32 devices in a mesh: win: 2 (over y), sta: 8 (over z, x), freq: 2 (over core).
Axes of the slice: x: 2, y: 2, z: 4, core: 2. Of those that a mesh axis runs over, the one named last changes fastest.
Arguments:
- traces: bfloat16 [256, 5120], P(('win', 'sta'), 'freq'), parts along dimension 0, may hold values from -6 to 6
- tables: float32 [16, 32768], replicated, may hold values from 0 to 20
- corrections: bfloat16 [128, 32768], P('sta'), may hold values from -1.5 to 1.5
- station_table: int32 [128], replicated, may hold values from 0 to 15
- node_ids: int32 [32768], replicated, may hold values from 0 to 32767, each once
- freq_bins: int32 [16], replicated, may hold values from 64 to 511
Outputs:
- spectrum: float32 [32, 32768], P('win', ('sta', 'freq')), parts along dimension 0
- beam_power: float32 [65536], P(('win', 'sta', 'freq')), parts along dimension 0
The draws below stay inside these ranges and needn't reach their ends.
There are 2 independent parts, one for each index of `win`. The reference program is written for one: setup_inputs(seed, part) draws one part's arguments, and reference() takes and returns one part's arrays. A program takes and returns all parts, laid end to end along the dimension named above; an argument that names none is the same for every part. Nothing has to cross between parts.
Inputs may be any that keep to these rules, and one draw needn't show every extreme that they name: `node_ids`: a permutation of 0 to 32767.
All inputs are finite; a program needn't handle non-finite values.
Results may differ from the reference program's by a relative error of at most 0.0003.
Values may be sent and summed in bfloat16 or wider, within the bound.
No kernel may reach another device: no remote copies, remote signals or barrier semaphores. Data moves between devices by JAX's collectives and lax.ppermute only.
A program may use at most 320 MiB of HBM per device.

```python
import math
import jax
import jax.numpy as jnp
from jax import lax

NT = 5120
NF = 16
GRID = 32768
NTAB = 16
STATIONS = 128


def set_ends(result, own_key, low, high):
    extent = result.shape
    spot = [jax.random.randint(jax.random.fold_in(own_key, axis), (), 0, extent[axis]) for axis in range(len(extent))]
    result = result.at[tuple(spot)].set(low)
    longest = extent.index(max(extent))
    spot[longest] = (spot[longest] + 1) % extent[longest]
    return result.at[tuple(spot)].set(high)


def level_of(rng, extent, shards, low, high):
    loudness = 1.0
    for axis_at, blocks in shards:
        draws = jax.random.uniform(jax.random.fold_in(jax.random.fold_in(rng, 6), axis_at), (blocks,), jnp.float32, low / len(shards), high / len(shards))
        loudness = loudness * jnp.repeat(jnp.exp(draws), extent[axis_at] // blocks).reshape((-1,) + (1,) * (len(extent) - 1 - axis_at))
    return loudness


def gaussian(rng, dims, spread, reach, cuts=(), held_as=jnp.bfloat16):
    entries = spread * jax.random.normal(rng, dims, jnp.float32)
    if cuts:
        entries = entries * level_of(rng, dims, cuts, -0.22, 0.18)
    return jnp.clip(entries, -reach, reach).astype(held_as)


def setup_inputs(seed: int = 0, part: int = 0) -> dict:
    streams_of = jax.random.split(jax.random.key(seed), 7)
    own_keys = jax.random.split(jax.random.fold_in(streams_of[6], part), 7)
    return {
        "traces": gaussian(own_keys[0], (STATIONS, NT), 1.0, 6.0, ((0, 8), (1, 2))),
        "tables": jnp.clip(jax.random.uniform(streams_of[1], (NTAB, GRID), jnp.float32, 0.0, 20.0), 0.0, 20.0),
        "corrections": gaussian(streams_of[2], (STATIONS, GRID), 0.3, 1.5, ((0, 8),)),
        "station_table": set_ends(jax.random.randint(streams_of[3], (STATIONS,), 0, NTAB), jax.random.fold_in(streams_of[3], 1), 0, NTAB - 1).astype(jnp.int32),
        "node_ids": jax.random.permutation(streams_of[4], GRID).astype(jnp.int32),
        "freq_bins": set_ends(jax.random.randint(streams_of[5], (NF,), NT // 80, NT // 10), jax.random.fold_in(streams_of[5], 1), NT // 80, (NT // 10) - 1).astype(jnp.int32),
    }


sample_rate = 20.0

def dft_table(sample_pos, freq_bins):
    turn_count = freq_bins[None, :] * sample_pos[:, None] % NT
    angles = 2.0 * math.pi / NT * turn_count.astype(jnp.float32)
    return jnp.concatenate([jnp.cos(angles), -jnp.sin(angles)], axis=1) / math.sqrt(NT)

def reference(traces, tables, corrections, station_table, node_ids, freq_bins):
    sample_pos = jnp.arange(NT, dtype=jnp.int32)
    spectra = jnp.dot(traces.astype(jnp.float32), dft_table(sample_pos, freq_bins), precision=lax.Precision.HIGHEST)
    spec_real = spectra[:, :NF]
    spec_imag = spectra[:, NF:]
    node_cols = jnp.take(tables, node_ids, axis=1)
    omegas = 2.0 * math.pi * sample_rate / NT * freq_bins.astype(jnp.float32)
    block_rows = math.gcd(STATIONS, 32)
    block_count = STATIONS // block_rows

    def add_block(sums_carry, pieces):
        real_part, imag_part = sums_carry
        table_idx, corr_block, real_block, imag_block = pieces
        travel_rows = jnp.take(node_cols, table_idx, axis=0) + corr_block.astype(jnp.float32)
        phases = omegas[:, None, None] * travel_rows[None]
        cosine = jnp.cos(phases)
        sine_val = jnp.sin(phases)
        weight_real = real_block.T[:, :, None]
        weight_imag = imag_block.T[:, :, None]
        real_part = real_part + lax.optimization_barrier(jnp.sum(weight_real * cosine - weight_imag * sine_val, axis=1))
        imag_part = imag_part + lax.optimization_barrier(jnp.sum(weight_real * sine_val + weight_imag * cosine, axis=1))
        return ((real_part, imag_part), None)
    zero_grid = jnp.zeros((NF, GRID), jnp.float32)
    pieces = (station_table.reshape(block_count, block_rows), corrections.reshape(block_count, block_rows, GRID), spec_real.reshape(block_count, block_rows, NF), spec_imag.reshape(block_count, block_rows, NF))
    (real_part, imag_part), leftover = lax.scan(add_block, (zero_grid, zero_grid), pieces)
    power_grid = real_part * real_part + imag_part * imag_part
    power_total = lax.optimization_barrier(jnp.sum(power_grid, axis=0))
    spectrum = NF * power_grid / power_total[None, :]
    beam_power = power_total / (NF * STATIONS)
    return (spectrum, beam_power)
```

```python
import functools
import math

import jax
import jax.numpy as jnp
import numpy as np
from jax import lax
from jax.experimental import pallas as pl
from jax.experimental.pallas import tpu as pltpu
from jax.sharding import PartitionSpec as P

NT = 5120
NF = 16
LANES = 128
VMEM_LIMIT = 48 * 1024 * 1024


def chebyshev_fit(func, degree, low, high):
    fit = np.polynomial.chebyshev.Chebyshev.interpolate(func, degree, domain=[low, high])
    return [float(v) for v in fit.convert(kind=np.polynomial.Polynomial).coef]


SIN_HALF = chebyshev_fit(lambda z: np.pi * np.sinc(np.sqrt(z)), 4, 0.0, 0.25)
COS_HALF = chebyshev_fit(lambda z: np.cos(np.pi * np.sqrt(z)), 4, 0.0, 0.25)


def horner(coefs, arg):
    total = coefs[-1]
    for coef in coefs[-2::-1]:
        total = total * arg + coef
    return total


def turn_parts(rest):
    square = rest * rest
    root = math.sqrt(2.0)
    sine_half = rest * horner([root * c for c in SIN_HALF], square)
    cos_half = horner([root * c for c in COS_HALF], square)
    return sine_half * sine_half, sine_half * cos_half


def dft_kernel(half_length, bins_ref, traces_ref, out_ref):
    start = lax.axis_index("freq") * half_length
    bins = bins_ref[...].astype(jnp.float32)
    pos = (start + lax.broadcasted_iota(jnp.int32, (NF, half_length), 1)).astype(jnp.float32)
    product = bins * pos
    turns = jnp.round(product * (1.0 / NT))
    rest = (product - turns * NT) * (1.0 / NT)
    versine, sine = turn_parts(rest)
    scale = 1.0 / math.sqrt(NT)
    table = jnp.concatenate([(1.0 - versine) * scale, sine * -scale], axis=0)
    high = table.astype(jnp.bfloat16)
    low = (table - high.astype(jnp.float32)).astype(jnp.bfloat16)
    both = jnp.concatenate([high, low], axis=0)
    sums = lax.dot_general(
        traces_ref[...], both, (((1,), (1,)), ((), ())), preferred_element_type=jnp.float32
    )
    out_ref[...] = sums[:, : 2 * NF] + sums[:, 2 * NF :]


def gather_kernel(ids_ref, tables_ref, out_ref):
    count = ids_ref.shape[1] // LANES
    rows = tables_ref.shape[0]
    blocks = tables_ref.shape[1] // LANES
    low = []
    high = []
    for tile in range(count):
        ids = jnp.broadcast_to(ids_ref[:, tile * LANES : (tile + 1) * LANES], (rows, LANES))
        low.append(ids & (LANES - 1))
        high.append(ids >> 7)

    def body(block, found):
        piece = tables_ref[:, pl.ds(pl.multiple_of(block * LANES, LANES), LANES)]
        result = []
        for tile in range(count):
            picked = jnp.take_along_axis(piece, low[tile], axis=1, mode="promise_in_bounds")
            result.append(jnp.where(high[tile] == block, picked, found[tile]))
        return tuple(result)

    zero = jnp.zeros((rows, LANES), jnp.float32)
    found = lax.fori_loop(0, blocks, body, (zero,) * count)
    for tile in range(count):
        out_ref[:, tile * LANES : (tile + 1) * LANES] = found[tile]


def image_kernel(table_of, bins_ref, spectra_ref, corr_ref, times_ref, out_ref, turns_ref, weight_ref):
    stations, nodes = corr_ref.shape
    windows = spectra_ref.shape[0]
    for win in range(windows):
        weight_ref[win] = spectra_ref[win, 0] + spectra_ref[win, 1]
    turns_ref[...] = corr_ref[...].astype(jnp.float32)

    def add_times(station, carry):
        row = pl.ds(station, 1)
        travel = turns_ref[row, :] + times_ref[pl.ds(table_of[station], 1), :]
        turns_ref[row, :] = travel * (1.0 / 256.0)
        return carry

    lax.fori_loop(0, stations, add_times, 0)

    powers = [[] for _ in range(windows)]
    for freq in range(NF):
        bin_at = bins_ref[freq].astype(jnp.float32)

        def body(group, sums):
            rows = pl.ds(pl.multiple_of(group * 8, 8), 8)
            turns = turns_ref[rows, :] * bin_at
            rest = turns - jnp.round(turns)
            versine, sine = turn_parts(rest)
            result = []
            for win in range(windows):
                real = weight_ref[win, rows, freq : freq + 1]
                imag = weight_ref[win, rows, NF + freq : NF + freq + 1]
                result.append(sums[2 * win] + (real - real * versine - imag * sine))
                result.append(sums[2 * win + 1] + (real * sine + imag - imag * versine))
            return tuple(result)

        zero = jnp.zeros((8, nodes), jnp.float32)
        sums = lax.fori_loop(0, stations // 8, body, (zero,) * (2 * windows))
        for win in range(windows):
            real = jnp.sum(sums[2 * win], axis=0, keepdims=True)
            imag = jnp.sum(sums[2 * win + 1], axis=0, keepdims=True)
            powers[win].append(real * real + imag * imag)
    for win in range(windows):
        power = jnp.concatenate(powers[win], axis=0)
        total = jnp.sum(power, axis=0, keepdims=True)
        out_ref[win, :NF, :] = power * (NF / total)
        out_ref[win, NF :, :] = jnp.broadcast_to(total * (1.0 / (NF * stations)), (8, nodes))


def on_device(traces, tables, corrections, station_table, node_ids, freq_bins):
    windows, groups, cores = (lax.axis_size(a) for a in ("win", "sta", "freq"))
    win, sta, core = (lax.axis_index(a) for a in ("win", "sta", "freq"))
    stations_dev, grid = corrections.shape
    stations = stations_dev * groups
    nodes = grid // (windows * groups * cores)
    params = pltpu.CompilerParams(vmem_limit_bytes=VMEM_LIMIT)
    vmem = pl.BlockSpec(memory_space=pltpu.VMEM)
    smem = pl.BlockSpec(memory_space=pltpu.SMEM)

    blocks = corrections.reshape(stations_dev, groups, cores * windows, nodes)
    mine = lax.dynamic_index_in_dim(blocks, core * windows + win, axis=2, keepdims=False)
    corr = lax.all_to_all(mine.transpose(1, 0, 2), "sta", split_axis=0, concat_axis=0, tiled=True)
    corr = corr.reshape(stations, nodes)

    partial = pl.pallas_call(
        functools.partial(dft_kernel, traces.shape[1]),
        out_shape=jax.ShapeDtypeStruct((stations_dev, 2 * NF), jnp.float32),
        in_specs=[vmem, vmem],
        out_specs=vmem,
        compiler_params=params,
        name="dft",
    )(freq_bins.reshape(NF, 1), traces)
    copies = jnp.broadcast_to(partial[None], (windows * groups * cores, stations_dev, 2 * NF))
    spectra = lax.all_to_all(copies, ("win", "sta", "freq"), split_axis=0, concat_axis=0, tiled=True)
    spectra = spectra.reshape(windows, groups, cores, stations_dev, 2 * NF)
    spectra = spectra.transpose(0, 2, 1, 3, 4).reshape(windows, cores, stations, 2 * NF)

    first = ((sta * cores + core) * windows + win) * nodes
    my_ids = lax.dynamic_slice_in_dim(node_ids, first, nodes).reshape(1, nodes)
    times = pl.pallas_call(
        gather_kernel,
        out_shape=jax.ShapeDtypeStruct((tables.shape[0], nodes), jnp.float32),
        in_specs=[vmem, vmem],
        out_specs=vmem,
        compiler_params=params,
        name="gather",
    )(my_ids, tables)

    result = pl.pallas_call(
        image_kernel,
        out_shape=jax.ShapeDtypeStruct((windows, NF + 8, nodes), jnp.float32),
        in_specs=[smem, smem, vmem, vmem, vmem],
        out_specs=vmem,
        scratch_shapes=[
            pltpu.VMEM((stations, nodes), jnp.float32),
            pltpu.VMEM((windows, stations, 2 * NF), jnp.float32),
        ],
        compiler_params=params,
        name="image",
    )(station_table, freq_bins, spectra, corr, times)
    halves = lax.all_to_all(result, "win", split_axis=0, concat_axis=0, tiled=True)
    spectrum = halves[:, :NF, :].transpose(1, 0, 2).reshape(NF, windows * nodes)
    beam_power = halves[:, NF, :].reshape(windows * nodes)
    return spectrum, beam_power


def solution(mesh):
    return jax.shard_map(
        on_device,
        mesh=mesh,
        in_specs=(P(("win", "sta"), "freq"), P(), P("sta", None), P(), P(), P()),
        out_specs=(P("win", ("sta", "freq")), P(("win", "sta", "freq"))),
        check_vma=False,
    )
```

```python
import functools
import math

import jax
import jax.numpy as jnp
import numpy as np
from jax import lax
from jax.experimental import pallas as pl
from jax.experimental.pallas import tpu as pltpu
from jax.sharding import PartitionSpec as P

NT = 5120
NF = 16
LANES = 128
VMEM_LIMIT = 48 * 1024 * 1024


def chebyshev_fit(func, degree, low, high):
    fit = np.polynomial.chebyshev.Chebyshev.interpolate(func, degree, domain=[low, high])
    return [float(v) for v in fit.convert(kind=np.polynomial.Polynomial).coef]


SIN_HALF = chebyshev_fit(lambda z: np.pi * np.sinc(np.sqrt(z)), 4, 0.0, 0.25)
COS_HALF = chebyshev_fit(lambda z: np.cos(np.pi * np.sqrt(z)), 4, 0.0, 0.25)


def horner(coefs, arg):
    total = coefs[-1]
    for coef in coefs[-2::-1]:
        total = total * arg + coef
    return total


def turn_parts(rest):
    square = rest * rest
    root = math.sqrt(2.0)
    sine_half = rest * horner([root * c for c in SIN_HALF], square)
    cos_half = horner([root * c for c in COS_HALF], square)
    return sine_half * sine_half, sine_half * cos_half


def bins_column(bins_ref):
    rows = lax.broadcasted_iota(jnp.int32, (NF, NF), 0)
    lanes = lax.broadcasted_iota(jnp.int32, (NF, NF), 1)
    square = jnp.broadcast_to(bins_ref[...].astype(jnp.float32), (NF, NF))
    return jnp.sum(jnp.where(rows == lanes, square, 0.0), axis=1, keepdims=True)


def split_bf16(value, terms):
    pieces = []
    for term in range(terms):
        piece = value.astype(jnp.bfloat16)
        pieces.append(piece)
        if term < terms - 1:
            value = value - piece.astype(jnp.float32)
    return pieces


def dft_kernel(half_length, bins_ref, traces_ref, out_ref):
    start = lax.axis_index("freq") * half_length
    bins = bins_column(bins_ref)
    pos = (start + lax.broadcasted_iota(jnp.int32, (NF, half_length), 1)).astype(jnp.float32)
    product = bins * pos
    turns = jnp.round(product * (1.0 / NT))
    rest = (product - turns * NT) * (1.0 / NT)
    versine, sine = turn_parts(rest)
    scale = 1.0 / math.sqrt(NT)
    table = jnp.concatenate([(1.0 - versine) * scale, sine * -scale], axis=0)
    both = jnp.concatenate(split_bf16(table, 2), axis=0)
    sums = lax.dot_general(
        traces_ref[...], both, (((1,), (1,)), ((), ())), preferred_element_type=jnp.float32
    )
    sums = sums[:, : 2 * NF] + sums[:, 2 * NF :]
    pieces = [sums[at : at + 8] for at in range(0, sums.shape[0], 8)]
    pieces.append(jnp.zeros((8, LANES - 2 * NF * len(pieces)), jnp.float32))
    tile = jnp.concatenate(pieces, axis=1)
    for copy in range(out_ref.shape[0]):
        out_ref[copy] = tile


def pick_kernel(nodes, corr_ref, *rest):
    outs, sem = rest[:-1], rest[-1]
    cores, windows = lax.axis_size("freq"), lax.axis_size("win")
    place = lax.axis_index("freq") * windows + lax.axis_index("win")
    groups = lax.axis_size("sta")
    copies = []
    for step, out in enumerate(outs):
        owner = lax.rem(lax.axis_index("sta") + step, groups)
        first = pl.multiple_of((owner * (cores * windows) + place) * nodes, LANES)
        copies.append(pltpu.make_async_copy(corr_ref.at[:, pl.ds(first, nodes)], out, sem.at[step]))
    for copy in copies:
        copy.start()
    for copy in copies:
        copy.wait()


def gather_kernel(ids_ref, tables_ref, out_ref, left_ref, right_ref):
    ntab, grid = tables_ref.shape
    nodes = out_ref.shape[1]
    count = nodes // LANES
    wide = right_ref.shape[0] // 3
    blocks = grid // wide
    windows, cores = lax.axis_size("win"), lax.axis_size("freq")
    place = (lax.axis_index("sta") * cores + lax.axis_index("freq")) * windows + lax.axis_index("win")
    ids = ids_ref[pl.ds(place * count, count), :]
    ids = jnp.concatenate([ids[at : at + 1] for at in range(count)], axis=1)
    low, high = ids & (wide - 1), ids >> (wide.bit_length() - 1)
    spots = lax.broadcasted_iota(jnp.int32, (wide, nodes), 0)
    ones = jnp.where(spots == low, 1.0, 0.0).astype(jnp.bfloat16)
    for term in range(3):
        right_ref[term * wide : (term + 1) * wide, :] = ones
    for block in range(blocks):
        pieces = split_bf16(tables_ref[:, block * wide : (block + 1) * wide], 3)
        left_ref[block * ntab : (block + 1) * ntab, :] = jnp.concatenate(pieces, axis=1)
    found = jnp.zeros((ntab, nodes), jnp.float32)
    step = 16
    for first in range(0, blocks, step):
        rows = left_ref[first * ntab : (first + step) * ntab, :]
        picked = jnp.dot(rows, right_ref[...], preferred_element_type=jnp.float32)
        for block in range(step):
            part = picked[block * ntab : (block + 1) * ntab]
            found = jnp.where(high == first + block, part, found)
    out_ref[...] = found


def image_kernel(stations_dev, table_of, bins_ref, spectra_ref, times_ref, *rest):
    keep_ref, send_ref, turns_ref, weight_ref = rest[-4:]
    corr_refs = rest[:-4]
    stations, nodes = turns_ref.shape
    windows, groups, cores = (lax.axis_size(a) for a in ("win", "sta", "freq"))
    for win in range(windows):
        for group in range(groups):
            at = (win * groups + group) * cores
            tile = spectra_ref[at]
            for core in range(1, cores):
                tile = tile + spectra_ref[at + core]
            for piece in range(stations_dev // 8):
                first = group * stations_dev + piece * 8
                weight_ref[win, first : first + 8, :] = tile[:, piece * 2 * NF : (piece + 1) * 2 * NF]
    for step, corr_ref in enumerate(corr_refs):
        owner = lax.rem(lax.axis_index("sta") + (groups - step), groups)
        rows = corr_ref.shape[0]
        first = pl.multiple_of(owner * stations_dev, 16) if len(corr_refs) > 1 else 0
        turns_ref[pl.ds(first, rows), :] = corr_ref[...].astype(jnp.float32)

    def add_times(station, carry):
        row = pl.ds(station, 1)
        travel = turns_ref[row, :] + times_ref[pl.ds(table_of[station], 1), :]
        turns_ref[row, :] = travel * (1.0 / 256.0)
        return carry

    lax.fori_loop(0, stations, add_times, 0)

    powers = [[] for _ in range(windows)]
    for freq in range(NF):
        bin_at = bins_ref[freq].astype(jnp.float32)

        def body(group, sums):
            rows = pl.ds(pl.multiple_of(group * 8, 8), 8)
            turns = turns_ref[rows, :] * bin_at
            rest = turns - jnp.round(turns)
            versine, sine = turn_parts(rest)
            result = []
            for win in range(windows):
                real = weight_ref[win, rows, freq : freq + 1]
                imag = weight_ref[win, rows, NF + freq : NF + freq + 1]
                result.append(sums[2 * win] + (real * versine + imag * sine))
                result.append(sums[2 * win + 1] + (real * sine - imag * versine))
            return tuple(result)

        zero = jnp.zeros((8, nodes), jnp.float32)
        sums = lax.fori_loop(0, stations // 8, body, (zero,) * (2 * windows))
        for win in range(windows):
            constant = jnp.sum(weight_ref[win, :, freq : freq + 1], axis=0, keepdims=True)
            constant_imag = jnp.sum(weight_ref[win, :, NF + freq : NF + freq + 1], axis=0, keepdims=True)
            real = constant - jnp.sum(sums[2 * win], axis=0, keepdims=True)
            imag = constant_imag + jnp.sum(sums[2 * win + 1], axis=0, keepdims=True)
            powers[win].append(real * real + imag * imag)
    powers = [jnp.concatenate(rows, axis=0) for rows in powers]
    mine = lax.axis_index("win") == 0
    keep_ref[...] = jnp.where(mine, powers[0], powers[1])
    send_ref[...] = jnp.where(mine, powers[1], powers[0])


def finish_kernel(stations, keep_ref, got_ref, spectrum_ref, beam_ref):
    nodes = keep_ref.shape[1]
    win = lax.axis_index("win")
    for place, ref in ((win, keep_ref), (1 - win, got_ref)):
        power = ref[...]
        total = jnp.sum(power, axis=0, keepdims=True)
        at = pl.ds(pl.multiple_of(place * nodes, LANES), nodes)
        spectrum_ref[:, at] = power * (NF / total)
        beam_ref[:, at] = total * (1.0 / (NF * stations))


def on_device(traces, tables, corrections, station_table, node_ids, freq_bins):
    windows, groups, cores = (lax.axis_size(a) for a in ("win", "sta", "freq"))
    stations_dev, grid = corrections.shape
    stations = stations_dev * groups
    devices = windows * groups * cores
    nodes = grid // devices
    ntab = tables.shape[0]
    params = pltpu.CompilerParams(vmem_limit_bytes=VMEM_LIMIT)
    vmem = pl.BlockSpec(memory_space=pltpu.VMEM)
    smem = pl.BlockSpec(memory_space=pltpu.SMEM)
    anywhere = pl.BlockSpec(memory_space=pl.ANY)

    block = jax.ShapeDtypeStruct((stations_dev, nodes), jnp.bfloat16)
    blocks = pl.pallas_call(
        functools.partial(pick_kernel, nodes),
        out_shape=[block] * groups,
        in_specs=[anywhere],
        out_specs=[anywhere] * groups,
        scratch_shapes=[pltpu.SemaphoreType.DMA((groups,))],
        compiler_params=params,
        name="pick",
    )(corrections)
    if groups <= 8:
        corr = [blocks[0]]
        for step in range(1, groups):
            pairs = [(at, (at + step) % groups) for at in range(groups)]
            corr.append(lax.ppermute(blocks[step], "sta", pairs))
    else:
        ordered = jnp.roll(jnp.stack(blocks), lax.axis_index("sta"), axis=0)
        corr = lax.all_to_all(ordered, "sta", split_axis=0, concat_axis=0, tiled=True)
        corr = [corr.reshape(stations, nodes)]

    copies = pl.pallas_call(
        functools.partial(dft_kernel, traces.shape[1]),
        out_shape=jax.ShapeDtypeStruct((devices, 8, LANES), jnp.float32),
        in_specs=[vmem, vmem],
        out_specs=vmem,
        compiler_params=params,
        name="dft",
    )(freq_bins.reshape(1, NF), traces)
    spectra = lax.all_to_all(copies, ("win", "sta", "freq"), split_axis=0, concat_axis=0, tiled=True)

    wide = 512
    times = pl.pallas_call(
        gather_kernel,
        out_shape=jax.ShapeDtypeStruct((ntab, nodes), jnp.float32),
        in_specs=[vmem, vmem],
        out_specs=vmem,
        scratch_shapes=[
            pltpu.VMEM((grid // wide * ntab, 3 * wide), jnp.bfloat16),
            pltpu.VMEM((3 * wide, nodes), jnp.bfloat16),
        ],
        compiler_params=params,
        name="gather",
    )(node_ids.reshape(grid // LANES, LANES), tables)

    half = jax.ShapeDtypeStruct((NF, nodes), jnp.float32)
    keep, send = pl.pallas_call(
        functools.partial(image_kernel, stations_dev),
        out_shape=[half, half],
        in_specs=[smem, smem, vmem, vmem] + [vmem] * len(corr),
        out_specs=[vmem, vmem],
        scratch_shapes=[
            pltpu.VMEM((stations, nodes), jnp.float32),
            pltpu.VMEM((windows, stations, 2 * NF), jnp.float32),
        ],
        compiler_params=params,
        name="image",
    )(station_table, freq_bins, spectra, times, *corr)
    got = lax.ppermute(send, "win", [(0, 1), (1, 0)])
    spectrum, beam_power = pl.pallas_call(
        functools.partial(finish_kernel, stations),
        out_shape=[
            jax.ShapeDtypeStruct((NF, windows * nodes), jnp.float32),
            jax.ShapeDtypeStruct((1, windows * nodes), jnp.float32),
        ],
        in_specs=[vmem, vmem],
        out_specs=[vmem, vmem],
        compiler_params=params,
        name="finish",
    )(keep, got)
    return spectrum, beam_power.reshape(windows * nodes)


def solution(mesh):
    return jax.shard_map(
        on_device,
        mesh=mesh,
        in_specs=(P(("win", "sta"), "freq"), P(), P("sta", None), P(), P(), P()),
        out_specs=(P("win", ("sta", "freq")), P(("win", "sta", "freq"))),
        check_vma=False,
    )
```

```python
import functools
import math

import jax
import jax.numpy as jnp
import numpy as np
from jax import lax
from jax.experimental import pallas as pl
from jax.experimental.pallas import tpu as pltpu
from jax.sharding import PartitionSpec as P

NT = 5120
NF = 16
LANES = 128
DEGREES = 32
REACH = 1.5
TERMS = 3
VMEM_LIMIT = 48 * 1024 * 1024


def chebyshev_fit(func, degree, low, high):
    fit = np.polynomial.chebyshev.Chebyshev.interpolate(func, degree, domain=[low, high])
    return [float(v) for v in fit.convert(kind=np.polynomial.Polynomial).coef]


SIN_HALF = chebyshev_fit(lambda z: np.pi * np.sinc(np.sqrt(z)), 4, 0.0, 0.25)
COS_HALF = chebyshev_fit(lambda z: np.cos(np.pi * np.sqrt(z)), 4, 0.0, 0.25)


def horner(coefs, arg):
    total = coefs[-1]
    for coef in coefs[-2::-1]:
        total = total * arg + coef
    return total


def turn_parts(rest):
    square = rest * rest
    root = math.sqrt(2.0)
    sine_half = rest * horner([root * c for c in SIN_HALF], square)
    cos_half = horner([root * c for c in COS_HALF], square)
    return sine_half * sine_half, sine_half * cos_half


def cos_sin(turns):
    versine, sine = turn_parts(turns - jnp.round(turns))
    return 1.0 - versine, sine


def bins_column(bins_ref):
    rows = lax.broadcasted_iota(jnp.int32, (NF, NF), 0)
    lanes = lax.broadcasted_iota(jnp.int32, (NF, NF), 1)
    square = jnp.broadcast_to(bins_ref[...].astype(jnp.float32), (NF, NF))
    return jnp.sum(jnp.where(rows == lanes, square, 0.0), axis=1, keepdims=True)


def split_bf16(value, terms):
    pieces = []
    for term in range(terms):
        piece = value.astype(jnp.bfloat16)
        pieces.append(piece)
        if term < terms - 1:
            value = value - piece.astype(jnp.float32)
    return pieces


def send_kernel(nodes, bins_ref, traces_ref, corr_ref, out_ref, *rest):
    sems = rest[-1]
    devices, rows, width = out_ref.shape
    share = width - LANES
    half_length = traces_ref.shape[1]
    copies = []
    if share:
        windows, groups, cores = (lax.axis_size(a) for a in ("win", "sta", "freq"))
        place = lax.axis_index("win") * cores + lax.axis_index("freq")
        for dev in range(devices):
            win, sta, core = dev // (groups * cores), dev // cores % groups, dev % cores
            first = ((sta * cores + core) * windows + win) * nodes
            first = pl.multiple_of(first + place * share, LANES)
            copies.append(
                pltpu.make_async_copy(
                    corr_ref.at[:, pl.ds(first, share)], out_ref.at[dev, :, pl.ds(0, share)], sems.at[dev]
                )
            )
    for copy in copies:
        copy.start()
    start = lax.axis_index("freq") * half_length
    bins = bins_column(bins_ref)
    pos = (start + lax.broadcasted_iota(jnp.int32, (NF, half_length), 1)).astype(jnp.float32)
    product = bins * pos
    turns = jnp.round(product * (1.0 / NT))
    rest = (product - turns * NT) * (1.0 / NT)
    versine, sine = turn_parts(rest)
    scale = 1.0 / math.sqrt(NT)
    table = jnp.concatenate([(1.0 - versine) * scale, sine * -scale], axis=0)
    both = jnp.concatenate(split_bf16(table, 2), axis=0)
    sums = lax.dot_general(
        traces_ref[...], both, (((1,), (1,)), ((), ())), preferred_element_type=jnp.float32
    )
    sums = sums[:, : 2 * NF] + sums[:, 2 * NF :]
    pieces = split_bf16(sums, TERMS) + [jnp.zeros((rows, LANES - 2 * NF * TERMS), jnp.bfloat16)]
    tile = jnp.concatenate([piece.astype(jnp.float32) for piece in pieces], axis=1).astype(jnp.bfloat16)
    for dev in range(devices):
        out_ref[dev, :, share:] = tile
    for copy in copies:
        copy.wait()


def pick_columns(ids_ref, tables_ref, nodes, left_ref, right_ref):
    ntab, grid = tables_ref.shape
    count = nodes // LANES
    wide = right_ref.shape[0] // 3
    blocks = grid // wide
    windows, cores = lax.axis_size("win"), lax.axis_size("freq")
    place = (lax.axis_index("sta") * cores + lax.axis_index("freq")) * windows + lax.axis_index("win")
    ids = ids_ref[pl.ds(place * count, count), :]
    ids = jnp.concatenate([ids[at : at + 1] for at in range(count)], axis=1)
    low, high = ids & (wide - 1), ids >> (wide.bit_length() - 1)
    spots = lax.broadcasted_iota(jnp.int32, (wide, nodes), 0)
    ones = jnp.where(spots == low, 1.0, 0.0).astype(jnp.bfloat16)
    for term in range(3):
        right_ref[term * wide : (term + 1) * wide, :] = ones
    for block in range(blocks):
        pieces = split_bf16(tables_ref[:, block * wide : (block + 1) * wide], 3)
        left_ref[block * ntab : (block + 1) * ntab, :] = jnp.concatenate(pieces, axis=1)
    found = jnp.zeros((ntab, nodes), jnp.float32)
    step = 16
    for first in range(0, blocks, step):
        rows = left_ref[first * ntab : (first + step) * ntab, :]
        picked = jnp.dot(rows, right_ref[...], preferred_element_type=jnp.float32)
        for block in range(step):
            part = picked[block * ntab : (block + 1) * ntab]
            found = jnp.where(high == first + block, part, found)
    return found


def chebyshev_coefs(bins_ref):
    shape = (DEGREES, DEGREES)
    degree = lax.broadcasted_iota(jnp.int32, shape, 0)
    node = lax.broadcasted_iota(jnp.int32, shape, 1)
    period = 4 * DEGREES
    weight, _ = cos_sin((degree * (2 * node + 1) & (period - 1)).astype(jnp.float32) * (1.0 / period))
    weight = weight * jnp.where(degree == 0, 1.0 / DEGREES, 2.0 / DEGREES)
    even = jnp.where(degree % 2 == 0, weight, 0.0)
    odd = jnp.where(degree % 2 == 1, weight, 0.0)
    row = bins_ref[...].astype(jnp.float32)
    bins = jnp.concatenate([row] * (LANES // NF), axis=1)
    at = lax.broadcasted_iota(jnp.int32, (DEGREES, LANES), 0).astype(jnp.float32)
    spot, _ = cos_sin((2.0 * at + 1.0) * (1.0 / period))
    cosine, sine = cos_sin(bins * (spot * (REACH / 256.0)))
    dot = functools.partial(jnp.dot, precision=lax.Precision.HIGHEST, preferred_element_type=jnp.float32)
    return dot(even, cosine) + dot(odd, sine)


def station_order(table_row):
    count = table_row.shape[1]
    shape = (count, count)
    here = lax.broadcasted_iota(jnp.int32, shape, 0)
    there = lax.broadcasted_iota(jnp.int32, shape, 1)
    key_row = table_row * count + there[:1]
    spread = jnp.broadcast_to(key_row, shape)
    key_column = jnp.sum(jnp.where(here == there, spread, 0), axis=1, keepdims=True)
    rank = jnp.sum(jnp.where(key_column < key_row, 1, 0), axis=0, keepdims=True)
    table_column = key_column // count
    bound = lax.broadcasted_iota(jnp.int32, (count, LANES), 1)
    starts = jnp.sum(jnp.where(table_column < bound, 1, 0), axis=0, keepdims=True)
    first = lax.broadcasted_iota(jnp.int32, (count, LANES), 1) * 8
    place_column = jnp.sum(jnp.where(here == there, jnp.broadcast_to(rank, shape), 0), axis=1, keepdims=True)
    low = jnp.sum(jnp.where(place_column == first, table_column, 0), axis=0, keepdims=True)
    high = jnp.sum(jnp.where(place_column == first + 7, table_column, 0), axis=0, keepdims=True)
    plan = jnp.concatenate([starts, low, high, jnp.zeros((5, LANES), jnp.int32)], axis=0)
    return rank, plan


def prepare_kernel(
    bins_ref, table_ref, ids_ref, tables_ref, cos_ref, sin_ref, coef_ref, sorter_ref, plan_ref, left_ref, right_ref
):
    nodes = cos_ref.shape[2]
    coef_ref[...] = chebyshev_coefs(bins_ref)
    rank, plan = station_order(table_ref[...])
    plan_ref[...] = plan
    count = table_ref.shape[1]
    place = lax.broadcasted_iota(jnp.int32, (count, count), 0)
    sorter_ref[...] = jnp.where(place == rank, 1.0, 0.0).astype(jnp.bfloat16)
    turns = pick_columns(ids_ref, tables_ref, nodes, left_ref, right_ref) * (1.0 / 256.0)
    bins = bins_column(bins_ref)
    for table in range(tables_ref.shape[0]):
        cosine, sine = cos_sin(bins * turns[table : table + 1])
        cos_ref[table] = cosine
        sin_ref[table] = sine


def image_kernel(merged, stations_dev, plan_ref, sorter_ref, coef_ref, cos_ref, sin_ref, *rest):
    keep_ref, send_ref, place_ref, weight_ref, sums_ref, basis_a, left_a, basis_b, left_b = rest[-9:]
    stations, nodes = place_ref.shape
    windows, groups, cores = (lax.axis_size(a) for a in ("win", "sta", "freq"))
    ntab = cos_ref.shape[0]
    sorter = sorter_ref[...]
    block_ref = rest[0]
    width = block_ref.shape[2]
    rows_of = lambda win, core: [(win * groups + group) * cores + core for group in range(groups)]

    scale = 1.0 / REACH
    if merged:
        share = width - LANES
        for win in range(windows):
            for core in range(cores):
                part = jnp.concatenate([block_ref[at, :, :share] for at in rows_of(win, core)], axis=0)
                found = jnp.dot(sorter, part, preferred_element_type=jnp.float32)
                first = (win * cores + core) * share
                place_ref[:, first : first + share] = found * scale
    else:
        found = jnp.dot(sorter, rest[1][...], preferred_element_type=jnp.float32)
        place_ref[...] = found * scale

    even, odd = [], []
    for win in range(windows):
        total = None
        for core in range(cores):
            part = jnp.concatenate([block_ref[at, :, width - LANES :] for at in rows_of(win, core)], axis=0)
            part = part.astype(jnp.float32)
            total = part if total is None else total + part
        value = sum(total[:, 2 * NF * term : 2 * NF * (term + 1)] for term in range(TERMS))
        even.append(value)
        odd.append(jnp.concatenate([-value[:, NF:], value[:, :NF]], axis=1))
    both = jnp.concatenate(even + even + odd + odd, axis=1)
    found = None
    for piece in split_bf16(both, 3):
        part = jnp.dot(sorter, piece, preferred_element_type=jnp.float32)
        found = part if found is None else found + part
    weight_ref[...] = found
    sums_ref[...] = jnp.zeros_like(sums_ref)
    chunk = min(256, nodes)
    lanes = 2 * windows * 2 * NF
    slot = lax.broadcasted_iota(jnp.int32, (8, lanes), 1) // (lanes // 2)
    spot = lax.broadcasted_iota(jnp.int32, (8, lanes), 0)

    def make_left(group, table, left_ref):
        here = spot + group * 8
        low = jnp.where(slot == 0, plan_ref[0, table], plan_ref[0, table + 1])
        high = jnp.where(slot == 0, plan_ref[0, table + 1], plan_ref[0, table + 2])
        mask = (here >= low) & (here < high)
        rows = pl.ds(pl.multiple_of(group * 8, 8), 8)
        sides = [
            jnp.where(mask, weight_ref[rows, :lanes], 0.0),
            jnp.where(mask, weight_ref[rows, lanes:], 0.0),
        ]
        for half in range(DEGREES * 8 // LANES):
            per = LANES // 8
            tall = jnp.concatenate(
                [sides[k % 2] * coef_ref[k : k + 1, :lanes] for k in range(half * per, (half + 1) * per)], axis=0
            )
            high, low = split_bf16(tall.T, 2)
            at = half * LANES
            left_ref[:, at : at + LANES] = high
            left_ref[:, DEGREES * 8 + at : DEGREES * 8 + at + LANES] = low

    def make_basis(group, basis_ref):
        arg = place_ref[pl.ds(pl.multiple_of(group * 8, 8), 8), :]
        twice = arg + arg
        before, now = jnp.ones_like(arg), arg
        for degree in range(0, DEGREES, 2):
            pair = jnp.concatenate([before, now], axis=0)
            high, low = split_bf16(pair, 2)
            basis_ref[degree * 8 : degree * 8 + 16, :] = high
            basis_ref[(DEGREES + degree) * 8 : (DEGREES + degree) * 8 + 16, :] = low
            before = twice * now - before
            now = twice * before - now

    def add_tables(table, basis_ref, left_ref):
        depth = DEGREES * 8
        other = jnp.minimum(table + 1, ntab - 1)
        half = lanes // 2
        for first in range(0, nodes, chunk):
            at = slice(first, first + chunk)
            high = left_ref[:, :depth]
            got = jnp.dot(high, basis_ref[:depth, at], preferred_element_type=jnp.float32)
            got = got + jnp.dot(high, basis_ref[depth:, at], preferred_element_type=jnp.float32)
            got = got + jnp.dot(left_ref[:, depth:], basis_ref[:depth, at], preferred_element_type=jnp.float32)
            cos_a, sin_a = cos_ref[table, :, at], sin_ref[table, :, at]
            cos_b, sin_b = cos_ref[other, :, at], sin_ref[other, :, at]
            for win in range(windows):
                row = win * 2 * NF
                real_a, imag_a = got[row : row + NF], got[row + NF : row + 2 * NF]
                real_b, imag_b = got[half + row : half + row + NF], got[half + row + NF : half + row + 2 * NF]
                sums_ref[row : row + NF, at] += (real_a * cos_a - imag_a * sin_a) + (real_b * cos_b - imag_b * sin_b)
                sums_ref[row + NF : row + 2 * NF, at] += (real_a * sin_a + imag_a * cos_a) + (
                    real_b * sin_b + imag_b * cos_b
                )

    def more_tables(group, basis_ref, left_ref):
        first, last = plan_ref[1, group], plan_ref[2, group]

        def step(turn, carry):
            table = first + 2 * turn
            make_left(group, table, left_ref)
            add_tables(table, basis_ref, left_ref)
            return carry

        lax.fori_loop(1, (last - first) // 2 + 1, step, 0)

    total_groups = stations // 8
    make_left(0, plan_ref[1, 0], left_a)
    make_basis(0, basis_a)

    def body(pair, carry):
        group = pair * 2
        make_left(group + 1, plan_ref[1, group + 1], left_b)
        make_basis(group + 1, basis_b)
        add_tables(plan_ref[1, group], basis_a, left_a)
        more_tables(group, basis_a, left_a)
        after = jnp.minimum(group + 2, total_groups - 1)
        make_left(after, plan_ref[1, after], left_a)
        make_basis(after, basis_a)
        add_tables(plan_ref[1, group + 1], basis_b, left_b)
        more_tables(group + 1, basis_b, left_b)
        return carry

    lax.fori_loop(0, total_groups // 2, body, 0)
    powers = []
    for win in range(windows):
        row = win * 2 * NF
        real, imag = sums_ref[row : row + NF, :], sums_ref[row + NF : row + 2 * NF, :]
        powers.append(real * real + imag * imag)
    mine = lax.axis_index("win") == 0
    keep_ref[...] = jnp.where(mine, powers[0], powers[1])
    send_ref[...] = jnp.where(mine, powers[1], powers[0])


def finish_kernel(stations, keep_ref, got_ref, spectrum_ref, beam_ref):
    nodes = keep_ref.shape[1]
    win = lax.axis_index("win")
    for place, ref in ((win, keep_ref), (1 - win, got_ref)):
        power = ref[...]
        total = jnp.sum(power, axis=0, keepdims=True)
        at = pl.ds(pl.multiple_of(place * nodes, LANES), nodes)
        spectrum_ref[:, at] = power * (NF / total)
        beam_ref[:, at] = total * (1.0 / (NF * stations))


def on_device(traces, tables, corrections, station_table, node_ids, freq_bins):
    windows, groups, cores = (lax.axis_size(a) for a in ("win", "sta", "freq"))
    stations_dev, grid = corrections.shape
    stations = stations_dev * groups
    devices = windows * groups * cores
    nodes = grid // devices
    ntab = tables.shape[0]
    params = pltpu.CompilerParams(vmem_limit_bytes=VMEM_LIMIT)
    vmem = pl.BlockSpec(memory_space=pltpu.VMEM)
    smem = pl.BlockSpec(memory_space=pltpu.SMEM)
    anywhere = pl.BlockSpec(memory_space=pl.ANY)
    bins = freq_bins.reshape(1, NF)

    holders = windows * cores
    merged = nodes % (holders * LANES) == 0
    width = LANES + (nodes // holders if merged else 0)
    blocks = pl.pallas_call(
        functools.partial(send_kernel, nodes),
        out_shape=jax.ShapeDtypeStruct((devices, stations_dev, width), jnp.bfloat16),
        in_specs=[vmem, vmem, anywhere],
        out_specs=vmem,
        scratch_shapes=[pltpu.SemaphoreType.DMA((devices,))],
        compiler_params=params,
        name="send",
    )(bins, traces, corrections)
    received = [lax.all_to_all(blocks, ("win", "sta", "freq"), split_axis=0, concat_axis=0, tiled=True)]
    if not merged:
        parts = corrections.reshape(stations_dev, groups, holders, nodes)
        place = lax.axis_index("freq") * windows + lax.axis_index("win")
        mine = lax.dynamic_index_in_dim(parts, place, axis=2, keepdims=False)
        corr = lax.all_to_all(mine.transpose(1, 0, 2), "sta", split_axis=0, concat_axis=0, tiled=True)
        received.append(corr.reshape(stations, nodes))

    wide = 512
    phasors = jax.ShapeDtypeStruct((ntab, NF, nodes), jnp.float32)
    cosine, sine, coefs, sorter, plan = pl.pallas_call(
        prepare_kernel,
        out_shape=[
            phasors,
            phasors,
            jax.ShapeDtypeStruct((DEGREES, LANES), jnp.float32),
            jax.ShapeDtypeStruct((stations, stations), jnp.bfloat16),
            jax.ShapeDtypeStruct((8, LANES), jnp.int32),
        ],
        in_specs=[vmem] * 4,
        out_specs=[vmem] * 5,
        scratch_shapes=[
            pltpu.VMEM((grid // wide * ntab, 3 * wide), jnp.bfloat16),
            pltpu.VMEM((3 * wide, nodes), jnp.bfloat16),
        ],
        compiler_params=params,
        name="prepare",
    )(bins, station_table.reshape(1, stations), node_ids.reshape(grid // LANES, LANES), tables)

    half = jax.ShapeDtypeStruct((NF, nodes), jnp.float32)
    rows = 2 * windows * 2 * NF
    basis = pltpu.VMEM((2 * DEGREES * 8, nodes), jnp.bfloat16)
    left = pltpu.VMEM((rows, 2 * DEGREES * 8), jnp.bfloat16)
    keep, send = pl.pallas_call(
        functools.partial(image_kernel, merged, stations_dev),
        out_shape=[half, half],
        in_specs=[smem] + [vmem] * (4 + len(received)),
        out_specs=[vmem, vmem],
        scratch_shapes=[
            pltpu.VMEM((stations, nodes), jnp.float32),
            pltpu.VMEM((stations, 2 * rows), jnp.float32),
            pltpu.VMEM((rows // 2, nodes), jnp.float32),
            basis,
            left,
            basis,
            left,
        ],
        compiler_params=params,
        name="image",
    )(plan, sorter, coefs, cosine, sine, *received)
    got = lax.ppermute(send, "win", [(0, 1), (1, 0)])
    spectrum, beam_power = pl.pallas_call(
        functools.partial(finish_kernel, stations),
        out_shape=[
            jax.ShapeDtypeStruct((NF, windows * nodes), jnp.float32),
            jax.ShapeDtypeStruct((1, windows * nodes), jnp.float32),
        ],
        in_specs=[vmem, vmem],
        out_specs=[vmem, vmem],
        compiler_params=params,
        name="finish",
    )(keep, got)
    return spectrum, beam_power.reshape(windows * nodes)


def solution(mesh):
    return jax.shard_map(
        on_device,
        mesh=mesh,
        in_specs=(P(("win", "sta"), "freq"), P(), P("sta", None), P(), P(), P()),
        out_specs=(P("win", ("sta", "freq")), P(("win", "sta", "freq"))),
        check_vma=False,
    )
```

```python
import functools
import math

import jax
import jax.numpy as jnp
import numpy as np
from jax import lax
from jax.experimental import pallas as pl
from jax.experimental.pallas import tpu as pltpu
from jax.sharding import PartitionSpec as P

NT = 5120
NF = 16
LANES = 128
DEGREES = 32
REACH = 1.5
TABLE_PIECES = 8
VMEM_LIMIT = 64 * 1024 * 1024 - 64 * 1024


def chebyshev_fit(func, degree, low, high):
    fit = np.polynomial.chebyshev.Chebyshev.interpolate(func, degree, domain=[low, high])
    return [float(v) for v in fit.convert(kind=np.polynomial.Polynomial).coef]


SIN_HALF = chebyshev_fit(lambda z: np.pi * np.sinc(np.sqrt(z)), 4, 0.0, 0.25)
COS_HALF = chebyshev_fit(lambda z: np.cos(np.pi * np.sqrt(z)), 4, 0.0, 0.25)


def horner(coefs, arg):
    total = coefs[-1]
    for coef in coefs[-2::-1]:
        total = total * arg + coef
    return total


def turn_parts(rest):
    square = rest * rest
    root = math.sqrt(2.0)
    sine_half = rest * horner([root * c for c in SIN_HALF], square)
    cos_half = horner([root * c for c in COS_HALF], square)
    return sine_half * sine_half, sine_half * cos_half


def cos_sin(turns):
    versine, sine = turn_parts(turns - jnp.round(turns))
    return 1.0 - versine, sine


def bins_column(bins_ref):
    rows = lax.broadcasted_iota(jnp.int32, (NF, NF), 0)
    lanes = lax.broadcasted_iota(jnp.int32, (NF, NF), 1)
    square = jnp.broadcast_to(bins_ref[...].astype(jnp.float32), (NF, NF))
    return jnp.sum(jnp.where(rows == lanes, square, 0.0), axis=1, keepdims=True)


def split_bf16(value, terms):
    pieces = []
    for term in range(terms):
        piece = value.astype(jnp.bfloat16)
        pieces.append(piece)
        if term < terms - 1:
            value = value - piece.astype(jnp.float32)
    return pieces


def start_all(copies):
    for copy in copies:
        copy.start()
    return copies


def send_kernel(nodes, bins_hbm, traces_hbm, corr_hbm, corr_out, spectra_out, bins_ref, traces_ref, sems):
    groups, _, _ = corr_out.shape
    windows, cores = lax.axis_size("win"), lax.axis_size("freq")
    place = lax.axis_index("freq") * windows + lax.axis_index("win")
    half_length = traces_ref.shape[1]
    small = start_all(
        [
            pltpu.make_async_copy(bins_hbm, bins_ref, sems.at[groups]),
            pltpu.make_async_copy(traces_hbm, traces_ref, sems.at[groups + 1]),
        ]
    )
    copies = []
    for group in range(groups):
        first = pl.multiple_of((group * cores * windows + place) * nodes, LANES)
        copies.append(
            pltpu.make_async_copy(corr_hbm.at[:, pl.ds(first, nodes)], corr_out.at[group], sems.at[group])
        )
    start_all(copies)
    start = lax.axis_index("freq") * half_length
    small[0].wait()
    bins = bins_column(bins_ref)
    pos = (start + lax.broadcasted_iota(jnp.int32, (NF, half_length), 1)).astype(jnp.float32)
    product = bins * pos
    turns = jnp.round(product * (1.0 / NT))
    rest = (product - turns * NT) * (1.0 / NT)
    versine, sine = turn_parts(rest)
    scale = 1.0 / math.sqrt(NT)
    table = jnp.concatenate([(1.0 - versine) * scale, sine * -scale], axis=0)
    both = jnp.concatenate(split_bf16(table, 2), axis=0)
    small[1].wait()
    sums = lax.dot_general(
        traces_ref[...], both, (((1,), (1,)), ((), ())), preferred_element_type=jnp.float32
    )
    sums = sums[:, : 2 * NF] + sums[:, 2 * NF :]
    rows = spectra_out.shape[1]
    tile = jnp.concatenate([sums[at : at + rows] for at in range(0, sums.shape[0], rows)], axis=1)
    for dev in range(spectra_out.shape[0]):
        spectra_out[dev] = tile
    for copy in copies:
        copy.wait()


def own_place():
    windows, cores = lax.axis_size("win"), lax.axis_size("freq")
    return (lax.axis_index("sta") * cores + lax.axis_index("freq")) * windows + lax.axis_index("win")


def pick_columns(ids_ref, tables_ref, table_copies, nodes, left_ref, right_ref):
    ntab, grid = tables_ref.shape
    count = nodes // LANES
    wide = right_ref.shape[0] // 3
    blocks = grid // wide
    ids = ids_ref[pl.ds(own_place() * count % ids_ref.shape[0], count), :]
    ids = jnp.concatenate([ids[at : at + 1] for at in range(count)], axis=1)
    low, high = ids & (wide - 1), ids >> (wide.bit_length() - 1)
    spots = lax.broadcasted_iota(jnp.int32, (wide, nodes), 0)
    ones = jnp.where(spots == low, 1.0, 0.0).astype(jnp.bfloat16)
    for term in range(3):
        right_ref[term * wide : (term + 1) * wide, :] = ones
    for block in range(blocks):
        if block % (blocks // len(table_copies)) == 0:
            table_copies[block // (blocks // len(table_copies))].wait()
        pieces = split_bf16(tables_ref[:, block * wide : (block + 1) * wide], 3)
        left_ref[block * ntab : (block + 1) * ntab, :] = jnp.concatenate(pieces, axis=1)
    found = jnp.zeros((ntab, nodes), jnp.float32)
    step = 16
    for first in range(0, blocks, step):
        rows = left_ref[first * ntab : (first + step) * ntab, :]
        picked = jnp.dot(rows, right_ref[...], preferred_element_type=jnp.float32)
        for block in range(step):
            part = picked[block * ntab : (block + 1) * ntab]
            found = jnp.where(high == first + block, part, found)
    return found


def chebyshev_coefs(bins_ref):
    shape = (DEGREES, DEGREES)
    degree = lax.broadcasted_iota(jnp.int32, shape, 0)
    node = lax.broadcasted_iota(jnp.int32, shape, 1)
    period = 4 * DEGREES
    weight, _ = cos_sin((degree * (2 * node + 1) & (period - 1)).astype(jnp.float32) * (1.0 / period))
    weight = weight * jnp.where(degree == 0, 1.0 / DEGREES, 2.0 / DEGREES)
    even = jnp.where(degree % 2 == 0, weight, 0.0)
    odd = jnp.where(degree % 2 == 1, weight, 0.0)
    row = bins_ref[...].astype(jnp.float32)
    bins = jnp.concatenate([row] * (LANES // NF), axis=1)
    at = lax.broadcasted_iota(jnp.int32, (DEGREES, LANES), 0).astype(jnp.float32)
    spot, _ = cos_sin((2.0 * at + 1.0) * (1.0 / period))
    cosine, sine = cos_sin(bins * (spot * (REACH / 256.0)))
    dot = functools.partial(jnp.dot, precision=lax.Precision.HIGHEST, preferred_element_type=jnp.float32)
    return dot(even, cosine) + dot(odd, sine)


def station_order(table_row):
    count = table_row.shape[1]
    shape = (count, count)
    here = lax.broadcasted_iota(jnp.int32, shape, 0)
    there = lax.broadcasted_iota(jnp.int32, shape, 1)
    key_row = table_row * count + there[:1]
    spread = jnp.broadcast_to(key_row, shape)
    key_column = jnp.sum(jnp.where(here == there, spread, 0), axis=1, keepdims=True)
    rank = jnp.sum(jnp.where(key_column < key_row, 1, 0), axis=0, keepdims=True)
    table_column = key_column // count
    bound = lax.broadcasted_iota(jnp.int32, (count, LANES), 1)
    starts = jnp.sum(jnp.where(table_column < bound, 1, 0), axis=0, keepdims=True)
    first = lax.broadcasted_iota(jnp.int32, (count, LANES), 1) * 8
    place_column = jnp.sum(jnp.where(here == there, jnp.broadcast_to(rank, shape), 0), axis=1, keepdims=True)
    low = jnp.sum(jnp.where(place_column == first, table_column, 0), axis=0, keepdims=True)
    high = jnp.sum(jnp.where(place_column == first + 7, table_column, 0), axis=0, keepdims=True)
    plan = jnp.concatenate([starts, low, high, jnp.zeros((5, LANES), jnp.int32)], axis=0)
    return rank, plan


def prepare_kernel(
    bins_hbm, table_hbm, ids_hbm, tables_hbm, cos_hbm, sin_hbm, coef_hbm, sorter_hbm, plan_hbm, *rest
):
    bins_ref, table_ref, ids_ref, tables_ref, cos_ref, sin_ref, coef_ref, sorter_ref, plan_ref = rest[:9]
    left_ref, right_ref, sems, table_sems = rest[9:]
    ntab, _, nodes = cos_ref.shape
    near = ids_ref.shape[0]
    first = pl.multiple_of(own_place() * (nodes // LANES) // near * near, 8)
    ins = start_all(
        [
            pltpu.make_async_copy(ids_hbm.at[pl.ds(first, near), :], ids_ref, sems.at[0]),
            pltpu.make_async_copy(bins_hbm, bins_ref, sems.at[1]),
            pltpu.make_async_copy(table_hbm, table_ref, sems.at[2]),
        ]
    )
    piece = tables_ref.shape[1] // TABLE_PIECES
    table_copies = []
    for at in range(TABLE_PIECES):
        part = (slice(None), pl.ds(at * piece, piece))
        table_copies.append(pltpu.make_async_copy(tables_hbm.at[part], tables_ref.at[part], table_sems.at[at]))
    start_all(table_copies)
    for copy in ins:
        copy.wait()
    coef_ref[...] = chebyshev_coefs(bins_ref)
    rank, plan = station_order(table_ref[...])
    plan_ref[...] = plan
    count = table_ref.shape[1]
    place = lax.broadcasted_iota(jnp.int32, (count, count), 0)
    sorter_ref[...] = jnp.where(place == rank, 1.0, 0.0).astype(jnp.bfloat16)
    outs = start_all(
        [
            pltpu.make_async_copy(coef_ref, coef_hbm, sems.at[0]),
            pltpu.make_async_copy(plan_ref, plan_hbm, sems.at[1]),
            pltpu.make_async_copy(sorter_ref, sorter_hbm, sems.at[2]),
        ]
    )
    turns = pick_columns(ids_ref, tables_ref, table_copies, nodes, left_ref, right_ref) * (1.0 / 256.0)
    bins = bins_column(bins_ref)
    for table in range(ntab):
        cosine, sine = cos_sin(bins * turns[table : table + 1])
        cos_ref[table] = cosine
        sin_ref[table] = sine
        outs += start_all(
            [
                pltpu.make_async_copy(cos_ref.at[table], cos_hbm.at[table], sems.at[3 + 2 * table]),
                pltpu.make_async_copy(sin_ref.at[table], sin_hbm.at[table], sems.at[4 + 2 * table]),
            ]
        )
    for copy in outs:
        copy.wait()


def image_kernel(
    stations_dev, plan_hbm, sorter_hbm, coef_hbm, spectra_hbm, corr_hbm, cos_hbm, sin_hbm, keep_ref, send_ref, *rest
):
    plan_ref, sorter_ref, coef_ref, spectra_ref, corr_ref, cos_ref, sin_ref, sems = rest[:8]
    place_ref, weight_ref, sums_ref, basis_a, left_a, basis_b, left_b = rest[8:]
    pairs = [
        (sorter_hbm, sorter_ref), (corr_hbm, corr_ref), (spectra_hbm, spectra_ref), (plan_hbm, plan_ref),
        (coef_hbm, coef_ref), (cos_hbm, cos_ref), (sin_hbm, sin_ref),
    ]
    copies = [pltpu.make_async_copy(src, dst, sems.at[at]) for at, (src, dst) in enumerate(pairs)]
    start_all(copies)
    stations, nodes = place_ref.shape
    windows, groups, cores = (lax.axis_size(a) for a in ("win", "sta", "freq"))
    ntab = cos_ref.shape[0]
    for copy in copies[:2]:
        copy.wait()
    sorter = sorter_ref[...]

    place_ref[...] = jnp.dot(sorter, corr_ref[...], preferred_element_type=jnp.float32) * (1.0 / REACH)

    for copy in copies[2:5]:
        copy.wait()
    even, odd = [], []
    rows = spectra_ref.shape[1]
    for win in range(windows):
        value = []
        for group in range(groups):
            at = (win * groups + group) * cores
            tile = spectra_ref[at]
            for core in range(1, cores):
                tile = tile + spectra_ref[at + core]
            value += [tile[:, 2 * NF * piece : 2 * NF * (piece + 1)] for piece in range(stations_dev // rows)]
        value = jnp.concatenate(value, axis=0)
        even.append(value)
        odd.append(jnp.concatenate([-value[:, NF:], value[:, :NF]], axis=1))
    both = jnp.concatenate(even + even + odd + odd, axis=1)
    found = None
    for piece in split_bf16(both, 3):
        part = jnp.dot(sorter, piece, preferred_element_type=jnp.float32)
        found = part if found is None else found + part
    weight_ref[...] = found
    sums_ref[...] = jnp.zeros_like(sums_ref)
    chunk = min(256, nodes)
    depth = DEGREES * 8
    lanes = 2 * windows * 2 * NF
    slot = lax.broadcasted_iota(jnp.int32, (8, lanes), 1) // (lanes // 2)
    spot = lax.broadcasted_iota(jnp.int32, (8, lanes), 0)

    def left_steps(group, table, left_ref):
        here = spot + group * 8
        low = jnp.where(slot == 0, plan_ref[0, table], plan_ref[0, table + 1])
        high = jnp.where(slot == 0, plan_ref[0, table + 1], plan_ref[0, table + 2])
        mask = (here >= low) & (here < high)
        rows = pl.ds(pl.multiple_of(group * 8, 8), 8)
        sides = [
            jnp.where(mask, weight_ref[rows, :lanes], 0.0),
            jnp.where(mask, weight_ref[rows, lanes:], 0.0),
        ]
        per = LANES // 8
        for half in range(DEGREES // per):
            tall = jnp.concatenate(
                [sides[k % 2] * coef_ref[k : k + 1, :lanes] for k in range(half * per, (half + 1) * per)], axis=0
            )
            high, low = split_bf16(tall.T, 2)
            at = half * LANES
            left_ref[:, at : at + LANES] = high
            left_ref[:, depth + at : depth + at + LANES] = high
            left_ref[:, 2 * depth + at : 2 * depth + at + LANES] = low
            yield

    def basis_steps(group, basis_ref):
        arg = place_ref[pl.ds(pl.multiple_of(group * 8, 8), 8), :]
        twice = arg + arg
        before, now = jnp.ones_like(arg), arg
        for degree in range(0, DEGREES, 2):
            pair = jnp.concatenate([before, now], axis=0)
            high, low = split_bf16(pair, 2)
            basis_ref[degree * 8 : degree * 8 + 16, :] = high
            basis_ref[depth + degree * 8 : depth + degree * 8 + 16, :] = low
            before = twice * now - before
            now = twice * before - now
            if degree % 8 == 6:
                yield

    def run(steps):
        for _ in steps:
            pass

    def add_tables(table, basis_ref, left_ref, steps):
        other = jnp.minimum(table + 1, ntab - 1)
        half = lanes // 2
        for first in range(0, nodes, chunk):
            at = slice(first, first + chunk)
            right = jnp.concatenate([basis_ref[:, at], basis_ref[:depth, at]], axis=0)
            got = jnp.dot(left_ref[...], right, preferred_element_type=jnp.float32)
            for step in steps:
                next(step, None)
            cos_a, sin_a = cos_ref[table, :, at], sin_ref[table, :, at]
            cos_b, sin_b = cos_ref[other, :, at], sin_ref[other, :, at]
            for win in range(windows):
                row = win * 2 * NF
                real_a, imag_a = got[row : row + NF], got[row + NF : row + 2 * NF]
                real_b, imag_b = got[half + row : half + row + NF], got[half + row + NF : half + row + 2 * NF]
                sums_ref[row : row + NF, at] += (real_a * cos_a - imag_a * sin_a) + (real_b * cos_b - imag_b * sin_b)
                sums_ref[row + NF : row + 2 * NF, at] += (real_a * sin_a + imag_a * cos_a) + (
                    real_b * sin_b + imag_b * cos_b
                )
        for step in steps:
            run(step)

    def more_tables(group, basis_ref, left_ref):
        first, last = plan_ref[1, group], plan_ref[2, group]

        def step(turn, carry):
            table = first + 2 * turn
            run(left_steps(group, table, left_ref))
            add_tables(table, basis_ref, left_ref, [])
            return carry

        lax.fori_loop(1, (last - first) // 2 + 1, step, 0)

    total_groups = stations // 8
    run(left_steps(0, plan_ref[1, 0], left_a))
    run(basis_steps(0, basis_a))
    for copy in copies[5:]:
        copy.wait()

    def stage(group, after, basis_ref, left_ref, next_basis, next_left):
        steps = [left_steps(after, plan_ref[1, after], next_left), basis_steps(after, next_basis)]
        add_tables(plan_ref[1, group], basis_ref, left_ref, steps)
        more_tables(group, basis_ref, left_ref)

    def body(pair, carry):
        group = pair * 2
        after = jnp.minimum(group + 2, total_groups - 1)
        stage(group, group + 1, basis_a, left_a, basis_b, left_b)
        stage(group + 1, after, basis_b, left_b, basis_a, left_a)
        return carry

    lax.fori_loop(0, total_groups // 2, body, 0)
    powers = []
    for win in range(windows):
        row = win * 2 * NF
        real, imag = sums_ref[row : row + NF, :], sums_ref[row + NF : row + 2 * NF, :]
        powers.append(real * real + imag * imag)
    mine = lax.axis_index("win") == 0
    keep_ref[...] = jnp.where(mine, powers[0], powers[1])
    send_ref[...] = jnp.where(mine, powers[1], powers[0])


def finish_kernel(stations, keep_ref, got_ref, spectrum_ref, beam_ref):
    nodes = keep_ref.shape[1]
    win = lax.axis_index("win")
    for place, ref in ((win, keep_ref), (1 - win, got_ref)):
        power = ref[...]
        total = jnp.sum(power, axis=0, keepdims=True)
        at = pl.ds(pl.multiple_of(place * nodes, LANES), nodes)
        spectrum_ref[:, at] = power * (NF / total)
        beam_ref[:, at] = total * (1.0 / (NF * stations))


def on_device(traces, tables, corrections, station_table, node_ids, freq_bins):
    windows, groups, cores = (lax.axis_size(a) for a in ("win", "sta", "freq"))
    stations_dev, grid = corrections.shape
    stations = stations_dev * groups
    devices = windows * groups * cores
    nodes = grid // devices
    ntab = tables.shape[0]
    params = pltpu.CompilerParams(vmem_limit_bytes=VMEM_LIMIT)
    vmem = pl.BlockSpec(memory_space=pltpu.VMEM)
    hbm = pl.BlockSpec(memory_space=pltpu.HBM)
    bins = freq_bins.reshape(1, NF)
    bins_scratch = pltpu.VMEM((1, NF), jnp.int32)

    corr, copies = pl.pallas_call(
        functools.partial(send_kernel, nodes),
        out_shape=[
            jax.ShapeDtypeStruct((groups, stations_dev, nodes), jnp.bfloat16),
            jax.ShapeDtypeStruct((devices, stations_dev * 2 * NF // LANES, LANES), jnp.float32),
        ],
        in_specs=[hbm] * 3,
        out_specs=[hbm, vmem],
        scratch_shapes=[
            bins_scratch,
            pltpu.VMEM(traces.shape, traces.dtype),
            pltpu.SemaphoreType.DMA((groups + 2,)),
        ],
        compiler_params=params,
        name="send",
    )(bins, traces, corrections)
    corr = lax.all_to_all(corr, "sta", split_axis=0, concat_axis=0, tiled=True)
    spectra = lax.all_to_all(copies, ("win", "sta", "freq"), split_axis=0, concat_axis=0, tiled=True)

    wide = 512
    products = [
        ((ntab, NF, nodes), jnp.float32),
        ((ntab, NF, nodes), jnp.float32),
        ((DEGREES, LANES), jnp.float32),
        ((stations, stations), jnp.bfloat16),
        ((8, LANES), jnp.int32),
    ]
    cosine, sine, coefs, sorter, plan = pl.pallas_call(
        prepare_kernel,
        out_shape=[jax.ShapeDtypeStruct(*product) for product in products],
        in_specs=[hbm] * 4,
        out_specs=[hbm] * 5,
        scratch_shapes=[
            bins_scratch,
            pltpu.VMEM((1, stations), jnp.int32),
            pltpu.VMEM((max(nodes // LANES, 8), LANES), jnp.int32),
            pltpu.VMEM(tables.shape, tables.dtype),
        ]
        + [pltpu.VMEM(*product) for product in products]
        + [
            pltpu.VMEM((grid // wide * ntab, 3 * wide), jnp.bfloat16),
            pltpu.VMEM((3 * wide, nodes), jnp.bfloat16),
            pltpu.SemaphoreType.DMA((3 + 2 * ntab,)),
            pltpu.SemaphoreType.DMA((TABLE_PIECES,)),
        ],
        compiler_params=params,
        name="prepare",
    )(bins, station_table.reshape(1, stations), node_ids.reshape(grid // LANES, LANES), tables)

    half = jax.ShapeDtypeStruct((NF, nodes), jnp.float32)
    rows = 2 * windows * 2 * NF
    basis = pltpu.VMEM((2 * DEGREES * 8, nodes), jnp.bfloat16)
    left = pltpu.VMEM((rows, 3 * DEGREES * 8), jnp.bfloat16)
    keep, send = pl.pallas_call(
        functools.partial(image_kernel, stations_dev),
        out_shape=[half, half],
        in_specs=[hbm] * 7,
        out_specs=[vmem, vmem],
        scratch_shapes=[
            pltpu.SMEM(*products[4]),
            pltpu.VMEM(*products[3]),
            pltpu.VMEM(*products[2]),
            pltpu.VMEM(spectra.shape, spectra.dtype),
            pltpu.VMEM((stations, nodes), corr.dtype),
            pltpu.VMEM(*products[0]),
            pltpu.VMEM(*products[1]),
            pltpu.SemaphoreType.DMA((7,)),
            pltpu.VMEM((stations, nodes), jnp.float32),
            pltpu.VMEM((stations, 2 * rows), jnp.float32),
            pltpu.VMEM((rows // 2, nodes), jnp.float32),
            basis,
            left,
            basis,
            left,
        ],
        compiler_params=params,
        name="image",
    )(plan, sorter, coefs, spectra, corr.reshape(stations, nodes), cosine, sine)
    got = lax.ppermute(send, "win", [(0, 1), (1, 0)])
    spectrum, beam_power = pl.pallas_call(
        functools.partial(finish_kernel, stations),
        out_shape=[
            jax.ShapeDtypeStruct((NF, windows * nodes), jnp.float32),
            jax.ShapeDtypeStruct((1, windows * nodes), jnp.float32),
        ],
        in_specs=[vmem, vmem],
        out_specs=[vmem, vmem],
        compiler_params=params,
        name="finish",
    )(keep, got)
    return spectrum, beam_power.reshape(windows * nodes)


def solution(mesh):
    return jax.shard_map(
        on_device,
        mesh=mesh,
        in_specs=(P(("win", "sta"), "freq"), P(), P("sta", None), P(), P(), P()),
        out_specs=(P("win", ("sta", "freq")), P(("win", "sta", "freq"))),
        check_vma=False,
    )
```

```python
import functools
import math

import jax
import jax.numpy as jnp
import numpy as np
from jax import lax
from jax.experimental import pallas as pl
from jax.experimental.pallas import tpu as pltpu
from jax.sharding import PartitionSpec as P

NT = 5120
NF = 16
LANES = 128
DEGREES = 32
REACH = 1.5
TABLE_PIECES = 4
VMEM_LIMIT = 64 * 1024 * 1024 - 64 * 1024


def chebyshev_fit(func, degree, low, high):
    fit = np.polynomial.chebyshev.Chebyshev.interpolate(func, degree, domain=[low, high])
    return [float(v) for v in fit.convert(kind=np.polynomial.Polynomial).coef]


SIN_HALF = chebyshev_fit(lambda z: np.pi * np.sinc(np.sqrt(z)), 4, 0.0, 0.25)
COS_HALF = chebyshev_fit(lambda z: np.cos(np.pi * np.sqrt(z)), 4, 0.0, 0.25)


def horner(coefs, arg):
    total = coefs[-1]
    for coef in coefs[-2::-1]:
        total = total * arg + coef
    return total


def turn_parts(rest):
    square = rest * rest
    root = math.sqrt(2.0)
    sine_half = rest * horner([root * c for c in SIN_HALF], square)
    cos_half = horner([root * c for c in COS_HALF], square)
    return sine_half * sine_half, sine_half * cos_half


def cos_sin(turns):
    versine, sine = turn_parts(turns - jnp.round(turns))
    return 1.0 - versine, sine


def bins_column(bins_ref):
    rows = lax.broadcasted_iota(jnp.int32, (NF, NF), 0)
    lanes = lax.broadcasted_iota(jnp.int32, (NF, NF), 1)
    square = jnp.broadcast_to(bins_ref[...].astype(jnp.float32), (NF, NF))
    return jnp.sum(jnp.where(rows == lanes, square, 0.0), axis=1, keepdims=True)


def split_bf16(value, terms):
    pieces = []
    for term in range(terms):
        piece = value.astype(jnp.bfloat16)
        pieces.append(piece)
        if term < terms - 1:
            value = value - piece.astype(jnp.float32)
    return pieces


def start_all(copies):
    for copy in copies:
        copy.start()
    return copies


def send_kernel(nodes, bins_hbm, traces_hbm, corr_hbm, out_ref, bins_ref, traces_ref, sems):
    devices, height, _ = out_ref.shape
    stations_dev, half_length = traces_ref.shape
    pieces = (height - 8) // stations_dev
    windows, groups, cores = (lax.axis_size(a) for a in ("win", "sta", "freq"))
    place = lax.axis_index("win") * cores + lax.axis_index("freq")
    small = start_all(
        [
            pltpu.make_async_copy(bins_hbm, bins_ref, sems.at[0]),
            pltpu.make_async_copy(traces_hbm, traces_ref, sems.at[1]),
        ]
    )
    copies = []
    for dev in range(devices):
        win, sta, core = dev // (groups * cores), dev // cores % groups, dev % cores
        first = ((sta * cores + core) * windows + win) * nodes
        for piece in range(pieces):
            at = pl.multiple_of(first + (place * pieces + piece) * LANES, LANES)
            to = out_ref.at[dev, pl.ds(piece * stations_dev, stations_dev), :]
            sem = sems.at[2 + dev * pieces + piece]
            copies.append(pltpu.make_async_copy(corr_hbm.at[:, pl.ds(at, LANES)], to, sem))
    start_all(copies)
    start = lax.axis_index("freq") * half_length
    small[0].wait()
    bins = bins_column(bins_ref)
    pos = (start + lax.broadcasted_iota(jnp.int32, (NF, half_length), 1)).astype(jnp.float32)
    product = bins * pos
    turns = jnp.round(product * (1.0 / NT))
    rest = (product - turns * NT) * (1.0 / NT)
    versine, sine = turn_parts(rest)
    scale = 1.0 / math.sqrt(NT)
    table = jnp.concatenate([(1.0 - versine) * scale, sine * -scale], axis=0)
    both = jnp.concatenate(split_bf16(table, 2), axis=0)
    small[1].wait()
    sums = lax.dot_general(
        traces_ref[...], both, (((1,), (1,)), ((), ())), preferred_element_type=jnp.float32
    )
    sums = sums[:, : 2 * NF] + sums[:, 2 * NF :]
    terms = [term.astype(jnp.float32) for term in split_bf16(sums, 2)]
    tile = jnp.concatenate([term[at : at + 8] for term in terms for at in range(0, stations_dev, 8)], axis=1)
    tile = tile.astype(jnp.bfloat16)
    for dev in range(devices):
        out_ref[dev, height - 8 :, :] = tile
    for copy in copies:
        copy.wait()


def own_place():
    windows, cores = lax.axis_size("win"), lax.axis_size("freq")
    return (lax.axis_index("sta") * cores + lax.axis_index("freq")) * windows + lax.axis_index("win")


def pick_columns(ids_ref, tables_ref, table_copies, nodes, left_ref, right_ref):
    ntab, grid = tables_ref.shape
    count = nodes // LANES
    wide = right_ref.shape[0] // 3
    blocks = grid // wide
    ids = ids_ref[pl.ds(own_place() * count % ids_ref.shape[0], count), :]
    ids = jnp.concatenate([ids[at : at + 1] for at in range(count)], axis=1)
    low, high = ids & (wide - 1), ids >> (wide.bit_length() - 1)
    spots = lax.broadcasted_iota(jnp.int32, (wide, nodes), 0)
    ones = jnp.where(spots == low, 1.0, 0.0).astype(jnp.bfloat16)
    for term in range(3):
        right_ref[term * wide : (term + 1) * wide, :] = ones
    found = jnp.zeros((ntab, nodes), jnp.float32)
    step = blocks // len(table_copies)
    for at, copy in enumerate(table_copies):
        copy.wait()
        for block in range(at * step, (at + 1) * step):
            pieces = split_bf16(tables_ref[:, block * wide : (block + 1) * wide], 3)
            left_ref[block * ntab : (block + 1) * ntab, :] = jnp.concatenate(pieces, axis=1)
        rows = left_ref[at * step * ntab : (at + 1) * step * ntab, :]
        picked = jnp.dot(rows, right_ref[...], preferred_element_type=jnp.float32)
        for block in range(step):
            part = picked[block * ntab : (block + 1) * ntab]
            found = jnp.where(high == at * step + block, part, found)
    return found


def chebyshev_coefs(bins_ref):
    shape = (DEGREES, DEGREES)
    degree = lax.broadcasted_iota(jnp.int32, shape, 0)
    node = lax.broadcasted_iota(jnp.int32, shape, 1)
    period = 4 * DEGREES
    weight, _ = cos_sin((degree * (2 * node + 1) & (period - 1)).astype(jnp.float32) * (1.0 / period))
    weight = weight * jnp.where(degree == 0, 1.0 / DEGREES, 2.0 / DEGREES)
    even = jnp.where(degree % 2 == 0, weight, 0.0)
    odd = jnp.where(degree % 2 == 1, weight, 0.0)
    row = bins_ref[...].astype(jnp.float32)
    bins = jnp.concatenate([row] * (LANES // NF), axis=1)
    at = lax.broadcasted_iota(jnp.int32, (DEGREES, LANES), 0).astype(jnp.float32)
    spot, _ = cos_sin((2.0 * at + 1.0) * (1.0 / period))
    cosine, sine = cos_sin(bins * (spot * (REACH / 256.0)))
    dot = functools.partial(jnp.dot, precision=lax.Precision.HIGHEST, preferred_element_type=jnp.float32)
    return dot(even, cosine) + dot(odd, sine)


def station_order(table_row):
    count = table_row.shape[1]
    shape = (count, count)
    here = lax.broadcasted_iota(jnp.int32, shape, 0)
    there = lax.broadcasted_iota(jnp.int32, shape, 1)
    key_row = table_row * count + there[:1]
    spread = jnp.broadcast_to(key_row, shape)
    key_column = jnp.sum(jnp.where(here == there, spread, 0), axis=1, keepdims=True)
    rank = jnp.sum(jnp.where(key_column < key_row, 1, 0), axis=0, keepdims=True)
    table_column = key_column // count
    bound = lax.broadcasted_iota(jnp.int32, (count, LANES), 1)
    starts = jnp.sum(jnp.where(table_column < bound, 1, 0), axis=0, keepdims=True)
    first = lax.broadcasted_iota(jnp.int32, (count, LANES), 1) * 8
    place_column = jnp.sum(jnp.where(here == there, jnp.broadcast_to(rank, shape), 0), axis=1, keepdims=True)
    low = jnp.sum(jnp.where(place_column == first, table_column, 0), axis=0, keepdims=True)
    high = jnp.sum(jnp.where(place_column == first + 7, table_column, 0), axis=0, keepdims=True)
    plan = jnp.concatenate([starts, low, high, jnp.zeros((5, LANES), jnp.int32)], axis=0)
    return rank, plan


def prepare_kernel(
    bins_hbm, table_hbm, ids_hbm, tables_hbm, cos_hbm, sin_hbm, coef_hbm, sorter_hbm, plan_hbm, *rest
):
    bins_ref, table_ref, ids_ref, tables_ref, cos_ref, sin_ref, coef_ref, sorter_ref, plan_ref = rest[:9]
    left_ref, right_ref, sems, table_sems = rest[9:]
    ntab, _, nodes = cos_ref.shape
    near = ids_ref.shape[0]
    first = pl.multiple_of(own_place() * (nodes // LANES) // near * near, 8)
    ins = start_all(
        [
            pltpu.make_async_copy(ids_hbm.at[pl.ds(first, near), :], ids_ref, sems.at[0]),
            pltpu.make_async_copy(bins_hbm, bins_ref, sems.at[1]),
            pltpu.make_async_copy(table_hbm, table_ref, sems.at[2]),
        ]
    )
    piece = tables_ref.shape[1] // TABLE_PIECES
    table_copies = []
    for at in range(TABLE_PIECES):
        part = (slice(None), pl.ds(at * piece, piece))
        table_copies.append(pltpu.make_async_copy(tables_hbm.at[part], tables_ref.at[part], table_sems.at[at]))
    start_all(table_copies)
    for copy in ins:
        copy.wait()
    coef_ref[...] = chebyshev_coefs(bins_ref)
    rank, plan = station_order(table_ref[...])
    plan_ref[...] = plan
    count = table_ref.shape[1]
    place = lax.broadcasted_iota(jnp.int32, (count, count), 0)
    sorter_ref[...] = jnp.where(place == rank, 1.0, 0.0).astype(jnp.bfloat16)
    outs = start_all(
        [
            pltpu.make_async_copy(coef_ref, coef_hbm, sems.at[0]),
            pltpu.make_async_copy(plan_ref, plan_hbm, sems.at[1]),
            pltpu.make_async_copy(sorter_ref, sorter_hbm, sems.at[2]),
        ]
    )
    turns = pick_columns(ids_ref, tables_ref, table_copies, nodes, left_ref, right_ref) * (1.0 / 256.0)
    bins = bins_column(bins_ref)
    for table in range(ntab):
        cosine, sine = cos_sin(bins * turns[table : table + 1])
        cos_ref[table] = cosine
        sin_ref[table] = sine
        outs += start_all(
            [
                pltpu.make_async_copy(cos_ref.at[table], cos_hbm.at[table], sems.at[3 + 2 * table]),
                pltpu.make_async_copy(sin_ref.at[table], sin_hbm.at[table], sems.at[4 + 2 * table]),
            ]
        )
    for copy in outs:
        copy.wait()


def image_kernel(merged, stations_dev, plan_hbm, sorter_hbm, coef_hbm, cos_hbm, sin_hbm, block_hbm, *rest):
    corr_hbm, rest = (None, rest) if merged else (rest[0], rest[1:])
    keep_ref, send_ref, plan_ref, sorter_ref, coef_ref, block_ref, corr_ref, cos_ref, sin_ref, sems = rest[:10]
    place_ref, weight_ref, left_ref, sums_ref, basis_a, basis_b = rest[10:]
    pairs = [
        (sorter_hbm, sorter_ref), (block_hbm, block_ref), (plan_hbm, plan_ref), (coef_hbm, coef_ref),
        (cos_hbm, cos_ref), (sin_hbm, sin_ref),
    ]
    if not merged:
        pairs.append((corr_hbm, corr_ref))
    copies = [pltpu.make_async_copy(src, dst, sems.at[at]) for at, (src, dst) in enumerate(pairs)]
    start_all(copies)
    stations, nodes = place_ref.shape
    windows, groups, cores = (lax.axis_size(a) for a in ("win", "sta", "freq"))
    ntab = cos_ref.shape[0]
    for copy in copies[:4] + copies[6:]:
        copy.wait()
    sorter = sorter_ref[...]
    height = block_ref.shape[1]
    rows_of = lambda win, core: [(win * groups + group) * cores + core for group in range(groups)]

    if merged:
        parts = []
        for win in range(windows):
            for core in range(cores):
                for first in range(0, height - 8, stations_dev):
                    rows = [block_ref[at, first : first + stations_dev, :] for at in rows_of(win, core)]
                    parts.append(jnp.concatenate(rows, axis=0))
        corr = jnp.concatenate(parts, axis=1)
    else:
        corr = corr_ref[...]
    place_ref[...] = jnp.dot(sorter, corr, preferred_element_type=jnp.float32) * (1.0 / REACH)

    even, odd = [], []
    for win in range(windows):
        value = []
        for group in range(groups):
            tile = None
            for core in range(cores):
                part = block_ref[(win * groups + group) * cores + core, height - 8 :, :].astype(jnp.float32)
                tile = part if tile is None else tile + part
            tile = tile[:, : LANES // 2] + tile[:, LANES // 2 :]
            value += [tile[:, 2 * NF * piece : 2 * NF * (piece + 1)] for piece in range(stations_dev // 8)]
        value = jnp.concatenate(value, axis=0)
        even.append(value)
        odd.append(jnp.concatenate([-value[:, NF:], value[:, :NF]], axis=1))
    found = None
    for piece in split_bf16(jnp.concatenate(even + odd, axis=1), 3):
        part = jnp.dot(sorter, piece, preferred_element_type=jnp.float32)
        found = part if found is None else found + part
    weight_ref[...] = found
    sums_ref[...] = jnp.zeros_like(sums_ref)
    chunk = min(256, nodes)
    depth = DEGREES * 8
    lanes = windows * 2 * NF
    total_groups = stations // 8

    def make_left(pair, carry):
        top = weight_ref[pl.ds(pl.multiple_of(pair * 16, 16), 8), :]
        bottom = weight_ref[pl.ds(pl.multiple_of(pair * 16 + 8, 8), 8), :]
        sides = [
            jnp.concatenate([top[:, :lanes], bottom[:, :lanes]], axis=1),
            jnp.concatenate([top[:, lanes:], bottom[:, lanes:]], axis=1),
        ]
        per = LANES // 8
        for half in range(DEGREES // per):
            tall = jnp.concatenate(
                [sides[k % 2] * coef_ref[k : k + 1, :] for k in range(half * per, (half + 1) * per)], axis=0
            )
            at = slice(half * LANES, (half + 1) * LANES)
            for term, value in enumerate(split_bf16(tall.T, 2)):
                left_ref[2 * pair, term * lanes : (term + 1) * lanes, at] = value[:lanes]
                left_ref[2 * pair + 1, term * lanes : (term + 1) * lanes, at] = value[lanes:]
        return carry

    lax.fori_loop(0, total_groups // 2, make_left, 0)
    spot = lax.broadcasted_iota(jnp.int32, (16, depth), 1) % 8

    def left_of(group, table):
        here = spot + group * 8
        mask = (here >= plan_ref[0, table]) & (here < plan_ref[0, table + 1])
        mask = jnp.where(mask, 1.0, 0.0).astype(jnp.bfloat16)
        return left_ref[group] * jnp.concatenate([mask] * (2 * lanes // 16), axis=0)

    def basis_steps(group, basis_ref):
        arg = place_ref[pl.ds(pl.multiple_of(group * 8, 8), 8), :]
        twice = arg + arg
        before, now = jnp.ones_like(arg), arg
        for degree in range(0, DEGREES, 2):
            pair = jnp.concatenate([before, now], axis=0)
            high, low = split_bf16(pair, 2)
            basis_ref[degree * 8 : degree * 8 + 16, :] = high
            basis_ref[depth + degree * 8 : depth + degree * 8 + 16, :] = low
            before = twice * now - before
            now = twice * before - now
            if degree % 8 == 6:
                yield

    def run(steps):
        for _ in steps:
            pass

    def add_tables(group, table, basis_ref, steps):
        other = jnp.minimum(table + 1, ntab - 1)
        left_a, left_b = left_of(group, table), left_of(group, table + 1)
        both = jnp.concatenate([left_a, left_b], axis=0)
        high = jnp.concatenate([left_a[:lanes], left_b[:lanes]], axis=0)
        for first in range(0, nodes, chunk):
            at = slice(first, first + chunk)
            got = jnp.dot(both, basis_ref[:depth, at], preferred_element_type=jnp.float32)
            more = jnp.dot(high, basis_ref[depth:, at], preferred_element_type=jnp.float32)
            next(steps, None)
            for slot, place in enumerate((table, other)):
                row = slot * 2 * lanes
                value = got[row : row + lanes] + got[row + lanes : row + 2 * lanes]
                value = value + more[slot * lanes : (slot + 1) * lanes]
                cosine, sine = cos_ref[place, :, at], sin_ref[place, :, at]
                for win in range(windows):
                    row = win * 2 * NF
                    real, imag = value[row : row + NF], value[row + NF : row + 2 * NF]
                    sums_ref[row : row + NF, at] += real * cosine - imag * sine
                    sums_ref[row + NF : row + 2 * NF, at] += real * sine + imag * cosine
        run(steps)

    def more_tables(group, basis_ref):
        first, last = plan_ref[1, group], plan_ref[2, group]

        def step(turn, carry):
            add_tables(group, first + 2 * turn, basis_ref, iter(()))
            return carry

        lax.fori_loop(1, (last - first) // 2 + 1, step, 0)

    run(basis_steps(0, basis_a))
    for copy in copies[4:6]:
        copy.wait()

    def stage(group, after, basis_ref, next_basis):
        add_tables(group, plan_ref[1, group], basis_ref, basis_steps(after, next_basis))
        more_tables(group, basis_ref)

    def body(pair, carry):
        group = pair * 2
        after = jnp.minimum(group + 2, total_groups - 1)
        stage(group, group + 1, basis_a, basis_b)
        stage(group + 1, after, basis_b, basis_a)
        return carry

    lax.fori_loop(0, total_groups // 2, body, 0)
    powers = []
    for win in range(windows):
        row = win * 2 * NF
        real, imag = sums_ref[row : row + NF, :], sums_ref[row + NF : row + 2 * NF, :]
        powers.append(real * real + imag * imag)
    mine = lax.axis_index("win") == 0
    keep_ref[...] = jnp.where(mine, powers[0], powers[1])
    send_ref[...] = jnp.where(mine, powers[1], powers[0])


def finish_kernel(stations, keep_ref, got_ref, spectrum_ref, beam_ref):
    nodes = keep_ref.shape[1]
    win = lax.axis_index("win")
    for place, ref in ((win, keep_ref), (1 - win, got_ref)):
        power = ref[...]
        total = jnp.sum(power, axis=0, keepdims=True)
        at = pl.ds(pl.multiple_of(place * nodes, LANES), nodes)
        spectrum_ref[:, at] = power * (NF / total)
        beam_ref[:, at] = total * (1.0 / (NF * stations))


def on_device(traces, tables, corrections, station_table, node_ids, freq_bins):
    windows, groups, cores = (lax.axis_size(a) for a in ("win", "sta", "freq"))
    stations_dev, grid = corrections.shape
    stations = stations_dev * groups
    devices = windows * groups * cores
    nodes = grid // devices
    ntab = tables.shape[0]
    params = pltpu.CompilerParams(vmem_limit_bytes=VMEM_LIMIT)
    vmem = pl.BlockSpec(memory_space=pltpu.VMEM)
    hbm = pl.BlockSpec(memory_space=pltpu.HBM)
    bins = freq_bins.reshape(1, NF)
    bins_scratch = pltpu.VMEM((1, NF), jnp.int32)

    holders = windows * cores
    merged = nodes % (holders * LANES) == 0
    pieces = nodes // (holders * LANES) if merged else 0
    height = pieces * stations_dev + 8
    blocks = pl.pallas_call(
        functools.partial(send_kernel, nodes),
        out_shape=jax.ShapeDtypeStruct((devices, height, LANES), jnp.bfloat16),
        in_specs=[hbm] * 3,
        out_specs=vmem,
        scratch_shapes=[
            bins_scratch,
            pltpu.VMEM(traces.shape, traces.dtype),
            pltpu.SemaphoreType.DMA((2 + devices * max(pieces, 1),)),
        ],
        compiler_params=params,
        name="send",
    )(bins, traces, corrections)
    received = [lax.all_to_all(blocks, ("win", "sta", "freq"), split_axis=0, concat_axis=0, tiled=True)]
    if not merged:
        parts = corrections.reshape(stations_dev, groups, holders, nodes)
        place = lax.axis_index("freq") * windows + lax.axis_index("win")
        mine = lax.dynamic_index_in_dim(parts, place, axis=2, keepdims=False)
        corr = lax.all_to_all(mine.transpose(1, 0, 2), "sta", split_axis=0, concat_axis=0, tiled=True)
        received.append(corr.reshape(stations, nodes))

    wide = 512
    products = [
        ((ntab, NF, nodes), jnp.float32),
        ((ntab, NF, nodes), jnp.float32),
        ((DEGREES, LANES), jnp.float32),
        ((stations, stations), jnp.bfloat16),
        ((8, LANES), jnp.int32),
    ]
    cosine, sine, coefs, sorter, plan = pl.pallas_call(
        prepare_kernel,
        out_shape=[jax.ShapeDtypeStruct(*product) for product in products],
        in_specs=[hbm] * 4,
        out_specs=[hbm] * 5,
        scratch_shapes=[
            bins_scratch,
            pltpu.VMEM((1, stations), jnp.int32),
            pltpu.VMEM((max(nodes // LANES, 8), LANES), jnp.int32),
            pltpu.VMEM(tables.shape, tables.dtype),
        ]
        + [pltpu.VMEM(*product) for product in products]
        + [
            pltpu.VMEM((grid // wide * ntab, 3 * wide), jnp.bfloat16),
            pltpu.VMEM((3 * wide, nodes), jnp.bfloat16),
            pltpu.SemaphoreType.DMA((3 + 2 * ntab,)),
            pltpu.SemaphoreType.DMA((TABLE_PIECES,)),
        ],
        compiler_params=params,
        name="prepare",
    )(bins, station_table.reshape(1, stations), node_ids.reshape(grid // LANES, LANES), tables)

    half = jax.ShapeDtypeStruct((NF, nodes), jnp.float32)
    rows = 2 * windows * 2 * NF
    basis = pltpu.VMEM((2 * DEGREES * 8, nodes), jnp.bfloat16)
    keep, send = pl.pallas_call(
        functools.partial(image_kernel, merged, stations_dev),
        out_shape=[half, half],
        in_specs=[hbm] * (5 + len(received)),
        out_specs=[vmem, vmem],
        scratch_shapes=[
            pltpu.SMEM(*products[4]),
            pltpu.VMEM(*products[3]),
            pltpu.VMEM(*products[2]),
            pltpu.VMEM((devices, height, LANES), jnp.bfloat16),
            pltpu.VMEM((16, LANES) if merged else (stations, nodes), jnp.bfloat16),
            pltpu.VMEM(*products[0]),
            pltpu.VMEM(*products[1]),
            pltpu.SemaphoreType.DMA((7,)),
            pltpu.VMEM((stations, nodes), jnp.float32),
            pltpu.VMEM((stations, rows), jnp.float32),
            pltpu.VMEM((stations // 8, rows, DEGREES * 8), jnp.bfloat16),
            pltpu.VMEM((rows // 2, nodes), jnp.float32),
            basis,
            basis,
        ],
        compiler_params=params,
        name="image",
    )(plan, sorter, coefs, cosine, sine, *received)
    got = lax.ppermute(send, "win", [(0, 1), (1, 0)])
    spectrum, beam_power = pl.pallas_call(
        functools.partial(finish_kernel, stations),
        out_shape=[
            jax.ShapeDtypeStruct((NF, windows * nodes), jnp.float32),
            jax.ShapeDtypeStruct((1, windows * nodes), jnp.float32),
        ],
        in_specs=[vmem, vmem],
        out_specs=[vmem, vmem],
        compiler_params=params,
        name="finish",
    )(keep, got)
    return spectrum, beam_power.reshape(windows * nodes)


def solution(mesh):
    return jax.shard_map(
        on_device,
        mesh=mesh,
        in_specs=(P(("win", "sta"), "freq"), P(), P("sta", None), P(), P(), P()),
        out_specs=(P("win", ("sta", "freq")), P(("win", "sta", "freq"))),
        check_vma=False,
    )
```

```python
import functools
import math

import jax
import jax.numpy as jnp
import numpy as np
from jax import lax
from jax.experimental import pallas as pl
from jax.experimental.pallas import tpu as pltpu
from jax.sharding import PartitionSpec as P

NT = 5120
NF = 16
NTAB = 16
LANES = 128
DEGREES = 32
REACH = 1.5
TABLE_PIECES = 4
VMEM_LIMIT = 64 * 1024 * 1024 - 64 * 1024


def chebyshev_fit(func, degree, low, high):
    fit = np.polynomial.chebyshev.Chebyshev.interpolate(func, degree, domain=[low, high])
    return [float(v) for v in fit.convert(kind=np.polynomial.Polynomial).coef]


SIN_HALF = chebyshev_fit(lambda z: np.pi * np.sinc(np.sqrt(z)), 4, 0.0, 0.25)
COS_HALF = chebyshev_fit(lambda z: np.cos(np.pi * np.sqrt(z)), 4, 0.0, 0.25)


def horner(coefs, arg):
    total = coefs[-1]
    for coef in coefs[-2::-1]:
        total = total * arg + coef
    return total


def turn_parts(rest):
    square = rest * rest
    root = math.sqrt(2.0)
    sine_half = rest * horner([root * c for c in SIN_HALF], square)
    cos_half = horner([root * c for c in COS_HALF], square)
    return sine_half * sine_half, sine_half * cos_half


def cos_sin(turns):
    versine, sine = turn_parts(turns - jnp.round(turns))
    return 1.0 - versine, sine


def bins_column(bins_ref):
    rows = lax.broadcasted_iota(jnp.int32, (NF, NF), 0)
    lanes = lax.broadcasted_iota(jnp.int32, (NF, NF), 1)
    square = jnp.broadcast_to(bins_ref[...].astype(jnp.float32), (NF, NF))
    return jnp.sum(jnp.where(rows == lanes, square, 0.0), axis=1, keepdims=True)


def split_bf16(value, terms):
    pieces = []
    for term in range(terms):
        piece = value.astype(jnp.bfloat16)
        pieces.append(piece)
        if term < terms - 1:
            value = value - piece.astype(jnp.float32)
    return pieces


def start_all(copies):
    for copy in copies:
        copy.start()
    return copies


def send_kernel(nodes, bins_hbm, traces_hbm, corr_hbm, out_ref, bins_ref, traces_ref, sems):
    devices, height, _ = out_ref.shape
    stations_dev, half_length = traces_ref.shape
    pieces = (height - 8) // stations_dev
    windows, groups, cores = (lax.axis_size(a) for a in ("win", "sta", "freq"))
    place = lax.axis_index("win") * cores + lax.axis_index("freq")
    small = start_all(
        [
            pltpu.make_async_copy(bins_hbm, bins_ref, sems.at[0]),
            pltpu.make_async_copy(traces_hbm, traces_ref, sems.at[1]),
        ]
    )
    copies = []
    for dev in range(devices):
        win, sta, core = dev // (groups * cores), dev // cores % groups, dev % cores
        first = ((sta * cores + core) * windows + win) * nodes
        for piece in range(pieces):
            at = pl.multiple_of(first + (place * pieces + piece) * LANES, LANES)
            to = out_ref.at[dev, pl.ds(piece * stations_dev, stations_dev), :]
            sem = sems.at[2 + dev * pieces + piece]
            copies.append(pltpu.make_async_copy(corr_hbm.at[:, pl.ds(at, LANES)], to, sem))
    start_all(copies)
    start = lax.axis_index("freq") * half_length
    small[0].wait()
    bins = bins_column(bins_ref)
    pos = (start + lax.broadcasted_iota(jnp.int32, (NF, half_length), 1)).astype(jnp.float32)
    product = bins * pos
    turns = jnp.round(product * (1.0 / NT))
    rest = (product - turns * NT) * (1.0 / NT)
    versine, sine = turn_parts(rest)
    scale = 1.0 / math.sqrt(NT)
    table = jnp.concatenate([(1.0 - versine) * scale, sine * -scale], axis=0)
    both = jnp.concatenate(split_bf16(table, 2), axis=0)
    small[1].wait()
    sums = lax.dot_general(
        traces_ref[...], both, (((1,), (1,)), ((), ())), preferred_element_type=jnp.float32
    )
    sums = sums[:, : 2 * NF] + sums[:, 2 * NF :]
    terms = [term.astype(jnp.float32) for term in split_bf16(sums, 2)]
    tile = jnp.concatenate([term[at : at + 8] for term in terms for at in range(0, stations_dev, 8)], axis=1)
    tile = tile.astype(jnp.bfloat16)
    for dev in range(devices):
        out_ref[dev, height - 8 :, :] = tile
    for copy in copies:
        copy.wait()


def own_place():
    windows, cores = lax.axis_size("win"), lax.axis_size("freq")
    return (lax.axis_index("sta") * cores + lax.axis_index("freq")) * windows + lax.axis_index("win")


def pick_columns(ids_ref, tables_ref, table_copies, nodes, left_ref, right_ref):
    ntab, grid = tables_ref.shape
    count = nodes // LANES
    wide = right_ref.shape[0] // 3
    blocks = grid // wide
    ids = ids_ref[pl.ds(own_place() * count % ids_ref.shape[0], count), :]
    ids = jnp.concatenate([ids[at : at + 1] for at in range(count)], axis=1)
    low, high = ids & (wide - 1), ids >> (wide.bit_length() - 1)
    spots = lax.broadcasted_iota(jnp.int32, (wide, nodes), 0)
    ones = jnp.where(spots == low, 1.0, 0.0).astype(jnp.bfloat16)
    for term in range(3):
        right_ref[term * wide : (term + 1) * wide, :] = ones
    found = jnp.zeros((ntab, nodes), jnp.float32)
    step = blocks // len(table_copies)
    for at, copy in enumerate(table_copies):
        copy.wait()
        for block in range(at * step, (at + 1) * step):
            pieces = split_bf16(tables_ref[:, block * wide : (block + 1) * wide], 3)
            left_ref[block * ntab : (block + 1) * ntab, :] = jnp.concatenate(pieces, axis=1)
        rows = left_ref[at * step * ntab : (at + 1) * step * ntab, :]
        picked = jnp.dot(rows, right_ref[...], preferred_element_type=jnp.float32)
        for block in range(step):
            part = picked[block * ntab : (block + 1) * ntab]
            found = jnp.where(high == at * step + block, part, found)
    return found


def chebyshev_coefs(bins_ref):
    shape = (DEGREES, DEGREES)
    degree = lax.broadcasted_iota(jnp.int32, shape, 0)
    node = lax.broadcasted_iota(jnp.int32, shape, 1)
    period = 4 * DEGREES
    weight, _ = cos_sin((degree * (2 * node + 1) & (period - 1)).astype(jnp.float32) * (1.0 / period))
    weight = weight * jnp.where(degree == 0, 1.0 / DEGREES, 2.0 / DEGREES)
    even = jnp.where(degree % 2 == 0, weight, 0.0)
    odd = jnp.where(degree % 2 == 1, weight, 0.0)
    row = bins_ref[...].astype(jnp.float32)
    bins = jnp.concatenate([row] * (LANES // NF), axis=1)
    at = lax.broadcasted_iota(jnp.int32, (DEGREES, LANES), 0).astype(jnp.float32)
    spot, _ = cos_sin((2.0 * at + 1.0) * (1.0 / period))
    cosine, sine = cos_sin(bins * (spot * (REACH / 256.0)))
    dot = functools.partial(jnp.dot, precision=lax.Precision.HIGHEST, preferred_element_type=jnp.float32)
    return dot(even, cosine) + dot(odd, sine)


def station_plan(table_row, width):
    count = table_row.shape[1]
    shape = (count, count)
    here = lax.broadcasted_iota(jnp.int32, shape, 0)
    there = lax.broadcasted_iota(jnp.int32, shape, 1)
    column_of = lambda row: jnp.sum(jnp.where(here == there, jnp.broadcast_to(row, shape), 0), axis=1, keepdims=True)
    table_column = column_of(table_row)
    same = (table_column == table_row) & (here < there)
    within = jnp.sum(jnp.where(same, 1, 0), axis=0, keepdims=True)
    place_row = within
    spot = jnp.zeros((1, 1), jnp.int32)
    held = jnp.zeros((1, 1), jnp.int32)
    for table in range(NTAB):
        size = jnp.sum(jnp.where(table_row == table, 1, 0), axis=1, keepdims=True)
        some = size > 0
        edge = (spot & 7) == 0
        skip = some & (held >= 2) & ~edge
        spot = jnp.where(skip, (spot + 7) >> 3 << 3, spot)
        held = jnp.where(skip | edge, 0, held)
        after = spot + size
        place_row = place_row + jnp.where(table_row == table, spot, 0)
        held = jnp.where(some, jnp.where(after >> 3 == spot >> 3, held + 1, 1), held)
        spot = after
    groups = (spot + 7) >> 3
    place_column = column_of(place_row)
    group = lax.broadcasted_iota(jnp.int32, (count, width), 1)
    inside = place_column >> 3 == group
    first = jnp.sum(jnp.where(place_column == group * 8, table_column, 0), axis=0, keepdims=True)
    last = jnp.max(jnp.where(inside, table_column, 0), axis=0, keepdims=True)
    length = jnp.sum(jnp.where(inside & (table_column == first), 1, 0), axis=0, keepdims=True)
    rows = [first, last, length, jnp.broadcast_to(groups, (1, width))]
    if width > count:
        place_row = jnp.concatenate([place_row, jnp.zeros((1, width - count), jnp.int32)], axis=1)
    rows += [place_row, jnp.zeros((3, width), jnp.int32)]
    return jnp.concatenate(rows, axis=0).astype(jnp.float32)


def packed_rows(ntab):
    ends = [ntab * NF, 2 * ntab * NF, 2 * ntab * NF + DEGREES, 2 * ntab * NF + DEGREES + 8]
    return [slice(start, end) for start, end in zip([0] + ends, ends)]


def prepare_kernel(bins_hbm, table_hbm, ids_hbm, tables_hbm, out_hbm, *rest):
    bins_ref, table_ref, ids_ref, tables_ref, cos_ref, sin_ref, coef_ref, plan_ref = rest[:8]
    left_ref, right_ref, sems, table_sems = rest[8:]
    ntab = tables_ref.shape[0]
    nodes = cos_ref.shape[1]
    near = ids_ref.shape[0]
    first = pl.multiple_of(own_place() * (nodes // LANES) // near * near, 8)
    ins = start_all(
        [
            pltpu.make_async_copy(ids_hbm.at[pl.ds(first, near), :], ids_ref, sems.at[0]),
            pltpu.make_async_copy(bins_hbm, bins_ref, sems.at[1]),
            pltpu.make_async_copy(table_hbm, table_ref, sems.at[2]),
        ]
    )
    piece = tables_ref.shape[1] // TABLE_PIECES
    table_copies = []
    for at in range(TABLE_PIECES):
        part = (slice(None), pl.ds(at * piece, piece))
        table_copies.append(pltpu.make_async_copy(tables_hbm.at[part], tables_ref.at[part], table_sems.at[at]))
    start_all(table_copies)
    for copy in ins:
        copy.wait()
    cos_at, sin_at, coef_at, plan_at = packed_rows(ntab)
    coef_ref[...] = chebyshev_coefs(bins_ref)
    plan_ref[...] = station_plan(table_ref[...], plan_ref.shape[1])
    outs = start_all(
        [
            pltpu.make_async_copy(coef_ref, out_hbm.at[coef_at, pl.ds(0, LANES)], sems.at[0]),
            pltpu.make_async_copy(plan_ref, out_hbm.at[plan_at, pl.ds(0, plan_ref.shape[1])], sems.at[1]),
        ]
    )
    turns = pick_columns(ids_ref, tables_ref, table_copies, nodes, left_ref, right_ref) * (1.0 / 256.0)
    bins = bins_column(bins_ref)
    for table in range(ntab):
        cosine, sine = cos_sin(bins * turns[table : table + 1])
        at = pl.ds(table * NF, NF)
        cos_ref[at, :] = cosine
        sin_ref[at, :] = sine
        outs += start_all(
            [
                pltpu.make_async_copy(
                    cos_ref.at[at, :], out_hbm.at[pl.ds(cos_at.start + table * NF, NF), pl.ds(0, nodes)],
                    sems.at[3 + 2 * table],
                ),
                pltpu.make_async_copy(
                    sin_ref.at[at, :], out_hbm.at[pl.ds(sin_at.start + table * NF, NF), pl.ds(0, nodes)],
                    sems.at[4 + 2 * table],
                ),
            ]
        )
    for copy in outs:
        copy.wait()


def image_kernel(merged, stations_dev, packed_hbm, block_ref, *rest):
    corr_ref, rest = (None, rest) if merged else (rest[0], rest[1:])
    keep_ref, send_ref, plan_ref, place_of_ref, coef_ref, cos_ref, sin_ref, sems = rest[:8]
    place_ref, weight_ref, left_ref, sums_ref, basis_a, basis_b = rest[8:]
    places, nodes = place_ref.shape
    windows, groups, cores = (lax.axis_size(a) for a in ("win", "sta", "freq"))
    stations = stations_dev * groups
    cos_at, sin_at, coef_at, plan_at = packed_rows(cos_ref.shape[0] // NF)
    width = plan_ref.shape[1]
    copies = start_all(
        [
            pltpu.make_async_copy(packed_hbm.at[plan_at, pl.ds(0, width)], place_of_ref, sems.at[0]),
            pltpu.make_async_copy(packed_hbm.at[plan_at, pl.ds(0, width)], plan_ref, sems.at[1]),
            pltpu.make_async_copy(packed_hbm.at[coef_at, pl.ds(0, LANES)], coef_ref, sems.at[2]),
            pltpu.make_async_copy(packed_hbm.at[cos_at, pl.ds(0, nodes)], cos_ref, sems.at[3]),
            pltpu.make_async_copy(packed_hbm.at[sin_at, pl.ds(0, nodes)], sin_ref, sems.at[4]),
        ]
    )
    height = block_ref.shape[1]
    rows_of = lambda win, core: [(win * groups + group) * cores + core for group in range(groups)]

    even, odd = [], []
    for win in range(windows):
        value = []
        for group in range(groups):
            tile = None
            for core in range(cores):
                part = block_ref[(win * groups + group) * cores + core, height - 8 :, :].astype(jnp.float32)
                tile = part if tile is None else tile + part
            tile = tile[:, : LANES // 2] + tile[:, LANES // 2 :]
            value += [tile[:, 2 * NF * piece : 2 * NF * (piece + 1)] for piece in range(stations_dev // 8)]
        value = jnp.concatenate(value, axis=0)
        even.append(value)
        odd.append(jnp.concatenate([-value[:, NF:], value[:, :NF]], axis=1))
    spectra = jnp.concatenate(even + odd, axis=1)
    if merged:
        parts = []
        for win in range(windows):
            for core in range(cores):
                for first in range(0, height - 8, stations_dev):
                    rows = [block_ref[at, first : first + stations_dev, :] for at in rows_of(win, core)]
                    parts.append(jnp.concatenate(rows, axis=0))
        corr = jnp.concatenate(parts, axis=1)
    else:
        corr = corr_ref[...]

    copies[0].wait()
    place_row = place_of_ref[4:5, :stations].astype(jnp.int32)
    sorter = lax.broadcasted_iota(jnp.int32, (places, stations), 0) == place_row
    sorter = jnp.where(sorter, 1.0, 0.0).astype(jnp.bfloat16)
    found = None
    for piece in split_bf16(spectra, 3):
        part = jnp.dot(sorter, piece, preferred_element_type=jnp.float32)
        found = part if found is None else found + part
    weight_ref[...] = found
    place_ref[...] = jnp.dot(sorter, corr, preferred_element_type=jnp.float32) * (1.0 / REACH)
    sums_ref[...] = jnp.zeros_like(sums_ref)
    chunk = min(256, nodes)
    depth = DEGREES * 8
    lanes = windows * 2 * NF
    for copy in copies[1:3]:
        copy.wait()

    def make_left(pair):
        top = weight_ref[pl.ds(pl.multiple_of(pair * 16, 16), 8), :]
        bottom = weight_ref[pl.ds(pl.multiple_of(pair * 16 + 8, 8), 8), :]
        sides = [
            jnp.concatenate([top[:, :lanes], bottom[:, :lanes]], axis=1),
            jnp.concatenate([top[:, lanes:], bottom[:, lanes:]], axis=1),
        ]
        per = LANES // 8
        for half in range(DEGREES // per):
            tall = jnp.concatenate(
                [sides[k % 2] * coef_ref[k : k + 1, :] for k in range(half * per, (half + 1) * per)], axis=0
            )
            at = slice(half * LANES, (half + 1) * LANES)
            for term, value in enumerate(split_bf16(tall.T, 2)):
                left_ref[2 * pair, term * lanes : (term + 1) * lanes, at] = value[:lanes]
                left_ref[2 * pair + 1, term * lanes : (term + 1) * lanes, at] = value[lanes:]

    used = plan_ref[3, 0].astype(jnp.int32)
    sure = stations // 16
    if sure <= 8:
        for pair in range(sure):
            make_left(pair)
    else:
        lax.fori_loop(0, sure, lambda pair, carry: (make_left(pair), carry)[1], 0)
    lax.fori_loop(sure, (used + 1) // 2, lambda pair, carry: (make_left(pair), carry)[1], 0)
    spot = (lax.broadcasted_iota(jnp.int32, (16, depth), 1) & 7).astype(jnp.float32)

    def left_of(group):
        mask = spot < plan_ref[2, group]
        results = []
        for keep, drop in ((1.0, 0.0), (0.0, 1.0)):
            side = jnp.where(mask, keep, drop).astype(jnp.bfloat16)
            results.append(left_ref[group] * jnp.concatenate([side] * (2 * lanes // 16), axis=0))
        high = jnp.concatenate([result[:lanes] for result in results], axis=0)
        low = jnp.concatenate([result[lanes:] for result in results], axis=0)
        return jnp.concatenate([high, high, low], axis=1)

    def basis_steps(group, basis_ref):
        arg = place_ref[pl.ds(pl.multiple_of(group * 8, 8), 8), :]
        twice = arg + arg
        before, now = jnp.ones_like(arg), arg
        for degree in range(0, DEGREES, 2):
            pair = jnp.concatenate([before, now], axis=0)
            high, low = split_bf16(pair, 2)
            basis_ref[degree * 8 : degree * 8 + 16, :] = high
            basis_ref[depth + degree * 8 : depth + degree * 8 + 16, :] = low
            before = twice * now - before
            now = twice * before - now
            if degree % 8 == 6:
                yield

    def run(steps):
        for _ in steps:
            pass

    def add_group(group, basis_ref, steps):
        left = left_of(group)
        tables = [plan_ref[slot, group].astype(jnp.int32) for slot in range(2)]
        phasor_rows = [pl.ds(pl.multiple_of(table * NF, NF), NF) for table in tables]
        for first in range(0, nodes, chunk):
            at = slice(first, first + chunk)
            right = jnp.concatenate([basis_ref[:, at], basis_ref[:depth, at]], axis=0)
            got = jnp.dot(left, right, preferred_element_type=jnp.float32)
            next(steps, None)
            for win in range(windows):
                row = win * 2 * NF
                real_sum, imag_sum = sums_ref[row : row + NF, at], sums_ref[row + NF : row + 2 * NF, at]
                for slot, rows in enumerate(phasor_rows):
                    cosine, sine = cos_ref[rows, at], sin_ref[rows, at]
                    real = got[slot * lanes + row : slot * lanes + row + NF]
                    imag = got[slot * lanes + row + NF : slot * lanes + row + 2 * NF]
                    real_sum += real * cosine - imag * sine
                    imag_sum += real * sine + imag * cosine
                sums_ref[row : row + NF, at], sums_ref[row + NF : row + 2 * NF, at] = real_sum, imag_sum
        run(steps)

    run(basis_steps(0, basis_a))
    for copy in copies[3:]:
        copy.wait()

    def body(pair, carry):
        group = pair * 2
        add_group(group, basis_a, basis_steps(group + 1, basis_b))
        add_group(group + 1, basis_b, basis_steps(jnp.minimum(group + 2, places // 8 - 1), basis_a))
        return carry

    lax.fori_loop(0, (used + 1) // 2, body, 0)
    powers = []
    for win in range(windows):
        row = win * 2 * NF
        real, imag = sums_ref[row : row + NF, :], sums_ref[row + NF : row + 2 * NF, :]
        powers.append(real * real + imag * imag)
    mine = lax.axis_index("win") == 0
    keep_ref[...] = jnp.where(mine, powers[0], powers[1])
    send_ref[...] = jnp.where(mine, powers[1], powers[0])


def finish_kernel(stations, keep_ref, got_ref, spectrum_ref, beam_ref):
    nodes = keep_ref.shape[1]
    win = lax.axis_index("win")
    for place, ref in ((win, keep_ref), (1 - win, got_ref)):
        power = ref[...]
        total = jnp.sum(power, axis=0, keepdims=True)
        at = pl.ds(pl.multiple_of(place * nodes, LANES), nodes)
        spectrum_ref[:, at] = power * (NF / total)
        beam_ref[:, at] = total * (1.0 / (NF * stations))


def on_device(traces, tables, corrections, station_table, node_ids, freq_bins):
    windows, groups, cores = (lax.axis_size(a) for a in ("win", "sta", "freq"))
    stations_dev, grid = corrections.shape
    stations = stations_dev * groups
    devices = windows * groups * cores
    nodes = grid // devices
    ntab = tables.shape[0]
    params = lambda free: pltpu.CompilerParams(vmem_limit_bytes=VMEM_LIMIT - free)
    vmem = pl.BlockSpec(memory_space=pltpu.VMEM)
    hbm = pl.BlockSpec(memory_space=pltpu.HBM)
    bins = freq_bins.reshape(1, NF)
    bins_scratch = pltpu.VMEM((1, NF), jnp.int32)

    holders = windows * cores
    merged = nodes % (holders * LANES) == 0
    pieces = nodes // (holders * LANES) if merged else 0
    height = pieces * stations_dev + 8
    blocks = pl.pallas_call(
        functools.partial(send_kernel, nodes),
        out_shape=jax.ShapeDtypeStruct((devices, height, LANES), jnp.bfloat16),
        in_specs=[hbm] * 3,
        out_specs=vmem,
        scratch_shapes=[
            bins_scratch,
            pltpu.VMEM(traces.shape, traces.dtype),
            pltpu.SemaphoreType.DMA((2 + devices * max(pieces, 1),)),
        ],
        compiler_params=params(0),
        name="send",
    )(bins, traces, corrections)
    received = [lax.all_to_all(blocks, ("win", "sta", "freq"), split_axis=0, concat_axis=0, tiled=True)]
    if not merged:
        parts = corrections.reshape(stations_dev, groups, holders, nodes)
        place = lax.axis_index("freq") * windows + lax.axis_index("win")
        mine = lax.dynamic_index_in_dim(parts, place, axis=2, keepdims=False)
        corr = lax.all_to_all(mine.transpose(1, 0, 2), "sta", split_axis=0, concat_axis=0, tiled=True)
        received.append(corr.reshape(stations, nodes))

    wide = 512
    plan_width = max(LANES, stations)
    phasors = pltpu.VMEM((ntab * NF, nodes), jnp.float32)
    coefs = pltpu.VMEM((DEGREES, LANES), jnp.float32)
    plan = pltpu.VMEM((8, plan_width), jnp.float32)
    packed_shape = (packed_rows(ntab)[-1].stop, max(nodes, plan_width))
    packed = pl.pallas_call(
        prepare_kernel,
        out_shape=jax.ShapeDtypeStruct(packed_shape, jnp.float32),
        in_specs=[hbm] * 4,
        out_specs=hbm,
        scratch_shapes=[
            bins_scratch,
            pltpu.VMEM((1, stations), jnp.int32),
            pltpu.VMEM((max(nodes // LANES, 8), LANES), jnp.int32),
            pltpu.VMEM(tables.shape, tables.dtype),
            phasors,
            phasors,
            coefs,
            plan,
            pltpu.VMEM((grid // wide * ntab, 3 * wide), jnp.bfloat16),
            pltpu.VMEM((3 * wide, nodes), jnp.bfloat16),
            pltpu.SemaphoreType.DMA((3 + 2 * ntab,)),
            pltpu.SemaphoreType.DMA((TABLE_PIECES,)),
        ],
        compiler_params=params(blocks.size * 2 + 16 * 1024),
        name="prepare",
    )(bins, station_table.reshape(1, stations), node_ids.reshape(grid // LANES, LANES), tables)

    places = (stations // 8 + ntab // 2 + 2) // 2 * 16
    half = jax.ShapeDtypeStruct((NF, nodes), jnp.float32)
    rows = 2 * windows * 2 * NF
    basis = pltpu.VMEM((2 * DEGREES * 8, nodes), jnp.bfloat16)
    keep, send = pl.pallas_call(
        functools.partial(image_kernel, merged, stations_dev),
        out_shape=[half, half],
        in_specs=[hbm] + [vmem] * len(received),
        out_specs=[vmem, vmem],
        scratch_shapes=[
            pltpu.SMEM((8, plan_width), jnp.float32),
            plan,
            coefs,
            phasors,
            phasors,
            pltpu.SemaphoreType.DMA((5,)),
            pltpu.VMEM((places, nodes), jnp.float32),
            pltpu.VMEM((places, rows), jnp.float32),
            pltpu.VMEM((places // 8, rows, DEGREES * 8), jnp.bfloat16),
            pltpu.VMEM((rows // 2, nodes), jnp.float32),
            basis,
            basis,
        ],
        compiler_params=params(blocks.size * 2 + half.size * 8 + 16 * 1024),
        name="image",
    )(packed, *received)
    got = lax.ppermute(send, "win", [(0, 1), (1, 0)])
    spectrum, beam_power = pl.pallas_call(
        functools.partial(finish_kernel, stations),
        out_shape=[
            jax.ShapeDtypeStruct((NF, windows * nodes), jnp.float32),
            jax.ShapeDtypeStruct((1, windows * nodes), jnp.float32),
        ],
        in_specs=[vmem, vmem],
        out_specs=[vmem, vmem],
        compiler_params=params(32 * 1024 * 1024),
        name="finish",
    )(keep, got)
    return spectrum, beam_power.reshape(windows * nodes)


def solution(mesh):
    return jax.shard_map(
        on_device,
        mesh=mesh,
        in_specs=(P(("win", "sta"), "freq"), P(), P("sta", None), P(), P(), P()),
        out_specs=(P("win", ("sta", "freq")), P(("win", "sta", "freq"))),
        check_vma=False,
    )
```

```python
import functools
import math

import jax
import jax.numpy as jnp
import numpy as np
from jax import lax
from jax.experimental import pallas as pl
from jax.experimental.pallas import tpu as pltpu
from jax.sharding import PartitionSpec as P

NT = 5120
NF = 16
NTAB = 16
LANES = 128
DEGREES = 32
REACH = 1.5
TABLE_PIECES = 4
VMEM_LIMIT = 64 * 1024 * 1024 - 64 * 1024


def chebyshev_fit(func, degree, low, high):
    fit = np.polynomial.chebyshev.Chebyshev.interpolate(func, degree, domain=[low, high])
    return [float(v) for v in fit.convert(kind=np.polynomial.Polynomial).coef]


SIN_HALF = chebyshev_fit(lambda z: np.pi * np.sinc(np.sqrt(z)), 4, 0.0, 0.25)
COS_HALF = chebyshev_fit(lambda z: np.cos(np.pi * np.sqrt(z)), 4, 0.0, 0.25)


def horner(coefs, arg):
    total = coefs[-1]
    for coef in coefs[-2::-1]:
        total = total * arg + coef
    return total


def turn_parts(rest):
    square = rest * rest
    root = math.sqrt(2.0)
    sine_half = rest * horner([root * c for c in SIN_HALF], square)
    cos_half = horner([root * c for c in COS_HALF], square)
    return sine_half * sine_half, sine_half * cos_half


def cos_sin(turns):
    versine, sine = turn_parts(turns - jnp.round(turns))
    return 1.0 - versine, sine


def bins_column(bins_ref):
    rows = lax.broadcasted_iota(jnp.int32, (NF, NF), 0)
    lanes = lax.broadcasted_iota(jnp.int32, (NF, NF), 1)
    square = jnp.broadcast_to(bins_ref[...].astype(jnp.float32), (NF, NF))
    return jnp.sum(jnp.where(rows == lanes, square, 0.0), axis=1, keepdims=True)


def split_bf16(value, terms):
    pieces = []
    for term in range(terms):
        piece = value.astype(jnp.bfloat16)
        pieces.append(piece)
        if term < terms - 1:
            value = value - piece.astype(jnp.float32)
    return pieces


def start_all(copies):
    for copy in copies:
        copy.start()
    return copies


def send_kernel(nodes, bins_hbm, traces_hbm, corr_hbm, out_ref, bins_ref, traces_ref, sems):
    devices, height, _ = out_ref.shape
    stations_dev, half_length = traces_ref.shape
    pieces = (height - 8) // stations_dev
    windows, groups, cores = (lax.axis_size(a) for a in ("win", "sta", "freq"))
    place = lax.axis_index("win") * cores + lax.axis_index("freq")
    small = start_all(
        [
            pltpu.make_async_copy(bins_hbm, bins_ref, sems.at[0]),
            pltpu.make_async_copy(traces_hbm, traces_ref, sems.at[1]),
        ]
    )
    copies = []
    for dev in range(devices):
        win, sta, core = dev // (groups * cores), dev // cores % groups, dev % cores
        first = ((sta * cores + core) * windows + win) * nodes
        for piece in range(pieces):
            at = pl.multiple_of(first + (place * pieces + piece) * LANES, LANES)
            to = out_ref.at[dev, pl.ds(piece * stations_dev, stations_dev), :]
            sem = sems.at[2 + dev * pieces + piece]
            copies.append(pltpu.make_async_copy(corr_hbm.at[:, pl.ds(at, LANES)], to, sem))
    start_all(copies)
    start = lax.axis_index("freq") * half_length
    small[0].wait()
    bins = bins_column(bins_ref)
    pos = (start + lax.broadcasted_iota(jnp.int32, (NF, half_length), 1)).astype(jnp.float32)
    product = bins * pos
    turns = jnp.round(product * (1.0 / NT))
    rest = (product - turns * NT) * (1.0 / NT)
    versine, sine = turn_parts(rest)
    scale = 1.0 / math.sqrt(NT)
    table = jnp.concatenate([(1.0 - versine) * scale, sine * -scale], axis=0)
    both = jnp.concatenate(split_bf16(table, 2), axis=0)
    small[1].wait()
    sums = lax.dot_general(
        traces_ref[...], both, (((1,), (1,)), ((), ())), preferred_element_type=jnp.float32
    )
    sums = sums[:, : 2 * NF] + sums[:, 2 * NF :]
    terms = [term.astype(jnp.float32) for term in split_bf16(sums, 2)]
    tile = jnp.concatenate([term[at : at + 8] for term in terms for at in range(0, stations_dev, 8)], axis=1)
    tile = tile.astype(jnp.bfloat16)
    for dev in range(devices):
        out_ref[dev, height - 8 :, :] = tile
    for copy in copies:
        copy.wait()


def own_place():
    windows, cores = lax.axis_size("win"), lax.axis_size("freq")
    return (lax.axis_index("sta") * cores + lax.axis_index("freq")) * windows + lax.axis_index("win")


def pick_columns(ids_ref, tables_ref, table_copies, nodes, left_ref, right_ref):
    ntab, grid = tables_ref.shape
    count = nodes // LANES
    wide = right_ref.shape[0] // 3
    blocks = grid // wide
    ids = ids_ref[pl.ds(own_place() * count % ids_ref.shape[0], count), :]
    ids = jnp.concatenate([ids[at : at + 1] for at in range(count)], axis=1)
    low, high = ids & (wide - 1), ids >> (wide.bit_length() - 1)
    spots = lax.broadcasted_iota(jnp.int32, (wide, nodes), 0)
    ones = jnp.where(spots == low, 1.0, 0.0).astype(jnp.bfloat16)
    for term in range(3):
        right_ref[term * wide : (term + 1) * wide, :] = ones
    found = jnp.zeros((ntab, nodes), jnp.float32)
    step = blocks // len(table_copies)
    for at, copy in enumerate(table_copies):
        copy.wait()
        for block in range(at * step, (at + 1) * step):
            pieces = split_bf16(tables_ref[:, block * wide : (block + 1) * wide], 3)
            left_ref[block * ntab : (block + 1) * ntab, :] = jnp.concatenate(pieces, axis=1)
        rows = left_ref[at * step * ntab : (at + 1) * step * ntab, :]
        picked = jnp.dot(rows, right_ref[...], preferred_element_type=jnp.float32)
        for block in range(step):
            part = picked[block * ntab : (block + 1) * ntab]
            found = jnp.where(high == at * step + block, part, found)
    return found


def chebyshev_coefs(bins_ref):
    shape = (DEGREES, DEGREES)
    degree = lax.broadcasted_iota(jnp.int32, shape, 0)
    node = lax.broadcasted_iota(jnp.int32, shape, 1)
    period = 4 * DEGREES
    weight, _ = cos_sin((degree * (2 * node + 1) & (period - 1)).astype(jnp.float32) * (1.0 / period))
    weight = weight * jnp.where(degree == 0, 1.0 / DEGREES, 2.0 / DEGREES)
    even = jnp.where(degree % 2 == 0, weight, 0.0)
    odd = jnp.where(degree % 2 == 1, weight, 0.0)
    row = bins_ref[...].astype(jnp.float32)
    bins = jnp.concatenate([row] * (LANES // NF), axis=1)
    at = lax.broadcasted_iota(jnp.int32, (DEGREES, LANES), 0).astype(jnp.float32)
    spot, _ = cos_sin((2.0 * at + 1.0) * (1.0 / period))
    cosine, sine = cos_sin(bins * (spot * (REACH / 256.0)))
    dot = functools.partial(jnp.dot, precision=lax.Precision.HIGHEST, preferred_element_type=jnp.float32)
    return dot(even, cosine) + dot(odd, sine)


def station_plan(table_row, width):
    count = table_row.shape[1]
    shape = (count, count)
    here = lax.broadcasted_iota(jnp.int32, shape, 0)
    there = lax.broadcasted_iota(jnp.int32, shape, 1)
    column_of = lambda row: jnp.sum(jnp.where(here == there, jnp.broadcast_to(row, shape), 0), axis=1, keepdims=True)
    table_column = column_of(table_row)
    same = (table_column == table_row) & (here < there)
    within = jnp.sum(jnp.where(same, 1, 0), axis=0, keepdims=True)
    place_row = within
    spot = jnp.zeros((1, 1), jnp.int32)
    held = jnp.zeros((1, 1), jnp.int32)
    for table in range(NTAB):
        size = jnp.sum(jnp.where(table_row == table, 1, 0), axis=1, keepdims=True)
        some = size > 0
        edge = (spot & 7) == 0
        skip = some & (held >= 2) & ~edge
        spot = jnp.where(skip, (spot + 7) >> 3 << 3, spot)
        held = jnp.where(skip | edge, 0, held)
        after = spot + size
        place_row = place_row + jnp.where(table_row == table, spot, 0)
        held = jnp.where(some, jnp.where(after >> 3 == spot >> 3, held + 1, 1), held)
        spot = after
    groups = (spot + 7) >> 3
    place_column = column_of(place_row)
    group = lax.broadcasted_iota(jnp.int32, (count, width), 1)
    inside = place_column >> 3 == group
    first = jnp.sum(jnp.where(place_column == group * 8, table_column, 0), axis=0, keepdims=True)
    last = jnp.max(jnp.where(inside, table_column, 0), axis=0, keepdims=True)
    length = jnp.sum(jnp.where(inside & (table_column == first), 1, 0), axis=0, keepdims=True)
    rows = [first, last, length, jnp.broadcast_to(groups, (1, width))]
    if width > count:
        place_row = jnp.concatenate([place_row, jnp.zeros((1, width - count), jnp.int32)], axis=1)
    rows += [place_row, jnp.zeros((3, width), jnp.int32)]
    return jnp.concatenate(rows, axis=0).astype(jnp.float32)


def packed_rows(ntab):
    ends = [ntab * NF, 2 * ntab * NF, 2 * ntab * NF + DEGREES, 2 * ntab * NF + DEGREES + 8]
    return [slice(start, end) for start, end in zip([0] + ends, ends)]


def prepare_kernel(bins_hbm, table_hbm, ids_hbm, tables_hbm, out_hbm, *rest):
    bins_ref, table_ref, ids_ref, tables_ref, cos_ref, sin_ref, coef_ref, plan_ref = rest[:8]
    left_ref, right_ref, sems, table_sems = rest[8:]
    ntab = tables_ref.shape[0]
    nodes = cos_ref.shape[1]
    near = ids_ref.shape[0]
    first = pl.multiple_of(own_place() * (nodes // LANES) // near * near, 8)
    ins = start_all(
        [
            pltpu.make_async_copy(ids_hbm.at[pl.ds(first, near), :], ids_ref, sems.at[0]),
            pltpu.make_async_copy(bins_hbm, bins_ref, sems.at[1]),
            pltpu.make_async_copy(table_hbm, table_ref, sems.at[2]),
        ]
    )
    piece = tables_ref.shape[1] // TABLE_PIECES
    table_copies = []
    for at in range(TABLE_PIECES):
        part = (slice(None), pl.ds(at * piece, piece))
        table_copies.append(pltpu.make_async_copy(tables_hbm.at[part], tables_ref.at[part], table_sems.at[at]))
    start_all(table_copies)
    for copy in ins:
        copy.wait()
    cos_at, sin_at, coef_at, plan_at = packed_rows(ntab)
    coef_ref[...] = chebyshev_coefs(bins_ref)
    plan_ref[...] = station_plan(table_ref[...], plan_ref.shape[1])
    outs = start_all(
        [
            pltpu.make_async_copy(coef_ref, out_hbm.at[coef_at, pl.ds(0, LANES)], sems.at[0]),
            pltpu.make_async_copy(plan_ref, out_hbm.at[plan_at, pl.ds(0, plan_ref.shape[1])], sems.at[1]),
        ]
    )
    turns = pick_columns(ids_ref, tables_ref, table_copies, nodes, left_ref, right_ref) * (1.0 / 256.0)
    bins = bins_column(bins_ref)
    for table in range(ntab):
        cosine, sine = cos_sin(bins * turns[table : table + 1])
        at = pl.ds(table * NF, NF)
        cos_ref[at, :] = cosine
        sin_ref[at, :] = sine
        outs += start_all(
            [
                pltpu.make_async_copy(
                    cos_ref.at[at, :], out_hbm.at[pl.ds(cos_at.start + table * NF, NF), pl.ds(0, nodes)],
                    sems.at[3 + 2 * table],
                ),
                pltpu.make_async_copy(
                    sin_ref.at[at, :], out_hbm.at[pl.ds(sin_at.start + table * NF, NF), pl.ds(0, nodes)],
                    sems.at[4 + 2 * table],
                ),
            ]
        )
    for copy in outs:
        copy.wait()


def image_kernel(merged, stations_dev, packed_hbm, block_ref, *rest):
    corr_ref, rest = (None, rest) if merged else (rest[0], rest[1:])
    keep_ref, send_ref, plan_ref, place_of_ref, coef_ref, cos_ref, sin_ref, sems = rest[:8]
    place_ref, weight_ref, left_ref, sums_ref, basis_a, basis_b = rest[8:]
    places, nodes = place_ref.shape
    windows, groups, cores = (lax.axis_size(a) for a in ("win", "sta", "freq"))
    stations = stations_dev * groups
    cos_at, sin_at, coef_at, plan_at = packed_rows(cos_ref.shape[0] // NF)
    width = plan_ref.shape[1]
    copies = start_all(
        [
            pltpu.make_async_copy(packed_hbm.at[plan_at, pl.ds(0, width)], place_of_ref, sems.at[0]),
            pltpu.make_async_copy(packed_hbm.at[plan_at, pl.ds(0, width)], plan_ref, sems.at[1]),
            pltpu.make_async_copy(packed_hbm.at[coef_at, pl.ds(0, LANES)], coef_ref, sems.at[2]),
            pltpu.make_async_copy(packed_hbm.at[cos_at, pl.ds(0, nodes)], cos_ref, sems.at[3]),
            pltpu.make_async_copy(packed_hbm.at[sin_at, pl.ds(0, nodes)], sin_ref, sems.at[4]),
        ]
    )
    height = block_ref.shape[1]
    rows_of = lambda win, core: [(win * groups + group) * cores + core for group in range(groups)]

    even, odd = [], []
    for win in range(windows):
        value = []
        for group in range(groups):
            tile = None
            for core in range(cores):
                part = block_ref[(win * groups + group) * cores + core, height - 8 :, :].astype(jnp.float32)
                tile = part if tile is None else tile + part
            tile = tile[:, : LANES // 2] + tile[:, LANES // 2 :]
            value += [tile[:, 2 * NF * piece : 2 * NF * (piece + 1)] for piece in range(stations_dev // 8)]
        value = jnp.concatenate(value, axis=0)
        even.append(value)
        odd.append(jnp.concatenate([-value[:, NF:], value[:, :NF]], axis=1))
    spectra = jnp.concatenate(even + odd, axis=1)
    if merged:
        parts = []
        for win in range(windows):
            for core in range(cores):
                for first in range(0, height - 8, stations_dev):
                    rows = [block_ref[at, first : first + stations_dev, :] for at in rows_of(win, core)]
                    parts.append(jnp.concatenate(rows, axis=0))
        corr = jnp.concatenate(parts, axis=1)
    else:
        corr = corr_ref[...]

    copies[0].wait()
    place_row = place_of_ref[4:5, :stations].astype(jnp.int32)
    sorter = lax.broadcasted_iota(jnp.int32, (places, stations), 0) == place_row
    sorter = jnp.where(sorter, 1.0, 0.0).astype(jnp.bfloat16)
    found = None
    for piece in split_bf16(spectra, 3):
        part = jnp.dot(sorter, piece, preferred_element_type=jnp.float32)
        found = part if found is None else found + part
    weight_ref[...] = found
    place_ref[...] = jnp.dot(sorter, corr, preferred_element_type=jnp.float32) * (1.0 / REACH)
    sums_ref[...] = jnp.zeros_like(sums_ref)
    chunk = min(256, nodes)
    depth = DEGREES * 8
    lanes = windows * 2 * NF
    for copy in copies[1:3]:
        copy.wait()

    def make_left(pair):
        top = weight_ref[pl.ds(pl.multiple_of(pair * 16, 16), 8), :]
        bottom = weight_ref[pl.ds(pl.multiple_of(pair * 16 + 8, 8), 8), :]
        sides = [
            jnp.concatenate([top[:, :lanes], bottom[:, :lanes]], axis=1),
            jnp.concatenate([top[:, lanes:], bottom[:, lanes:]], axis=1),
        ]
        per = LANES // 8
        for half in range(DEGREES // per):
            tall = jnp.concatenate(
                [sides[k % 2] * coef_ref[k : k + 1, :] for k in range(half * per, (half + 1) * per)], axis=0
            )
            at = slice(half * LANES, (half + 1) * LANES)
            for term, value in enumerate(split_bf16(tall.T, 2)):
                left_ref[2 * pair, term * lanes : (term + 1) * lanes, at] = value[:lanes]
                left_ref[2 * pair + 1, term * lanes : (term + 1) * lanes, at] = value[lanes:]

    used = plan_ref[3, 0].astype(jnp.int32)
    sure = stations // 16
    if sure <= 8:
        for pair in range(sure):
            make_left(pair)
    else:
        lax.fori_loop(0, sure, lambda pair, carry: (make_left(pair), carry)[1], 0)
    lax.fori_loop(sure, (used + 1) // 2, lambda pair, carry: (make_left(pair), carry)[1], 0)
    spot = (lax.broadcasted_iota(jnp.int32, (16, depth), 1) & 7).astype(jnp.float32)

    def left_of(group):
        mask = spot < plan_ref[2, group]
        results = []
        for keep, drop in ((1.0, 0.0), (0.0, 1.0)):
            side = jnp.where(mask, keep, drop).astype(jnp.bfloat16)
            results.append(left_ref[group] * jnp.concatenate([side] * (2 * lanes // 16), axis=0))
        high = jnp.concatenate([result[:lanes] for result in results], axis=0)
        low = jnp.concatenate([result[lanes:] for result in results], axis=0)
        return jnp.concatenate([high, high, low], axis=1)

    def basis_steps(group, basis_ref):
        arg = place_ref[pl.ds(pl.multiple_of(group * 8, 8), 8), :]
        twice = arg + arg
        before, now = jnp.ones_like(arg), arg
        for degree in range(0, DEGREES, 2):
            pair = jnp.concatenate([before, now], axis=0)
            high, low = split_bf16(pair, 2)
            basis_ref[degree * 8 : degree * 8 + 16, :] = high
            basis_ref[depth + degree * 8 : depth + degree * 8 + 16, :] = low
            before = twice * now - before
            now = twice * before - now
            if degree % 8 == 6:
                yield

    def run(steps):
        for _ in steps:
            pass

    def add_group(group, basis_ref, steps):
        left = left_of(group)
        tables = [plan_ref[slot, group].astype(jnp.int32) for slot in range(2)]
        phasor_rows = [pl.ds(pl.multiple_of(table * NF, NF), NF) for table in tables]
        for first in range(0, nodes, chunk):
            at = slice(first, first + chunk)
            right = jnp.concatenate([basis_ref[:, at], basis_ref[:depth, at]], axis=0)
            got = jnp.dot(left, right, preferred_element_type=jnp.float32)
            next(steps, None)
            for win in range(windows):
                row = win * 2 * NF
                real_sum, imag_sum = sums_ref[row : row + NF, at], sums_ref[row + NF : row + 2 * NF, at]
                for slot, rows in enumerate(phasor_rows):
                    cosine, sine = cos_ref[rows, at], sin_ref[rows, at]
                    real = got[slot * lanes + row : slot * lanes + row + NF]
                    imag = got[slot * lanes + row + NF : slot * lanes + row + 2 * NF]
                    real_sum += real * cosine - imag * sine
                    imag_sum += real * sine + imag * cosine
                sums_ref[row : row + NF, at], sums_ref[row + NF : row + 2 * NF, at] = real_sum, imag_sum
        run(steps)

    run(basis_steps(0, basis_a))
    for copy in copies[3:]:
        copy.wait()

    def body(pair, carry):
        group = pair * 2
        add_group(group, basis_a, basis_steps(group + 1, basis_b))
        add_group(group + 1, basis_b, basis_steps(jnp.minimum(group + 2, places // 8 - 1), basis_a))
        return carry

    lax.fori_loop(0, (used + 1) // 2, body, 0)
    powers = []
    for win in range(windows):
        row = win * 2 * NF
        real, imag = sums_ref[row : row + NF, :], sums_ref[row + NF : row + 2 * NF, :]
        powers.append(real * real + imag * imag)
    mine = lax.axis_index("win") == 0
    keep_ref[...] = jnp.where(mine, powers[0], powers[1])
    send_ref[...] = jnp.where(mine, powers[1], powers[0])


def finish_kernel(stations, keep_ref, got_ref, spectrum_ref, beam_ref):
    nodes = keep_ref.shape[1]
    win = lax.axis_index("win")
    for place, ref in ((win, keep_ref), (1 - win, got_ref)):
        power = ref[...]
        total = jnp.sum(power, axis=0, keepdims=True)
        at = pl.ds(pl.multiple_of(place * nodes, LANES), nodes)
        spectrum_ref[:, at] = power * (NF / total)
        beam_ref[:, at] = total * (1.0 / (NF * stations))


def on_device(traces, tables, corrections, station_table, node_ids, freq_bins):
    windows, groups, cores = (lax.axis_size(a) for a in ("win", "sta", "freq"))
    stations_dev, grid = corrections.shape
    stations = stations_dev * groups
    devices = windows * groups * cores
    nodes = grid // devices
    ntab = tables.shape[0]
    params = lambda free: pltpu.CompilerParams(vmem_limit_bytes=VMEM_LIMIT - free)
    vmem = pl.BlockSpec(memory_space=pltpu.VMEM)
    hbm = pl.BlockSpec(memory_space=pltpu.HBM)
    bins = freq_bins.reshape(1, NF)
    bins_scratch = pltpu.VMEM((1, NF), jnp.int32)

    holders = windows * cores
    merged = nodes % (holders * LANES) == 0
    pieces = nodes // (holders * LANES) if merged else 0
    height = pieces * stations_dev + 8
    blocks = pl.pallas_call(
        functools.partial(send_kernel, nodes),
        out_shape=jax.ShapeDtypeStruct((devices, height, LANES), jnp.bfloat16),
        in_specs=[hbm] * 3,
        out_specs=vmem,
        scratch_shapes=[
            bins_scratch,
            pltpu.VMEM(traces.shape, traces.dtype),
            pltpu.SemaphoreType.DMA((2 + devices * max(pieces, 1),)),
        ],
        compiler_params=params(0),
        name="send",
    )(bins, traces, corrections)
    received = [lax.all_to_all(blocks, ("win", "sta", "freq"), split_axis=0, concat_axis=0, tiled=True)]
    if not merged:
        parts = corrections.reshape(stations_dev, groups, holders, nodes)
        place = lax.axis_index("freq") * windows + lax.axis_index("win")
        mine = lax.dynamic_index_in_dim(parts, place, axis=2, keepdims=False)
        corr = lax.all_to_all(mine.transpose(1, 0, 2), "sta", split_axis=0, concat_axis=0, tiled=True)
        received.append(corr.reshape(stations, nodes))

    wide = 512
    plan_width = max(LANES, stations)
    phasors = pltpu.VMEM((ntab * NF, nodes), jnp.float32)
    coefs = pltpu.VMEM((DEGREES, LANES), jnp.float32)
    plan = pltpu.VMEM((8, plan_width), jnp.float32)
    packed_shape = (packed_rows(ntab)[-1].stop, max(nodes, plan_width))
    packed = pl.pallas_call(
        prepare_kernel,
        out_shape=jax.ShapeDtypeStruct(packed_shape, jnp.float32),
        in_specs=[hbm] * 4,
        out_specs=hbm,
        scratch_shapes=[
            bins_scratch,
            pltpu.VMEM((1, stations), jnp.int32),
            pltpu.VMEM((max(nodes // LANES, 8), LANES), jnp.int32),
            pltpu.VMEM(tables.shape, tables.dtype),
            phasors,
            phasors,
            coefs,
            plan,
            pltpu.VMEM((grid // wide * ntab, 3 * wide), jnp.bfloat16),
            pltpu.VMEM((3 * wide, nodes), jnp.bfloat16),
            pltpu.SemaphoreType.DMA((3 + 2 * ntab,)),
            pltpu.SemaphoreType.DMA((TABLE_PIECES,)),
        ],
        compiler_params=params(512 * 1024),
        name="prepare",
    )(bins, station_table.reshape(1, stations), node_ids.reshape(grid // LANES, LANES), tables)

    places = (stations // 8 + ntab // 2 + 2) // 2 * 16
    half = jax.ShapeDtypeStruct((NF, nodes), jnp.float32)
    rows = 2 * windows * 2 * NF
    basis = pltpu.VMEM((2 * DEGREES * 8, nodes), jnp.bfloat16)
    keep, send = pl.pallas_call(
        functools.partial(image_kernel, merged, stations_dev),
        out_shape=[half, half],
        in_specs=[hbm] + [vmem] * len(received),
        out_specs=[vmem, vmem],
        scratch_shapes=[
            pltpu.SMEM((8, plan_width), jnp.float32),
            plan,
            coefs,
            phasors,
            phasors,
            pltpu.SemaphoreType.DMA((5,)),
            pltpu.VMEM((places, nodes), jnp.float32),
            pltpu.VMEM((places, rows), jnp.float32),
            pltpu.VMEM((places // 8, rows, DEGREES * 8), jnp.bfloat16),
            pltpu.VMEM((rows // 2, nodes), jnp.float32),
            basis,
            basis,
        ],
        compiler_params=params(1024 * 1024),
        name="image",
    )(packed, *received)
    got = lax.ppermute(send, "win", [(0, 1), (1, 0)])
    spectrum, beam_power = pl.pallas_call(
        functools.partial(finish_kernel, stations),
        out_shape=[
            jax.ShapeDtypeStruct((NF, windows * nodes), jnp.float32),
            jax.ShapeDtypeStruct((1, windows * nodes), jnp.float32),
        ],
        in_specs=[vmem, vmem],
        out_specs=[vmem, vmem],
        compiler_params=params(32 * 1024 * 1024),
        name="finish",
    )(keep, got)
    return spectrum, beam_power.reshape(windows * nodes)


def solution(mesh):
    return jax.shard_map(
        on_device,
        mesh=mesh,
        in_specs=(P(("win", "sta"), "freq"), P(), P("sta", None), P(), P(), P()),
        out_specs=(P("win", ("sta", "freq")), P(("win", "sta", "freq"))),
        check_vma=False,
    )
```

```python
import functools
import math

import jax
import jax.numpy as jnp
import numpy as np
from jax import lax
from jax.experimental import pallas as pl
from jax.experimental.pallas import tpu as pltpu
from jax.sharding import PartitionSpec as P

NT = 5120
NF = 16
NTAB = 16
LANES = 128
DEGREES = 32
REACH = 1.5
TABLE_PIECES = 4
VMEM_LIMIT = 64 * 1024 * 1024 - 64 * 1024


def chebyshev_fit(func, degree, low, high):
    fit = np.polynomial.chebyshev.Chebyshev.interpolate(func, degree, domain=[low, high])
    return [float(v) for v in fit.convert(kind=np.polynomial.Polynomial).coef]


SIN_HALF = chebyshev_fit(lambda z: np.pi * np.sinc(np.sqrt(z)), 4, 0.0, 0.25)
COS_HALF = chebyshev_fit(lambda z: np.cos(np.pi * np.sqrt(z)), 4, 0.0, 0.25)


def horner(coefs, arg):
    total = coefs[-1]
    for coef in coefs[-2::-1]:
        total = total * arg + coef
    return total


def turn_parts(rest):
    square = rest * rest
    root = math.sqrt(2.0)
    sine_half = rest * horner([root * c for c in SIN_HALF], square)
    cos_half = horner([root * c for c in COS_HALF], square)
    return sine_half * sine_half, sine_half * cos_half


def cos_sin(turns):
    versine, sine = turn_parts(turns - jnp.round(turns))
    return 1.0 - versine, sine


def bins_column(bins_ref):
    rows = lax.broadcasted_iota(jnp.int32, (NF, NF), 0)
    lanes = lax.broadcasted_iota(jnp.int32, (NF, NF), 1)
    square = jnp.broadcast_to(bins_ref[...].astype(jnp.float32), (NF, NF))
    return jnp.sum(jnp.where(rows == lanes, square, 0.0), axis=1, keepdims=True)


def split_bf16(value, terms):
    pieces = []
    for term in range(terms):
        piece = value.astype(jnp.bfloat16)
        pieces.append(piece)
        if term < terms - 1:
            value = value - piece.astype(jnp.float32)
    return pieces


def start_all(copies):
    for copy in copies:
        copy.start()
    return copies


def send_kernel(nodes, bins_hbm, traces_hbm, corr_hbm, out_ref, bins_ref, traces_ref, sems):
    devices, height, _ = out_ref.shape
    stations_dev, half_length = traces_ref.shape
    pieces = (height - 8) // stations_dev
    windows, groups, cores = (lax.axis_size(a) for a in ("win", "sta", "freq"))
    place = lax.axis_index("win") * cores + lax.axis_index("freq")
    small = start_all(
        [
            pltpu.make_async_copy(bins_hbm, bins_ref, sems.at[0]),
            pltpu.make_async_copy(traces_hbm, traces_ref, sems.at[1]),
        ]
    )
    copies = []
    for dev in range(devices):
        win, sta, core = dev // (groups * cores), dev // cores % groups, dev % cores
        first = ((sta * cores + core) * windows + win) * nodes
        for piece in range(pieces):
            at = pl.multiple_of(first + (place * pieces + piece) * LANES, LANES)
            to = out_ref.at[dev, pl.ds(piece * stations_dev, stations_dev), :]
            sem = sems.at[2 + dev * pieces + piece]
            copies.append(pltpu.make_async_copy(corr_hbm.at[:, pl.ds(at, LANES)], to, sem))
    start_all(copies)
    start = lax.axis_index("freq") * half_length
    small[0].wait()
    bins = bins_column(bins_ref)
    pos = (start + lax.broadcasted_iota(jnp.int32, (NF, half_length), 1)).astype(jnp.float32)
    product = bins * pos
    turns = jnp.round(product * (1.0 / NT))
    rest = (product - turns * NT) * (1.0 / NT)
    versine, sine = turn_parts(rest)
    scale = 1.0 / math.sqrt(NT)
    table = jnp.concatenate([(1.0 - versine) * scale, sine * -scale], axis=0)
    both = jnp.concatenate(split_bf16(table, 2), axis=0)
    small[1].wait()
    sums = lax.dot_general(
        traces_ref[...], both, (((1,), (1,)), ((), ())), preferred_element_type=jnp.float32
    )
    sums = sums[:, : 2 * NF] + sums[:, 2 * NF :]
    terms = [term.astype(jnp.float32) for term in split_bf16(sums, 2)]
    tile = jnp.concatenate([term[at : at + 8] for term in terms for at in range(0, stations_dev, 8)], axis=1)
    tile = tile.astype(jnp.bfloat16)
    for dev in range(devices):
        out_ref[dev, height - 8 :, :] = tile
    for copy in copies:
        copy.wait()


def own_place():
    windows, cores = lax.axis_size("win"), lax.axis_size("freq")
    return (lax.axis_index("sta") * cores + lax.axis_index("freq")) * windows + lax.axis_index("win")


def pick_columns(ids_ref, tables_ref, table_copies, nodes, left_ref, right_ref):
    ntab, grid = tables_ref.shape
    count = nodes // LANES
    wide = right_ref.shape[0] // 3
    blocks = grid // wide
    ids = ids_ref[pl.ds(own_place() * count % ids_ref.shape[0], count), :]
    ids = jnp.concatenate([ids[at : at + 1] for at in range(count)], axis=1)
    low, high = ids & (wide - 1), ids >> (wide.bit_length() - 1)
    spots = lax.broadcasted_iota(jnp.int32, (wide, nodes), 0)
    ones = jnp.where(spots == low, 1.0, 0.0).astype(jnp.bfloat16)
    for term in range(3):
        right_ref[term * wide : (term + 1) * wide, :] = ones
    found = jnp.zeros((ntab, nodes), jnp.float32)
    step = blocks // len(table_copies)
    for at, copy in enumerate(table_copies):
        copy.wait()
        for block in range(at * step, (at + 1) * step):
            pieces = split_bf16(tables_ref[:, block * wide : (block + 1) * wide], 3)
            left_ref[block * ntab : (block + 1) * ntab, :] = jnp.concatenate(pieces, axis=1)
        rows = left_ref[at * step * ntab : (at + 1) * step * ntab, :]
        picked = jnp.dot(rows, right_ref[...], preferred_element_type=jnp.float32)
        for block in range(step):
            part = picked[block * ntab : (block + 1) * ntab]
            found = jnp.where(high == at * step + block, part, found)
    return found


def chebyshev_coefs(bins_ref):
    shape = (DEGREES, DEGREES)
    degree = lax.broadcasted_iota(jnp.int32, shape, 0)
    node = lax.broadcasted_iota(jnp.int32, shape, 1)
    period = 4 * DEGREES
    weight, _ = cos_sin((degree * (2 * node + 1) & (period - 1)).astype(jnp.float32) * (1.0 / period))
    weight = weight * jnp.where(degree == 0, 1.0 / DEGREES, 2.0 / DEGREES)
    even = jnp.where(degree % 2 == 0, weight, 0.0)
    odd = jnp.where(degree % 2 == 1, weight, 0.0)
    row = bins_ref[...].astype(jnp.float32)
    bins = jnp.concatenate([row] * (LANES // NF), axis=1)
    at = lax.broadcasted_iota(jnp.int32, (DEGREES, LANES), 0).astype(jnp.float32)
    spot, _ = cos_sin((2.0 * at + 1.0) * (1.0 / period))
    cosine, sine = cos_sin(bins * (spot * (REACH / 256.0)))
    dot = functools.partial(jnp.dot, precision=lax.Precision.HIGHEST, preferred_element_type=jnp.float32)
    return dot(even, cosine) + dot(odd, sine)


def station_plan(table_row, width):
    count = table_row.shape[1]
    shape = (count, count)
    here = lax.broadcasted_iota(jnp.int32, shape, 0)
    there = lax.broadcasted_iota(jnp.int32, shape, 1)
    column_of = lambda row: jnp.sum(jnp.where(here == there, jnp.broadcast_to(row, shape), 0), axis=1, keepdims=True)
    table_column = column_of(table_row)
    same = (table_column == table_row) & (here < there)
    within = jnp.sum(jnp.where(same, 1, 0), axis=0, keepdims=True)
    place_row = within
    spot = jnp.zeros((1, 1), jnp.int32)
    held = jnp.zeros((1, 1), jnp.int32)
    for table in range(NTAB):
        size = jnp.sum(jnp.where(table_row == table, 1, 0), axis=1, keepdims=True)
        some = size > 0
        edge = (spot & 7) == 0
        skip = some & (held >= 2) & ~edge
        spot = jnp.where(skip, (spot + 7) >> 3 << 3, spot)
        held = jnp.where(skip | edge, 0, held)
        after = spot + size
        place_row = place_row + jnp.where(table_row == table, spot, 0)
        held = jnp.where(some, jnp.where(after >> 3 == spot >> 3, held + 1, 1), held)
        spot = after
    groups = (spot + 7) >> 3
    place_column = column_of(place_row)
    group = lax.broadcasted_iota(jnp.int32, (count, width), 1)
    inside = place_column >> 3 == group
    first = jnp.sum(jnp.where(place_column == group * 8, table_column, 0), axis=0, keepdims=True)
    last = jnp.max(jnp.where(inside, table_column, 0), axis=0, keepdims=True)
    length = jnp.sum(jnp.where(inside & (table_column == first), 1, 0), axis=0, keepdims=True)
    rows = [first, last, length, jnp.broadcast_to(groups, (1, width))]
    if width > count:
        place_row = jnp.concatenate([place_row, jnp.zeros((1, width - count), jnp.int32)], axis=1)
    rows += [place_row, jnp.zeros((3, width), jnp.int32)]
    return jnp.concatenate(rows, axis=0).astype(jnp.float32)


def packed_rows(ntab):
    ends = [ntab * NF, 2 * ntab * NF, 2 * ntab * NF + DEGREES, 2 * ntab * NF + DEGREES + 8]
    return [slice(start, end) for start, end in zip([0] + ends, ends)]


def prepare_kernel(bins_hbm, table_hbm, ids_hbm, tables_hbm, out_hbm, *rest):
    bins_ref, table_ref, ids_ref, tables_ref, cos_ref, sin_ref, coef_ref, plan_ref = rest[:8]
    left_ref, right_ref, sems, table_sems = rest[8:]
    ntab = tables_ref.shape[0]
    nodes = cos_ref.shape[1]
    near = ids_ref.shape[0]
    first = pl.multiple_of(own_place() * (nodes // LANES) // near * near, 8)
    ins = start_all(
        [
            pltpu.make_async_copy(ids_hbm.at[pl.ds(first, near), :], ids_ref, sems.at[0]),
            pltpu.make_async_copy(bins_hbm, bins_ref, sems.at[1]),
            pltpu.make_async_copy(table_hbm, table_ref, sems.at[2]),
        ]
    )
    piece = tables_ref.shape[1] // TABLE_PIECES
    table_copies = []
    for at in range(TABLE_PIECES):
        part = (slice(None), pl.ds(at * piece, piece))
        table_copies.append(pltpu.make_async_copy(tables_hbm.at[part], tables_ref.at[part], table_sems.at[at]))
    start_all(table_copies)
    for copy in ins:
        copy.wait()
    cos_at, sin_at, coef_at, plan_at = packed_rows(ntab)
    coef_ref[...] = chebyshev_coefs(bins_ref)
    plan_ref[...] = station_plan(table_ref[...], plan_ref.shape[1])
    outs = start_all(
        [
            pltpu.make_async_copy(coef_ref, out_hbm.at[coef_at, pl.ds(0, LANES)], sems.at[0]),
            pltpu.make_async_copy(plan_ref, out_hbm.at[plan_at, pl.ds(0, plan_ref.shape[1])], sems.at[1]),
        ]
    )
    turns = pick_columns(ids_ref, tables_ref, table_copies, nodes, left_ref, right_ref) * (1.0 / 256.0)
    bins = bins_column(bins_ref)
    for table in range(ntab):
        cosine, sine = cos_sin(bins * turns[table : table + 1])
        at = pl.ds(table * NF, NF)
        cos_ref[at, :] = cosine
        sin_ref[at, :] = sine
        outs += start_all(
            [
                pltpu.make_async_copy(
                    cos_ref.at[at, :], out_hbm.at[pl.ds(cos_at.start + table * NF, NF), pl.ds(0, nodes)],
                    sems.at[3 + 2 * table],
                ),
                pltpu.make_async_copy(
                    sin_ref.at[at, :], out_hbm.at[pl.ds(sin_at.start + table * NF, NF), pl.ds(0, nodes)],
                    sems.at[4 + 2 * table],
                ),
            ]
        )
    for copy in outs:
        copy.wait()


def image_kernel(merged, stations_dev, packed_hbm, block_ref, *rest):
    corr_ref, rest = (None, rest) if merged else (rest[0], rest[1:])
    keep_ref, send_ref, plan_ref, place_of_ref, coef_ref, cos_ref, sin_ref, sems = rest[:8]
    place_ref, weight_ref, left_ref, sums_ref, basis_a, basis_b = rest[8:]
    places, nodes = place_ref.shape
    windows, groups, cores = (lax.axis_size(a) for a in ("win", "sta", "freq"))
    stations = stations_dev * groups
    cos_at, sin_at, coef_at, plan_at = packed_rows(cos_ref.shape[0] // NF)
    width = plan_ref.shape[1]
    copies = start_all(
        [
            pltpu.make_async_copy(packed_hbm.at[plan_at, pl.ds(0, width)], place_of_ref, sems.at[0]),
            pltpu.make_async_copy(packed_hbm.at[plan_at, pl.ds(0, width)], plan_ref, sems.at[1]),
            pltpu.make_async_copy(packed_hbm.at[coef_at, pl.ds(0, LANES)], coef_ref, sems.at[2]),
            pltpu.make_async_copy(packed_hbm.at[cos_at, pl.ds(0, nodes)], cos_ref, sems.at[3]),
            pltpu.make_async_copy(packed_hbm.at[sin_at, pl.ds(0, nodes)], sin_ref, sems.at[4]),
        ]
    )
    height = block_ref.shape[1]
    rows_of = lambda win, core: [(win * groups + group) * cores + core for group in range(groups)]

    even, odd = [], []
    for win in range(windows):
        value = []
        for group in range(groups):
            tile = None
            for core in range(cores):
                part = block_ref[(win * groups + group) * cores + core, height - 8 :, :].astype(jnp.float32)
                tile = part if tile is None else tile + part
            tile = tile[:, : LANES // 2] + tile[:, LANES // 2 :]
            value += [tile[:, 2 * NF * piece : 2 * NF * (piece + 1)] for piece in range(stations_dev // 8)]
        value = jnp.concatenate(value, axis=0)
        even.append(value)
        odd.append(jnp.concatenate([-value[:, NF:], value[:, :NF]], axis=1))
    spectra = jnp.concatenate(even + odd, axis=1)
    if merged:
        parts = []
        for win in range(windows):
            for core in range(cores):
                for first in range(0, height - 8, stations_dev):
                    rows = [block_ref[at, first : first + stations_dev, :] for at in rows_of(win, core)]
                    parts.append(jnp.concatenate(rows, axis=0))
        corr = jnp.concatenate(parts, axis=1)
    else:
        corr = corr_ref[...]

    copies[0].wait()
    place_row = place_of_ref[4:5, :stations].astype(jnp.int32)
    sorter = lax.broadcasted_iota(jnp.int32, (places, stations), 0) == place_row
    sorter = jnp.where(sorter, 1.0, 0.0).astype(jnp.bfloat16)
    found = None
    for piece in split_bf16(spectra, 3):
        part = jnp.dot(sorter, piece, preferred_element_type=jnp.float32)
        found = part if found is None else found + part
    weight_ref[...] = found
    place_ref[...] = jnp.dot(sorter, corr, preferred_element_type=jnp.float32) * (1.0 / REACH)
    sums_ref[...] = jnp.zeros_like(sums_ref)
    chunk = min(256, nodes)
    depth = DEGREES * 8
    lanes = windows * 2 * NF
    for copy in copies[1:3]:
        copy.wait()

    def make_left(pair):
        top = weight_ref[pl.ds(pl.multiple_of(pair * 16, 16), 8), :]
        bottom = weight_ref[pl.ds(pl.multiple_of(pair * 16 + 8, 8), 8), :]
        sides = [
            jnp.concatenate([top[:, :lanes], bottom[:, :lanes]], axis=1),
            jnp.concatenate([top[:, lanes:], bottom[:, lanes:]], axis=1),
        ]
        per = LANES // 8
        for half in range(DEGREES // per):
            tall = jnp.concatenate(
                [sides[k % 2] * coef_ref[k : k + 1, :] for k in range(half * per, (half + 1) * per)], axis=0
            )
            at = slice(half * LANES, (half + 1) * LANES)
            for term, value in enumerate(split_bf16(tall.T, 2)):
                left_ref[2 * pair, term * lanes : (term + 1) * lanes, at] = value[:lanes]
                left_ref[2 * pair + 1, term * lanes : (term + 1) * lanes, at] = value[lanes:]

    used = plan_ref[3, 0].astype(jnp.int32)
    sure = stations // 16
    if sure <= 8:
        for pair in range(sure):
            make_left(pair)
    else:
        lax.fori_loop(0, sure, lambda pair, carry: (make_left(pair), carry)[1], 0)
    lax.fori_loop(sure, (used + 1) // 2, lambda pair, carry: (make_left(pair), carry)[1], 0)
    spot = (lax.broadcasted_iota(jnp.int32, (16, depth), 1) & 7).astype(jnp.float32)

    def left_of(group):
        mask = spot < plan_ref[2, group]
        results = []
        for keep, drop in ((1.0, 0.0), (0.0, 1.0)):
            side = jnp.where(mask, keep, drop).astype(jnp.bfloat16)
            results.append(left_ref[group] * jnp.concatenate([side] * (2 * lanes // 16), axis=0))
        high = jnp.concatenate([result[:lanes] for result in results], axis=0)
        return jnp.concatenate(results, axis=0), high

    def basis_steps(group, basis_ref):
        arg = place_ref[pl.ds(pl.multiple_of(group * 8, 8), 8), :]
        twice = arg + arg
        before, now = jnp.ones_like(arg), arg
        for degree in range(0, DEGREES, 2):
            pair = jnp.concatenate([before, now], axis=0)
            high, low = split_bf16(pair, 2)
            basis_ref[degree * 8 : degree * 8 + 16, :] = high
            basis_ref[depth + degree * 8 : depth + degree * 8 + 16, :] = low
            before = twice * now - before
            now = twice * before - now
            if degree % 8 == 6:
                yield

    def run(steps):
        for _ in steps:
            pass

    def add_group(group, basis_ref, steps):
        both, high = left_of(group)
        tables = [plan_ref[slot, group].astype(jnp.int32) for slot in range(2)]
        phasor_rows = [pl.ds(pl.multiple_of(table * NF, NF), NF) for table in tables]
        for first in range(0, nodes, chunk):
            at = slice(first, first + chunk)
            got = jnp.dot(both, basis_ref[:depth, at], preferred_element_type=jnp.float32)
            more = jnp.dot(high, basis_ref[depth:, at], preferred_element_type=jnp.float32)
            next(steps, None)
            got = [
                got[2 * slot * lanes : (2 * slot + 1) * lanes]
                + got[(2 * slot + 1) * lanes : (2 * slot + 2) * lanes]
                + more[slot * lanes : (slot + 1) * lanes]
                for slot in range(2)
            ]
            for win in range(windows):
                row = win * 2 * NF
                real_sum, imag_sum = sums_ref[row : row + NF, at], sums_ref[row + NF : row + 2 * NF, at]
                for slot, rows in enumerate(phasor_rows):
                    cosine, sine = cos_ref[rows, at], sin_ref[rows, at]
                    real, imag = got[slot][row : row + NF], got[slot][row + NF : row + 2 * NF]
                    real_sum += real * cosine - imag * sine
                    imag_sum += real * sine + imag * cosine
                sums_ref[row : row + NF, at], sums_ref[row + NF : row + 2 * NF, at] = real_sum, imag_sum
        run(steps)

    run(basis_steps(0, basis_a))
    for copy in copies[3:]:
        copy.wait()

    def body(pair, carry):
        group = pair * 2
        add_group(group, basis_a, basis_steps(group + 1, basis_b))
        add_group(group + 1, basis_b, basis_steps(jnp.minimum(group + 2, places // 8 - 1), basis_a))
        return carry

    lax.fori_loop(0, (used + 1) // 2, body, 0)
    powers = []
    for win in range(windows):
        row = win * 2 * NF
        real, imag = sums_ref[row : row + NF, :], sums_ref[row + NF : row + 2 * NF, :]
        powers.append(real * real + imag * imag)
    mine = lax.axis_index("win") == 0
    keep_ref[...] = jnp.where(mine, powers[0], powers[1])
    send_ref[...] = jnp.where(mine, powers[1], powers[0])


def finish_kernel(stations, keep_ref, got_ref, spectrum_ref, beam_ref):
    nodes = keep_ref.shape[1]
    win = lax.axis_index("win")
    for place, ref in ((win, keep_ref), (1 - win, got_ref)):
        power = ref[...]
        total = jnp.sum(power, axis=0, keepdims=True)
        at = pl.ds(pl.multiple_of(place * nodes, LANES), nodes)
        spectrum_ref[:, at] = power * (NF / total)
        beam_ref[:, at] = total * (1.0 / (NF * stations))


def on_device(traces, tables, corrections, station_table, node_ids, freq_bins):
    windows, groups, cores = (lax.axis_size(a) for a in ("win", "sta", "freq"))
    stations_dev, grid = corrections.shape
    stations = stations_dev * groups
    devices = windows * groups * cores
    nodes = grid // devices
    ntab = tables.shape[0]
    params = lambda free: pltpu.CompilerParams(vmem_limit_bytes=VMEM_LIMIT - free)
    vmem = pl.BlockSpec(memory_space=pltpu.VMEM)
    hbm = pl.BlockSpec(memory_space=pltpu.HBM)
    bins = freq_bins.reshape(1, NF)
    bins_scratch = pltpu.VMEM((1, NF), jnp.int32)

    holders = windows * cores
    merged = nodes % (holders * LANES) == 0
    pieces = nodes // (holders * LANES) if merged else 0
    height = pieces * stations_dev + 8
    blocks = pl.pallas_call(
        functools.partial(send_kernel, nodes),
        out_shape=jax.ShapeDtypeStruct((devices, height, LANES), jnp.bfloat16),
        in_specs=[hbm] * 3,
        out_specs=vmem,
        scratch_shapes=[
            bins_scratch,
            pltpu.VMEM(traces.shape, traces.dtype),
            pltpu.SemaphoreType.DMA((2 + devices * max(pieces, 1),)),
        ],
        compiler_params=params(0),
        name="send",
    )(bins, traces, corrections)
    received = [lax.all_to_all(blocks, ("win", "sta", "freq"), split_axis=0, concat_axis=0, tiled=True)]
    if not merged:
        parts = corrections.reshape(stations_dev, groups, holders, nodes)
        place = lax.axis_index("freq") * windows + lax.axis_index("win")
        mine = lax.dynamic_index_in_dim(parts, place, axis=2, keepdims=False)
        corr = lax.all_to_all(mine.transpose(1, 0, 2), "sta", split_axis=0, concat_axis=0, tiled=True)
        received.append(corr.reshape(stations, nodes))

    wide = 512
    plan_width = max(LANES, stations)
    phasors = pltpu.VMEM((ntab * NF, nodes), jnp.float32)
    coefs = pltpu.VMEM((DEGREES, LANES), jnp.float32)
    plan = pltpu.VMEM((8, plan_width), jnp.float32)
    packed_shape = (packed_rows(ntab)[-1].stop, max(nodes, plan_width))
    packed = pl.pallas_call(
        prepare_kernel,
        out_shape=jax.ShapeDtypeStruct(packed_shape, jnp.float32),
        in_specs=[hbm] * 4,
        out_specs=hbm,
        scratch_shapes=[
            bins_scratch,
            pltpu.VMEM((1, stations), jnp.int32),
            pltpu.VMEM((max(nodes // LANES, 8), LANES), jnp.int32),
            pltpu.VMEM(tables.shape, tables.dtype),
            phasors,
            phasors,
            coefs,
            plan,
            pltpu.VMEM((grid // wide * ntab, 3 * wide), jnp.bfloat16),
            pltpu.VMEM((3 * wide, nodes), jnp.bfloat16),
            pltpu.SemaphoreType.DMA((3 + 2 * ntab,)),
            pltpu.SemaphoreType.DMA((TABLE_PIECES,)),
        ],
        compiler_params=params(512 * 1024),
        name="prepare",
    )(bins, station_table.reshape(1, stations), node_ids.reshape(grid // LANES, LANES), tables)

    places = (stations // 8 + ntab // 2 + 2) // 2 * 16
    half = jax.ShapeDtypeStruct((NF, nodes), jnp.float32)
    rows = 2 * windows * 2 * NF
    basis = pltpu.VMEM((2 * DEGREES * 8, nodes), jnp.bfloat16)
    keep, send = pl.pallas_call(
        functools.partial(image_kernel, merged, stations_dev),
        out_shape=[half, half],
        in_specs=[hbm] + [vmem] * len(received),
        out_specs=[vmem, vmem],
        scratch_shapes=[
            pltpu.SMEM((8, plan_width), jnp.float32),
            plan,
            coefs,
            phasors,
            phasors,
            pltpu.SemaphoreType.DMA((5,)),
            pltpu.VMEM((places, nodes), jnp.float32),
            pltpu.VMEM((places, rows), jnp.float32),
            pltpu.VMEM((places // 8, rows, DEGREES * 8), jnp.bfloat16),
            pltpu.VMEM((rows // 2, nodes), jnp.float32),
            basis,
            basis,
        ],
        compiler_params=params(23 * 512 * 1024),
        name="image",
    )(packed, *received)
    got = lax.ppermute(send, "win", [(0, 1), (1, 0)])
    spectrum, beam_power = pl.pallas_call(
        functools.partial(finish_kernel, stations),
        out_shape=[
            jax.ShapeDtypeStruct((NF, windows * nodes), jnp.float32),
            jax.ShapeDtypeStruct((1, windows * nodes), jnp.float32),
        ],
        in_specs=[vmem, vmem],
        out_specs=[vmem, vmem],
        compiler_params=params(32 * 1024 * 1024),
        name="finish",
    )(keep, got)
    return spectrum, beam_power.reshape(windows * nodes)


def solution(mesh):
    return jax.shard_map(
        on_device,
        mesh=mesh,
        in_specs=(P(("win", "sta"), "freq"), P(), P("sta", None), P(), P(), P()),
        out_specs=(P("win", ("sta", "freq")), P(("win", "sta", "freq"))),
        check_vma=False,
    )
```

```python
import functools
import math

import jax
import jax.numpy as jnp
import numpy as np
from jax import lax
from jax.experimental import pallas as pl
from jax.experimental.pallas import tpu as pltpu
from jax.sharding import PartitionSpec as P

NT = 5120
NF = 16
NTAB = 16
LANES = 128
DEGREES = 32
REACH = 1.5
TABLE_PIECES = 4
VMEM_LIMIT = 64 * 1024 * 1024 - 64 * 1024


def chebyshev_fit(func, degree, low, high):
    fit = np.polynomial.chebyshev.Chebyshev.interpolate(func, degree, domain=[low, high])
    return [float(v) for v in fit.convert(kind=np.polynomial.Polynomial).coef]


SIN_HALF = chebyshev_fit(lambda z: np.pi * np.sinc(np.sqrt(z)), 4, 0.0, 0.25)
COS_HALF = chebyshev_fit(lambda z: np.cos(np.pi * np.sqrt(z)), 4, 0.0, 0.25)


def horner(coefs, arg):
    total = coefs[-1]
    for coef in coefs[-2::-1]:
        total = total * arg + coef
    return total


def turn_parts(rest):
    square = rest * rest
    root = math.sqrt(2.0)
    sine_half = rest * horner([root * c for c in SIN_HALF], square)
    cos_half = horner([root * c for c in COS_HALF], square)
    return sine_half * sine_half, sine_half * cos_half


def cos_sin(turns):
    versine, sine = turn_parts(turns - jnp.round(turns))
    return 1.0 - versine, sine


def bins_column(bins_ref):
    rows = lax.broadcasted_iota(jnp.int32, (NF, NF), 0)
    lanes = lax.broadcasted_iota(jnp.int32, (NF, NF), 1)
    square = jnp.broadcast_to(bins_ref[...].astype(jnp.float32), (NF, NF))
    return jnp.sum(jnp.where(rows == lanes, square, 0.0), axis=1, keepdims=True)


def split_bf16(value, terms):
    pieces = []
    for term in range(terms):
        piece = value.astype(jnp.bfloat16)
        pieces.append(piece)
        if term < terms - 1:
            value = value - piece.astype(jnp.float32)
    return pieces


def start_all(copies):
    for copy in copies:
        copy.start()
    return copies


def send_kernel(nodes, bins_hbm, traces_hbm, corr_hbm, out_ref, bins_ref, traces_ref, sems):
    devices, height, _ = out_ref.shape
    stations_dev, half_length = traces_ref.shape
    pieces = (height - 8) // stations_dev
    windows, groups, cores = (lax.axis_size(a) for a in ("win", "sta", "freq"))
    place = lax.axis_index("win") * cores + lax.axis_index("freq")
    small = start_all(
        [
            pltpu.make_async_copy(bins_hbm, bins_ref, sems.at[0]),
            pltpu.make_async_copy(traces_hbm, traces_ref, sems.at[1]),
        ]
    )
    copies = []
    for dev in range(devices):
        win, sta, core = dev // (groups * cores), dev // cores % groups, dev % cores
        first = ((sta * cores + core) * windows + win) * nodes
        for piece in range(pieces):
            at = pl.multiple_of(first + (place * pieces + piece) * LANES, LANES)
            to = out_ref.at[dev, pl.ds(piece * stations_dev, stations_dev), :]
            sem = sems.at[2 + dev * pieces + piece]
            copies.append(pltpu.make_async_copy(corr_hbm.at[:, pl.ds(at, LANES)], to, sem))
    start_all(copies)
    start = lax.axis_index("freq") * half_length
    small[0].wait()
    bins = bins_column(bins_ref)
    pos = (start + lax.broadcasted_iota(jnp.int32, (NF, half_length), 1)).astype(jnp.float32)
    product = bins * pos
    turns = jnp.round(product * (1.0 / NT))
    rest = (product - turns * NT) * (1.0 / NT)
    versine, sine = turn_parts(rest)
    scale = 1.0 / math.sqrt(NT)
    table = jnp.concatenate([(1.0 - versine) * scale, sine * -scale], axis=0)
    both = jnp.concatenate(split_bf16(table, 2), axis=0)
    small[1].wait()
    sums = lax.dot_general(
        traces_ref[...], both, (((1,), (1,)), ((), ())), preferred_element_type=jnp.float32
    )
    sums = sums[:, : 2 * NF] + sums[:, 2 * NF :]
    terms = [term.astype(jnp.float32) for term in split_bf16(sums, 2)]
    tile = jnp.concatenate([term[at : at + 8] for term in terms for at in range(0, stations_dev, 8)], axis=1)
    tile = tile.astype(jnp.bfloat16)
    for dev in range(devices):
        out_ref[dev, height - 8 :, :] = tile
    for copy in copies:
        copy.wait()


def own_place():
    windows, cores = lax.axis_size("win"), lax.axis_size("freq")
    return (lax.axis_index("sta") * cores + lax.axis_index("freq")) * windows + lax.axis_index("win")


def pick_columns(ids_ref, tables_ref, table_copies, nodes, left_ref, right_ref):
    ntab, grid = tables_ref.shape
    count = nodes // LANES
    wide = right_ref.shape[0] // 3
    blocks = grid // wide
    ids = ids_ref[pl.ds(own_place() * count % ids_ref.shape[0], count), :]
    ids = jnp.concatenate([ids[at : at + 1] for at in range(count)], axis=1)
    low, high = ids & (wide - 1), ids >> (wide.bit_length() - 1)
    spots = lax.broadcasted_iota(jnp.int32, (wide, nodes), 0)
    ones = jnp.where(spots == low, 1.0, 0.0).astype(jnp.bfloat16)
    for term in range(3):
        right_ref[term * wide : (term + 1) * wide, :] = ones
    found = jnp.zeros((ntab, nodes), jnp.float32)
    step = blocks // len(table_copies)
    for at, copy in enumerate(table_copies):
        copy.wait()
        for block in range(at * step, (at + 1) * step):
            pieces = split_bf16(tables_ref[:, block * wide : (block + 1) * wide], 3)
            left_ref[block * ntab : (block + 1) * ntab, :] = jnp.concatenate(pieces, axis=1)
        rows = left_ref[at * step * ntab : (at + 1) * step * ntab, :]
        picked = jnp.dot(rows, right_ref[...], preferred_element_type=jnp.float32)
        for block in range(step):
            part = picked[block * ntab : (block + 1) * ntab]
            found = jnp.where(high == at * step + block, part, found)
    return found


def chebyshev_coefs(bins_ref):
    shape = (DEGREES, DEGREES)
    degree = lax.broadcasted_iota(jnp.int32, shape, 0)
    node = lax.broadcasted_iota(jnp.int32, shape, 1)
    period = 4 * DEGREES
    weight, _ = cos_sin((degree * (2 * node + 1) & (period - 1)).astype(jnp.float32) * (1.0 / period))
    weight = weight * jnp.where(degree == 0, 1.0 / DEGREES, 2.0 / DEGREES)
    even = jnp.where(degree % 2 == 0, weight, 0.0)
    odd = jnp.where(degree % 2 == 1, weight, 0.0)
    row = bins_ref[...].astype(jnp.float32)
    bins = jnp.concatenate([row] * (LANES // NF), axis=1)
    at = lax.broadcasted_iota(jnp.int32, (DEGREES, LANES), 0).astype(jnp.float32)
    spot, _ = cos_sin((2.0 * at + 1.0) * (1.0 / period))
    cosine, sine = cos_sin(bins * (spot * (REACH / 256.0)))
    dot = functools.partial(jnp.dot, precision=lax.Precision.HIGHEST, preferred_element_type=jnp.float32)
    return dot(even, cosine) + dot(odd, sine)


def station_plan(table_row, width):
    count = table_row.shape[1]
    shape = (count, count)
    here = lax.broadcasted_iota(jnp.int32, shape, 0)
    there = lax.broadcasted_iota(jnp.int32, shape, 1)
    column_of = lambda row: jnp.sum(jnp.where(here == there, jnp.broadcast_to(row, shape), 0), axis=1, keepdims=True)
    table_column = column_of(table_row)
    same = (table_column == table_row) & (here < there)
    within = jnp.sum(jnp.where(same, 1, 0), axis=0, keepdims=True)
    place_row = within
    spot = jnp.zeros((1, 1), jnp.int32)
    held = jnp.zeros((1, 1), jnp.int32)
    for table in range(NTAB):
        size = jnp.sum(jnp.where(table_row == table, 1, 0), axis=1, keepdims=True)
        some = size > 0
        edge = (spot & 7) == 0
        skip = some & (held >= 2) & ~edge
        spot = jnp.where(skip, (spot + 7) >> 3 << 3, spot)
        held = jnp.where(skip | edge, 0, held)
        after = spot + size
        place_row = place_row + jnp.where(table_row == table, spot, 0)
        held = jnp.where(some, jnp.where(after >> 3 == spot >> 3, held + 1, 1), held)
        spot = after
    groups = (spot + 7) >> 3
    place_column = column_of(place_row)
    group = lax.broadcasted_iota(jnp.int32, (count, width), 1)
    inside = place_column >> 3 == group
    first = jnp.sum(jnp.where(place_column == group * 8, table_column, 0), axis=0, keepdims=True)
    last = jnp.max(jnp.where(inside, table_column, 0), axis=0, keepdims=True)
    length = jnp.sum(jnp.where(inside & (table_column == first), 1, 0), axis=0, keepdims=True)
    rows = [first, last, length, jnp.broadcast_to(groups, (1, width))]
    if width > count:
        place_row = jnp.concatenate([place_row, jnp.zeros((1, width - count), jnp.int32)], axis=1)
    rows += [place_row, jnp.zeros((3, width), jnp.int32)]
    return jnp.concatenate(rows, axis=0).astype(jnp.float32)


def packed_rows(ntab):
    ends = [ntab * NF, 2 * ntab * NF, 2 * ntab * NF + DEGREES, 2 * ntab * NF + DEGREES + 8]
    return [slice(start, end) for start, end in zip([0] + ends, ends)]


def prepare_kernel(bins_hbm, table_hbm, ids_hbm, tables_hbm, out_hbm, *rest):
    bins_ref, table_ref, ids_ref, tables_ref, cos_ref, sin_ref, coef_ref, plan_ref = rest[:8]
    left_ref, right_ref, sems, table_sems = rest[8:]
    ntab = tables_ref.shape[0]
    nodes = cos_ref.shape[1]
    near = ids_ref.shape[0]
    first = pl.multiple_of(own_place() * (nodes // LANES) // near * near, 8)
    ins = start_all(
        [
            pltpu.make_async_copy(ids_hbm.at[pl.ds(first, near), :], ids_ref, sems.at[0]),
            pltpu.make_async_copy(bins_hbm, bins_ref, sems.at[1]),
            pltpu.make_async_copy(table_hbm, table_ref, sems.at[2]),
        ]
    )
    piece = tables_ref.shape[1] // TABLE_PIECES
    table_copies = []
    for at in range(TABLE_PIECES):
        part = (slice(None), pl.ds(at * piece, piece))
        table_copies.append(pltpu.make_async_copy(tables_hbm.at[part], tables_ref.at[part], table_sems.at[at]))
    start_all(table_copies)
    for copy in ins:
        copy.wait()
    cos_at, sin_at, coef_at, plan_at = packed_rows(ntab)
    coef_ref[...] = chebyshev_coefs(bins_ref)
    plan_ref[...] = station_plan(table_ref[...], plan_ref.shape[1])
    outs = start_all(
        [
            pltpu.make_async_copy(coef_ref, out_hbm.at[coef_at, pl.ds(0, LANES)], sems.at[0]),
            pltpu.make_async_copy(plan_ref, out_hbm.at[plan_at, pl.ds(0, plan_ref.shape[1])], sems.at[1]),
        ]
    )
    turns = pick_columns(ids_ref, tables_ref, table_copies, nodes, left_ref, right_ref) * (1.0 / 256.0)
    bins = bins_column(bins_ref)
    for table in range(ntab):
        cosine, sine = cos_sin(bins * turns[table : table + 1])
        at = pl.ds(table * NF, NF)
        cos_ref[at, :] = cosine
        sin_ref[at, :] = sine
        outs += start_all(
            [
                pltpu.make_async_copy(
                    cos_ref.at[at, :], out_hbm.at[pl.ds(cos_at.start + table * NF, NF), pl.ds(0, nodes)],
                    sems.at[3 + 2 * table],
                ),
                pltpu.make_async_copy(
                    sin_ref.at[at, :], out_hbm.at[pl.ds(sin_at.start + table * NF, NF), pl.ds(0, nodes)],
                    sems.at[4 + 2 * table],
                ),
            ]
        )
    for copy in outs:
        copy.wait()


def image_kernel(merged, stations_dev, packed_hbm, block_ref, *rest):
    corr_ref, rest = (None, rest) if merged else (rest[0], rest[1:])
    keep_ref, send_ref, plan_ref, place_of_ref, coef_ref, cos_ref, sin_ref, sems = rest[:8]
    place_ref, weight_ref, left_ref, sums_ref, basis_a, basis_b = rest[8:]
    places, nodes = place_ref.shape
    windows, groups, cores = (lax.axis_size(a) for a in ("win", "sta", "freq"))
    stations = stations_dev * groups
    cos_at, sin_at, coef_at, plan_at = packed_rows(cos_ref.shape[0] // NF)
    width = plan_ref.shape[1]
    copies = start_all(
        [
            pltpu.make_async_copy(packed_hbm.at[plan_at, pl.ds(0, width)], place_of_ref, sems.at[0]),
            pltpu.make_async_copy(packed_hbm.at[plan_at, pl.ds(0, width)], plan_ref, sems.at[1]),
            pltpu.make_async_copy(packed_hbm.at[coef_at, pl.ds(0, LANES)], coef_ref, sems.at[2]),
            pltpu.make_async_copy(packed_hbm.at[cos_at, pl.ds(0, nodes)], cos_ref, sems.at[3]),
            pltpu.make_async_copy(packed_hbm.at[sin_at, pl.ds(0, nodes)], sin_ref, sems.at[4]),
        ]
    )
    height = block_ref.shape[1]
    rows_of = lambda win, core: [(win * groups + group) * cores + core for group in range(groups)]

    even, odd = [], []
    for win in range(windows):
        value = []
        for group in range(groups):
            tile = None
            for core in range(cores):
                part = block_ref[(win * groups + group) * cores + core, height - 8 :, :].astype(jnp.float32)
                tile = part if tile is None else tile + part
            tile = tile[:, : LANES // 2] + tile[:, LANES // 2 :]
            value += [tile[:, 2 * NF * piece : 2 * NF * (piece + 1)] for piece in range(stations_dev // 8)]
        value = jnp.concatenate(value, axis=0)
        even.append(value)
        odd.append(jnp.concatenate([-value[:, NF:], value[:, :NF]], axis=1))
    spectra = jnp.concatenate(even + odd, axis=1)
    if merged:
        parts = []
        for win in range(windows):
            for core in range(cores):
                for first in range(0, height - 8, stations_dev):
                    rows = [block_ref[at, first : first + stations_dev, :] for at in rows_of(win, core)]
                    parts.append(jnp.concatenate(rows, axis=0))
        corr = jnp.concatenate(parts, axis=1)
    else:
        corr = corr_ref[...]

    copies[0].wait()
    place_row = place_of_ref[4:5, :stations].astype(jnp.int32)
    sorter = lax.broadcasted_iota(jnp.int32, (places, stations), 0) == place_row
    sorter = jnp.where(sorter, 1.0, 0.0).astype(jnp.bfloat16)
    found = None
    for piece in split_bf16(spectra, 3):
        part = jnp.dot(sorter, piece, preferred_element_type=jnp.float32)
        found = part if found is None else found + part
    weight_ref[...] = found
    place_ref[...] = jnp.dot(sorter, corr, preferred_element_type=jnp.float32) * (1.0 / REACH)
    sums_ref[...] = jnp.zeros_like(sums_ref)
    chunk = nodes
    depth = DEGREES * 8
    lanes = windows * 2 * NF
    for copy in copies[1:3]:
        copy.wait()

    def make_left(pair):
        top = weight_ref[pl.ds(pl.multiple_of(pair * 16, 16), 8), :]
        bottom = weight_ref[pl.ds(pl.multiple_of(pair * 16 + 8, 8), 8), :]
        sides = [
            jnp.concatenate([top[:, :lanes], bottom[:, :lanes]], axis=1),
            jnp.concatenate([top[:, lanes:], bottom[:, lanes:]], axis=1),
        ]
        per = LANES // 8
        for half in range(DEGREES // per):
            tall = jnp.concatenate(
                [sides[k % 2] * coef_ref[k : k + 1, :] for k in range(half * per, (half + 1) * per)], axis=0
            )
            at = slice(half * LANES, (half + 1) * LANES)
            for term, value in enumerate(split_bf16(tall.T, 2)):
                left_ref[2 * pair, term * lanes : (term + 1) * lanes, at] = value[:lanes]
                left_ref[2 * pair + 1, term * lanes : (term + 1) * lanes, at] = value[lanes:]

    used = plan_ref[3, 0].astype(jnp.int32)
    sure = stations // 16
    if sure <= 8:
        for pair in range(sure):
            make_left(pair)
    else:
        lax.fori_loop(0, sure, lambda pair, carry: (make_left(pair), carry)[1], 0)
    lax.fori_loop(sure, (used + 1) // 2, lambda pair, carry: (make_left(pair), carry)[1], 0)
    spot = (lax.broadcasted_iota(jnp.int32, (16, depth), 1) & 7).astype(jnp.float32)

    def left_of(group):
        mask = spot < plan_ref[2, group]
        results = []
        for keep, drop in ((1.0, 0.0), (0.0, 1.0)):
            side = jnp.where(mask, keep, drop).astype(jnp.bfloat16)
            results.append(left_ref[group] * jnp.concatenate([side] * (2 * lanes // 16), axis=0))
        high = jnp.concatenate([result[:lanes] for result in results], axis=0)
        low = jnp.concatenate([result[lanes:] for result in results], axis=0)
        return jnp.concatenate([high, high, low], axis=1)

    def basis_steps(group, basis_ref):
        arg = place_ref[pl.ds(pl.multiple_of(group * 8, 8), 8), :]
        twice = arg + arg
        before, now = jnp.ones_like(arg), arg
        for degree in range(0, DEGREES, 2):
            pair = jnp.concatenate([before, now], axis=0)
            high, low = split_bf16(pair, 2)
            basis_ref[degree * 8 : degree * 8 + 16, :] = high
            basis_ref[depth + degree * 8 : depth + degree * 8 + 16, :] = low
            before = twice * now - before
            now = twice * before - now
            if degree % 8 == 6:
                yield

    def run(steps):
        for _ in steps:
            pass

    def add_group(group, basis_ref, steps):
        left = left_of(group)
        tables = [plan_ref[slot, group].astype(jnp.int32) for slot in range(2)]
        phasor_rows = [pl.ds(pl.multiple_of(table * NF, NF), NF) for table in tables]
        for first in range(0, nodes, chunk):
            at = slice(first, first + chunk)
            right = jnp.concatenate([basis_ref[:, at], basis_ref[:depth, at]], axis=0)
            got = jnp.dot(left, right, preferred_element_type=jnp.float32)
            run(steps)
            for win in range(windows):
                row = win * 2 * NF
                real_sum, imag_sum = sums_ref[row : row + NF, at], sums_ref[row + NF : row + 2 * NF, at]
                for slot, rows in enumerate(phasor_rows):
                    cosine, sine = cos_ref[rows, at], sin_ref[rows, at]
                    real = got[slot * lanes + row : slot * lanes + row + NF]
                    imag = got[slot * lanes + row + NF : slot * lanes + row + 2 * NF]
                    real_sum += real * cosine - imag * sine
                    imag_sum += real * sine + imag * cosine
                sums_ref[row : row + NF, at], sums_ref[row + NF : row + 2 * NF, at] = real_sum, imag_sum
        run(steps)

    run(basis_steps(0, basis_a))
    for copy in copies[3:]:
        copy.wait()

    def body(pair, carry):
        group = pair * 2
        add_group(group, basis_a, basis_steps(group + 1, basis_b))
        add_group(group + 1, basis_b, basis_steps(jnp.minimum(group + 2, places // 8 - 1), basis_a))
        return carry

    lax.fori_loop(0, (used + 1) // 2, body, 0)
    powers = []
    for win in range(windows):
        row = win * 2 * NF
        real, imag = sums_ref[row : row + NF, :], sums_ref[row + NF : row + 2 * NF, :]
        powers.append(real * real + imag * imag)
    mine = lax.axis_index("win") == 0
    keep_ref[...] = jnp.where(mine, powers[0], powers[1])
    send_ref[...] = jnp.where(mine, powers[1], powers[0])


def finish_kernel(stations, keep_ref, got_ref, spectrum_ref, beam_ref):
    nodes = keep_ref.shape[1]
    win = lax.axis_index("win")
    for place, ref in ((win, keep_ref), (1 - win, got_ref)):
        power = ref[...]
        total = jnp.sum(power, axis=0, keepdims=True)
        at = pl.ds(pl.multiple_of(place * nodes, LANES), nodes)
        spectrum_ref[:, at] = power * (NF / total)
        beam_ref[:, at] = total * (1.0 / (NF * stations))


def on_device(traces, tables, corrections, station_table, node_ids, freq_bins):
    windows, groups, cores = (lax.axis_size(a) for a in ("win", "sta", "freq"))
    stations_dev, grid = corrections.shape
    stations = stations_dev * groups
    devices = windows * groups * cores
    nodes = grid // devices
    ntab = tables.shape[0]
    params = lambda free: pltpu.CompilerParams(vmem_limit_bytes=VMEM_LIMIT - free)
    vmem = pl.BlockSpec(memory_space=pltpu.VMEM)
    hbm = pl.BlockSpec(memory_space=pltpu.HBM)
    bins = freq_bins.reshape(1, NF)
    bins_scratch = pltpu.VMEM((1, NF), jnp.int32)

    holders = windows * cores
    merged = nodes % (holders * LANES) == 0
    pieces = nodes // (holders * LANES) if merged else 0
    height = pieces * stations_dev + 8
    blocks = pl.pallas_call(
        functools.partial(send_kernel, nodes),
        out_shape=jax.ShapeDtypeStruct((devices, height, LANES), jnp.bfloat16),
        in_specs=[hbm] * 3,
        out_specs=vmem,
        scratch_shapes=[
            bins_scratch,
            pltpu.VMEM(traces.shape, traces.dtype),
            pltpu.SemaphoreType.DMA((2 + devices * max(pieces, 1),)),
        ],
        compiler_params=params(0),
        name="send",
    )(bins, traces, corrections)
    received = [lax.all_to_all(blocks, ("win", "sta", "freq"), split_axis=0, concat_axis=0, tiled=True)]
    if not merged:
        parts = corrections.reshape(stations_dev, groups, holders, nodes)
        place = lax.axis_index("freq") * windows + lax.axis_index("win")
        mine = lax.dynamic_index_in_dim(parts, place, axis=2, keepdims=False)
        corr = lax.all_to_all(mine.transpose(1, 0, 2), "sta", split_axis=0, concat_axis=0, tiled=True)
        received.append(corr.reshape(stations, nodes))

    wide = 512
    plan_width = max(LANES, stations)
    phasors = pltpu.VMEM((ntab * NF, nodes), jnp.float32)
    coefs = pltpu.VMEM((DEGREES, LANES), jnp.float32)
    plan = pltpu.VMEM((8, plan_width), jnp.float32)
    packed_shape = (packed_rows(ntab)[-1].stop, max(nodes, plan_width))
    packed = pl.pallas_call(
        prepare_kernel,
        out_shape=jax.ShapeDtypeStruct(packed_shape, jnp.float32),
        in_specs=[hbm] * 4,
        out_specs=hbm,
        scratch_shapes=[
            bins_scratch,
            pltpu.VMEM((1, stations), jnp.int32),
            pltpu.VMEM((max(nodes // LANES, 8), LANES), jnp.int32),
            pltpu.VMEM(tables.shape, tables.dtype),
            phasors,
            phasors,
            coefs,
            plan,
            pltpu.VMEM((grid // wide * ntab, 3 * wide), jnp.bfloat16),
            pltpu.VMEM((3 * wide, nodes), jnp.bfloat16),
            pltpu.SemaphoreType.DMA((3 + 2 * ntab,)),
            pltpu.SemaphoreType.DMA((TABLE_PIECES,)),
        ],
        compiler_params=params(512 * 1024),
        name="prepare",
    )(bins, station_table.reshape(1, stations), node_ids.reshape(grid // LANES, LANES), tables)

    places = (stations // 8 + ntab // 2 + 2) // 2 * 16
    half = jax.ShapeDtypeStruct((NF, nodes), jnp.float32)
    rows = 2 * windows * 2 * NF
    basis = pltpu.VMEM((2 * DEGREES * 8, nodes), jnp.bfloat16)
    keep, send = pl.pallas_call(
        functools.partial(image_kernel, merged, stations_dev),
        out_shape=[half, half],
        in_specs=[hbm] + [vmem] * len(received),
        out_specs=[vmem, vmem],
        scratch_shapes=[
            pltpu.SMEM((8, plan_width), jnp.float32),
            plan,
            coefs,
            phasors,
            phasors,
            pltpu.SemaphoreType.DMA((5,)),
            pltpu.VMEM((places, nodes), jnp.float32),
            pltpu.VMEM((places, rows), jnp.float32),
            pltpu.VMEM((places // 8, rows, DEGREES * 8), jnp.bfloat16),
            pltpu.VMEM((rows // 2, nodes), jnp.float32),
            basis,
            basis,
        ],
        compiler_params=params(23 * 512 * 1024),
        name="image",
    )(packed, *received)
    got = lax.ppermute(send, "win", [(0, 1), (1, 0)])
    spectrum, beam_power = pl.pallas_call(
        functools.partial(finish_kernel, stations),
        out_shape=[
            jax.ShapeDtypeStruct((NF, windows * nodes), jnp.float32),
            jax.ShapeDtypeStruct((1, windows * nodes), jnp.float32),
        ],
        in_specs=[vmem, vmem],
        out_specs=[vmem, vmem],
        compiler_params=params(32 * 1024 * 1024),
        name="finish",
    )(keep, got)
    return spectrum, beam_power.reshape(windows * nodes)


def solution(mesh):
    return jax.shard_map(
        on_device,
        mesh=mesh,
        in_specs=(P(("win", "sta"), "freq"), P(), P("sta", None), P(), P(), P()),
        out_specs=(P("win", ("sta", "freq")), P(("win", "sta", "freq"))),
        check_vma=False,
    )
```

```python
import functools
import math

import jax
import jax.numpy as jnp
import numpy as np
from jax import lax
from jax.experimental import pallas as pl
from jax.experimental.pallas import tpu as pltpu
from jax.sharding import PartitionSpec as P

NT = 5120
NF = 16
NTAB = 16
LANES = 128
DEGREES = 32
REACH = 1.5
TABLE_PIECES = 4
VMEM_LIMIT = 64 * 1024 * 1024 - 64 * 1024


def chebyshev_fit(func, degree, low, high):
    fit = np.polynomial.chebyshev.Chebyshev.interpolate(func, degree, domain=[low, high])
    return [float(v) for v in fit.convert(kind=np.polynomial.Polynomial).coef]


SIN_HALF = chebyshev_fit(lambda z: np.pi * np.sinc(np.sqrt(z)), 4, 0.0, 0.25)
COS_HALF = chebyshev_fit(lambda z: np.cos(np.pi * np.sqrt(z)), 4, 0.0, 0.25)


def horner(coefs, arg):
    total = coefs[-1]
    for coef in coefs[-2::-1]:
        total = total * arg + coef
    return total


def turn_parts(rest):
    square = rest * rest
    root = math.sqrt(2.0)
    sine_half = rest * horner([root * c for c in SIN_HALF], square)
    cos_half = horner([root * c for c in COS_HALF], square)
    return sine_half * sine_half, sine_half * cos_half


def cos_sin(turns):
    versine, sine = turn_parts(turns - jnp.round(turns))
    return 1.0 - versine, sine


def bins_column(row):
    rows = lax.broadcasted_iota(jnp.int32, (NF, NF), 0)
    lanes = lax.broadcasted_iota(jnp.int32, (NF, NF), 1)
    square = jnp.broadcast_to(row, (NF, NF))
    return jnp.sum(jnp.where(rows == lanes, square, 0.0), axis=1, keepdims=True)


def split_bf16(value, terms):
    pieces = []
    for term in range(terms):
        piece = value.astype(jnp.bfloat16)
        pieces.append(piece)
        if term < terms - 1:
            value = value - piece.astype(jnp.float32)
    return pieces


def start_all(copies):
    for copy in copies:
        copy.start()
    return copies


def send_kernel(nodes, bins_hbm, traces_hbm, corr_hbm, out_ref, bins_ref, traces_ref, sems):
    peers, height, _ = out_ref.shape
    stations_dev, half_length = traces_ref.shape
    pieces = (height - 8) // stations_dev
    windows, groups, cores = (lax.axis_size(a) for a in ("win", "sta", "freq"))
    small = start_all(
        [
            pltpu.make_async_copy(bins_hbm, bins_ref, sems.at[0]),
            pltpu.make_async_copy(traces_hbm, traces_ref, sems.at[1]),
        ]
    )
    copies = []
    for peer in range(peers):
        first = ((peer % groups * cores + lax.axis_index("freq")) * windows + peer // groups) * nodes
        for piece in range(pieces):
            at = pl.multiple_of(first + (lax.axis_index("win") * pieces + piece) * LANES, LANES)
            to = out_ref.at[peer, pl.ds(piece * stations_dev, stations_dev), :]
            sem = sems.at[2 + peer * pieces + piece]
            copies.append(pltpu.make_async_copy(corr_hbm.at[:, pl.ds(at, LANES)], to, sem))
    start_all(copies)
    start = lax.axis_index("freq") * half_length
    small[0].wait()
    bins = bins_column(bins_ref[...].astype(jnp.float32))
    pos = (start + lax.broadcasted_iota(jnp.int32, (NF, half_length), 1)).astype(jnp.float32)
    product = bins * pos
    turns = jnp.round(product * (1.0 / NT))
    rest = (product - turns * NT) * (1.0 / NT)
    versine, sine = turn_parts(rest)
    scale = 1.0 / math.sqrt(NT)
    table = jnp.concatenate([(1.0 - versine) * scale, sine * -scale], axis=0)
    both = jnp.concatenate(split_bf16(table, 2), axis=0)
    small[1].wait()
    sums = lax.dot_general(
        traces_ref[...], both, (((1,), (1,)), ((), ())), preferred_element_type=jnp.float32
    )
    sums = sums[:, : 2 * NF] + sums[:, 2 * NF :]
    terms = [term.astype(jnp.float32) for term in split_bf16(sums, 2)]
    tile = jnp.concatenate([term[at : at + 8] for term in terms for at in range(0, stations_dev, 8)], axis=1)
    tile = tile.astype(jnp.bfloat16)
    for peer in range(peers):
        out_ref[peer, height - 8 :, :] = tile
    for copy in copies:
        copy.wait()


def own_place():
    windows, cores = lax.axis_size("win"), lax.axis_size("freq")
    return (lax.axis_index("sta") * cores + lax.axis_index("freq")) * windows + lax.axis_index("win")


def pick_columns(ids_ref, tables_ref, table_copies, nodes, left_ref, right_ref, beside):
    ntab, grid = tables_ref.shape
    count = nodes // LANES
    wide = right_ref.shape[0] // 3
    blocks = grid // wide
    ids = ids_ref[pl.ds(own_place() * count % ids_ref.shape[0], count), :]
    ids = jnp.concatenate([ids[at : at + 1] for at in range(count)], axis=1)
    low, high = ids & (wide - 1), ids >> (wide.bit_length() - 1)
    spots = lax.broadcasted_iota(jnp.int32, (wide, nodes), 0)
    ones = jnp.where(spots == low, 1.0, 0.0).astype(jnp.bfloat16)
    for term in range(3):
        right_ref[term * wide : (term + 1) * wide, :] = ones
    found = jnp.zeros((ntab, nodes), jnp.float32)
    step = blocks // len(table_copies)
    for at, copy in enumerate(table_copies):
        copy.wait()
        for block in range(at * step, (at + 1) * step):
            pieces = split_bf16(tables_ref[:, block * wide : (block + 1) * wide], 3)
            left_ref[block * ntab : (block + 1) * ntab, :] = jnp.concatenate(pieces, axis=1)
        if at < len(beside):
            beside[at]()
        rows = left_ref[at * step * ntab : (at + 1) * step * ntab, :]
        picked = jnp.dot(rows, right_ref[...], preferred_element_type=jnp.float32)
        for block in range(step):
            part = picked[block * ntab : (block + 1) * ntab]
            found = jnp.where(high == at * step + block, part, found)
    return found


def chebyshev_coefs(bins_ref):
    shape = (DEGREES, DEGREES)
    degree = lax.broadcasted_iota(jnp.int32, shape, 0)
    node = lax.broadcasted_iota(jnp.int32, shape, 1)
    period = 4 * DEGREES
    weight, _ = cos_sin((degree * (2 * node + 1) & (period - 1)).astype(jnp.float32) * (1.0 / period))
    weight = weight * jnp.where(degree == 0, 1.0 / DEGREES, 2.0 / DEGREES)
    even = jnp.where(degree % 2 == 0, weight, 0.0)
    odd = jnp.where(degree % 2 == 1, weight, 0.0)
    row = bins_ref[...].astype(jnp.float32)
    bins = jnp.concatenate([row] * (LANES // NF), axis=1)
    at = lax.broadcasted_iota(jnp.int32, (DEGREES, LANES), 0).astype(jnp.float32)
    spot, _ = cos_sin((2.0 * at + 1.0) * (1.0 / period))
    cosine, sine = cos_sin(bins * (spot * (REACH / 256.0)))
    dot = functools.partial(jnp.dot, precision=lax.Precision.HIGHEST, preferred_element_type=jnp.float32)
    return dot(even, cosine) + dot(odd, sine)


def station_plan(table_row, bins_row, width):
    count = table_row.shape[1]
    shape = (count, count)
    here = lax.broadcasted_iota(jnp.int32, shape, 0)
    there = lax.broadcasted_iota(jnp.int32, shape, 1)
    column_of = lambda row: jnp.sum(jnp.where(here == there, jnp.broadcast_to(row, shape), 0), axis=1, keepdims=True)
    table_column = column_of(table_row)
    same = (table_column == table_row) & (here < there)
    within = jnp.sum(jnp.where(same, 1, 0), axis=0, keepdims=True)
    place_row = within
    spot = jnp.zeros((1, 1), jnp.int32)
    held = jnp.zeros((1, 1), jnp.int32)
    for table in range(NTAB):
        size = jnp.sum(jnp.where(table_row == table, 1, 0), axis=1, keepdims=True)
        some = size > 0
        edge = (spot & 7) == 0
        skip = some & (held >= 2) & ~edge
        spot = jnp.where(skip, (spot + 7) >> 3 << 3, spot)
        held = jnp.where(skip | edge, 0, held)
        after = spot + size
        place_row = place_row + jnp.where(table_row == table, spot, 0)
        held = jnp.where(some, jnp.where(after >> 3 == spot >> 3, held + 1, 1), held)
        spot = after
    groups = (spot + 7) >> 3
    place_column = column_of(place_row)
    group = lax.broadcasted_iota(jnp.int32, (count, width), 1)
    inside = place_column >> 3 == group
    first = jnp.sum(jnp.where(place_column == group * 8, table_column, 0), axis=0, keepdims=True)
    last = jnp.max(jnp.where(inside, table_column, 0), axis=0, keepdims=True)
    length = jnp.sum(jnp.where(inside & (table_column == first), 1, 0), axis=0, keepdims=True)
    rows = [first, last, length, jnp.broadcast_to(groups, (1, width))]
    if width > count:
        place_row = jnp.concatenate([place_row, jnp.zeros((1, width - count), jnp.int32)], axis=1)
    bins_row = jnp.concatenate([bins_row, jnp.zeros((1, width - NF), jnp.int32)], axis=1)
    rows += [place_row, bins_row, jnp.zeros((2, width), jnp.int32)]
    return jnp.concatenate(rows, axis=0).astype(jnp.float32)


TURNS_AT, COEF_AT, PLAN_AT, PACKED_ROWS = slice(0, NTAB), slice(16, 48), slice(48, 56), 640


def prepare_kernel(bins_hbm, table_hbm, ids_hbm, tables_hbm, out_hbm, *rest):
    bins_ref, table_ref, ids_ref, tables_ref, turns_ref, coef_ref, plan_ref = rest[:7]
    left_ref, right_ref, sems, table_sems = rest[7:]
    nodes = turns_ref.shape[1]
    near = ids_ref.shape[0]
    first = pl.multiple_of(own_place() * (nodes // LANES) // near * near, 8)
    ins = start_all(
        [
            pltpu.make_async_copy(ids_hbm.at[pl.ds(first, near), :], ids_ref, sems.at[0]),
            pltpu.make_async_copy(bins_hbm, bins_ref, sems.at[1]),
            pltpu.make_async_copy(table_hbm, table_ref, sems.at[2]),
        ]
    )
    piece = tables_ref.shape[1] // TABLE_PIECES
    table_copies = []
    for at in range(TABLE_PIECES):
        part = (slice(None), pl.ds(at * piece, piece))
        table_copies.append(pltpu.make_async_copy(tables_hbm.at[part], tables_ref.at[part], table_sems.at[at]))
    start_all(table_copies)
    for copy in ins:
        copy.wait()

    def make_coefs():
        coef_ref[...] = chebyshev_coefs(bins_ref)

    def make_plan():
        plan_ref[...] = station_plan(table_ref[...], bins_ref[...], plan_ref.shape[1])

    beside = [make_coefs, make_plan]
    turns_ref[...] = pick_columns(ids_ref, tables_ref, table_copies, nodes, left_ref, right_ref, beside) * (1.0 / 256.0)
    outs = start_all(
        [
            pltpu.make_async_copy(coef_ref, out_hbm.at[COEF_AT, pl.ds(0, LANES)], sems.at[0]),
            pltpu.make_async_copy(plan_ref, out_hbm.at[PLAN_AT, pl.ds(0, plan_ref.shape[1])], sems.at[1]),
            pltpu.make_async_copy(turns_ref, out_hbm.at[TURNS_AT, pl.ds(0, nodes)], sems.at[2]),
        ]
    )
    for copy in outs:
        copy.wait()


def image_kernel(merged, stations_dev, packed_hbm, other_ref, block_ref, *rest):
    corr_ref, rest = (None, rest) if merged else (rest[0], rest[1:])
    keep_ref, send_ref, plan_ref, place_of_ref, coef_ref, turns_ref, cos_ref, sin_ref, sems = rest[:9]
    place_ref, weight_ref, left_ref, sums_ref, basis_a, basis_b = rest[9:]
    places, nodes = place_ref.shape
    windows, groups = lax.axis_size("win"), lax.axis_size("sta")
    stations = stations_dev * groups
    width = plan_ref.shape[1]
    copies = start_all(
        [
            pltpu.make_async_copy(packed_hbm.at[PLAN_AT, pl.ds(0, width)], place_of_ref, sems.at[0]),
            pltpu.make_async_copy(packed_hbm.at[TURNS_AT, pl.ds(0, nodes)], turns_ref, sems.at[1]),
            pltpu.make_async_copy(packed_hbm.at[COEF_AT, pl.ds(0, LANES)], coef_ref, sems.at[2]),
            pltpu.make_async_copy(packed_hbm.at[PLAN_AT, pl.ds(0, width)], plan_ref, sems.at[3]),
        ]
    )
    height = block_ref.shape[1]

    even, odd = [], []
    for win in range(windows):
        value = []
        for group in range(groups):
            at = win * groups + group
            tile = block_ref[at, height - 8 :, :].astype(jnp.float32) + other_ref[at].astype(jnp.float32)
            tile = tile[:, : LANES // 2] + tile[:, LANES // 2 :]
            value += [tile[:, 2 * NF * piece : 2 * NF * (piece + 1)] for piece in range(stations_dev // 8)]
        value = jnp.concatenate(value, axis=0)
        even.append(value)
        odd.append(jnp.concatenate([-value[:, NF:], value[:, :NF]], axis=1))
    spectra = jnp.concatenate(even + odd, axis=1)
    if merged:
        parts = []
        for win in range(windows):
            for first in range(0, height - 8, stations_dev):
                rows = slice(first, first + stations_dev)
                parts.append(jnp.concatenate([block_ref[win * groups + at, rows, :] for at in range(groups)], axis=0))
        corr = jnp.concatenate(parts, axis=1)
    else:
        corr = corr_ref[...]

    copies[0].wait()
    place_row = place_of_ref[4:5, :stations].astype(jnp.int32)
    sorter = lax.broadcasted_iota(jnp.int32, (places, stations), 0) == place_row
    sorter = jnp.where(sorter, 1.0, 0.0).astype(jnp.bfloat16)
    found = None
    for piece in split_bf16(spectra, 3):
        part = jnp.dot(sorter, piece, preferred_element_type=jnp.float32)
        found = part if found is None else found + part
    weight_ref[...] = found
    place_ref[...] = jnp.dot(sorter, corr, preferred_element_type=jnp.float32) * (1.0 / REACH)
    sums_ref[...] = jnp.zeros_like(sums_ref)
    chunk = min(256, nodes)
    depth = DEGREES * 8
    lanes = windows * 2 * NF
    for copy in copies[1:]:
        copy.wait()

    bins = bins_column(place_of_ref[5:6, :NF])
    for table in range(NTAB):
        cosine, sine = cos_sin(bins * turns_ref[table : table + 1, :])
        cos_ref[table * NF : (table + 1) * NF, :] = cosine
        sin_ref[table * NF : (table + 1) * NF, :] = sine

    def make_left(pair):
        top = weight_ref[pl.ds(pl.multiple_of(pair * 16, 16), 8), :]
        bottom = weight_ref[pl.ds(pl.multiple_of(pair * 16 + 8, 8), 8), :]
        sides = [
            jnp.concatenate([top[:, :lanes], bottom[:, :lanes]], axis=1),
            jnp.concatenate([top[:, lanes:], bottom[:, lanes:]], axis=1),
        ]
        per = LANES // 8
        for half in range(DEGREES // per):
            tall = jnp.concatenate(
                [sides[k % 2] * coef_ref[k : k + 1, :] for k in range(half * per, (half + 1) * per)], axis=0
            )
            at = slice(half * LANES, (half + 1) * LANES)
            for term, value in enumerate(split_bf16(tall.T, 2)):
                left_ref[2 * pair, term * lanes : (term + 1) * lanes, at] = value[:lanes]
                left_ref[2 * pair + 1, term * lanes : (term + 1) * lanes, at] = value[lanes:]

    used = plan_ref[3, 0].astype(jnp.int32)
    sure = stations // 16
    if sure <= 8:
        for pair in range(sure):
            make_left(pair)
    else:
        lax.fori_loop(0, sure, lambda pair, carry: (make_left(pair), carry)[1], 0)
    lax.fori_loop(sure, (used + 1) // 2, lambda pair, carry: (make_left(pair), carry)[1], 0)
    spot = (lax.broadcasted_iota(jnp.int32, (16, depth), 1) & 7).astype(jnp.float32)

    def left_of(group):
        mask = spot < plan_ref[2, group]
        results = []
        for keep, drop in ((1.0, 0.0), (0.0, 1.0)):
            side = jnp.where(mask, keep, drop).astype(jnp.bfloat16)
            results.append(left_ref[group] * jnp.concatenate([side] * (2 * lanes // 16), axis=0))
        high = jnp.concatenate([result[:lanes] for result in results], axis=0)
        return jnp.concatenate(results, axis=0), high

    def basis_steps(group, basis_ref):
        arg = place_ref[pl.ds(pl.multiple_of(group * 8, 8), 8), :]
        twice = arg + arg
        before, now = jnp.ones_like(arg), arg
        for degree in range(0, DEGREES, 2):
            pair = jnp.concatenate([before, now], axis=0)
            high, low = split_bf16(pair, 2)
            basis_ref[degree * 8 : degree * 8 + 16, :] = high
            basis_ref[depth + degree * 8 : depth + degree * 8 + 16, :] = low
            before = twice * now - before
            now = twice * before - now
            if degree % 8 == 6:
                yield

    def run(steps):
        for _ in steps:
            pass

    def add_group(group, basis_ref, steps):
        both, high = left_of(group)
        tables = [plan_ref[slot, group].astype(jnp.int32) for slot in range(2)]
        phasor_rows = [pl.ds(pl.multiple_of(table * NF, NF), NF) for table in tables]
        for first in range(0, nodes, chunk):
            at = slice(first, first + chunk)
            got = jnp.dot(both, basis_ref[:depth, at], preferred_element_type=jnp.float32)
            more = jnp.dot(high, basis_ref[depth:, at], preferred_element_type=jnp.float32)
            next(steps, None)
            got = [
                got[2 * slot * lanes : (2 * slot + 1) * lanes]
                + got[(2 * slot + 1) * lanes : (2 * slot + 2) * lanes]
                + more[slot * lanes : (slot + 1) * lanes]
                for slot in range(2)
            ]
            for win in range(windows):
                row = win * 2 * NF
                real_sum, imag_sum = sums_ref[row : row + NF, at], sums_ref[row + NF : row + 2 * NF, at]
                for slot, rows in enumerate(phasor_rows):
                    cosine, sine = cos_ref[rows, at], sin_ref[rows, at]
                    real, imag = got[slot][row : row + NF], got[slot][row + NF : row + 2 * NF]
                    real_sum += real * cosine - imag * sine
                    imag_sum += real * sine + imag * cosine
                sums_ref[row : row + NF, at], sums_ref[row + NF : row + 2 * NF, at] = real_sum, imag_sum
        run(steps)

    run(basis_steps(0, basis_a))

    def body(pair, carry):
        group = pair * 2
        add_group(group, basis_a, basis_steps(group + 1, basis_b))
        add_group(group + 1, basis_b, basis_steps(jnp.minimum(group + 2, places // 8 - 1), basis_a))
        return carry

    lax.fori_loop(0, (used + 1) // 2, body, 0)
    powers = []
    for win in range(windows):
        row = win * 2 * NF
        real, imag = sums_ref[row : row + NF, :], sums_ref[row + NF : row + 2 * NF, :]
        powers.append(real * real + imag * imag)
    mine = lax.axis_index("win") == 0
    keep_ref[...] = jnp.where(mine, powers[0], powers[1])
    send_ref[...] = jnp.where(mine, powers[1], powers[0])


def finish_kernel(stations, keep_ref, got_ref, spectrum_ref, beam_ref):
    nodes = keep_ref.shape[1]
    win = lax.axis_index("win")
    for place, ref in ((win, keep_ref), (1 - win, got_ref)):
        power = ref[...]
        total = jnp.sum(power, axis=0, keepdims=True)
        at = pl.ds(pl.multiple_of(place * nodes, LANES), nodes)
        spectrum_ref[:, at] = power * (NF / total)
        beam_ref[:, at] = total * (1.0 / (NF * stations))


def on_device(traces, tables, corrections, station_table, node_ids, freq_bins):
    windows, groups, cores = (lax.axis_size(a) for a in ("win", "sta", "freq"))
    stations_dev, grid = corrections.shape
    stations = stations_dev * groups
    devices = windows * groups * cores
    nodes = grid // devices
    ntab = tables.shape[0]
    params = lambda free: pltpu.CompilerParams(vmem_limit_bytes=VMEM_LIMIT - free)
    vmem = pl.BlockSpec(memory_space=pltpu.VMEM)
    hbm = pl.BlockSpec(memory_space=pltpu.HBM)
    bins = freq_bins.reshape(1, NF)
    bins_scratch = pltpu.VMEM((1, NF), jnp.int32)

    peers = windows * groups
    merged = nodes % (windows * LANES) == 0
    pieces = nodes // (windows * LANES) if merged else 0
    height = pieces * stations_dev + 8
    blocks = pl.pallas_call(
        functools.partial(send_kernel, nodes),
        out_shape=jax.ShapeDtypeStruct((peers, height, LANES), jnp.bfloat16),
        in_specs=[hbm] * 3,
        out_specs=vmem,
        scratch_shapes=[
            bins_scratch,
            pltpu.VMEM(traces.shape, traces.dtype),
            pltpu.SemaphoreType.DMA((2 + peers * max(pieces, 1),)),
        ],
        compiler_params=params(0),
        name="send",
    )(bins, traces, corrections)
    received = [lax.all_to_all(blocks, ("win", "sta"), split_axis=0, concat_axis=0, tiled=True)]
    other = lax.ppermute(received[0][:, height - 8 :, :], "freq", [(0, 1), (1, 0)])
    if not merged:
        parts = corrections.reshape(stations_dev, groups, cores * windows, nodes)
        place = lax.axis_index("freq") * windows + lax.axis_index("win")
        mine = lax.dynamic_index_in_dim(parts, place, axis=2, keepdims=False)
        corr = lax.all_to_all(mine.transpose(1, 0, 2), "sta", split_axis=0, concat_axis=0, tiled=True)
        received.append(corr.reshape(stations, nodes))

    wide = 512
    plan_width = max(LANES, stations)
    turns = pltpu.VMEM((ntab, nodes), jnp.float32)
    phasors = pltpu.VMEM((ntab * NF, nodes), jnp.float32)
    coefs = pltpu.VMEM((DEGREES, LANES), jnp.float32)
    plan = pltpu.VMEM((8, plan_width), jnp.float32)
    packed_shape = (PACKED_ROWS, max(nodes, plan_width))
    packed = pl.pallas_call(
        prepare_kernel,
        out_shape=jax.ShapeDtypeStruct(packed_shape, jnp.float32),
        in_specs=[hbm] * 4,
        out_specs=hbm,
        scratch_shapes=[
            bins_scratch,
            pltpu.VMEM((1, stations), jnp.int32),
            pltpu.VMEM((max(nodes // LANES, 8), LANES), jnp.int32),
            pltpu.VMEM(tables.shape, tables.dtype),
            turns,
            coefs,
            plan,
            pltpu.VMEM((grid // wide * ntab, 3 * wide), jnp.bfloat16),
            pltpu.VMEM((3 * wide, nodes), jnp.bfloat16),
            pltpu.SemaphoreType.DMA((3,)),
            pltpu.SemaphoreType.DMA((TABLE_PIECES,)),
        ],
        compiler_params=params(512 * 1024),
        name="prepare",
    )(bins, station_table.reshape(1, stations), node_ids.reshape(grid // LANES, LANES), tables)

    places = (stations // 8 + ntab // 2 + 2) // 2 * 16
    half = jax.ShapeDtypeStruct((NF, nodes), jnp.float32)
    rows = 2 * windows * 2 * NF
    basis = pltpu.VMEM((2 * DEGREES * 8, nodes), jnp.bfloat16)
    keep, send = pl.pallas_call(
        functools.partial(image_kernel, merged, stations_dev),
        out_shape=[half, half],
        in_specs=[hbm] + [vmem] * (1 + len(received)),
        out_specs=[vmem, vmem],
        scratch_shapes=[
            pltpu.SMEM((8, plan_width), jnp.float32),
            plan,
            coefs,
            turns,
            phasors,
            phasors,
            pltpu.SemaphoreType.DMA((4,)),
            pltpu.VMEM((places, nodes), jnp.float32),
            pltpu.VMEM((places, rows), jnp.float32),
            pltpu.VMEM((places // 8, rows, DEGREES * 8), jnp.bfloat16),
            pltpu.VMEM((rows // 2, nodes), jnp.float32),
            basis,
            basis,
        ],
        compiler_params=params(23 * 512 * 1024),
        name="image",
    )(packed, other, *received)
    got = lax.ppermute(send, "win", [(0, 1), (1, 0)])
    spectrum, beam_power = pl.pallas_call(
        functools.partial(finish_kernel, stations),
        out_shape=[
            jax.ShapeDtypeStruct((NF, windows * nodes), jnp.float32),
            jax.ShapeDtypeStruct((1, windows * nodes), jnp.float32),
        ],
        in_specs=[vmem, vmem],
        out_specs=[vmem, vmem],
        compiler_params=params(32 * 1024 * 1024),
        name="finish",
    )(keep, got)
    return spectrum, beam_power.reshape(windows * nodes)


def solution(mesh):
    return jax.shard_map(
        on_device,
        mesh=mesh,
        in_specs=(P(("win", "sta"), "freq"), P(), P("sta", None), P(), P(), P()),
        out_specs=(P("win", ("sta", "freq")), P(("win", "sta", "freq"))),
        check_vma=False,
    )
```

```python
import functools
import math

import jax
import jax.numpy as jnp
import numpy as np
from jax import lax
from jax.experimental import pallas as pl
from jax.experimental.pallas import tpu as pltpu
from jax.sharding import PartitionSpec as P

NT = 5120
NF = 16
NTAB = 16
LANES = 128
DEGREES = 32
REACH = 1.5
TABLE_PIECES = 4
VMEM_LIMIT = 64 * 1024 * 1024 - 64 * 1024


def chebyshev_fit(func, degree, low, high):
    fit = np.polynomial.chebyshev.Chebyshev.interpolate(func, degree, domain=[low, high])
    return [float(v) for v in fit.convert(kind=np.polynomial.Polynomial).coef]


SIN_HALF = chebyshev_fit(lambda z: np.pi * np.sinc(np.sqrt(z)), 4, 0.0, 0.25)
COS_HALF = chebyshev_fit(lambda z: np.cos(np.pi * np.sqrt(z)), 4, 0.0, 0.25)


def horner(coefs, arg):
    total = coefs[-1]
    for coef in coefs[-2::-1]:
        total = total * arg + coef
    return total


def turn_parts(rest):
    square = rest * rest
    root = math.sqrt(2.0)
    sine_half = rest * horner([root * c for c in SIN_HALF], square)
    cos_half = horner([root * c for c in COS_HALF], square)
    return sine_half * sine_half, sine_half * cos_half


def cos_sin(turns):
    versine, sine = turn_parts(turns - jnp.round(turns))
    return 1.0 - versine, sine


def bins_column(bins_ref):
    rows = lax.broadcasted_iota(jnp.int32, (NF, NF), 0)
    lanes = lax.broadcasted_iota(jnp.int32, (NF, NF), 1)
    square = jnp.broadcast_to(bins_ref[...].astype(jnp.float32), (NF, NF))
    return jnp.sum(jnp.where(rows == lanes, square, 0.0), axis=1, keepdims=True)


def split_bf16(value, terms):
    pieces = []
    for term in range(terms):
        piece = value.astype(jnp.bfloat16)
        pieces.append(piece)
        if term < terms - 1:
            value = value - piece.astype(jnp.float32)
    return pieces


def start_all(copies):
    for copy in copies:
        copy.start()
    return copies


def send_kernel(nodes, bins_hbm, traces_hbm, corr_hbm, out_ref, bins_ref, traces_ref, sems):
    devices, height, _ = out_ref.shape
    stations_dev, half_length = traces_ref.shape
    pieces = (height - 8) // stations_dev
    windows, groups, cores = (lax.axis_size(a) for a in ("win", "sta", "freq"))
    place = lax.axis_index("win") * cores + lax.axis_index("freq")
    small = start_all(
        [
            pltpu.make_async_copy(bins_hbm, bins_ref, sems.at[0]),
            pltpu.make_async_copy(traces_hbm, traces_ref, sems.at[1]),
        ]
    )
    copies = []
    for dev in range(devices):
        win, sta, core = dev // (groups * cores), dev // cores % groups, dev % cores
        first = ((sta * cores + core) * windows + win) * nodes
        for piece in range(pieces):
            at = pl.multiple_of(first + (place * pieces + piece) * LANES, LANES)
            to = out_ref.at[dev, pl.ds(piece * stations_dev, stations_dev), :]
            sem = sems.at[2 + dev * pieces + piece]
            copies.append(pltpu.make_async_copy(corr_hbm.at[:, pl.ds(at, LANES)], to, sem))
    start_all(copies)
    start = lax.axis_index("freq") * half_length
    small[0].wait()
    bins = bins_column(bins_ref)
    pos = (start + lax.broadcasted_iota(jnp.int32, (NF, half_length), 1)).astype(jnp.float32)
    product = bins * pos
    turns = jnp.round(product * (1.0 / NT))
    rest = (product - turns * NT) * (1.0 / NT)
    versine, sine = turn_parts(rest)
    scale = 1.0 / math.sqrt(NT)
    table = jnp.concatenate([(1.0 - versine) * scale, sine * -scale], axis=0)
    both = jnp.concatenate(split_bf16(table, 2), axis=0)
    small[1].wait()
    sums = lax.dot_general(
        traces_ref[...], both, (((1,), (1,)), ((), ())), preferred_element_type=jnp.float32
    )
    sums = sums[:, : 2 * NF] + sums[:, 2 * NF :]
    terms = [term.astype(jnp.float32) for term in split_bf16(sums, 2)]
    tile = jnp.concatenate([term[at : at + 8] for term in terms for at in range(0, stations_dev, 8)], axis=1)
    tile = tile.astype(jnp.bfloat16)
    for dev in range(devices):
        out_ref[dev, height - 8 :, :] = tile
    for copy in copies:
        copy.wait()


def own_place():
    windows, cores = lax.axis_size("win"), lax.axis_size("freq")
    return (lax.axis_index("sta") * cores + lax.axis_index("freq")) * windows + lax.axis_index("win")


def pick_columns(ids_ref, tables_ref, table_copies, nodes, left_ref, right_ref):
    ntab, grid = tables_ref.shape
    count = nodes // LANES
    wide = right_ref.shape[0] // 3
    blocks = grid // wide
    ids = ids_ref[pl.ds(own_place() * count % ids_ref.shape[0], count), :]
    ids = jnp.concatenate([ids[at : at + 1] for at in range(count)], axis=1)
    low, high = ids & (wide - 1), ids >> (wide.bit_length() - 1)
    spots = lax.broadcasted_iota(jnp.int32, (wide, nodes), 0)
    ones = jnp.where(spots == low, 1.0, 0.0).astype(jnp.bfloat16)
    for term in range(3):
        right_ref[term * wide : (term + 1) * wide, :] = ones
    found = jnp.zeros((ntab, nodes), jnp.float32)
    step = blocks // len(table_copies)
    for at, copy in enumerate(table_copies):
        copy.wait()
        for block in range(at * step, (at + 1) * step):
            pieces = split_bf16(tables_ref[:, block * wide : (block + 1) * wide], 3)
            left_ref[block * ntab : (block + 1) * ntab, :] = jnp.concatenate(pieces, axis=1)
        rows = left_ref[at * step * ntab : (at + 1) * step * ntab, :]
        picked = jnp.dot(rows, right_ref[...], preferred_element_type=jnp.float32)
        for block in range(step):
            part = picked[block * ntab : (block + 1) * ntab]
            found = jnp.where(high == at * step + block, part, found)
    return found


def chebyshev_coefs(bins_ref):
    shape = (DEGREES, DEGREES)
    degree = lax.broadcasted_iota(jnp.int32, shape, 0)
    node = lax.broadcasted_iota(jnp.int32, shape, 1)
    period = 4 * DEGREES
    weight, _ = cos_sin((degree * (2 * node + 1) & (period - 1)).astype(jnp.float32) * (1.0 / period))
    weight = weight * jnp.where(degree == 0, 1.0 / DEGREES, 2.0 / DEGREES)
    even = jnp.where(degree % 2 == 0, weight, 0.0)
    odd = jnp.where(degree % 2 == 1, weight, 0.0)
    row = bins_ref[...].astype(jnp.float32)
    bins = jnp.concatenate([row] * (LANES // NF), axis=1)
    at = lax.broadcasted_iota(jnp.int32, (DEGREES, LANES), 0).astype(jnp.float32)
    spot, _ = cos_sin((2.0 * at + 1.0) * (1.0 / period))
    cosine, sine = cos_sin(bins * (spot * (REACH / 256.0)))
    dot = functools.partial(jnp.dot, precision=lax.Precision.HIGHEST, preferred_element_type=jnp.float32)
    return dot(even, cosine) + dot(odd, sine)


def station_plan(table_row, width):
    count = table_row.shape[1]
    shape = (count, count)
    here = lax.broadcasted_iota(jnp.int32, shape, 0)
    there = lax.broadcasted_iota(jnp.int32, shape, 1)
    column_of = lambda row: jnp.sum(jnp.where(here == there, jnp.broadcast_to(row, shape), 0), axis=1, keepdims=True)
    table_column = column_of(table_row)
    same = (table_column == table_row) & (here < there)
    within = jnp.sum(jnp.where(same, 1, 0), axis=0, keepdims=True)
    place_row = within
    spot = jnp.zeros((1, 1), jnp.int32)
    held = jnp.zeros((1, 1), jnp.int32)
    for table in range(NTAB):
        size = jnp.sum(jnp.where(table_row == table, 1, 0), axis=1, keepdims=True)
        some = size > 0
        edge = (spot & 7) == 0
        skip = some & (held >= 2) & ~edge
        spot = jnp.where(skip, (spot + 7) >> 3 << 3, spot)
        held = jnp.where(skip | edge, 0, held)
        after = spot + size
        place_row = place_row + jnp.where(table_row == table, spot, 0)
        held = jnp.where(some, jnp.where(after >> 3 == spot >> 3, held + 1, 1), held)
        spot = after
    groups = (spot + 7) >> 3
    place_column = column_of(place_row)
    group = lax.broadcasted_iota(jnp.int32, (count, width), 1)
    inside = place_column >> 3 == group
    first = jnp.sum(jnp.where(place_column == group * 8, table_column, 0), axis=0, keepdims=True)
    last = jnp.max(jnp.where(inside, table_column, 0), axis=0, keepdims=True)
    length = jnp.sum(jnp.where(inside & (table_column == first), 1, 0), axis=0, keepdims=True)
    rows = [first, last, length, jnp.broadcast_to(groups, (1, width))]
    if width > count:
        place_row = jnp.concatenate([place_row, jnp.zeros((1, width - count), jnp.int32)], axis=1)
    rows += [place_row, jnp.zeros((3, width), jnp.int32)]
    return jnp.concatenate(rows, axis=0).astype(jnp.float32)


def packed_rows(ntab):
    ends = [ntab * NF, 2 * ntab * NF, 2 * ntab * NF + DEGREES, 2 * ntab * NF + DEGREES + 8]
    return [slice(start, end) for start, end in zip([0] + ends, ends)]


def prepare_kernel(bins_hbm, table_hbm, ids_hbm, tables_hbm, out_hbm, *rest):
    bins_ref, table_ref, ids_ref, tables_ref, cos_ref, sin_ref, coef_ref, plan_ref = rest[:8]
    left_ref, right_ref, sems, table_sems = rest[8:]
    ntab = tables_ref.shape[0]
    nodes = cos_ref.shape[1]
    near = ids_ref.shape[0]
    first = pl.multiple_of(own_place() * (nodes // LANES) // near * near, 8)
    ins = start_all(
        [
            pltpu.make_async_copy(ids_hbm.at[pl.ds(first, near), :], ids_ref, sems.at[0]),
            pltpu.make_async_copy(bins_hbm, bins_ref, sems.at[1]),
            pltpu.make_async_copy(table_hbm, table_ref, sems.at[2]),
        ]
    )
    piece = tables_ref.shape[1] // TABLE_PIECES
    table_copies = []
    for at in range(TABLE_PIECES):
        part = (slice(None), pl.ds(at * piece, piece))
        table_copies.append(pltpu.make_async_copy(tables_hbm.at[part], tables_ref.at[part], table_sems.at[at]))
    start_all(table_copies)
    for copy in ins:
        copy.wait()
    cos_at, sin_at, coef_at, plan_at = packed_rows(ntab)
    coef_ref[...] = chebyshev_coefs(bins_ref)
    plan_ref[...] = station_plan(table_ref[...], plan_ref.shape[1])
    outs = start_all(
        [
            pltpu.make_async_copy(coef_ref, out_hbm.at[coef_at, pl.ds(0, LANES)], sems.at[0]),
            pltpu.make_async_copy(plan_ref, out_hbm.at[plan_at, pl.ds(0, plan_ref.shape[1])], sems.at[1]),
        ]
    )
    turns = pick_columns(ids_ref, tables_ref, table_copies, nodes, left_ref, right_ref) * (1.0 / 256.0)
    bins = bins_column(bins_ref)
    for table in range(ntab):
        cosine, sine = cos_sin(bins * turns[table : table + 1])
        at = pl.ds(table * NF, NF)
        cos_ref[at, :] = cosine
        sin_ref[at, :] = sine
        outs += start_all(
            [
                pltpu.make_async_copy(
                    cos_ref.at[at, :], out_hbm.at[pl.ds(cos_at.start + table * NF, NF), pl.ds(0, nodes)],
                    sems.at[3 + 2 * table],
                ),
                pltpu.make_async_copy(
                    sin_ref.at[at, :], out_hbm.at[pl.ds(sin_at.start + table * NF, NF), pl.ds(0, nodes)],
                    sems.at[4 + 2 * table],
                ),
            ]
        )
    for copy in outs:
        copy.wait()


def image_kernel(merged, stations_dev, packed_hbm, block_ref, *rest):
    corr_ref, rest = (None, rest) if merged else (rest[0], rest[1:])
    keep_ref, send_ref, plan_ref, place_of_ref, coef_ref, cos_ref, sin_ref, sems = rest[:8]
    place_ref, weight_ref, left_ref, sums_ref, basis_a, basis_b, got_a, got_b = rest[8:]
    places, nodes = place_ref.shape
    windows, groups, cores = (lax.axis_size(a) for a in ("win", "sta", "freq"))
    stations = stations_dev * groups
    cos_at, sin_at, coef_at, plan_at = packed_rows(cos_ref.shape[0] // NF)
    width = plan_ref.shape[1]
    copies = start_all(
        [
            pltpu.make_async_copy(packed_hbm.at[plan_at, pl.ds(0, width)], place_of_ref, sems.at[0]),
            pltpu.make_async_copy(packed_hbm.at[plan_at, pl.ds(0, width)], plan_ref, sems.at[1]),
            pltpu.make_async_copy(packed_hbm.at[coef_at, pl.ds(0, LANES)], coef_ref, sems.at[2]),
            pltpu.make_async_copy(packed_hbm.at[cos_at, pl.ds(0, nodes)], cos_ref, sems.at[3]),
            pltpu.make_async_copy(packed_hbm.at[sin_at, pl.ds(0, nodes)], sin_ref, sems.at[4]),
        ]
    )
    height = block_ref.shape[1]
    rows_of = lambda win, core: [(win * groups + group) * cores + core for group in range(groups)]

    even, odd = [], []
    for win in range(windows):
        value = []
        for group in range(groups):
            tile = None
            for core in range(cores):
                part = block_ref[(win * groups + group) * cores + core, height - 8 :, :].astype(jnp.float32)
                tile = part if tile is None else tile + part
            tile = tile[:, : LANES // 2] + tile[:, LANES // 2 :]
            value += [tile[:, 2 * NF * piece : 2 * NF * (piece + 1)] for piece in range(stations_dev // 8)]
        value = jnp.concatenate(value, axis=0)
        even.append(value)
        odd.append(jnp.concatenate([-value[:, NF:], value[:, :NF]], axis=1))
    spectra = jnp.concatenate(even + odd, axis=1)
    if merged:
        parts = []
        for win in range(windows):
            for core in range(cores):
                for first in range(0, height - 8, stations_dev):
                    rows = [block_ref[at, first : first + stations_dev, :] for at in rows_of(win, core)]
                    parts.append(jnp.concatenate(rows, axis=0))
        corr = jnp.concatenate(parts, axis=1)
    else:
        corr = corr_ref[...]

    copies[0].wait()
    place_row = place_of_ref[4:5, :stations].astype(jnp.int32)
    sorter = lax.broadcasted_iota(jnp.int32, (places, stations), 0) == place_row
    sorter = jnp.where(sorter, 1.0, 0.0).astype(jnp.bfloat16)
    found = None
    for piece in split_bf16(spectra, 3):
        part = jnp.dot(sorter, piece, preferred_element_type=jnp.float32)
        found = part if found is None else found + part
    weight_ref[...] = found
    place_ref[...] = jnp.dot(sorter, corr, preferred_element_type=jnp.float32) * (1.0 / REACH)
    sums_ref[...] = jnp.zeros_like(sums_ref)
    chunk = min(256, nodes)
    depth = DEGREES * 8
    lanes = windows * 2 * NF
    for copy in copies[1:3]:
        copy.wait()

    def make_left(pair):
        top = weight_ref[pl.ds(pl.multiple_of(pair * 16, 16), 8), :]
        bottom = weight_ref[pl.ds(pl.multiple_of(pair * 16 + 8, 8), 8), :]
        sides = [
            jnp.concatenate([top[:, :lanes], bottom[:, :lanes]], axis=1),
            jnp.concatenate([top[:, lanes:], bottom[:, lanes:]], axis=1),
        ]
        per = LANES // 8
        for half in range(DEGREES // per):
            tall = jnp.concatenate(
                [sides[k % 2] * coef_ref[k : k + 1, :] for k in range(half * per, (half + 1) * per)], axis=0
            )
            at = slice(half * LANES, (half + 1) * LANES)
            for term, value in enumerate(split_bf16(tall.T, 2)):
                left_ref[2 * pair, term * lanes : (term + 1) * lanes, at] = value[:lanes]
                left_ref[2 * pair + 1, term * lanes : (term + 1) * lanes, at] = value[lanes:]

    used = plan_ref[3, 0].astype(jnp.int32)
    sure = stations // 16
    if sure <= 8:
        for pair in range(sure):
            make_left(pair)
    else:
        lax.fori_loop(0, sure, lambda pair, carry: (make_left(pair), carry)[1], 0)
    lax.fori_loop(sure, (used + 1) // 2, lambda pair, carry: (make_left(pair), carry)[1], 0)
    spot = (lax.broadcasted_iota(jnp.int32, (16, depth), 1) & 7).astype(jnp.float32)

    def left_of(group):
        mask = spot < plan_ref[2, group]
        results = []
        for keep, drop in ((1.0, 0.0), (0.0, 1.0)):
            side = jnp.where(mask, keep, drop).astype(jnp.bfloat16)
            results.append(left_ref[group] * jnp.concatenate([side] * (2 * lanes // 16), axis=0))
        high = jnp.concatenate([result[:lanes] for result in results], axis=0)
        low = jnp.concatenate([result[lanes:] for result in results], axis=0)
        return jnp.concatenate([high, high, low], axis=1)

    def make_basis(group, basis_ref, at):
        arg = place_ref[pl.ds(pl.multiple_of(group * 8, 8), 8), at]
        twice = arg + arg
        before, now = jnp.ones_like(arg), arg
        for degree in range(0, DEGREES, 2):
            high, low = split_bf16(jnp.concatenate([before, now], axis=0), 2)
            basis_ref[degree * 8 : degree * 8 + 16, at] = high
            basis_ref[depth + degree * 8 : depth + degree * 8 + 16, at] = low
            before = twice * now - before
            now = twice * before - now

    def phasor_rows(group):
        tables = [plan_ref[slot, group].astype(jnp.int32) for slot in range(2)]
        return [pl.ds(pl.multiple_of(table * NF, NF), NF) for table in tables]

    def add_product(rows_of_slot, got_ref, at):
        for win in range(windows):
            row = win * 2 * NF
            real_sum, imag_sum = sums_ref[row : row + NF, at], sums_ref[row + NF : row + 2 * NF, at]
            for slot, rows in enumerate(rows_of_slot):
                cosine, sine = cos_ref[rows, at], sin_ref[rows, at]
                real = got_ref[slot * lanes + row : slot * lanes + row + NF, at]
                imag = got_ref[slot * lanes + row + NF : slot * lanes + row + 2 * NF, at]
                real_sum += real * cosine - imag * sine
                imag_sum += real * sine + imag * cosine
            sums_ref[row : row + NF, at], sums_ref[row + NF : row + 2 * NF, at] = real_sum, imag_sum

    chunks = [slice(first, first + chunk) for first in range(0, nodes, chunk)]

    def stage(group, basis_ref, next_basis, got_ref, last_got):
        left = left_of(group)
        rows_of_slot = phasor_rows(jnp.maximum(group - 1, 0))
        for at in chunks:
            right = jnp.concatenate([basis_ref[:, at], basis_ref[:depth, at]], axis=0)
            got_ref[:, at] = jnp.dot(left, right, preferred_element_type=jnp.float32)
            make_basis(group + 1, next_basis, at)
            add_product(rows_of_slot, last_got, at)

    got_b[...] = jnp.zeros_like(got_b)
    for at in chunks:
        make_basis(0, basis_a, at)
    for copy in copies[3:]:
        copy.wait()

    def body(pair, carry):
        stage(pair * 2, basis_a, basis_b, got_a, got_b)
        stage(pair * 2 + 1, basis_b, basis_a, got_b, got_a)
        return carry

    turns = (used + 1) // 2
    lax.fori_loop(0, turns, body, 0)
    for at in chunks:
        add_product(phasor_rows(turns * 2 - 1), got_b, at)
    powers = []
    for win in range(windows):
        row = win * 2 * NF
        real, imag = sums_ref[row : row + NF, :], sums_ref[row + NF : row + 2 * NF, :]
        powers.append(real * real + imag * imag)
    mine = lax.axis_index("win") == 0
    keep_ref[...] = jnp.where(mine, powers[0], powers[1])
    send_ref[...] = jnp.where(mine, powers[1], powers[0])


def finish_kernel(stations, keep_ref, got_ref, spectrum_ref, beam_ref):
    nodes = keep_ref.shape[1]
    win = lax.axis_index("win")
    for place, ref in ((win, keep_ref), (1 - win, got_ref)):
        power = ref[...]
        total = jnp.sum(power, axis=0, keepdims=True)
        at = pl.ds(pl.multiple_of(place * nodes, LANES), nodes)
        spectrum_ref[:, at] = power * (NF / total)
        beam_ref[:, at] = total * (1.0 / (NF * stations))


def on_device(traces, tables, corrections, station_table, node_ids, freq_bins):
    windows, groups, cores = (lax.axis_size(a) for a in ("win", "sta", "freq"))
    stations_dev, grid = corrections.shape
    stations = stations_dev * groups
    devices = windows * groups * cores
    nodes = grid // devices
    ntab = tables.shape[0]
    params = lambda free: pltpu.CompilerParams(vmem_limit_bytes=VMEM_LIMIT - free)
    vmem = pl.BlockSpec(memory_space=pltpu.VMEM)
    hbm = pl.BlockSpec(memory_space=pltpu.HBM)
    bins = freq_bins.reshape(1, NF)
    bins_scratch = pltpu.VMEM((1, NF), jnp.int32)

    holders = windows * cores
    merged = nodes % (holders * LANES) == 0
    pieces = nodes // (holders * LANES) if merged else 0
    height = pieces * stations_dev + 8
    blocks = pl.pallas_call(
        functools.partial(send_kernel, nodes),
        out_shape=jax.ShapeDtypeStruct((devices, height, LANES), jnp.bfloat16),
        in_specs=[hbm] * 3,
        out_specs=vmem,
        scratch_shapes=[
            bins_scratch,
            pltpu.VMEM(traces.shape, traces.dtype),
            pltpu.SemaphoreType.DMA((2 + devices * max(pieces, 1),)),
        ],
        compiler_params=params(0),
        name="send",
    )(bins, traces, corrections)
    received = [lax.all_to_all(blocks, ("win", "sta", "freq"), split_axis=0, concat_axis=0, tiled=True)]
    if not merged:
        parts = corrections.reshape(stations_dev, groups, holders, nodes)
        place = lax.axis_index("freq") * windows + lax.axis_index("win")
        mine = lax.dynamic_index_in_dim(parts, place, axis=2, keepdims=False)
        corr = lax.all_to_all(mine.transpose(1, 0, 2), "sta", split_axis=0, concat_axis=0, tiled=True)
        received.append(corr.reshape(stations, nodes))

    wide = 512
    plan_width = max(LANES, stations)
    phasors = pltpu.VMEM((ntab * NF, nodes), jnp.float32)
    coefs = pltpu.VMEM((DEGREES, LANES), jnp.float32)
    plan = pltpu.VMEM((8, plan_width), jnp.float32)
    packed_shape = (packed_rows(ntab)[-1].stop, max(nodes, plan_width))
    packed = pl.pallas_call(
        prepare_kernel,
        out_shape=jax.ShapeDtypeStruct(packed_shape, jnp.float32),
        in_specs=[hbm] * 4,
        out_specs=hbm,
        scratch_shapes=[
            bins_scratch,
            pltpu.VMEM((1, stations), jnp.int32),
            pltpu.VMEM((max(nodes // LANES, 8), LANES), jnp.int32),
            pltpu.VMEM(tables.shape, tables.dtype),
            phasors,
            phasors,
            coefs,
            plan,
            pltpu.VMEM((grid // wide * ntab, 3 * wide), jnp.bfloat16),
            pltpu.VMEM((3 * wide, nodes), jnp.bfloat16),
            pltpu.SemaphoreType.DMA((3 + 2 * ntab,)),
            pltpu.SemaphoreType.DMA((TABLE_PIECES,)),
        ],
        compiler_params=params(512 * 1024),
        name="prepare",
    )(bins, station_table.reshape(1, stations), node_ids.reshape(grid // LANES, LANES), tables)

    places = (stations // 8 + ntab // 2 + 3) // 2 * 16
    half = jax.ShapeDtypeStruct((NF, nodes), jnp.float32)
    rows = 2 * windows * 2 * NF
    basis = pltpu.VMEM((2 * DEGREES * 8, nodes), jnp.bfloat16)
    keep, send = pl.pallas_call(
        functools.partial(image_kernel, merged, stations_dev),
        out_shape=[half, half],
        in_specs=[hbm] + [vmem] * len(received),
        out_specs=[vmem, vmem],
        scratch_shapes=[
            pltpu.SMEM((8, plan_width), jnp.float32),
            plan,
            coefs,
            phasors,
            phasors,
            pltpu.SemaphoreType.DMA((5,)),
            pltpu.VMEM((places, nodes), jnp.float32),
            pltpu.VMEM((places, rows), jnp.float32),
            pltpu.VMEM((places // 8, rows, DEGREES * 8), jnp.bfloat16),
            pltpu.VMEM((rows // 2, nodes), jnp.float32),
            basis,
            basis,
            pltpu.VMEM((rows, nodes), jnp.float32),
            pltpu.VMEM((rows, nodes), jnp.float32),
        ],
        compiler_params=params(23 * 512 * 1024),
        name="image",
    )(packed, *received)
    got = lax.ppermute(send, "win", [(0, 1), (1, 0)])
    spectrum, beam_power = pl.pallas_call(
        functools.partial(finish_kernel, stations),
        out_shape=[
            jax.ShapeDtypeStruct((NF, windows * nodes), jnp.float32),
            jax.ShapeDtypeStruct((1, windows * nodes), jnp.float32),
        ],
        in_specs=[vmem, vmem],
        out_specs=[vmem, vmem],
        compiler_params=params(32 * 1024 * 1024),
        name="finish",
    )(keep, got)
    return spectrum, beam_power.reshape(windows * nodes)


def solution(mesh):
    return jax.shard_map(
        on_device,
        mesh=mesh,
        in_specs=(P(("win", "sta"), "freq"), P(), P("sta", None), P(), P(), P()),
        out_specs=(P("win", ("sta", "freq")), P(("win", "sta", "freq"))),
        check_vma=False,
    )
```

```python
import functools
import math

import jax
import jax.numpy as jnp
import numpy as np
from jax import lax
from jax.experimental import pallas as pl
from jax.experimental.pallas import tpu as pltpu
from jax.sharding import PartitionSpec as P

NT = 5120
NF = 16
NTAB = 16
LANES = 128
DEGREES = 32
REACH = 1.5
TABLE_PIECES = 4
VMEM_LIMIT = 64 * 1024 * 1024 - 64 * 1024


def chebyshev_fit(func, degree, low, high):
    fit = np.polynomial.chebyshev.Chebyshev.interpolate(func, degree, domain=[low, high])
    return [float(v) for v in fit.convert(kind=np.polynomial.Polynomial).coef]


SIN_HALF = chebyshev_fit(lambda z: np.pi * np.sinc(np.sqrt(z)), 4, 0.0, 0.25)
COS_HALF = chebyshev_fit(lambda z: np.cos(np.pi * np.sqrt(z)), 4, 0.0, 0.25)


def horner(coefs, arg):
    total = coefs[-1]
    for coef in coefs[-2::-1]:
        total = total * arg + coef
    return total


def turn_parts(rest):
    square = rest * rest
    root = math.sqrt(2.0)
    sine_half = rest * horner([root * c for c in SIN_HALF], square)
    cos_half = horner([root * c for c in COS_HALF], square)
    return sine_half * sine_half, sine_half * cos_half


def cos_sin(turns):
    versine, sine = turn_parts(turns - jnp.round(turns))
    return 1.0 - versine, sine


def bins_column(bins_ref):
    rows = lax.broadcasted_iota(jnp.int32, (NF, NF), 0)
    lanes = lax.broadcasted_iota(jnp.int32, (NF, NF), 1)
    square = jnp.broadcast_to(bins_ref[...].astype(jnp.float32), (NF, NF))
    return jnp.sum(jnp.where(rows == lanes, square, 0.0), axis=1, keepdims=True)


def split_bf16(value, terms):
    pieces = []
    for term in range(terms):
        piece = value.astype(jnp.bfloat16)
        pieces.append(piece)
        if term < terms - 1:
            value = value - piece.astype(jnp.float32)
    return pieces


def start_all(copies):
    for copy in copies:
        copy.start()
    return copies


def send_kernel(nodes, bins_hbm, traces_hbm, corr_hbm, out_ref, bins_ref, traces_ref, sems):
    devices, height, _ = out_ref.shape
    stations_dev, half_length = traces_ref.shape
    pieces = (height - 8) // stations_dev
    windows, groups, cores = (lax.axis_size(a) for a in ("win", "sta", "freq"))
    place = lax.axis_index("win") * cores + lax.axis_index("freq")
    small = start_all(
        [
            pltpu.make_async_copy(bins_hbm, bins_ref, sems.at[0]),
            pltpu.make_async_copy(traces_hbm, traces_ref, sems.at[1]),
        ]
    )
    copies = []
    for dev in range(devices):
        win, sta, core = dev // (groups * cores), dev // cores % groups, dev % cores
        first = ((sta * cores + core) * windows + win) * nodes
        for piece in range(pieces):
            at = pl.multiple_of(first + (place * pieces + piece) * LANES, LANES)
            to = out_ref.at[dev, pl.ds(piece * stations_dev, stations_dev), :]
            sem = sems.at[2 + dev * pieces + piece]
            copies.append(pltpu.make_async_copy(corr_hbm.at[:, pl.ds(at, LANES)], to, sem))
    start_all(copies)
    start = lax.axis_index("freq") * half_length
    small[0].wait()
    bins = bins_column(bins_ref)
    pos = (start + lax.broadcasted_iota(jnp.int32, (NF, half_length), 1)).astype(jnp.float32)
    product = bins * pos
    turns = jnp.round(product * (1.0 / NT))
    rest = (product - turns * NT) * (1.0 / NT)
    versine, sine = turn_parts(rest)
    scale = 1.0 / math.sqrt(NT)
    table = jnp.concatenate([(1.0 - versine) * scale, sine * -scale], axis=0)
    both = jnp.concatenate(split_bf16(table, 2), axis=0)
    small[1].wait()
    sums = lax.dot_general(
        traces_ref[...], both, (((1,), (1,)), ((), ())), preferred_element_type=jnp.float32
    )
    sums = sums[:, : 2 * NF] + sums[:, 2 * NF :]
    terms = [term.astype(jnp.float32) for term in split_bf16(sums, 2)]
    tile = jnp.concatenate([term[at : at + 8] for term in terms for at in range(0, stations_dev, 8)], axis=1)
    tile = tile.astype(jnp.bfloat16)
    for dev in range(devices):
        out_ref[dev, height - 8 :, :] = tile
    for copy in copies:
        copy.wait()


def own_place():
    windows, cores = lax.axis_size("win"), lax.axis_size("freq")
    return (lax.axis_index("sta") * cores + lax.axis_index("freq")) * windows + lax.axis_index("win")


def pick_columns(ids_ref, tables_ref, table_copies, nodes, left_ref, right_ref):
    ntab, grid = tables_ref.shape
    count = nodes // LANES
    wide = right_ref.shape[0] // 3
    blocks = grid // wide
    ids = ids_ref[pl.ds(own_place() * count % ids_ref.shape[0], count), :]
    ids = jnp.concatenate([ids[at : at + 1] for at in range(count)], axis=1)
    low, high = ids & (wide - 1), ids >> (wide.bit_length() - 1)
    spots = lax.broadcasted_iota(jnp.int32, (wide, nodes), 0)
    ones = jnp.where(spots == low, 1.0, 0.0).astype(jnp.bfloat16)
    for term in range(3):
        right_ref[term * wide : (term + 1) * wide, :] = ones
    found = jnp.zeros((ntab, nodes), jnp.float32)
    step = blocks // len(table_copies)
    for at, copy in enumerate(table_copies):
        copy.wait()
        for block in range(at * step, (at + 1) * step):
            pieces = split_bf16(tables_ref[:, block * wide : (block + 1) * wide], 3)
            left_ref[block * ntab : (block + 1) * ntab, :] = jnp.concatenate(pieces, axis=1)
        rows = left_ref[at * step * ntab : (at + 1) * step * ntab, :]
        picked = jnp.dot(rows, right_ref[...], preferred_element_type=jnp.float32)
        for block in range(step):
            part = picked[block * ntab : (block + 1) * ntab]
            found = jnp.where(high == at * step + block, part, found)
    return found


def chebyshev_coefs(bins_ref):
    shape = (DEGREES, DEGREES)
    degree = lax.broadcasted_iota(jnp.int32, shape, 0)
    node = lax.broadcasted_iota(jnp.int32, shape, 1)
    period = 4 * DEGREES
    weight, _ = cos_sin((degree * (2 * node + 1) & (period - 1)).astype(jnp.float32) * (1.0 / period))
    weight = weight * jnp.where(degree == 0, 1.0 / DEGREES, 2.0 / DEGREES)
    even = jnp.where(degree % 2 == 0, weight, 0.0)
    odd = jnp.where(degree % 2 == 1, weight, 0.0)
    row = bins_ref[...].astype(jnp.float32)
    bins = jnp.concatenate([row] * (LANES // NF), axis=1)
    at = lax.broadcasted_iota(jnp.int32, (DEGREES, LANES), 0).astype(jnp.float32)
    spot, _ = cos_sin((2.0 * at + 1.0) * (1.0 / period))
    cosine, sine = cos_sin(bins * (spot * (REACH / 256.0)))
    dot = functools.partial(jnp.dot, precision=lax.Precision.HIGHEST, preferred_element_type=jnp.float32)
    return dot(even, cosine) + dot(odd, sine)


def station_plan(table_row, width):
    count = table_row.shape[1]
    shape = (count, count)
    here = lax.broadcasted_iota(jnp.int32, shape, 0)
    there = lax.broadcasted_iota(jnp.int32, shape, 1)
    column_of = lambda row: jnp.sum(jnp.where(here == there, jnp.broadcast_to(row, shape), 0), axis=1, keepdims=True)
    table_column = column_of(table_row)
    same = (table_column == table_row) & (here < there)
    within = jnp.sum(jnp.where(same, 1, 0), axis=0, keepdims=True)
    place_row = within
    spot = jnp.zeros((1, 1), jnp.int32)
    held = jnp.zeros((1, 1), jnp.int32)
    for table in range(NTAB):
        size = jnp.sum(jnp.where(table_row == table, 1, 0), axis=1, keepdims=True)
        some = size > 0
        edge = (spot & 7) == 0
        skip = some & (held >= 2) & ~edge
        spot = jnp.where(skip, (spot + 7) >> 3 << 3, spot)
        held = jnp.where(skip | edge, 0, held)
        after = spot + size
        place_row = place_row + jnp.where(table_row == table, spot, 0)
        held = jnp.where(some, jnp.where(after >> 3 == spot >> 3, held + 1, 1), held)
        spot = after
    groups = (spot + 7) >> 3
    place_column = column_of(place_row)
    group = lax.broadcasted_iota(jnp.int32, (count, width), 1)
    inside = place_column >> 3 == group
    first = jnp.sum(jnp.where(place_column == group * 8, table_column, 0), axis=0, keepdims=True)
    last = jnp.max(jnp.where(inside, table_column, 0), axis=0, keepdims=True)
    length = jnp.sum(jnp.where(inside & (table_column == first), 1, 0), axis=0, keepdims=True)
    rows = [first, last, length, jnp.broadcast_to(groups, (1, width))]
    if width > count:
        place_row = jnp.concatenate([place_row, jnp.zeros((1, width - count), jnp.int32)], axis=1)
    rows += [place_row, jnp.zeros((3, width), jnp.int32)]
    return jnp.concatenate(rows, axis=0).astype(jnp.float32)


def packed_rows(ntab):
    ends = [ntab * NF, 2 * ntab * NF, 2 * ntab * NF + DEGREES, 2 * ntab * NF + DEGREES + 8]
    return [slice(start, end) for start, end in zip([0] + ends, ends)]


def prepare_kernel(bins_hbm, table_hbm, ids_hbm, tables_hbm, out_hbm, *rest):
    bins_ref, table_ref, ids_ref, tables_ref, cos_ref, sin_ref, coef_ref, plan_ref = rest[:8]
    left_ref, right_ref, sems, table_sems = rest[8:]
    ntab = tables_ref.shape[0]
    nodes = cos_ref.shape[1]
    near = ids_ref.shape[0]
    first = pl.multiple_of(own_place() * (nodes // LANES) // near * near, 8)
    ins = start_all(
        [
            pltpu.make_async_copy(ids_hbm.at[pl.ds(first, near), :], ids_ref, sems.at[0]),
            pltpu.make_async_copy(bins_hbm, bins_ref, sems.at[1]),
            pltpu.make_async_copy(table_hbm, table_ref, sems.at[2]),
        ]
    )
    piece = tables_ref.shape[1] // TABLE_PIECES
    table_copies = []
    for at in range(TABLE_PIECES):
        part = (slice(None), pl.ds(at * piece, piece))
        table_copies.append(pltpu.make_async_copy(tables_hbm.at[part], tables_ref.at[part], table_sems.at[at]))
    start_all(table_copies)
    for copy in ins:
        copy.wait()
    cos_at, sin_at, coef_at, plan_at = packed_rows(ntab)
    coef_ref[...] = chebyshev_coefs(bins_ref)
    plan_ref[...] = station_plan(table_ref[...], plan_ref.shape[1])
    outs = start_all(
        [
            pltpu.make_async_copy(coef_ref, out_hbm.at[coef_at, pl.ds(0, LANES)], sems.at[0]),
            pltpu.make_async_copy(plan_ref, out_hbm.at[plan_at, pl.ds(0, plan_ref.shape[1])], sems.at[1]),
        ]
    )
    turns = pick_columns(ids_ref, tables_ref, table_copies, nodes, left_ref, right_ref) * (1.0 / 256.0)
    bins = bins_column(bins_ref)
    for table in range(ntab):
        cosine, sine = cos_sin(bins * turns[table : table + 1])
        at = pl.ds(table * NF, NF)
        cos_ref[at, :] = cosine
        sin_ref[at, :] = sine
        outs += start_all(
            [
                pltpu.make_async_copy(
                    cos_ref.at[at, :], out_hbm.at[pl.ds(cos_at.start + table * NF, NF), pl.ds(0, nodes)],
                    sems.at[3 + 2 * table],
                ),
                pltpu.make_async_copy(
                    sin_ref.at[at, :], out_hbm.at[pl.ds(sin_at.start + table * NF, NF), pl.ds(0, nodes)],
                    sems.at[4 + 2 * table],
                ),
            ]
        )
    for copy in outs:
        copy.wait()


def weights_kernel(merged, stations_dev, packed_hbm, block_ref, *rest):
    corr_ref, rest = (None, rest) if merged else (rest[0], rest[1:])
    place_ref, left_ref, plan_ref, place_of_ref, coef_ref, weight_ref, sems = rest
    places, nodes = place_ref.shape
    windows, groups, cores = (lax.axis_size(a) for a in ("win", "sta", "freq"))
    stations = stations_dev * groups
    _, _, coef_at, plan_at = packed_rows(NTAB)
    width = plan_ref.shape[1]
    copies = start_all(
        [
            pltpu.make_async_copy(packed_hbm.at[plan_at, pl.ds(0, width)], place_of_ref, sems.at[0]),
            pltpu.make_async_copy(packed_hbm.at[plan_at, pl.ds(0, width)], plan_ref, sems.at[1]),
            pltpu.make_async_copy(packed_hbm.at[coef_at, pl.ds(0, LANES)], coef_ref, sems.at[2]),
        ]
    )
    height = block_ref.shape[1]
    rows_of = lambda win, core: [(win * groups + group) * cores + core for group in range(groups)]

    even, odd = [], []
    for win in range(windows):
        value = []
        for group in range(groups):
            tile = None
            for core in range(cores):
                part = block_ref[(win * groups + group) * cores + core, height - 8 :, :].astype(jnp.float32)
                tile = part if tile is None else tile + part
            tile = tile[:, : LANES // 2] + tile[:, LANES // 2 :]
            value += [tile[:, 2 * NF * piece : 2 * NF * (piece + 1)] for piece in range(stations_dev // 8)]
        value = jnp.concatenate(value, axis=0)
        even.append(value)
        odd.append(jnp.concatenate([-value[:, NF:], value[:, :NF]], axis=1))
    spectra = jnp.concatenate(even + odd, axis=1)
    if merged:
        parts = []
        for win in range(windows):
            for core in range(cores):
                for first in range(0, height - 8, stations_dev):
                    rows = [block_ref[at, first : first + stations_dev, :] for at in rows_of(win, core)]
                    parts.append(jnp.concatenate(rows, axis=0))
        corr = jnp.concatenate(parts, axis=1)
    else:
        corr = corr_ref[...]

    copies[0].wait()
    place_row = place_of_ref[4:5, :stations].astype(jnp.int32)
    sorter = lax.broadcasted_iota(jnp.int32, (places, stations), 0) == place_row
    sorter = jnp.where(sorter, 1.0, 0.0).astype(jnp.bfloat16)
    found = None
    for piece in split_bf16(spectra, 3):
        part = jnp.dot(sorter, piece, preferred_element_type=jnp.float32)
        found = part if found is None else found + part
    weight_ref[...] = found
    place_ref[...] = jnp.dot(sorter, corr, preferred_element_type=jnp.float32) * (1.0 / REACH)
    depth = DEGREES * 8
    lanes = windows * 2 * NF
    for copy in copies[1:3]:
        copy.wait()

    def make_left(pair):
        top = weight_ref[pl.ds(pl.multiple_of(pair * 16, 16), 8), :]
        bottom = weight_ref[pl.ds(pl.multiple_of(pair * 16 + 8, 8), 8), :]
        sides = [
            jnp.concatenate([top[:, :lanes], bottom[:, :lanes]], axis=1),
            jnp.concatenate([top[:, lanes:], bottom[:, lanes:]], axis=1),
        ]
        per = LANES // 8
        for half in range(DEGREES // per):
            tall = jnp.concatenate(
                [sides[k % 2] * coef_ref[k : k + 1, :] for k in range(half * per, (half + 1) * per)], axis=0
            )
            at = slice(half * LANES, (half + 1) * LANES)
            for term, value in enumerate(split_bf16(tall.T, 2)):
                left_ref[2 * pair, term * lanes : (term + 1) * lanes, at] = value[:lanes]
                left_ref[2 * pair + 1, term * lanes : (term + 1) * lanes, at] = value[lanes:]

    used = plan_ref[3, 0].astype(jnp.int32)
    sure = stations // 16
    if sure <= 8:
        for pair in range(sure):
            make_left(pair)
    else:
        lax.fori_loop(0, sure, lambda pair, carry: (make_left(pair), carry)[1], 0)
    lax.fori_loop(sure, (used + 1) // 2, lambda pair, carry: (make_left(pair), carry)[1], 0)


def image_kernel(stations, packed_hbm, place_ref, left_ref, keep_ref, send_ref, *rest):
    plan_ref, cos_ref, sin_ref, sems, sums_ref, basis_a, basis_b = rest
    places, nodes = place_ref.shape
    windows = lax.axis_size("win")
    cos_at, sin_at, _, plan_at = packed_rows(NTAB)
    width = plan_ref.shape[1]
    copies = start_all(
        [
            pltpu.make_async_copy(packed_hbm.at[plan_at, pl.ds(0, width)], plan_ref, sems.at[0]),
            pltpu.make_async_copy(packed_hbm.at[cos_at, pl.ds(0, nodes)], cos_ref, sems.at[1]),
            pltpu.make_async_copy(packed_hbm.at[sin_at, pl.ds(0, nodes)], sin_ref, sems.at[2]),
        ]
    )
    sums_ref[...] = jnp.zeros_like(sums_ref)
    chunk = min(256, nodes)
    depth = DEGREES * 8
    lanes = windows * 2 * NF
    spot = (lax.broadcasted_iota(jnp.int32, (16, depth), 1) & 7).astype(jnp.float32)

    def left_of(group):
        mask = spot < plan_ref[2, group]
        results = []
        for keep, drop in ((1.0, 0.0), (0.0, 1.0)):
            side = jnp.where(mask, keep, drop).astype(jnp.bfloat16)
            results.append(left_ref[group] * jnp.concatenate([side] * (2 * lanes // 16), axis=0))
        high = jnp.concatenate([result[:lanes] for result in results], axis=0)
        return jnp.concatenate(results, axis=0), high

    def basis_steps(group, basis_ref):
        arg = place_ref[pl.ds(pl.multiple_of(group * 8, 8), 8), :]
        twice = arg + arg
        before, now = jnp.ones_like(arg), arg
        for degree in range(0, DEGREES, 2):
            pair = jnp.concatenate([before, now], axis=0)
            high, low = split_bf16(pair, 2)
            basis_ref[degree * 8 : degree * 8 + 16, :] = high
            basis_ref[depth + degree * 8 : depth + degree * 8 + 16, :] = low
            before = twice * now - before
            now = twice * before - now
            if degree % 8 == 6:
                yield

    def run(steps):
        for _ in steps:
            pass

    def add_group(group, basis_ref, steps):
        both, high = left_of(group)
        tables = [plan_ref[slot, group].astype(jnp.int32) for slot in range(2)]
        phasor_rows = [pl.ds(pl.multiple_of(table * NF, NF), NF) for table in tables]
        for first in range(0, nodes, chunk):
            at = slice(first, first + chunk)
            got = jnp.dot(both, basis_ref[:depth, at], preferred_element_type=jnp.float32)
            more = jnp.dot(high, basis_ref[depth:, at], preferred_element_type=jnp.float32)
            next(steps, None)
            got = [
                got[2 * slot * lanes : (2 * slot + 1) * lanes]
                + got[(2 * slot + 1) * lanes : (2 * slot + 2) * lanes]
                + more[slot * lanes : (slot + 1) * lanes]
                for slot in range(2)
            ]
            for win in range(windows):
                row = win * 2 * NF
                real_sum, imag_sum = sums_ref[row : row + NF, at], sums_ref[row + NF : row + 2 * NF, at]
                for slot, rows in enumerate(phasor_rows):
                    cosine, sine = cos_ref[rows, at], sin_ref[rows, at]
                    real, imag = got[slot][row : row + NF], got[slot][row + NF : row + 2 * NF]
                    real_sum += real * cosine - imag * sine
                    imag_sum += real * sine + imag * cosine
                sums_ref[row : row + NF, at], sums_ref[row + NF : row + 2 * NF, at] = real_sum, imag_sum
        run(steps)

    run(basis_steps(0, basis_a))
    for copy in copies:
        copy.wait()
    used = plan_ref[3, 0].astype(jnp.int32)

    def body(pair, carry):
        group = pair * 2
        add_group(group, basis_a, basis_steps(group + 1, basis_b))
        add_group(group + 1, basis_b, basis_steps(jnp.minimum(group + 2, places // 8 - 1), basis_a))
        return carry

    lax.fori_loop(0, (used + 1) // 2, body, 0)
    powers = []
    for win in range(windows):
        row = win * 2 * NF
        real, imag = sums_ref[row : row + NF, :], sums_ref[row + NF : row + 2 * NF, :]
        powers.append(real * real + imag * imag)
    mine = lax.axis_index("win") == 0
    keep_ref[...] = jnp.where(mine, powers[0], powers[1])
    send_ref[...] = jnp.where(mine, powers[1], powers[0])


def finish_kernel(stations, keep_ref, got_ref, spectrum_ref, beam_ref):
    nodes = keep_ref.shape[1]
    win = lax.axis_index("win")
    for place, ref in ((win, keep_ref), (1 - win, got_ref)):
        power = ref[...]
        total = jnp.sum(power, axis=0, keepdims=True)
        at = pl.ds(pl.multiple_of(place * nodes, LANES), nodes)
        spectrum_ref[:, at] = power * (NF / total)
        beam_ref[:, at] = total * (1.0 / (NF * stations))


def on_device(traces, tables, corrections, station_table, node_ids, freq_bins):
    windows, groups, cores = (lax.axis_size(a) for a in ("win", "sta", "freq"))
    stations_dev, grid = corrections.shape
    stations = stations_dev * groups
    devices = windows * groups * cores
    nodes = grid // devices
    ntab = tables.shape[0]
    params = lambda free: pltpu.CompilerParams(vmem_limit_bytes=VMEM_LIMIT - free)
    vmem = pl.BlockSpec(memory_space=pltpu.VMEM)
    hbm = pl.BlockSpec(memory_space=pltpu.HBM)
    bins = freq_bins.reshape(1, NF)
    bins_scratch = pltpu.VMEM((1, NF), jnp.int32)

    holders = windows * cores
    merged = nodes % (holders * LANES) == 0
    pieces = nodes // (holders * LANES) if merged else 0
    height = pieces * stations_dev + 8
    blocks = pl.pallas_call(
        functools.partial(send_kernel, nodes),
        out_shape=jax.ShapeDtypeStruct((devices, height, LANES), jnp.bfloat16),
        in_specs=[hbm] * 3,
        out_specs=vmem,
        scratch_shapes=[
            bins_scratch,
            pltpu.VMEM(traces.shape, traces.dtype),
            pltpu.SemaphoreType.DMA((2 + devices * max(pieces, 1),)),
        ],
        compiler_params=params(0),
        name="send",
    )(bins, traces, corrections)
    received = [lax.all_to_all(blocks, ("win", "sta", "freq"), split_axis=0, concat_axis=0, tiled=True)]
    if not merged:
        parts = corrections.reshape(stations_dev, groups, holders, nodes)
        place = lax.axis_index("freq") * windows + lax.axis_index("win")
        mine = lax.dynamic_index_in_dim(parts, place, axis=2, keepdims=False)
        corr = lax.all_to_all(mine.transpose(1, 0, 2), "sta", split_axis=0, concat_axis=0, tiled=True)
        received.append(corr.reshape(stations, nodes))

    wide = 512
    plan_width = max(LANES, stations)
    phasors = pltpu.VMEM((ntab * NF, nodes), jnp.float32)
    coefs = pltpu.VMEM((DEGREES, LANES), jnp.float32)
    plan = pltpu.VMEM((8, plan_width), jnp.float32)
    packed_shape = (packed_rows(ntab)[-1].stop, max(nodes, plan_width))
    packed = pl.pallas_call(
        prepare_kernel,
        out_shape=jax.ShapeDtypeStruct(packed_shape, jnp.float32),
        in_specs=[hbm] * 4,
        out_specs=hbm,
        scratch_shapes=[
            bins_scratch,
            pltpu.VMEM((1, stations), jnp.int32),
            pltpu.VMEM((max(nodes // LANES, 8), LANES), jnp.int32),
            pltpu.VMEM(tables.shape, tables.dtype),
            phasors,
            phasors,
            coefs,
            plan,
            pltpu.VMEM((grid // wide * ntab, 3 * wide), jnp.bfloat16),
            pltpu.VMEM((3 * wide, nodes), jnp.bfloat16),
            pltpu.SemaphoreType.DMA((3 + 2 * ntab,)),
            pltpu.SemaphoreType.DMA((TABLE_PIECES,)),
        ],
        compiler_params=params(512 * 1024),
        name="prepare",
    )(bins, station_table.reshape(1, stations), node_ids.reshape(grid // LANES, LANES), tables)

    places = (stations // 8 + ntab // 2 + 2) // 2 * 16
    half = jax.ShapeDtypeStruct((NF, nodes), jnp.float32)
    rows = 2 * windows * 2 * NF
    basis = pltpu.VMEM((2 * DEGREES * 8, nodes), jnp.bfloat16)
    place, left = pl.pallas_call(
        functools.partial(weights_kernel, merged, stations_dev),
        out_shape=[
            jax.ShapeDtypeStruct((places, nodes), jnp.float32),
            jax.ShapeDtypeStruct((places // 8, rows, DEGREES * 8), jnp.bfloat16),
        ],
        in_specs=[hbm] + [vmem] * len(received),
        out_specs=[vmem, vmem],
        scratch_shapes=[
            pltpu.SMEM((8, plan_width), jnp.float32),
            plan,
            coefs,
            pltpu.VMEM((places, rows), jnp.float32),
            pltpu.SemaphoreType.DMA((3,)),
        ],
        compiler_params=params(27 * 512 * 1024),
        name="weights",
    )(packed, *received)
    keep, send = pl.pallas_call(
        functools.partial(image_kernel, stations),
        out_shape=[half, half],
        in_specs=[hbm, vmem, vmem],
        out_specs=[vmem, vmem],
        scratch_shapes=[
            pltpu.SMEM((8, plan_width), jnp.float32),
            phasors,
            phasors,
            pltpu.SemaphoreType.DMA((3,)),
            pltpu.VMEM((rows // 2, nodes), jnp.float32),
            basis,
            basis,
        ],
        compiler_params=params(27 * 512 * 1024),
        name="image",
    )(packed, place, left)
    got = lax.ppermute(send, "win", [(0, 1), (1, 0)])
    spectrum, beam_power = pl.pallas_call(
        functools.partial(finish_kernel, stations),
        out_shape=[
            jax.ShapeDtypeStruct((NF, windows * nodes), jnp.float32),
            jax.ShapeDtypeStruct((1, windows * nodes), jnp.float32),
        ],
        in_specs=[vmem, vmem],
        out_specs=[vmem, vmem],
        compiler_params=params(32 * 1024 * 1024),
        name="finish",
    )(keep, got)
    return spectrum, beam_power.reshape(windows * nodes)


def solution(mesh):
    return jax.shard_map(
        on_device,
        mesh=mesh,
        in_specs=(P(("win", "sta"), "freq"), P(), P("sta", None), P(), P(), P()),
        out_specs=(P("win", ("sta", "freq")), P(("win", "sta", "freq"))),
        check_vma=False,
    )
```

```python
import functools
import math

import jax
import jax.numpy as jnp
import numpy as np
from jax import lax
from jax.experimental import pallas as pl
from jax.experimental.pallas import tpu as pltpu
from jax.sharding import PartitionSpec as P

NT = 5120
NF = 16
NTAB = 16
LANES = 128
DEGREES = 32
FINE = 24
REACH = 1.5
TABLE_PIECES = 4
VMEM_LIMIT = 64 * 1024 * 1024 - 64 * 1024


def chebyshev_fit(func, degree, low, high):
    fit = np.polynomial.chebyshev.Chebyshev.interpolate(func, degree, domain=[low, high])
    return [float(v) for v in fit.convert(kind=np.polynomial.Polynomial).coef]


SIN_HALF = chebyshev_fit(lambda z: np.pi * np.sinc(np.sqrt(z)), 4, 0.0, 0.25)
COS_HALF = chebyshev_fit(lambda z: np.cos(np.pi * np.sqrt(z)), 4, 0.0, 0.25)


def horner(coefs, arg):
    total = coefs[-1]
    for coef in coefs[-2::-1]:
        total = total * arg + coef
    return total


def turn_parts(rest):
    square = rest * rest
    root = math.sqrt(2.0)
    sine_half = rest * horner([root * c for c in SIN_HALF], square)
    cos_half = horner([root * c for c in COS_HALF], square)
    return sine_half * sine_half, sine_half * cos_half


def cos_sin(turns):
    versine, sine = turn_parts(turns - jnp.round(turns))
    return 1.0 - versine, sine


def bins_column(bins_ref):
    rows = lax.broadcasted_iota(jnp.int32, (NF, NF), 0)
    lanes = lax.broadcasted_iota(jnp.int32, (NF, NF), 1)
    square = jnp.broadcast_to(bins_ref[...].astype(jnp.float32), (NF, NF))
    return jnp.sum(jnp.where(rows == lanes, square, 0.0), axis=1, keepdims=True)


def split_bf16(value, terms):
    pieces = []
    for term in range(terms):
        piece = value.astype(jnp.bfloat16)
        pieces.append(piece)
        if term < terms - 1:
            value = value - piece.astype(jnp.float32)
    return pieces


def start_all(copies):
    for copy in copies:
        copy.start()
    return copies


def send_kernel(nodes, bins_hbm, traces_hbm, corr_hbm, out_ref, bins_ref, traces_ref, sems):
    devices, height, _ = out_ref.shape
    stations_dev, half_length = traces_ref.shape
    pieces = (height - 8) // stations_dev
    windows, groups, cores = (lax.axis_size(a) for a in ("win", "sta", "freq"))
    place = lax.axis_index("win") * cores + lax.axis_index("freq")
    small = start_all(
        [
            pltpu.make_async_copy(bins_hbm, bins_ref, sems.at[0]),
            pltpu.make_async_copy(traces_hbm, traces_ref, sems.at[1]),
        ]
    )
    copies = []
    for dev in range(devices):
        win, sta, core = dev // (groups * cores), dev // cores % groups, dev % cores
        first = ((sta * cores + core) * windows + win) * nodes
        for piece in range(pieces):
            at = pl.multiple_of(first + (place * pieces + piece) * LANES, LANES)
            to = out_ref.at[dev, pl.ds(piece * stations_dev, stations_dev), :]
            sem = sems.at[2 + dev * pieces + piece]
            copies.append(pltpu.make_async_copy(corr_hbm.at[:, pl.ds(at, LANES)], to, sem))
    start_all(copies)
    start = lax.axis_index("freq") * half_length
    small[0].wait()
    bins = bins_column(bins_ref)
    pos = (start + lax.broadcasted_iota(jnp.int32, (NF, half_length), 1)).astype(jnp.float32)
    product = bins * pos
    turns = jnp.round(product * (1.0 / NT))
    rest = (product - turns * NT) * (1.0 / NT)
    versine, sine = turn_parts(rest)
    scale = 1.0 / math.sqrt(NT)
    table = jnp.concatenate([(1.0 - versine) * scale, sine * -scale], axis=0)
    both = jnp.concatenate(split_bf16(table, 2), axis=0)
    small[1].wait()
    sums = lax.dot_general(
        both, traces_ref[...], (((1,), (1,)), ((), ())), preferred_element_type=jnp.float32
    )
    sums = (sums[: 2 * NF] + sums[2 * NF :]).T
    terms = [term.astype(jnp.float32) for term in split_bf16(sums, 2)]
    tile = jnp.concatenate([term[at : at + 8] for term in terms for at in range(0, stations_dev, 8)], axis=1)
    tile = tile.astype(jnp.bfloat16)
    for dev in range(devices):
        out_ref[dev, height - 8 :, :] = tile
    for copy in copies:
        copy.wait()


def own_place():
    windows, cores = lax.axis_size("win"), lax.axis_size("freq")
    return (lax.axis_index("sta") * cores + lax.axis_index("freq")) * windows + lax.axis_index("win")


def pick_columns(ids_ref, tables_ref, table_copies, nodes, left_ref, right_ref):
    ntab, grid = tables_ref.shape
    count = nodes // LANES
    wide = right_ref.shape[0] // 3
    blocks = grid // wide
    ids = ids_ref[pl.ds(own_place() * count % ids_ref.shape[0], count), :]
    ids = jnp.concatenate([ids[at : at + 1] for at in range(count)], axis=1)
    low, high = ids & (wide - 1), ids >> (wide.bit_length() - 1)
    spots = lax.broadcasted_iota(jnp.int32, (wide, nodes), 0)
    ones = jnp.where(spots == low, 1.0, 0.0).astype(jnp.bfloat16)
    for term in range(3):
        right_ref[term * wide : (term + 1) * wide, :] = ones
    found = jnp.zeros((ntab, nodes), jnp.float32)
    step = blocks // len(table_copies)
    for at, copy in enumerate(table_copies):
        copy.wait()
        for block in range(at * step, (at + 1) * step):
            pieces = split_bf16(tables_ref[:, block * wide : (block + 1) * wide], 3)
            left_ref[block * ntab : (block + 1) * ntab, :] = jnp.concatenate(pieces, axis=1)
        rows = left_ref[at * step * ntab : (at + 1) * step * ntab, :]
        picked = jnp.dot(rows, right_ref[...], preferred_element_type=jnp.float32)
        for block in range(step):
            part = picked[block * ntab : (block + 1) * ntab]
            found = jnp.where(high == at * step + block, part, found)
    return found


def chebyshev_coefs(bins_ref):
    shape = (DEGREES, DEGREES)
    degree = lax.broadcasted_iota(jnp.int32, shape, 0)
    node = lax.broadcasted_iota(jnp.int32, shape, 1)
    period = 4 * DEGREES
    weight, _ = cos_sin((degree * (2 * node + 1) & (period - 1)).astype(jnp.float32) * (1.0 / period))
    weight = weight * jnp.where(degree == 0, 1.0 / DEGREES, 2.0 / DEGREES)
    even = jnp.where(degree % 2 == 0, weight, 0.0)
    odd = jnp.where(degree % 2 == 1, weight, 0.0)
    row = bins_ref[...].astype(jnp.float32)
    bins = jnp.concatenate([row] * (LANES // NF), axis=1)
    at = lax.broadcasted_iota(jnp.int32, (DEGREES, LANES), 0).astype(jnp.float32)
    spot, _ = cos_sin((2.0 * at + 1.0) * (1.0 / period))
    cosine, sine = cos_sin(bins * (spot * (REACH / 256.0)))
    dot = functools.partial(jnp.dot, precision=lax.Precision.HIGHEST, preferred_element_type=jnp.float32)
    return dot(even, cosine) + dot(odd, sine)


def station_plan(table_row, width):
    count = table_row.shape[1]
    shape = (count, count)
    here = lax.broadcasted_iota(jnp.int32, shape, 0)
    there = lax.broadcasted_iota(jnp.int32, shape, 1)
    column_of = lambda row: jnp.sum(jnp.where(here == there, jnp.broadcast_to(row, shape), 0), axis=1, keepdims=True)
    table_column = column_of(table_row)
    same = (table_column == table_row) & (here < there)
    within = jnp.sum(jnp.where(same, 1, 0), axis=0, keepdims=True)
    place_row = within
    spot = jnp.zeros((1, 1), jnp.int32)
    held = jnp.zeros((1, 1), jnp.int32)
    for table in range(NTAB):
        size = jnp.sum(jnp.where(table_row == table, 1, 0), axis=1, keepdims=True)
        some = size > 0
        edge = (spot & 7) == 0
        skip = some & (held >= 2) & ~edge
        spot = jnp.where(skip, (spot + 7) >> 3 << 3, spot)
        held = jnp.where(skip | edge, 0, held)
        after = spot + size
        place_row = place_row + jnp.where(table_row == table, spot, 0)
        held = jnp.where(some, jnp.where(after >> 3 == spot >> 3, held + 1, 1), held)
        spot = after
    groups = (spot + 7) >> 3
    place_column = column_of(place_row)
    group = lax.broadcasted_iota(jnp.int32, (count, width), 1)
    inside = place_column >> 3 == group
    first = jnp.sum(jnp.where(place_column == group * 8, table_column, 0), axis=0, keepdims=True)
    last = jnp.max(jnp.where(inside, table_column, 0), axis=0, keepdims=True)
    length = jnp.sum(jnp.where(inside & (table_column == first), 1, 0), axis=0, keepdims=True)
    rows = [first, last, length, jnp.broadcast_to(groups, (1, width))]
    if width > count:
        place_row = jnp.concatenate([place_row, jnp.zeros((1, width - count), jnp.int32)], axis=1)
    rows += [place_row, jnp.zeros((3, width), jnp.int32)]
    return jnp.concatenate(rows, axis=0).astype(jnp.float32)


def packed_rows(ntab):
    ends = [ntab * NF, 2 * ntab * NF, 2 * ntab * NF + DEGREES, 2 * ntab * NF + DEGREES + 8]
    return [slice(start, end) for start, end in zip([0] + ends, ends)]


def prepare_kernel(bins_hbm, table_hbm, ids_hbm, tables_hbm, out_hbm, *rest):
    bins_ref, table_ref, ids_ref, tables_ref, cos_ref, sin_ref, coef_ref, plan_ref = rest[:8]
    left_ref, right_ref, sems, table_sems = rest[8:]
    ntab = tables_ref.shape[0]
    nodes = cos_ref.shape[1]
    near = ids_ref.shape[0]
    first = pl.multiple_of(own_place() * (nodes // LANES) // near * near, 8)
    ins = start_all(
        [
            pltpu.make_async_copy(ids_hbm.at[pl.ds(first, near), :], ids_ref, sems.at[0]),
            pltpu.make_async_copy(bins_hbm, bins_ref, sems.at[1]),
            pltpu.make_async_copy(table_hbm, table_ref, sems.at[2]),
        ]
    )
    piece = tables_ref.shape[1] // TABLE_PIECES
    table_copies = []
    for at in range(TABLE_PIECES):
        part = (slice(None), pl.ds(at * piece, piece))
        table_copies.append(pltpu.make_async_copy(tables_hbm.at[part], tables_ref.at[part], table_sems.at[at]))
    start_all(table_copies)
    for copy in ins:
        copy.wait()
    cos_at, sin_at, coef_at, plan_at = packed_rows(ntab)
    coef_ref[...] = chebyshev_coefs(bins_ref)
    plan_ref[...] = station_plan(table_ref[...], plan_ref.shape[1])
    outs = start_all(
        [
            pltpu.make_async_copy(coef_ref, out_hbm.at[coef_at, pl.ds(0, LANES)], sems.at[0]),
            pltpu.make_async_copy(plan_ref, out_hbm.at[plan_at, pl.ds(0, plan_ref.shape[1])], sems.at[1]),
        ]
    )
    turns = pick_columns(ids_ref, tables_ref, table_copies, nodes, left_ref, right_ref) * (1.0 / 256.0)
    bins = bins_column(bins_ref)
    for table in range(ntab):
        cosine, sine = cos_sin(bins * turns[table : table + 1])
        at = pl.ds(table * NF, NF)
        cos_ref[at, :] = cosine
        sin_ref[at, :] = sine
        outs += start_all(
            [
                pltpu.make_async_copy(
                    cos_ref.at[at, :], out_hbm.at[pl.ds(cos_at.start + table * NF, NF), pl.ds(0, nodes)],
                    sems.at[3 + 2 * table],
                ),
                pltpu.make_async_copy(
                    sin_ref.at[at, :], out_hbm.at[pl.ds(sin_at.start + table * NF, NF), pl.ds(0, nodes)],
                    sems.at[4 + 2 * table],
                ),
            ]
        )
    for copy in outs:
        copy.wait()


def image_kernel(merged, stations_dev, packed_hbm, block_ref, *rest):
    corr_ref, rest = (None, rest) if merged else (rest[0], rest[1:])
    keep_ref, send_ref, plan_ref, place_of_ref, coef_ref, cos_ref, sin_ref, sems = rest[:8]
    place_ref, weight_ref, left_ref, sums_ref, basis_a, basis_b = rest[8:]
    places, nodes = place_ref.shape
    windows, groups, cores = (lax.axis_size(a) for a in ("win", "sta", "freq"))
    stations = stations_dev * groups
    cos_at, sin_at, coef_at, plan_at = packed_rows(cos_ref.shape[0] // NF)
    width = plan_ref.shape[1]
    copies = start_all(
        [
            pltpu.make_async_copy(packed_hbm.at[plan_at, pl.ds(0, width)], place_of_ref, sems.at[0]),
            pltpu.make_async_copy(packed_hbm.at[plan_at, pl.ds(0, width)], plan_ref, sems.at[1]),
            pltpu.make_async_copy(packed_hbm.at[coef_at, pl.ds(0, LANES)], coef_ref, sems.at[2]),
        ]
        + [
            pltpu.make_async_copy(
                packed_hbm.at[pl.ds(at.start + first, 4 * NF), pl.ds(0, nodes)],
                ref.at[pl.ds(first, 4 * NF), :],
                sems.at[3 + 2 * (first // (4 * NF)) + which],
            )
            for first in range(0, NTAB * NF, 4 * NF)
            for which, (at, ref) in enumerate(((cos_at, cos_ref), (sin_at, sin_ref)))
        ]
    )
    height = block_ref.shape[1]
    rows_of = lambda win, core: [(win * groups + group) * cores + core for group in range(groups)]

    even, odd = [], []
    for win in range(windows):
        value = []
        for group in range(groups):
            tile = None
            for core in range(cores):
                part = block_ref[(win * groups + group) * cores + core, height - 8 :, :].astype(jnp.float32)
                tile = part if tile is None else tile + part
            tile = tile[:, : LANES // 2] + tile[:, LANES // 2 :]
            value += [tile[:, 2 * NF * piece : 2 * NF * (piece + 1)] for piece in range(stations_dev // 8)]
        value = jnp.concatenate(value, axis=0)
        even.append(value)
        odd.append(jnp.concatenate([-value[:, NF:], value[:, :NF]], axis=1))
    spectra = jnp.concatenate(even + odd, axis=1)
    if merged:
        parts = []
        for win in range(windows):
            for core in range(cores):
                for first in range(0, height - 8, stations_dev):
                    rows = [block_ref[at, first : first + stations_dev, :] for at in rows_of(win, core)]
                    parts.append(jnp.concatenate(rows, axis=0))
        corr = jnp.concatenate(parts, axis=1)
    else:
        corr = corr_ref[...]

    copies[0].wait()
    place_row = place_of_ref[4:5, :stations].astype(jnp.int32)
    sorter = lax.broadcasted_iota(jnp.int32, (places, stations), 0) == place_row
    sorter = jnp.where(sorter, 1.0, 0.0).astype(jnp.bfloat16)
    found = None
    for piece in split_bf16(spectra, 3):
        part = jnp.dot(sorter, piece, preferred_element_type=jnp.float32)
        found = part if found is None else found + part
    weight_ref[...] = found
    place_ref[...] = jnp.dot(sorter, corr, preferred_element_type=jnp.float32) * (1.0 / REACH)
    sums_ref[...] = jnp.zeros_like(sums_ref)
    chunk = min(256, nodes)
    depth = DEGREES * 8
    lanes = windows * 2 * NF
    for copy in copies[1:3]:
        copy.wait()

    def make_left(pair):
        top = weight_ref[pl.ds(pl.multiple_of(pair * 16, 16), 8), :]
        bottom = weight_ref[pl.ds(pl.multiple_of(pair * 16 + 8, 8), 8), :]
        sides = [
            jnp.concatenate([top[:, :lanes], bottom[:, :lanes]], axis=1),
            jnp.concatenate([top[:, lanes:], bottom[:, lanes:]], axis=1),
        ]
        per = LANES // 8
        for half in range(DEGREES // per):
            tall = jnp.concatenate(
                [sides[k % 2] * coef_ref[k : k + 1, :] for k in range(half * per, (half + 1) * per)], axis=0
            )
            high, low = split_bf16(tall.T, 2)
            first = half * LANES
            fine = min(FINE * 8 - first, LANES)
            if fine == LANES:
                parts = [(first, high), (depth + first, high), (2 * FINE * 8 + first + LANES, low)]
            else:
                mixed = [high[:, :fine].astype(jnp.float32), low[:, :fine].astype(jnp.float32)]
                parts = [(first, high), (depth + first, jnp.concatenate(mixed, axis=1).astype(jnp.bfloat16))]
            for at, value in parts:
                left_ref[2 * pair, :, at : at + LANES] = value[:lanes]
                left_ref[2 * pair + 1, :, at : at + LANES] = value[lanes:]

    used = plan_ref[3, 0].astype(jnp.int32)
    sure = stations // 16
    if sure <= 8:
        for pair in range(sure):
            make_left(pair)
    else:
        lax.fori_loop(0, sure, lambda pair, carry: (make_left(pair), carry)[1], 0)
    lax.fori_loop(sure, (used + 1) // 2, lambda pair, carry: (make_left(pair), carry)[1], 0)
    spot = (lax.broadcasted_iota(jnp.int32, (16, left_ref.shape[2]), 1) & 7).astype(jnp.float32)

    def left_of(group):
        mask = spot < plan_ref[2, group]
        results = []
        for keep, drop in ((1.0, 0.0), (0.0, 1.0)):
            side = jnp.where(mask, keep, drop).astype(jnp.bfloat16)
            results.append(left_ref[group] * jnp.concatenate([side] * (lanes // 16), axis=0))
        return jnp.concatenate(results, axis=0)

    def basis_steps(group, basis_ref):
        arg = place_ref[pl.ds(pl.multiple_of(group * 8, 8), 8), :]
        twice = arg + arg
        before, now = jnp.ones_like(arg), arg
        for degree in range(0, DEGREES, 2):
            pair = jnp.concatenate([before, now], axis=0)
            terms = split_bf16(pair, 2 if degree < FINE else 1)
            for term, value in enumerate(terms):
                basis_ref[term * depth + degree * 8 : term * depth + degree * 8 + 16, :] = value
            before = twice * now - before
            now = twice * before - now
            if degree % 8 == 6:
                yield

    def run(steps):
        for _ in steps:
            pass

    def add_group(group, basis_ref, steps):
        left = left_of(group)
        tables = [plan_ref[slot, group].astype(jnp.int32) for slot in range(2)]
        phasor_rows = [pl.ds(pl.multiple_of(table * NF, NF), NF) for table in tables]
        fine = FINE * 8
        for first in range(0, nodes, chunk):
            at = slice(first, first + chunk)
            right = [
                basis_ref[: depth + fine, at],
                basis_ref[LANES:fine, at],
                basis_ref[:LANES, at],
            ]
            got = jnp.dot(left, jnp.concatenate(right, axis=0), preferred_element_type=jnp.float32)
            next(steps, None)
            for win in range(windows):
                row = win * 2 * NF
                real_sum, imag_sum = sums_ref[row : row + NF, at], sums_ref[row + NF : row + 2 * NF, at]
                for slot, rows in enumerate(phasor_rows):
                    cosine, sine = cos_ref[rows, at], sin_ref[rows, at]
                    real = got[slot * lanes + row : slot * lanes + row + NF]
                    imag = got[slot * lanes + row + NF : slot * lanes + row + 2 * NF]
                    real_sum += real * cosine - imag * sine
                    imag_sum += real * sine + imag * cosine
                sums_ref[row : row + NF, at], sums_ref[row + NF : row + 2 * NF, at] = real_sum, imag_sum
        run(steps)

    run(basis_steps(0, basis_a))
    for copy in copies[3:]:
        copy.wait()

    def body(pair, carry):
        group = pair * 2
        add_group(group, basis_a, basis_steps(group + 1, basis_b))
        add_group(group + 1, basis_b, basis_steps(jnp.minimum(group + 2, places // 8 - 1), basis_a))
        return carry

    lax.fori_loop(0, used // 2, body, 0)

    @pl.when(used % 2 == 1)
    def _():
        add_group(used - 1, basis_a, iter(()))

    powers = []
    for win in range(windows):
        row = win * 2 * NF
        real, imag = sums_ref[row : row + NF, :], sums_ref[row + NF : row + 2 * NF, :]
        powers.append(real * real + imag * imag)
    mine = lax.axis_index("win") == 0
    keep_ref[...] = jnp.where(mine, powers[0], powers[1])
    send_ref[...] = jnp.where(mine, powers[1], powers[0])


def finish_kernel(stations, keep_ref, got_ref, spectrum_ref, beam_ref):
    nodes = keep_ref.shape[1]
    win = lax.axis_index("win")
    for place, ref in ((win, keep_ref), (1 - win, got_ref)):
        power = ref[...]
        total = jnp.sum(power, axis=0, keepdims=True)
        at = pl.ds(pl.multiple_of(place * nodes, LANES), nodes)
        spectrum_ref[:, at] = power * (NF / total)
        beam_ref[:, at] = total * (1.0 / (NF * stations))


def on_device(traces, tables, corrections, station_table, node_ids, freq_bins):
    windows, groups, cores = (lax.axis_size(a) for a in ("win", "sta", "freq"))
    stations_dev, grid = corrections.shape
    stations = stations_dev * groups
    devices = windows * groups * cores
    nodes = grid // devices
    ntab = tables.shape[0]
    params = lambda free: pltpu.CompilerParams(vmem_limit_bytes=VMEM_LIMIT - free)
    vmem = pl.BlockSpec(memory_space=pltpu.VMEM)
    hbm = pl.BlockSpec(memory_space=pltpu.HBM)
    bins = freq_bins.reshape(1, NF)
    bins_scratch = pltpu.VMEM((1, NF), jnp.int32)

    holders = windows * cores
    merged = nodes % (holders * LANES) == 0
    pieces = nodes // (holders * LANES) if merged else 0
    height = pieces * stations_dev + 8
    blocks = pl.pallas_call(
        functools.partial(send_kernel, nodes),
        out_shape=jax.ShapeDtypeStruct((devices, height, LANES), jnp.bfloat16),
        in_specs=[hbm] * 3,
        out_specs=vmem,
        scratch_shapes=[
            bins_scratch,
            pltpu.VMEM(traces.shape, traces.dtype),
            pltpu.SemaphoreType.DMA((2 + devices * max(pieces, 1),)),
        ],
        compiler_params=params(0),
        name="send",
    )(bins, traces, corrections)
    received = [lax.all_to_all(blocks, ("win", "sta", "freq"), split_axis=0, concat_axis=0, tiled=True)]
    if not merged:
        parts = corrections.reshape(stations_dev, groups, holders, nodes)
        place = lax.axis_index("freq") * windows + lax.axis_index("win")
        mine = lax.dynamic_index_in_dim(parts, place, axis=2, keepdims=False)
        corr = lax.all_to_all(mine.transpose(1, 0, 2), "sta", split_axis=0, concat_axis=0, tiled=True)
        received.append(corr.reshape(stations, nodes))

    wide = 512
    plan_width = max(LANES, stations)
    phasors = pltpu.VMEM((ntab * NF, nodes), jnp.float32)
    coefs = pltpu.VMEM((DEGREES, LANES), jnp.float32)
    plan = pltpu.VMEM((8, plan_width), jnp.float32)
    packed_shape = (packed_rows(ntab)[-1].stop, max(nodes, plan_width))
    packed = pl.pallas_call(
        prepare_kernel,
        out_shape=jax.ShapeDtypeStruct(packed_shape, jnp.float32),
        in_specs=[hbm] * 4,
        out_specs=hbm,
        scratch_shapes=[
            bins_scratch,
            pltpu.VMEM((1, stations), jnp.int32),
            pltpu.VMEM((max(nodes // LANES, 8), LANES), jnp.int32),
            pltpu.VMEM(tables.shape, tables.dtype),
            phasors,
            phasors,
            coefs,
            plan,
            pltpu.VMEM((grid // wide * ntab, 3 * wide), jnp.bfloat16),
            pltpu.VMEM((3 * wide, nodes), jnp.bfloat16),
            pltpu.SemaphoreType.DMA((3 + 2 * ntab,)),
            pltpu.SemaphoreType.DMA((TABLE_PIECES,)),
        ],
        compiler_params=params(512 * 1024),
        name="prepare",
    )(bins, station_table.reshape(1, stations), node_ids.reshape(grid // LANES, LANES), tables)

    places = (stations // 8 + ntab // 2 + 2) // 2 * 16
    half = jax.ShapeDtypeStruct((NF, nodes), jnp.float32)
    rows = 2 * windows * 2 * NF
    basis = pltpu.VMEM(((DEGREES + FINE) * 8, nodes), jnp.bfloat16)
    keep, send = pl.pallas_call(
        functools.partial(image_kernel, merged, stations_dev),
        out_shape=[half, half],
        in_specs=[hbm] + [vmem] * len(received),
        out_specs=[vmem, vmem],
        scratch_shapes=[
            pltpu.SMEM((8, plan_width), jnp.float32),
            plan,
            coefs,
            phasors,
            phasors,
            pltpu.SemaphoreType.DMA((3 + ntab // 2,)),
            pltpu.VMEM((places, nodes), jnp.float32),
            pltpu.VMEM((places, rows), jnp.float32),
            pltpu.VMEM((places // 8, rows // 2, (DEGREES + 2 * FINE) * 8), jnp.bfloat16),
            pltpu.VMEM((rows // 2, nodes), jnp.float32),
            basis,
            basis,
        ],
        compiler_params=params(23 * 512 * 1024),
        name="image",
    )(packed, *received)
    got = lax.ppermute(send, "win", [(0, 1), (1, 0)])
    spectrum, beam_power = pl.pallas_call(
        functools.partial(finish_kernel, stations),
        out_shape=[
            jax.ShapeDtypeStruct((NF, windows * nodes), jnp.float32),
            jax.ShapeDtypeStruct((1, windows * nodes), jnp.float32),
        ],
        in_specs=[vmem, vmem],
        out_specs=[vmem, vmem],
        compiler_params=params(32 * 1024 * 1024),
        name="finish",
    )(keep, got)
    return spectrum, beam_power.reshape(windows * nodes)


def solution(mesh):
    return jax.shard_map(
        on_device,
        mesh=mesh,
        in_specs=(P(("win", "sta"), "freq"), P(), P("sta", None), P(), P(), P()),
        out_specs=(P("win", ("sta", "freq")), P(("win", "sta", "freq"))),
        check_vma=False,
    )
```

```python
import functools
import math

import jax
import jax.numpy as jnp
import numpy as np
from jax import lax
from jax.experimental import pallas as pl
from jax.experimental.pallas import tpu as pltpu
from jax.sharding import PartitionSpec as P

NT = 5120
NF = 16
NTAB = 16
LANES = 128
DEGREES = 32
FINE = 24
REACH = 1.5
TABLE_PIECES = 4
VMEM_LIMIT = 64 * 1024 * 1024 - 64 * 1024


def chebyshev_fit(func, degree, low, high):
    fit = np.polynomial.chebyshev.Chebyshev.interpolate(func, degree, domain=[low, high])
    return [float(v) for v in fit.convert(kind=np.polynomial.Polynomial).coef]


SIN_HALF = chebyshev_fit(lambda z: np.pi * np.sinc(np.sqrt(z)), 4, 0.0, 0.25)
COS_HALF = chebyshev_fit(lambda z: np.cos(np.pi * np.sqrt(z)), 4, 0.0, 0.25)


def horner(coefs, arg):
    total = coefs[-1]
    for coef in coefs[-2::-1]:
        total = total * arg + coef
    return total


def turn_parts(rest):
    square = rest * rest
    root = math.sqrt(2.0)
    sine_half = rest * horner([root * c for c in SIN_HALF], square)
    cos_half = horner([root * c for c in COS_HALF], square)
    return sine_half * sine_half, sine_half * cos_half


def cos_sin(turns):
    versine, sine = turn_parts(turns - jnp.round(turns))
    return 1.0 - versine, sine


def bins_column(bins_ref):
    rows = lax.broadcasted_iota(jnp.int32, (NF, NF), 0)
    lanes = lax.broadcasted_iota(jnp.int32, (NF, NF), 1)
    square = jnp.broadcast_to(bins_ref[...].astype(jnp.float32), (NF, NF))
    return jnp.sum(jnp.where(rows == lanes, square, 0.0), axis=1, keepdims=True)


def split_bf16(value, terms):
    pieces = []
    for term in range(terms):
        piece = value.astype(jnp.bfloat16)
        pieces.append(piece)
        if term < terms - 1:
            value = value - piece.astype(jnp.float32)
    return pieces


def start_all(copies):
    for copy in copies:
        copy.start()
    return copies


def send_kernel(nodes, bins_hbm, traces_hbm, corr_hbm, out_ref, bins_ref, traces_ref, sems):
    devices, height, _ = out_ref.shape
    stations_dev, half_length = traces_ref.shape
    pieces = (height - 8) // stations_dev
    windows, groups, cores = (lax.axis_size(a) for a in ("win", "sta", "freq"))
    place = lax.axis_index("win") * cores + lax.axis_index("freq")
    small = start_all(
        [
            pltpu.make_async_copy(bins_hbm, bins_ref, sems.at[0]),
            pltpu.make_async_copy(traces_hbm, traces_ref, sems.at[1]),
        ]
    )
    copies = []
    for dev in range(devices):
        win, sta, core = dev // (groups * cores), dev // cores % groups, dev % cores
        first = ((sta * cores + core) * windows + win) * nodes
        for piece in range(pieces):
            at = pl.multiple_of(first + (place * pieces + piece) * LANES, LANES)
            to = out_ref.at[dev, pl.ds(piece * stations_dev, stations_dev), :]
            sem = sems.at[2 + dev * pieces + piece]
            copies.append(pltpu.make_async_copy(corr_hbm.at[:, pl.ds(at, LANES)], to, sem))
    start_all(copies)
    start = lax.axis_index("freq") * half_length
    small[0].wait()
    bins = bins_column(bins_ref)
    pos = (start + lax.broadcasted_iota(jnp.int32, (NF, half_length), 1)).astype(jnp.float32)
    product = bins * pos
    turns = jnp.round(product * (1.0 / NT))
    rest = (product - turns * NT) * (1.0 / NT)
    versine, sine = turn_parts(rest)
    scale = 1.0 / math.sqrt(NT)
    table = jnp.concatenate([(1.0 - versine) * scale, sine * -scale], axis=0)
    both = jnp.concatenate(split_bf16(table, 2), axis=0)
    small[1].wait()
    sums = lax.dot_general(
        both, traces_ref[...], (((1,), (1,)), ((), ())), preferred_element_type=jnp.float32
    )
    sums = (sums[: 2 * NF] + sums[2 * NF :]).T
    terms = [term.astype(jnp.float32) for term in split_bf16(sums, 2)]
    tile = jnp.concatenate([term[at : at + 8] for term in terms for at in range(0, stations_dev, 8)], axis=1)
    tile = tile.astype(jnp.bfloat16)
    for dev in range(devices):
        out_ref[dev, height - 8 :, :] = tile
    for copy in copies:
        copy.wait()


def own_place():
    windows, cores = lax.axis_size("win"), lax.axis_size("freq")
    return (lax.axis_index("sta") * cores + lax.axis_index("freq")) * windows + lax.axis_index("win")


def pick_columns(ids_ref, tables_ref, table_copies, nodes, left_ref, right_ref):
    ntab, grid = tables_ref.shape
    count = nodes // LANES
    wide = right_ref.shape[0] // 3
    blocks = grid // wide
    ids = ids_ref[pl.ds(own_place() * count % ids_ref.shape[0], count), :]
    ids = jnp.concatenate([ids[at : at + 1] for at in range(count)], axis=1)
    low, high = ids & (wide - 1), ids >> (wide.bit_length() - 1)
    spots = lax.broadcasted_iota(jnp.int32, (wide, nodes), 0)
    ones = jnp.where(spots == low, 1.0, 0.0).astype(jnp.bfloat16)
    for term in range(3):
        right_ref[term * wide : (term + 1) * wide, :] = ones
    found = jnp.zeros((ntab, nodes), jnp.float32)
    step = blocks // len(table_copies)
    for at, copy in enumerate(table_copies):
        copy.wait()
        for block in range(at * step, (at + 1) * step):
            pieces = split_bf16(tables_ref[:, block * wide : (block + 1) * wide], 3)
            left_ref[block * ntab : (block + 1) * ntab, :] = jnp.concatenate(pieces, axis=1)
        rows = left_ref[at * step * ntab : (at + 1) * step * ntab, :]
        picked = jnp.dot(rows, right_ref[...], preferred_element_type=jnp.float32)
        for block in range(step):
            part = picked[block * ntab : (block + 1) * ntab]
            found = jnp.where(high == at * step + block, part, found)
    return found


def chebyshev_coefs(bins_ref):
    shape = (DEGREES, DEGREES)
    degree = lax.broadcasted_iota(jnp.int32, shape, 0)
    node = lax.broadcasted_iota(jnp.int32, shape, 1)
    period = 4 * DEGREES
    weight, _ = cos_sin((degree * (2 * node + 1) & (period - 1)).astype(jnp.float32) * (1.0 / period))
    weight = weight * jnp.where(degree == 0, 1.0 / DEGREES, 2.0 / DEGREES)
    even = jnp.where(degree % 2 == 0, weight, 0.0)
    odd = jnp.where(degree % 2 == 1, weight, 0.0)
    row = bins_ref[...].astype(jnp.float32)
    bins = jnp.concatenate([row] * (LANES // NF), axis=1)
    at = lax.broadcasted_iota(jnp.int32, (DEGREES, LANES), 0).astype(jnp.float32)
    spot, _ = cos_sin((2.0 * at + 1.0) * (1.0 / period))
    cosine, sine = cos_sin(bins * (spot * (REACH / 256.0)))
    dot = functools.partial(jnp.dot, precision=lax.Precision.HIGHEST, preferred_element_type=jnp.float32)
    return dot(even, cosine) + dot(odd, sine)


def station_plan(table_row, width):
    count = table_row.shape[1]
    shape = (count, count)
    here = lax.broadcasted_iota(jnp.int32, shape, 0)
    there = lax.broadcasted_iota(jnp.int32, shape, 1)
    column_of = lambda row: jnp.sum(jnp.where(here == there, jnp.broadcast_to(row, shape), 0), axis=1, keepdims=True)
    table_column = column_of(table_row)
    same = (table_column == table_row) & (here < there)
    within = jnp.sum(jnp.where(same, 1, 0), axis=0, keepdims=True)
    place_row = within
    spot = jnp.zeros((1, 1), jnp.int32)
    held = jnp.zeros((1, 1), jnp.int32)
    for table in range(NTAB):
        size = jnp.sum(jnp.where(table_row == table, 1, 0), axis=1, keepdims=True)
        some = size > 0
        edge = (spot & 7) == 0
        skip = some & (held >= 2) & ~edge
        spot = jnp.where(skip, (spot + 7) >> 3 << 3, spot)
        held = jnp.where(skip | edge, 0, held)
        after = spot + size
        place_row = place_row + jnp.where(table_row == table, spot, 0)
        held = jnp.where(some, jnp.where(after >> 3 == spot >> 3, held + 1, 1), held)
        spot = after
    groups = (spot + 7) >> 3
    place_column = column_of(place_row)
    group = lax.broadcasted_iota(jnp.int32, (count, width), 1)
    inside = place_column >> 3 == group
    first = jnp.sum(jnp.where(place_column == group * 8, table_column, 0), axis=0, keepdims=True)
    last = jnp.max(jnp.where(inside, table_column, 0), axis=0, keepdims=True)
    length = jnp.sum(jnp.where(inside & (table_column == first), 1, 0), axis=0, keepdims=True)
    rows = [first, last, length, jnp.broadcast_to(groups, (1, width))]
    if width > count:
        place_row = jnp.concatenate([place_row, jnp.zeros((1, width - count), jnp.int32)], axis=1)
    rows += [place_row, jnp.zeros((3, width), jnp.int32)]
    return jnp.concatenate(rows, axis=0).astype(jnp.float32)


def packed_rows(ntab):
    ends = [ntab * NF, 2 * ntab * NF, 2 * ntab * NF + DEGREES, 2 * ntab * NF + DEGREES + 8]
    return [slice(start, end) for start, end in zip([0] + ends, ends)]


def prepare_kernel(bins_hbm, table_hbm, ids_hbm, tables_hbm, out_hbm, *rest):
    bins_ref, table_ref, ids_ref, tables_ref, cos_ref, sin_ref, coef_ref, plan_ref = rest[:8]
    left_ref, right_ref, sems, table_sems = rest[8:]
    ntab = tables_ref.shape[0]
    nodes = cos_ref.shape[1]
    near = ids_ref.shape[0]
    first = pl.multiple_of(own_place() * (nodes // LANES) // near * near, 8)
    ins = start_all(
        [
            pltpu.make_async_copy(ids_hbm.at[pl.ds(first, near), :], ids_ref, sems.at[0]),
            pltpu.make_async_copy(bins_hbm, bins_ref, sems.at[1]),
            pltpu.make_async_copy(table_hbm, table_ref, sems.at[2]),
        ]
    )
    piece = tables_ref.shape[1] // TABLE_PIECES
    table_copies = []
    for at in range(TABLE_PIECES):
        part = (slice(None), pl.ds(at * piece, piece))
        table_copies.append(pltpu.make_async_copy(tables_hbm.at[part], tables_ref.at[part], table_sems.at[at]))
    start_all(table_copies)
    for copy in ins:
        copy.wait()
    cos_at, sin_at, coef_at, plan_at = packed_rows(ntab)
    coef_ref[...] = chebyshev_coefs(bins_ref)
    plan_ref[...] = station_plan(table_ref[...], plan_ref.shape[1])
    outs = start_all(
        [
            pltpu.make_async_copy(coef_ref, out_hbm.at[coef_at, pl.ds(0, LANES)], sems.at[0]),
            pltpu.make_async_copy(plan_ref, out_hbm.at[plan_at, pl.ds(0, plan_ref.shape[1])], sems.at[1]),
        ]
    )
    turns = pick_columns(ids_ref, tables_ref, table_copies, nodes, left_ref, right_ref) * (1.0 / 256.0)
    bins = bins_column(bins_ref)
    for table in range(ntab):
        cosine, sine = cos_sin(bins * turns[table : table + 1])
        at = pl.ds(table * NF, NF)
        cos_ref[at, :] = cosine
        sin_ref[at, :] = sine
        outs += start_all(
            [
                pltpu.make_async_copy(
                    cos_ref.at[at, :], out_hbm.at[pl.ds(cos_at.start + table * NF, NF), pl.ds(0, nodes)],
                    sems.at[3 + 2 * table],
                ),
                pltpu.make_async_copy(
                    sin_ref.at[at, :], out_hbm.at[pl.ds(sin_at.start + table * NF, NF), pl.ds(0, nodes)],
                    sems.at[4 + 2 * table],
                ),
            ]
        )
    for copy in outs:
        copy.wait()


def image_kernel(merged, stations_dev, packed_hbm, block_ref, *rest):
    corr_ref, rest = (None, rest) if merged else (rest[0], rest[1:])
    keep_ref, send_ref, plan_ref, place_of_ref, coef_ref, cos_ref, sin_ref, sems = rest[:8]
    place_ref, weight_ref, left_ref, sums_ref, basis_a, basis_b = rest[8:]
    places, nodes = place_ref.shape
    windows, groups, cores = (lax.axis_size(a) for a in ("win", "sta", "freq"))
    stations = stations_dev * groups
    cos_at, sin_at, coef_at, plan_at = packed_rows(cos_ref.shape[0] // NF)
    width = plan_ref.shape[1]
    copies = start_all(
        [
            pltpu.make_async_copy(packed_hbm.at[plan_at, pl.ds(0, width)], place_of_ref, sems.at[0]),
            pltpu.make_async_copy(packed_hbm.at[plan_at, pl.ds(0, width)], plan_ref, sems.at[1]),
            pltpu.make_async_copy(packed_hbm.at[coef_at, pl.ds(0, LANES)], coef_ref, sems.at[2]),
        ]
        + [
            pltpu.make_async_copy(
                packed_hbm.at[pl.ds(at.start + first, 4 * NF), pl.ds(0, nodes)],
                ref.at[pl.ds(first, 4 * NF), :],
                sems.at[3 + 2 * (first // (4 * NF)) + which],
            )
            for first in range(0, NTAB * NF, 4 * NF)
            for which, (at, ref) in enumerate(((cos_at, cos_ref), (sin_at, sin_ref)))
        ]
    )
    height = block_ref.shape[1]
    rows_of = lambda win, core: [(win * groups + group) * cores + core for group in range(groups)]

    even, odd = [], []
    for win in range(windows):
        value = []
        for group in range(groups):
            tile = None
            for core in range(cores):
                part = block_ref[(win * groups + group) * cores + core, height - 8 :, :].astype(jnp.float32)
                tile = part if tile is None else tile + part
            tile = tile[:, : LANES // 2] + tile[:, LANES // 2 :]
            value += [tile[:, 2 * NF * piece : 2 * NF * (piece + 1)] for piece in range(stations_dev // 8)]
        value = jnp.concatenate(value, axis=0)
        even.append(value)
        odd.append(jnp.concatenate([-value[:, NF:], value[:, :NF]], axis=1))
    spectra = jnp.concatenate(even + odd, axis=1)
    if merged:
        parts = []
        for win in range(windows):
            for core in range(cores):
                for first in range(0, height - 8, stations_dev):
                    rows = [block_ref[at, first : first + stations_dev, :] for at in rows_of(win, core)]
                    parts.append(jnp.concatenate(rows, axis=0))
        corr = jnp.concatenate(parts, axis=1)
    else:
        corr = corr_ref[...]

    copies[0].wait()
    place_row = place_of_ref[4:5, :stations].astype(jnp.int32)
    sorter = lax.broadcasted_iota(jnp.int32, (places, stations), 0) == place_row
    sorter = jnp.where(sorter, 1.0, 0.0).astype(jnp.bfloat16)
    found = None
    for piece in split_bf16(spectra, 3):
        part = jnp.dot(sorter, piece, preferred_element_type=jnp.float32)
        found = part if found is None else found + part
    weight_ref[...] = found
    place_ref[...] = jnp.dot(sorter, corr, preferred_element_type=jnp.float32) * (1.0 / REACH)
    sums_ref[...] = jnp.zeros_like(sums_ref)
    chunk = min(256, nodes)
    depth = DEGREES * 8
    lanes = windows * 2 * NF
    for copy in copies[1:3]:
        copy.wait()

    spot = (lax.broadcasted_iota(jnp.int32, (lanes, LANES), 1) & 7).astype(jnp.float32)

    def make_left(pair):
        top = weight_ref[pl.ds(pl.multiple_of(pair * 16, 16), 8), :]
        bottom = weight_ref[pl.ds(pl.multiple_of(pair * 16 + 8, 8), 8), :]
        sides = [
            jnp.concatenate([top[:, :lanes], bottom[:, :lanes]], axis=1),
            jnp.concatenate([top[:, lanes:], bottom[:, lanes:]], axis=1),
        ]
        per = LANES // 8
        for half in range(DEGREES // per):
            tall = jnp.concatenate(
                [sides[k % 2] * coef_ref[k : k + 1, :] for k in range(half * per, (half + 1) * per)], axis=0
            )
            turned = tall.T
            first = half * LANES
            fine = min(FINE * 8 - first, LANES)
            for which in range(2):
                group = 2 * pair + which
                mask = spot < plan_ref[2, group]
                value = turned[which * lanes : (which + 1) * lanes]
                value = jnp.concatenate([jnp.where(mask, value, 0.0), jnp.where(mask, 0.0, value)], axis=0)
                high, low = split_bf16(value, 2)
                if fine == LANES:
                    parts = [(first, high), (depth + first, high), (2 * FINE * 8 + first + LANES, low)]
                else:
                    mixed = [high[:, :fine].astype(jnp.float32), low[:, :fine].astype(jnp.float32)]
                    parts = [(first, high), (depth + first, jnp.concatenate(mixed, axis=1).astype(jnp.bfloat16))]
                for at, part in parts:
                    left_ref[group, :, at : at + LANES] = part

    used = plan_ref[3, 0].astype(jnp.int32)
    sure = stations // 16
    if sure <= 8:
        for pair in range(sure):
            make_left(pair)
    else:
        lax.fori_loop(0, sure, lambda pair, carry: (make_left(pair), carry)[1], 0)
    lax.fori_loop(sure, (used + 1) // 2, lambda pair, carry: (make_left(pair), carry)[1], 0)
    def basis_steps(group, basis_ref):
        arg = place_ref[pl.ds(pl.multiple_of(group * 8, 8), 8), :]
        twice = arg + arg
        before, now = jnp.ones_like(arg), arg
        for degree in range(0, DEGREES, 2):
            pair = jnp.concatenate([before, now], axis=0)
            terms = split_bf16(pair, 2 if degree < FINE else 1)
            for term, value in enumerate(terms):
                basis_ref[term * depth + degree * 8 : term * depth + degree * 8 + 16, :] = value
            before = twice * now - before
            now = twice * before - now
            if degree % 8 == 6:
                yield

    def run(steps):
        for _ in steps:
            pass

    def add_group(group, basis_ref, steps):
        left = left_ref[group]
        tables = [plan_ref[slot, group].astype(jnp.int32) for slot in range(2)]
        phasor_rows = [pl.ds(pl.multiple_of(table * NF, NF), NF) for table in tables]
        fine = FINE * 8
        for first in range(0, nodes, chunk):
            at = slice(first, first + chunk)
            right = [
                basis_ref[: depth + fine, at],
                basis_ref[LANES:fine, at],
                basis_ref[:LANES, at],
            ]
            got = jnp.dot(left, jnp.concatenate(right, axis=0), preferred_element_type=jnp.float32)
            next(steps, None)
            for win in range(windows):
                row = win * 2 * NF
                real_sum, imag_sum = sums_ref[row : row + NF, at], sums_ref[row + NF : row + 2 * NF, at]
                for slot, rows in enumerate(phasor_rows):
                    cosine, sine = cos_ref[rows, at], sin_ref[rows, at]
                    real = got[slot * lanes + row : slot * lanes + row + NF]
                    imag = got[slot * lanes + row + NF : slot * lanes + row + 2 * NF]
                    real_sum += real * cosine - imag * sine
                    imag_sum += real * sine + imag * cosine
                sums_ref[row : row + NF, at], sums_ref[row + NF : row + 2 * NF, at] = real_sum, imag_sum
        run(steps)

    run(basis_steps(0, basis_a))
    for copy in copies[3:]:
        copy.wait()

    def body(pair, carry):
        group = pair * 2
        add_group(group, basis_a, basis_steps(group + 1, basis_b))
        add_group(group + 1, basis_b, basis_steps(jnp.minimum(group + 2, places // 8 - 1), basis_a))
        return carry

    lax.fori_loop(0, used // 2, body, 0)

    @pl.when(used % 2 == 1)
    def _():
        add_group(used - 1, basis_a, iter(()))

    powers = []
    for win in range(windows):
        row = win * 2 * NF
        real, imag = sums_ref[row : row + NF, :], sums_ref[row + NF : row + 2 * NF, :]
        powers.append(real * real + imag * imag)
    mine = lax.axis_index("win") == 0
    keep_ref[...] = jnp.where(mine, powers[0], powers[1])
    send_ref[...] = jnp.where(mine, powers[1], powers[0])


def finish_kernel(stations, keep_ref, got_ref, spectrum_ref, beam_ref):
    nodes = keep_ref.shape[1]
    win = lax.axis_index("win")
    for place, ref in ((win, keep_ref), (1 - win, got_ref)):
        power = ref[...]
        total = jnp.sum(power, axis=0, keepdims=True)
        at = pl.ds(pl.multiple_of(place * nodes, LANES), nodes)
        spectrum_ref[:, at] = power * (NF / total)
        beam_ref[:, at] = total * (1.0 / (NF * stations))


def on_device(traces, tables, corrections, station_table, node_ids, freq_bins):
    windows, groups, cores = (lax.axis_size(a) for a in ("win", "sta", "freq"))
    stations_dev, grid = corrections.shape
    stations = stations_dev * groups
    devices = windows * groups * cores
    nodes = grid // devices
    ntab = tables.shape[0]
    params = lambda free: pltpu.CompilerParams(vmem_limit_bytes=VMEM_LIMIT - free)
    vmem = pl.BlockSpec(memory_space=pltpu.VMEM)
    hbm = pl.BlockSpec(memory_space=pltpu.HBM)
    bins = freq_bins.reshape(1, NF)
    bins_scratch = pltpu.VMEM((1, NF), jnp.int32)

    holders = windows * cores
    merged = nodes % (holders * LANES) == 0
    pieces = nodes // (holders * LANES) if merged else 0
    height = pieces * stations_dev + 8
    blocks = pl.pallas_call(
        functools.partial(send_kernel, nodes),
        out_shape=jax.ShapeDtypeStruct((devices, height, LANES), jnp.bfloat16),
        in_specs=[hbm] * 3,
        out_specs=vmem,
        scratch_shapes=[
            bins_scratch,
            pltpu.VMEM(traces.shape, traces.dtype),
            pltpu.SemaphoreType.DMA((2 + devices * max(pieces, 1),)),
        ],
        compiler_params=params(0),
        name="send",
    )(bins, traces, corrections)
    received = [lax.all_to_all(blocks, ("win", "sta", "freq"), split_axis=0, concat_axis=0, tiled=True)]
    if not merged:
        parts = corrections.reshape(stations_dev, groups, holders, nodes)
        place = lax.axis_index("freq") * windows + lax.axis_index("win")
        mine = lax.dynamic_index_in_dim(parts, place, axis=2, keepdims=False)
        corr = lax.all_to_all(mine.transpose(1, 0, 2), "sta", split_axis=0, concat_axis=0, tiled=True)
        received.append(corr.reshape(stations, nodes))

    wide = 512
    plan_width = max(LANES, stations)
    phasors = pltpu.VMEM((ntab * NF, nodes), jnp.float32)
    coefs = pltpu.VMEM((DEGREES, LANES), jnp.float32)
    plan = pltpu.VMEM((8, plan_width), jnp.float32)
    packed_shape = (packed_rows(ntab)[-1].stop, max(nodes, plan_width))
    packed = pl.pallas_call(
        prepare_kernel,
        out_shape=jax.ShapeDtypeStruct(packed_shape, jnp.float32),
        in_specs=[hbm] * 4,
        out_specs=hbm,
        scratch_shapes=[
            bins_scratch,
            pltpu.VMEM((1, stations), jnp.int32),
            pltpu.VMEM((max(nodes // LANES, 8), LANES), jnp.int32),
            pltpu.VMEM(tables.shape, tables.dtype),
            phasors,
            phasors,
            coefs,
            plan,
            pltpu.VMEM((grid // wide * ntab, 3 * wide), jnp.bfloat16),
            pltpu.VMEM((3 * wide, nodes), jnp.bfloat16),
            pltpu.SemaphoreType.DMA((3 + 2 * ntab,)),
            pltpu.SemaphoreType.DMA((TABLE_PIECES,)),
        ],
        compiler_params=params(512 * 1024),
        name="prepare",
    )(bins, station_table.reshape(1, stations), node_ids.reshape(grid // LANES, LANES), tables)

    places = (stations // 8 + ntab // 2 + 2) // 2 * 16
    half = jax.ShapeDtypeStruct((NF, nodes), jnp.float32)
    rows = 2 * windows * 2 * NF
    basis = pltpu.VMEM(((DEGREES + FINE) * 8, nodes), jnp.bfloat16)
    keep, send = pl.pallas_call(
        functools.partial(image_kernel, merged, stations_dev),
        out_shape=[half, half],
        in_specs=[hbm] + [vmem] * len(received),
        out_specs=[vmem, vmem],
        scratch_shapes=[
            pltpu.SMEM((8, plan_width), jnp.float32),
            plan,
            coefs,
            phasors,
            phasors,
            pltpu.SemaphoreType.DMA((3 + ntab // 2,)),
            pltpu.VMEM((places, nodes), jnp.float32),
            pltpu.VMEM((places, rows), jnp.float32),
            pltpu.VMEM((places // 8, rows, (DEGREES + 2 * FINE) * 8), jnp.bfloat16),
            pltpu.VMEM((rows // 2, nodes), jnp.float32),
            basis,
            basis,
        ],
        compiler_params=params(23 * 512 * 1024),
        name="image",
    )(packed, *received)
    got = lax.ppermute(send, "win", [(0, 1), (1, 0)])
    spectrum, beam_power = pl.pallas_call(
        functools.partial(finish_kernel, stations),
        out_shape=[
            jax.ShapeDtypeStruct((NF, windows * nodes), jnp.float32),
            jax.ShapeDtypeStruct((1, windows * nodes), jnp.float32),
        ],
        in_specs=[vmem, vmem],
        out_specs=[vmem, vmem],
        compiler_params=params(32 * 1024 * 1024),
        name="finish",
    )(keep, got)
    return spectrum, beam_power.reshape(windows * nodes)


def solution(mesh):
    return jax.shard_map(
        on_device,
        mesh=mesh,
        in_specs=(P(("win", "sta"), "freq"), P(), P("sta", None), P(), P(), P()),
        out_specs=(P("win", ("sta", "freq")), P(("win", "sta", "freq"))),
        check_vma=False,
    )
```

```python
import functools
import math

import jax
import jax.numpy as jnp
import numpy as np
from jax import lax
from jax.experimental import pallas as pl
from jax.experimental.pallas import tpu as pltpu
from jax.sharding import PartitionSpec as P

NT = 5120
NF = 16
NTAB = 16
LANES = 128
DEGREES = 32
FINE = 24
REACH = 1.5
TABLE_PIECES = 4
PARTS = 2
VMEM_LIMIT = 64 * 1024 * 1024 - 64 * 1024


def chebyshev_fit(func, degree, low, high):
    fit = np.polynomial.chebyshev.Chebyshev.interpolate(func, degree, domain=[low, high])
    return [float(v) for v in fit.convert(kind=np.polynomial.Polynomial).coef]


SIN_HALF = chebyshev_fit(lambda z: np.pi * np.sinc(np.sqrt(z)), 4, 0.0, 0.25)
COS_HALF = chebyshev_fit(lambda z: np.cos(np.pi * np.sqrt(z)), 4, 0.0, 0.25)


def horner(coefs, arg):
    total = coefs[-1]
    for coef in coefs[-2::-1]:
        total = total * arg + coef
    return total


def turn_parts(rest):
    square = rest * rest
    root = math.sqrt(2.0)
    sine_half = rest * horner([root * c for c in SIN_HALF], square)
    cos_half = horner([root * c for c in COS_HALF], square)
    return sine_half * sine_half, sine_half * cos_half


def cos_sin(turns):
    versine, sine = turn_parts(turns - jnp.round(turns))
    return 1.0 - versine, sine


def bins_column(bins_ref):
    rows = lax.broadcasted_iota(jnp.int32, (NF, NF), 0)
    lanes = lax.broadcasted_iota(jnp.int32, (NF, NF), 1)
    square = jnp.broadcast_to(bins_ref[...].astype(jnp.float32), (NF, NF))
    return jnp.sum(jnp.where(rows == lanes, square, 0.0), axis=1, keepdims=True)


def split_bf16(value, terms):
    pieces = []
    for term in range(terms):
        piece = value.astype(jnp.bfloat16)
        pieces.append(piece)
        if term < terms - 1:
            value = value - piece.astype(jnp.float32)
    return pieces


def start_all(copies):
    for copy in copies:
        copy.start()
    return copies


def send_kernel(nodes, bins_hbm, traces_hbm, corr_hbm, out_ref, bins_ref, traces_ref, sems):
    devices, height, _ = out_ref.shape
    stations_dev, half_length = traces_ref.shape
    pieces = (height - 8) // stations_dev
    windows, groups, cores = (lax.axis_size(a) for a in ("win", "sta", "freq"))
    place = lax.axis_index("win") * cores + lax.axis_index("freq")
    small = start_all(
        [
            pltpu.make_async_copy(bins_hbm, bins_ref, sems.at[0]),
            pltpu.make_async_copy(traces_hbm, traces_ref, sems.at[1]),
        ]
    )
    copies = []
    for dev in range(devices):
        win, sta, core = dev // (groups * cores), dev // cores % groups, dev % cores
        first = ((sta * cores + core) * windows + win) * nodes
        for piece in range(pieces):
            at = pl.multiple_of(first + (place * pieces + piece) * LANES, LANES)
            to = out_ref.at[dev, pl.ds(piece * stations_dev, stations_dev), :]
            copies.append(pltpu.make_async_copy(corr_hbm.at[:, pl.ds(at, LANES)], to, sems.at[2]))
    start_all(copies)
    start = lax.axis_index("freq") * half_length
    small[0].wait()
    bins = bins_column(bins_ref)
    pos = (start + lax.broadcasted_iota(jnp.int32, (NF, half_length), 1)).astype(jnp.float32)
    product = bins * pos
    turns = jnp.round(product * (1.0 / NT))
    rest = (product - turns * NT) * (1.0 / NT)
    versine, sine = turn_parts(rest)
    scale = 1.0 / math.sqrt(NT)
    table = jnp.concatenate([(1.0 - versine) * scale, sine * -scale], axis=0)
    both = jnp.concatenate(split_bf16(table, 2), axis=0)
    small[1].wait()
    sums = lax.dot_general(
        both, traces_ref[...], (((1,), (1,)), ((), ())), preferred_element_type=jnp.float32
    )
    sums = (sums[: 2 * NF] + sums[2 * NF :]).T
    terms = [term.astype(jnp.float32) for term in split_bf16(sums, 2)]
    tile = jnp.concatenate([term[at : at + 8] for term in terms for at in range(0, stations_dev, 8)], axis=1)
    tile = tile.astype(jnp.bfloat16)
    for dev in range(devices):
        out_ref[dev, height - 8 :, :] = tile
    if copies:
        filled = out_ref.at[:, pl.ds(0, height - 8), :]
        pltpu.make_async_copy(filled, filled, sems.at[2]).wait()


def own_place():
    windows, cores = lax.axis_size("win"), lax.axis_size("freq")
    return (lax.axis_index("sta") * cores + lax.axis_index("freq")) * windows + lax.axis_index("win")


def pick_columns(ids_ref, tables_ref, table_copies, nodes, left_ref, right_ref):
    ntab, grid = tables_ref.shape
    count = nodes // LANES
    wide = right_ref.shape[0] // 3
    blocks = grid // wide
    ids = ids_ref[pl.ds(own_place() * count % ids_ref.shape[0], count), :]
    ids = jnp.concatenate([ids[at : at + 1] for at in range(count)], axis=1)
    low, high = ids & (wide - 1), ids >> (wide.bit_length() - 1)
    spots = lax.broadcasted_iota(jnp.int32, (wide, nodes), 0)
    ones = jnp.where(spots == low, 1.0, 0.0).astype(jnp.bfloat16)
    for term in range(3):
        right_ref[term * wide : (term + 1) * wide, :] = ones
    found = jnp.zeros((ntab, nodes), jnp.float32)
    step = blocks // len(table_copies)
    for at, copy in enumerate(table_copies):
        copy.wait()
        for block in range(at * step, (at + 1) * step):
            pieces = split_bf16(tables_ref[:, block * wide : (block + 1) * wide], 3)
            left_ref[block * ntab : (block + 1) * ntab, :] = jnp.concatenate(pieces, axis=1)
        rows = left_ref[at * step * ntab : (at + 1) * step * ntab, :]
        picked = jnp.dot(rows, right_ref[...], preferred_element_type=jnp.float32)
        for block in range(step):
            part = picked[block * ntab : (block + 1) * ntab]
            found = jnp.where(high == at * step + block, part, found)
    return found


def chebyshev_coefs(bins_ref):
    shape = (DEGREES, DEGREES)
    degree = lax.broadcasted_iota(jnp.int32, shape, 0)
    node = lax.broadcasted_iota(jnp.int32, shape, 1)
    period = 4 * DEGREES
    weight, _ = cos_sin((degree * (2 * node + 1) & (period - 1)).astype(jnp.float32) * (1.0 / period))
    weight = weight * jnp.where(degree == 0, 1.0 / DEGREES, 2.0 / DEGREES)
    even = jnp.where(degree % 2 == 0, weight, 0.0)
    odd = jnp.where(degree % 2 == 1, weight, 0.0)
    row = bins_ref[...].astype(jnp.float32)
    bins = jnp.concatenate([row] * (LANES // NF), axis=1)
    at = lax.broadcasted_iota(jnp.int32, (DEGREES, LANES), 0).astype(jnp.float32)
    spot, _ = cos_sin((2.0 * at + 1.0) * (1.0 / period))
    cosine, sine = cos_sin(bins * (spot * (REACH / 256.0)))
    dot = functools.partial(jnp.dot, precision=lax.Precision.HIGHEST, preferred_element_type=jnp.float32)
    return dot(even, cosine) + dot(odd, sine)


def station_plan(table_row, width):
    count = table_row.shape[1]
    shape = (count, count)
    here = lax.broadcasted_iota(jnp.int32, shape, 0)
    there = lax.broadcasted_iota(jnp.int32, shape, 1)
    column_of = lambda row: jnp.sum(jnp.where(here == there, jnp.broadcast_to(row, shape), 0), axis=1, keepdims=True)
    table_column = column_of(table_row)
    same = (table_column == table_row) & (here < there)
    within = jnp.sum(jnp.where(same, 1, 0), axis=0, keepdims=True)
    place_row = within
    spot = jnp.zeros((1, 1), jnp.int32)
    held = jnp.zeros((1, 1), jnp.int32)
    for table in range(NTAB):
        size = jnp.sum(jnp.where(table_row == table, 1, 0), axis=1, keepdims=True)
        some = size > 0
        edge = (spot & 7) == 0
        skip = some & (held >= 2) & ~edge
        spot = jnp.where(skip, (spot + 7) >> 3 << 3, spot)
        held = jnp.where(skip | edge, 0, held)
        after = spot + size
        place_row = place_row + jnp.where(table_row == table, spot, 0)
        held = jnp.where(some, jnp.where(after >> 3 == spot >> 3, held + 1, 1), held)
        spot = after
    groups = (spot + 7) >> 3
    place_column = column_of(place_row)
    group = lax.broadcasted_iota(jnp.int32, (count, width), 1)
    inside = place_column >> 3 == group
    first = jnp.sum(jnp.where(place_column == group * 8, table_column, 0), axis=0, keepdims=True)
    last = jnp.max(jnp.where(inside, table_column, 0), axis=0, keepdims=True)
    length = jnp.sum(jnp.where(inside & (table_column == first), 1, 0), axis=0, keepdims=True)
    rows = [first, last, length, jnp.broadcast_to(groups, (1, width))]
    if width > count:
        place_row = jnp.concatenate([place_row, jnp.zeros((1, width - count), jnp.int32)], axis=1)
    rows += [place_row, jnp.zeros((3, width), jnp.int32)]
    return jnp.concatenate(rows, axis=0).astype(jnp.float32)


def packed_rows(ntab):
    ends = [ntab * NF, 2 * ntab * NF, 2 * ntab * NF + DEGREES, 2 * ntab * NF + DEGREES + 8]
    return [slice(start, end) for start, end in zip([0] + ends, ends)]


def prepare_kernel(bins_hbm, table_hbm, ids_hbm, tables_hbm, out_hbm, *rest):
    bins_ref, table_ref, ids_ref, tables_ref, cos_ref, sin_ref, coef_ref, plan_ref = rest[:8]
    left_ref, right_ref, sems, table_sems = rest[8:]
    ntab = tables_ref.shape[0]
    nodes = cos_ref.shape[1]
    near = ids_ref.shape[0]
    first = pl.multiple_of(own_place() * (nodes // LANES) // near * near, 8)
    ins = start_all(
        [
            pltpu.make_async_copy(ids_hbm.at[pl.ds(first, near), :], ids_ref, sems.at[0]),
            pltpu.make_async_copy(bins_hbm, bins_ref, sems.at[1]),
            pltpu.make_async_copy(table_hbm, table_ref, sems.at[2]),
        ]
    )
    piece = tables_ref.shape[1] // TABLE_PIECES
    table_copies = []
    for at in range(TABLE_PIECES):
        part = (slice(None), pl.ds(at * piece, piece))
        table_copies.append(pltpu.make_async_copy(tables_hbm.at[part], tables_ref.at[part], table_sems.at[at]))
    start_all(table_copies)
    for copy in ins:
        copy.wait()
    cos_at, sin_at, coef_at, plan_at = packed_rows(ntab)
    coef_ref[...] = chebyshev_coefs(bins_ref)
    plan_ref[...] = station_plan(table_ref[...], plan_ref.shape[1])
    outs = start_all(
        [
            pltpu.make_async_copy(coef_ref, out_hbm.at[coef_at, pl.ds(0, LANES)], sems.at[0]),
            pltpu.make_async_copy(plan_ref, out_hbm.at[plan_at, pl.ds(0, plan_ref.shape[1])], sems.at[1]),
        ]
    )
    turns = pick_columns(ids_ref, tables_ref, table_copies, nodes, left_ref, right_ref) * (1.0 / 256.0)
    bins = bins_column(bins_ref)
    for table in range(ntab):
        cosine, sine = cos_sin(bins * turns[table : table + 1])
        at = pl.ds(table * NF, NF)
        cos_ref[at, :] = cosine
        sin_ref[at, :] = sine
        outs += start_all(
            [
                pltpu.make_async_copy(
                    cos_ref.at[at, :], out_hbm.at[pl.ds(cos_at.start + table * NF, NF), pl.ds(0, nodes)],
                    sems.at[3 + 2 * table],
                ),
                pltpu.make_async_copy(
                    sin_ref.at[at, :], out_hbm.at[pl.ds(sin_at.start + table * NF, NF), pl.ds(0, nodes)],
                    sems.at[4 + 2 * table],
                ),
            ]
        )
    for copy in outs:
        copy.wait()


def image_kernel(merged, stations_dev, packed_hbm, block_ref, *rest):
    corr_ref, rest = (None, rest) if merged else (rest[0], rest[1:])
    keep_ref, *send_refs = rest[: 1 + PARTS]
    plan_ref, place_of_ref, coef_ref, cos_ref, sin_ref, sems = rest[1 + PARTS : 7 + PARTS]
    place_ref, weight_ref, left_ref, sums_ref, basis_a, basis_b = rest[7 + PARTS :]
    places, nodes = place_ref.shape
    windows, groups, cores = (lax.axis_size(a) for a in ("win", "sta", "freq"))
    stations = stations_dev * groups
    cos_at, sin_at, coef_at, plan_at = packed_rows(cos_ref.shape[0] // NF)
    width = plan_ref.shape[1]
    copies = start_all(
        [
            pltpu.make_async_copy(packed_hbm.at[plan_at, pl.ds(0, width)], place_of_ref, sems.at[0]),
            pltpu.make_async_copy(packed_hbm.at[plan_at, pl.ds(0, width)], plan_ref, sems.at[1]),
            pltpu.make_async_copy(packed_hbm.at[coef_at, pl.ds(0, LANES)], coef_ref, sems.at[2]),
        ]
        + [
            pltpu.make_async_copy(
                packed_hbm.at[pl.ds(at.start + first, 4 * NF), pl.ds(0, nodes)],
                ref.at[pl.ds(first, 4 * NF), :],
                sems.at[3 + 2 * (first // (4 * NF)) + which],
            )
            for first in range(0, NTAB * NF, 4 * NF)
            for which, (at, ref) in enumerate(((cos_at, cos_ref), (sin_at, sin_ref)))
        ]
    )
    height = block_ref.shape[1]
    rows_of = lambda win, core: [(win * groups + group) * cores + core for group in range(groups)]

    even, odd = [], []
    for win in range(windows):
        value = []
        for group in range(groups):
            tile = None
            for core in range(cores):
                part = block_ref[(win * groups + group) * cores + core, height - 8 :, :].astype(jnp.float32)
                tile = part if tile is None else tile + part
            tile = tile[:, : LANES // 2] + tile[:, LANES // 2 :]
            value += [tile[:, 2 * NF * piece : 2 * NF * (piece + 1)] for piece in range(stations_dev // 8)]
        value = jnp.concatenate(value, axis=0)
        even.append(value)
        odd.append(jnp.concatenate([-value[:, NF:], value[:, :NF]], axis=1))
    spectra = jnp.concatenate(even + odd, axis=1)
    if merged:
        parts = []
        for win in range(windows):
            for core in range(cores):
                for first in range(0, height - 8, stations_dev):
                    rows = [block_ref[at, first : first + stations_dev, :] for at in rows_of(win, core)]
                    parts.append(jnp.concatenate(rows, axis=0))
        corr = jnp.concatenate(parts, axis=1)
    else:
        corr = corr_ref[...]

    copies[0].wait()
    place_row = place_of_ref[4:5, :stations].astype(jnp.int32)
    sorter = lax.broadcasted_iota(jnp.int32, (places, stations), 0) == place_row
    sorter = jnp.where(sorter, 1.0, 0.0).astype(jnp.bfloat16)
    found = None
    for piece in split_bf16(spectra, 3):
        part = jnp.dot(sorter, piece, preferred_element_type=jnp.float32)
        found = part if found is None else found + part
    weight_ref[...] = found
    place_ref[...] = jnp.dot(sorter, corr, preferred_element_type=jnp.float32) * (1.0 / REACH)
    sums_ref[...] = jnp.zeros_like(sums_ref)
    chunk = min(256, nodes)
    depth = DEGREES * 8
    lanes = windows * 2 * NF
    for copy in copies[1:3]:
        copy.wait()

    spot = (lax.broadcasted_iota(jnp.int32, (lanes, LANES), 1) & 7).astype(jnp.float32)

    def make_left(pair):
        top = weight_ref[pl.ds(pl.multiple_of(pair * 16, 16), 8), :]
        bottom = weight_ref[pl.ds(pl.multiple_of(pair * 16 + 8, 8), 8), :]
        sides = [
            jnp.concatenate([top[:, :lanes], bottom[:, :lanes]], axis=1),
            jnp.concatenate([top[:, lanes:], bottom[:, lanes:]], axis=1),
        ]
        per = LANES // 8
        for half in range(DEGREES // per):
            tall = jnp.concatenate(
                [sides[k % 2] * coef_ref[k : k + 1, :] for k in range(half * per, (half + 1) * per)], axis=0
            )
            turned = tall.T
            first = half * LANES
            fine = min(FINE * 8 - first, LANES)
            for which in range(2):
                group = 2 * pair + which
                mask = spot < plan_ref[2, group]
                value = turned[which * lanes : (which + 1) * lanes]
                value = jnp.concatenate([jnp.where(mask, value, 0.0), jnp.where(mask, 0.0, value)], axis=0)
                high, low = split_bf16(value, 2)
                if fine == LANES:
                    parts = [(first, high), (depth + first, high), (2 * FINE * 8 + first + LANES, low)]
                else:
                    mixed = [high[:, :fine].astype(jnp.float32), low[:, :fine].astype(jnp.float32)]
                    parts = [(first, high), (depth + first, jnp.concatenate(mixed, axis=1).astype(jnp.bfloat16))]
                for at, part in parts:
                    left_ref[group, :, at : at + LANES] = part

    used = plan_ref[3, 0].astype(jnp.int32)
    sure = stations // 16
    if sure <= 8:
        for pair in range(sure):
            make_left(pair)
    else:
        lax.fori_loop(0, sure, lambda pair, carry: (make_left(pair), carry)[1], 0)
    lax.fori_loop(sure, (used + 1) // 2, lambda pair, carry: (make_left(pair), carry)[1], 0)
    def basis_steps(group, basis_ref):
        arg = place_ref[pl.ds(pl.multiple_of(group * 8, 8), 8), :]
        twice = arg + arg
        before, now = jnp.ones_like(arg), arg
        for degree in range(0, DEGREES, 2):
            pair = jnp.concatenate([before, now], axis=0)
            terms = split_bf16(pair, 2 if degree < FINE else 1)
            for term, value in enumerate(terms):
                basis_ref[term * depth + degree * 8 : term * depth + degree * 8 + 16, :] = value
            before = twice * now - before
            now = twice * before - now
            if degree % 8 == 6:
                yield

    def run(steps):
        for _ in steps:
            pass

    def add_group(group, basis_ref, steps):
        left = left_ref[group]
        tables = [plan_ref[slot, group].astype(jnp.int32) for slot in range(2)]
        phasor_rows = [pl.ds(pl.multiple_of(table * NF, NF), NF) for table in tables]
        fine = FINE * 8
        for first in range(0, nodes, chunk):
            at = slice(first, first + chunk)
            right = [
                basis_ref[: depth + fine, at],
                basis_ref[LANES:fine, at],
                basis_ref[:LANES, at],
            ]
            got = jnp.dot(left, jnp.concatenate(right, axis=0), preferred_element_type=jnp.float32)
            next(steps, None)
            for win in range(windows):
                row = win * 2 * NF
                real_sum, imag_sum = sums_ref[row : row + NF, at], sums_ref[row + NF : row + 2 * NF, at]
                for slot, rows in enumerate(phasor_rows):
                    cosine, sine = cos_ref[rows, at], sin_ref[rows, at]
                    real = got[slot * lanes + row : slot * lanes + row + NF]
                    imag = got[slot * lanes + row + NF : slot * lanes + row + 2 * NF]
                    real_sum += real * cosine - imag * sine
                    imag_sum += real * sine + imag * cosine
                sums_ref[row : row + NF, at], sums_ref[row + NF : row + 2 * NF, at] = real_sum, imag_sum
        run(steps)

    run(basis_steps(0, basis_a))
    for copy in copies[3:]:
        copy.wait()

    def body(pair, carry):
        group = pair * 2
        add_group(group, basis_a, basis_steps(group + 1, basis_b))
        add_group(group + 1, basis_b, basis_steps(jnp.minimum(group + 2, places // 8 - 1), basis_a))
        return carry

    lax.fori_loop(0, used // 2, body, 0)

    @pl.when(used % 2 == 1)
    def _():
        add_group(used - 1, basis_a, iter(()))

    powers = []
    for win in range(windows):
        row = win * 2 * NF
        real, imag = sums_ref[row : row + NF, :], sums_ref[row + NF : row + 2 * NF, :]
        powers.append(real * real + imag * imag)
    mine = lax.axis_index("win") == 0
    keep_ref[...] = jnp.where(mine, powers[0], powers[1])
    other = jnp.where(mine, powers[1], powers[0])
    for at, ref in enumerate(send_refs):
        ref[...] = other[at * ref.shape[0] : (at + 1) * ref.shape[0]]


def finish_kernel(stations, keep_ref, *rest):
    *got_refs, spectrum_ref, beam_ref = rest
    nodes = keep_ref.shape[1]
    win = lax.axis_index("win")
    for place, refs in ((win, [keep_ref]), (1 - win, got_refs)):
        power = jnp.concatenate([ref[...] for ref in refs], axis=0)
        total = jnp.sum(power, axis=0, keepdims=True)
        at = pl.ds(pl.multiple_of(place * nodes, LANES), nodes)
        spectrum_ref[:, at] = power * (NF / total)
        beam_ref[:, at] = total * (1.0 / (NF * stations))


def on_device(traces, tables, corrections, station_table, node_ids, freq_bins):
    windows, groups, cores = (lax.axis_size(a) for a in ("win", "sta", "freq"))
    stations_dev, grid = corrections.shape
    stations = stations_dev * groups
    devices = windows * groups * cores
    nodes = grid // devices
    ntab = tables.shape[0]
    params = lambda free: pltpu.CompilerParams(vmem_limit_bytes=VMEM_LIMIT - free)
    vmem = pl.BlockSpec(memory_space=pltpu.VMEM)
    hbm = pl.BlockSpec(memory_space=pltpu.HBM)
    bins = freq_bins.reshape(1, NF)
    bins_scratch = pltpu.VMEM((1, NF), jnp.int32)

    holders = windows * cores
    merged = nodes % (holders * LANES) == 0
    pieces = nodes // (holders * LANES) if merged else 0
    height = pieces * stations_dev + 8
    blocks = pl.pallas_call(
        functools.partial(send_kernel, nodes),
        out_shape=jax.ShapeDtypeStruct((devices, height, LANES), jnp.bfloat16),
        in_specs=[hbm] * 3,
        out_specs=vmem,
        scratch_shapes=[
            bins_scratch,
            pltpu.VMEM(traces.shape, traces.dtype),
            pltpu.SemaphoreType.DMA((3,)),
        ],
        compiler_params=params(0),
        name="send",
    )(bins, traces, corrections)
    received = [lax.all_to_all(blocks, ("win", "sta", "freq"), split_axis=0, concat_axis=0, tiled=True)]
    if not merged:
        parts = corrections.reshape(stations_dev, groups, holders, nodes)
        place = lax.axis_index("freq") * windows + lax.axis_index("win")
        mine = lax.dynamic_index_in_dim(parts, place, axis=2, keepdims=False)
        corr = lax.all_to_all(mine.transpose(1, 0, 2), "sta", split_axis=0, concat_axis=0, tiled=True)
        received.append(corr.reshape(stations, nodes))

    wide = 512
    plan_width = max(LANES, stations)
    phasors = pltpu.VMEM((ntab * NF, nodes), jnp.float32)
    coefs = pltpu.VMEM((DEGREES, LANES), jnp.float32)
    plan = pltpu.VMEM((8, plan_width), jnp.float32)
    packed_shape = (packed_rows(ntab)[-1].stop, max(nodes, plan_width))
    packed = pl.pallas_call(
        prepare_kernel,
        out_shape=jax.ShapeDtypeStruct(packed_shape, jnp.float32),
        in_specs=[hbm] * 4,
        out_specs=hbm,
        scratch_shapes=[
            bins_scratch,
            pltpu.VMEM((1, stations), jnp.int32),
            pltpu.VMEM((max(nodes // LANES, 8), LANES), jnp.int32),
            pltpu.VMEM(tables.shape, tables.dtype),
            phasors,
            phasors,
            coefs,
            plan,
            pltpu.VMEM((grid // wide * ntab, 3 * wide), jnp.bfloat16),
            pltpu.VMEM((3 * wide, nodes), jnp.bfloat16),
            pltpu.SemaphoreType.DMA((3 + 2 * ntab,)),
            pltpu.SemaphoreType.DMA((TABLE_PIECES,)),
        ],
        compiler_params=params(512 * 1024),
        name="prepare",
    )(bins, station_table.reshape(1, stations), node_ids.reshape(grid // LANES, LANES), tables)

    places = (stations // 8 + ntab // 2 + 2) // 2 * 16
    half = jax.ShapeDtypeStruct((NF, nodes), jnp.float32)
    rows = 2 * windows * 2 * NF
    basis = pltpu.VMEM(((DEGREES + FINE) * 8, nodes), jnp.bfloat16)
    part = jax.ShapeDtypeStruct((NF // PARTS, nodes), jnp.float32)
    keep, *sends = pl.pallas_call(
        functools.partial(image_kernel, merged, stations_dev),
        out_shape=[half] + [part] * PARTS,
        in_specs=[hbm] + [vmem] * len(received),
        out_specs=[vmem] * (1 + PARTS),
        scratch_shapes=[
            pltpu.SMEM((8, plan_width), jnp.float32),
            plan,
            coefs,
            phasors,
            phasors,
            pltpu.SemaphoreType.DMA((3 + ntab // 2,)),
            pltpu.VMEM((places, nodes), jnp.float32),
            pltpu.VMEM((places, rows), jnp.float32),
            pltpu.VMEM((places // 8, rows, (DEGREES + 2 * FINE) * 8), jnp.bfloat16),
            pltpu.VMEM((rows // 2, nodes), jnp.float32),
            basis,
            basis,
        ],
        compiler_params=params(23 * 512 * 1024),
        name="image",
    )(packed, *received)
    got = [lax.ppermute(send, "win", [(0, 1), (1, 0)]) for send in sends]
    spectrum, beam_power = pl.pallas_call(
        functools.partial(finish_kernel, stations),
        out_shape=[
            jax.ShapeDtypeStruct((NF, windows * nodes), jnp.float32),
            jax.ShapeDtypeStruct((1, windows * nodes), jnp.float32),
        ],
        in_specs=[vmem] * (1 + PARTS),
        out_specs=[vmem, vmem],
        compiler_params=params(32 * 1024 * 1024),
        name="finish",
    )(keep, *got)
    return spectrum, beam_power.reshape(windows * nodes)


def solution(mesh):
    return jax.shard_map(
        on_device,
        mesh=mesh,
        in_specs=(P(("win", "sta"), "freq"), P(), P("sta", None), P(), P(), P()),
        out_specs=(P("win", ("sta", "freq")), P(("win", "sta", "freq"))),
        check_vma=False,
    )
```

```python
import functools
import math

import jax
import jax.numpy as jnp
import numpy as np
from jax import lax
from jax.experimental import pallas as pl
from jax.experimental.pallas import tpu as pltpu
from jax.sharding import PartitionSpec as P

NT = 5120
NF = 16
NTAB = 16
LANES = 128
DEGREES = 32
FINE = 24
REACH = 1.5
TABLE_PIECES = 4
PARTS = 1
VMEM_LIMIT = 64 * 1024 * 1024 - 64 * 1024


def chebyshev_fit(func, degree, low, high):
    fit = np.polynomial.chebyshev.Chebyshev.interpolate(func, degree, domain=[low, high])
    return [float(v) for v in fit.convert(kind=np.polynomial.Polynomial).coef]


SIN_HALF = chebyshev_fit(lambda z: np.pi * np.sinc(np.sqrt(z)), 4, 0.0, 0.25)
COS_HALF = chebyshev_fit(lambda z: np.cos(np.pi * np.sqrt(z)), 4, 0.0, 0.25)


def horner(coefs, arg):
    total = coefs[-1]
    for coef in coefs[-2::-1]:
        total = total * arg + coef
    return total


def turn_parts(rest):
    square = rest * rest
    root = math.sqrt(2.0)
    sine_half = rest * horner([root * c for c in SIN_HALF], square)
    cos_half = horner([root * c for c in COS_HALF], square)
    return sine_half * sine_half, sine_half * cos_half


def cos_sin(turns):
    versine, sine = turn_parts(turns - jnp.round(turns))
    return 1.0 - versine, sine


def bins_column(bins_ref):
    rows = lax.broadcasted_iota(jnp.int32, (NF, NF), 0)
    lanes = lax.broadcasted_iota(jnp.int32, (NF, NF), 1)
    square = jnp.broadcast_to(bins_ref[...].astype(jnp.float32), (NF, NF))
    return jnp.sum(jnp.where(rows == lanes, square, 0.0), axis=1, keepdims=True)


def split_bf16(value, terms):
    pieces = []
    for term in range(terms):
        piece = value.astype(jnp.bfloat16)
        pieces.append(piece)
        if term < terms - 1:
            value = value - piece.astype(jnp.float32)
    return pieces


def start_all(copies):
    for copy in copies:
        copy.start()
    return copies


def send_kernel(nodes, bins_hbm, traces_hbm, corr_hbm, out_ref, bins_ref, traces_ref, sems):
    devices, height, _ = out_ref.shape
    stations_dev, half_length = traces_ref.shape
    pieces = (height - 8) // stations_dev
    windows, groups, cores = (lax.axis_size(a) for a in ("win", "sta", "freq"))
    place = lax.axis_index("win") * cores + lax.axis_index("freq")
    small = start_all(
        [
            pltpu.make_async_copy(bins_hbm, bins_ref, sems.at[0]),
            pltpu.make_async_copy(traces_hbm, traces_ref, sems.at[1]),
        ]
    )
    copies = []
    for dev in range(devices):
        win, sta, core = dev // (groups * cores), dev // cores % groups, dev % cores
        first = ((sta * cores + core) * windows + win) * nodes
        for piece in range(pieces):
            at = pl.multiple_of(first + (place * pieces + piece) * LANES, LANES)
            to = out_ref.at[dev, pl.ds(piece * stations_dev, stations_dev), :]
            copies.append(pltpu.make_async_copy(corr_hbm.at[:, pl.ds(at, LANES)], to, sems.at[2]))
    start_all(copies)
    start = lax.axis_index("freq") * half_length
    small[0].wait()
    bins = bins_column(bins_ref)
    pos = (start + lax.broadcasted_iota(jnp.int32, (NF, half_length), 1)).astype(jnp.float32)
    product = bins * pos
    turns = jnp.round(product * (1.0 / NT))
    rest = (product - turns * NT) * (1.0 / NT)
    versine, sine = turn_parts(rest)
    scale = 1.0 / math.sqrt(NT)
    table = jnp.concatenate([(1.0 - versine) * scale, sine * -scale], axis=0)
    both = jnp.concatenate(split_bf16(table, 2), axis=0)
    small[1].wait()
    sums = lax.dot_general(
        both, traces_ref[...], (((1,), (1,)), ((), ())), preferred_element_type=jnp.float32
    )
    sums = (sums[: 2 * NF] + sums[2 * NF :]).T
    terms = [term.astype(jnp.float32) for term in split_bf16(sums, 2)]
    tile = jnp.concatenate([term[at : at + 8] for term in terms for at in range(0, stations_dev, 8)], axis=1)
    tile = tile.astype(jnp.bfloat16)
    for dev in range(devices):
        out_ref[dev, height - 8 :, :] = tile
    if copies:
        filled = out_ref.at[:, pl.ds(0, height - 8), :]
        pltpu.make_async_copy(filled, filled, sems.at[2]).wait()


def own_place():
    windows, cores = lax.axis_size("win"), lax.axis_size("freq")
    return (lax.axis_index("sta") * cores + lax.axis_index("freq")) * windows + lax.axis_index("win")


def pick_columns(ids_ref, tables_ref, table_copies, nodes, left_ref, right_ref):
    ntab, grid = tables_ref.shape
    count = nodes // LANES
    wide = right_ref.shape[0] // 3
    blocks = grid // wide
    ids = ids_ref[pl.ds(own_place() * count % ids_ref.shape[0], count), :]
    ids = jnp.concatenate([ids[at : at + 1] for at in range(count)], axis=1)
    low, high = ids & (wide - 1), ids >> (wide.bit_length() - 1)
    spots = lax.broadcasted_iota(jnp.int32, (wide, nodes), 0)
    ones = jnp.where(spots == low, 1.0, 0.0).astype(jnp.bfloat16)
    for term in range(3):
        right_ref[term * wide : (term + 1) * wide, :] = ones
    found = jnp.zeros((ntab, nodes), jnp.float32)
    step = blocks // len(table_copies)
    for at, copy in enumerate(table_copies):
        copy.wait()
        for block in range(at * step, (at + 1) * step):
            pieces = split_bf16(tables_ref[:, block * wide : (block + 1) * wide], 3)
            left_ref[block * ntab : (block + 1) * ntab, :] = jnp.concatenate(pieces, axis=1)
        rows = left_ref[at * step * ntab : (at + 1) * step * ntab, :]
        picked = jnp.dot(rows, right_ref[...], preferred_element_type=jnp.float32)
        for block in range(step):
            part = picked[block * ntab : (block + 1) * ntab]
            found = jnp.where(high == at * step + block, part, found)
    return found


def chebyshev_coefs(bins_ref):
    shape = (DEGREES, DEGREES)
    degree = lax.broadcasted_iota(jnp.int32, shape, 0)
    node = lax.broadcasted_iota(jnp.int32, shape, 1)
    period = 4 * DEGREES
    weight, _ = cos_sin((degree * (2 * node + 1) & (period - 1)).astype(jnp.float32) * (1.0 / period))
    weight = weight * jnp.where(degree == 0, 1.0 / DEGREES, 2.0 / DEGREES)
    even = jnp.where(degree % 2 == 0, weight, 0.0)
    odd = jnp.where(degree % 2 == 1, weight, 0.0)
    row = bins_ref[...].astype(jnp.float32)
    bins = jnp.concatenate([row] * (LANES // NF), axis=1)
    at = lax.broadcasted_iota(jnp.int32, (DEGREES, LANES), 0).astype(jnp.float32)
    spot, _ = cos_sin((2.0 * at + 1.0) * (1.0 / period))
    cosine, sine = cos_sin(bins * (spot * (REACH / 256.0)))
    dot = functools.partial(jnp.dot, precision=lax.Precision.HIGHEST, preferred_element_type=jnp.float32)
    return dot(even, cosine) + dot(odd, sine)


def station_plan(table_row, width):
    count = table_row.shape[1]
    shape = (count, count)
    here = lax.broadcasted_iota(jnp.int32, shape, 0)
    there = lax.broadcasted_iota(jnp.int32, shape, 1)
    column_of = lambda row: jnp.sum(jnp.where(here == there, jnp.broadcast_to(row, shape), 0), axis=1, keepdims=True)
    table_column = column_of(table_row)
    same = (table_column == table_row) & (here < there)
    within = jnp.sum(jnp.where(same, 1, 0), axis=0, keepdims=True)
    place_row = within
    spot = jnp.zeros((1, 1), jnp.int32)
    held = jnp.zeros((1, 1), jnp.int32)
    for table in range(NTAB):
        size = jnp.sum(jnp.where(table_row == table, 1, 0), axis=1, keepdims=True)
        some = size > 0
        edge = (spot & 7) == 0
        skip = some & (held >= 2) & ~edge
        spot = jnp.where(skip, (spot + 7) >> 3 << 3, spot)
        held = jnp.where(skip | edge, 0, held)
        after = spot + size
        place_row = place_row + jnp.where(table_row == table, spot, 0)
        held = jnp.where(some, jnp.where(after >> 3 == spot >> 3, held + 1, 1), held)
        spot = after
    groups = (spot + 7) >> 3
    place_column = column_of(place_row)
    group = lax.broadcasted_iota(jnp.int32, (count, width), 1)
    inside = place_column >> 3 == group
    first = jnp.sum(jnp.where(place_column == group * 8, table_column, 0), axis=0, keepdims=True)
    last = jnp.max(jnp.where(inside, table_column, 0), axis=0, keepdims=True)
    length = jnp.sum(jnp.where(inside & (table_column == first), 1, 0), axis=0, keepdims=True)
    rows = [first, last, length, jnp.broadcast_to(groups, (1, width))]
    if width > count:
        place_row = jnp.concatenate([place_row, jnp.zeros((1, width - count), jnp.int32)], axis=1)
    rows += [place_row, jnp.zeros((3, width), jnp.int32)]
    return jnp.concatenate(rows, axis=0).astype(jnp.float32)


def packed_rows(ntab):
    ends = [ntab * NF, 2 * ntab * NF, 2 * ntab * NF + DEGREES, 2 * ntab * NF + DEGREES + 8]
    return [slice(start, end) for start, end in zip([0] + ends, ends)]


def prepare_kernel(bins_hbm, table_hbm, ids_hbm, tables_hbm, out_hbm, *rest):
    bins_ref, table_ref, ids_ref, tables_ref, cos_ref, sin_ref, coef_ref, plan_ref = rest[:8]
    left_ref, right_ref, sems, table_sems = rest[8:]
    ntab = tables_ref.shape[0]
    nodes = cos_ref.shape[1]
    near = ids_ref.shape[0]
    first = pl.multiple_of(own_place() * (nodes // LANES) // near * near, 8)
    ins = start_all(
        [
            pltpu.make_async_copy(ids_hbm.at[pl.ds(first, near), :], ids_ref, sems.at[0]),
            pltpu.make_async_copy(bins_hbm, bins_ref, sems.at[1]),
            pltpu.make_async_copy(table_hbm, table_ref, sems.at[2]),
        ]
    )
    piece = tables_ref.shape[1] // TABLE_PIECES
    table_copies = []
    for at in range(TABLE_PIECES):
        part = (slice(None), pl.ds(at * piece, piece))
        table_copies.append(pltpu.make_async_copy(tables_hbm.at[part], tables_ref.at[part], table_sems.at[at]))
    start_all(table_copies)
    for copy in ins:
        copy.wait()
    cos_at, sin_at, coef_at, plan_at = packed_rows(ntab)
    coef_ref[...] = chebyshev_coefs(bins_ref)
    plan_ref[...] = station_plan(table_ref[...], plan_ref.shape[1])
    outs = start_all(
        [
            pltpu.make_async_copy(coef_ref, out_hbm.at[coef_at, pl.ds(0, LANES)], sems.at[0]),
            pltpu.make_async_copy(plan_ref, out_hbm.at[plan_at, pl.ds(0, plan_ref.shape[1])], sems.at[1]),
        ]
    )
    turns = pick_columns(ids_ref, tables_ref, table_copies, nodes, left_ref, right_ref) * (1.0 / 256.0)
    bins = bins_column(bins_ref)
    for table in range(ntab):
        cosine, sine = cos_sin(bins * turns[table : table + 1])
        at = pl.ds(table * NF, NF)
        cos_ref[at, :] = cosine
        sin_ref[at, :] = sine
        outs += start_all(
            [
                pltpu.make_async_copy(
                    cos_ref.at[at, :], out_hbm.at[pl.ds(cos_at.start + table * NF, NF), pl.ds(0, nodes)],
                    sems.at[3 + 2 * table],
                ),
                pltpu.make_async_copy(
                    sin_ref.at[at, :], out_hbm.at[pl.ds(sin_at.start + table * NF, NF), pl.ds(0, nodes)],
                    sems.at[4 + 2 * table],
                ),
            ]
        )
    for copy in outs:
        copy.wait()


def image_kernel(merged, stations_dev, packed_hbm, block_ref, *rest):
    corr_ref, rest = (None, rest) if merged else (rest[0], rest[1:])
    keep_ref, *send_refs = rest[: 1 + PARTS]
    plan_ref, place_of_ref, coef_ref, cos_ref, sin_ref, sems = rest[1 + PARTS : 7 + PARTS]
    place_ref, weight_ref, left_ref, sums_ref, basis_a, basis_b = rest[7 + PARTS :]
    places, nodes = place_ref.shape
    windows, groups, cores = (lax.axis_size(a) for a in ("win", "sta", "freq"))
    stations = stations_dev * groups
    cos_at, sin_at, coef_at, plan_at = packed_rows(cos_ref.shape[0] // NF)
    width = plan_ref.shape[1]
    copies = start_all(
        [
            pltpu.make_async_copy(packed_hbm.at[plan_at, pl.ds(0, width)], place_of_ref, sems.at[0]),
            pltpu.make_async_copy(packed_hbm.at[plan_at, pl.ds(0, width)], plan_ref, sems.at[1]),
            pltpu.make_async_copy(packed_hbm.at[coef_at, pl.ds(0, LANES)], coef_ref, sems.at[2]),
        ]
        + [
            pltpu.make_async_copy(
                packed_hbm.at[pl.ds(at.start + first, 4 * NF), pl.ds(0, nodes)],
                ref.at[pl.ds(first, 4 * NF), :],
                sems.at[3 + 2 * (first // (4 * NF)) + which],
            )
            for first in range(0, NTAB * NF, 4 * NF)
            for which, (at, ref) in enumerate(((cos_at, cos_ref), (sin_at, sin_ref)))
        ]
    )
    height = block_ref.shape[1]
    rows_of = lambda win, core: [(win * groups + group) * cores + core for group in range(groups)]

    even, odd = [], []
    for win in range(windows):
        value = []
        for group in range(groups):
            tile = None
            for core in range(cores):
                part = block_ref[(win * groups + group) * cores + core, height - 8 :, :].astype(jnp.float32)
                tile = part if tile is None else tile + part
            tile = tile[:, : LANES // 2] + tile[:, LANES // 2 :]
            value += [tile[:, 2 * NF * piece : 2 * NF * (piece + 1)] for piece in range(stations_dev // 8)]
        value = jnp.concatenate(value, axis=0)
        even.append(value)
        odd.append(jnp.concatenate([-value[:, NF:], value[:, :NF]], axis=1))
    spectra = jnp.concatenate(even + odd, axis=1)
    if merged:
        parts = []
        for win in range(windows):
            for core in range(cores):
                for first in range(0, height - 8, stations_dev):
                    rows = [block_ref[at, first : first + stations_dev, :] for at in rows_of(win, core)]
                    parts.append(jnp.concatenate(rows, axis=0))
        corr = jnp.concatenate(parts, axis=1)
    else:
        corr = corr_ref[...]

    copies[0].wait()
    place_row = place_of_ref[4:5, :stations].astype(jnp.int32)
    sorter = lax.broadcasted_iota(jnp.int32, (places, stations), 0) == place_row
    sorter = jnp.where(sorter, 1.0, 0.0).astype(jnp.bfloat16)
    found = None
    for piece in split_bf16(spectra, 3):
        part = jnp.dot(sorter, piece, preferred_element_type=jnp.float32)
        found = part if found is None else found + part
    weight_ref[...] = found
    place_ref[...] = jnp.dot(sorter, corr, preferred_element_type=jnp.float32) * (1.0 / REACH)
    sums_ref[...] = jnp.zeros_like(sums_ref)
    chunk = min(256, nodes)
    depth = DEGREES * 8
    lanes = windows * 2 * NF
    for copy in copies[1:3]:
        copy.wait()

    rows = 2 * lanes
    spot = (lax.broadcasted_iota(jnp.int32, (lanes, LANES), 1) & 7).astype(jnp.float32)

    def make_left(pair):
        top = weight_ref[pl.ds(pl.multiple_of(pair * 16, 16), 8), :]
        bottom = weight_ref[pl.ds(pl.multiple_of(pair * 16 + 8, 8), 8), :]
        sides = [
            jnp.concatenate([top[:, :lanes], bottom[:, :lanes]], axis=1),
            jnp.concatenate([top[:, lanes:], bottom[:, lanes:]], axis=1),
        ]
        per = LANES // 8
        for half in range(DEGREES // per):
            tall = jnp.concatenate(
                [sides[k % 2] * coef_ref[k : k + 1, :] for k in range(half * per, (half + 1) * per)], axis=0
            )
            turned = tall.T
            first = half * LANES
            fine = min(FINE * 8 - first, LANES)
            for which in range(2):
                group = 2 * pair + which
                mask = spot < plan_ref[2, group]
                value = turned[which * lanes : (which + 1) * lanes]
                value = jnp.concatenate([jnp.where(mask, value, 0.0), jnp.where(mask, 0.0, value)], axis=0)
                high, low = split_bf16(value, 2)
                left_ref[group, :rows, first : first + LANES] = high
                left_ref[group, rows:, first : first + LANES] = low
                if fine < LANES:
                    lane = lax.broadcasted_iota(jnp.int32, high.shape, 1)
                    high = jnp.where(lane < fine, high.astype(jnp.float32), 0.0).astype(jnp.bfloat16)
                left_ref[group, :rows, depth + first : depth + first + LANES] = high
                left_ref[group, rows:, depth + first : depth + first + LANES] = jnp.zeros_like(low)

    used = plan_ref[3, 0].astype(jnp.int32)
    sure = stations // 16
    if sure <= 8:
        for pair in range(sure):
            make_left(pair)
    else:
        lax.fori_loop(0, sure, lambda pair, carry: (make_left(pair), carry)[1], 0)
    lax.fori_loop(sure, (used + 1) // 2, lambda pair, carry: (make_left(pair), carry)[1], 0)
    def basis_steps(group, basis_ref):
        arg = place_ref[pl.ds(pl.multiple_of(group * 8, 8), 8), :]
        twice = arg + arg
        before, now = jnp.ones_like(arg), arg
        for degree in range(0, DEGREES, 2):
            pair = jnp.concatenate([before, now], axis=0)
            terms = split_bf16(pair, 2 if degree < FINE else 1)
            for term, value in enumerate(terms):
                basis_ref[term * depth + degree * 8 : term * depth + degree * 8 + 16, :] = value
            before = twice * now - before
            now = twice * before - now
            if degree % 8 == 6:
                yield

    def run(steps):
        for _ in steps:
            pass

    def add_group(group, basis_ref, steps):
        left = left_ref[group]
        tables = [plan_ref[slot, group].astype(jnp.int32) for slot in range(2)]
        phasor_rows = [pl.ds(pl.multiple_of(table * NF, NF), NF) for table in tables]
        for first in range(0, nodes, chunk):
            at = slice(first, first + chunk)
            got = jnp.dot(left, basis_ref[:, at], preferred_element_type=jnp.float32)
            got = got[: 2 * lanes] + got[2 * lanes :]
            next(steps, None)
            for win in range(windows):
                row = win * 2 * NF
                real_sum, imag_sum = sums_ref[row : row + NF, at], sums_ref[row + NF : row + 2 * NF, at]
                for slot, rows in enumerate(phasor_rows):
                    cosine, sine = cos_ref[rows, at], sin_ref[rows, at]
                    real = got[slot * lanes + row : slot * lanes + row + NF]
                    imag = got[slot * lanes + row + NF : slot * lanes + row + 2 * NF]
                    real_sum += real * cosine - imag * sine
                    imag_sum += real * sine + imag * cosine
                sums_ref[row : row + NF, at], sums_ref[row + NF : row + 2 * NF, at] = real_sum, imag_sum
        run(steps)

    for ref in (basis_a, basis_b):
        ref[depth + FINE * 8 :, :] = jnp.zeros((depth - FINE * 8, nodes), jnp.bfloat16)
    run(basis_steps(0, basis_a))
    for copy in copies[3:]:
        copy.wait()

    def body(pair, carry):
        group = pair * 2
        add_group(group, basis_a, basis_steps(group + 1, basis_b))
        add_group(group + 1, basis_b, basis_steps(jnp.minimum(group + 2, places // 8 - 1), basis_a))
        return carry

    lax.fori_loop(0, used // 2, body, 0)

    @pl.when(used % 2 == 1)
    def _():
        add_group(used - 1, basis_a, iter(()))

    powers = []
    for win in range(windows):
        row = win * 2 * NF
        real, imag = sums_ref[row : row + NF, :], sums_ref[row + NF : row + 2 * NF, :]
        powers.append(real * real + imag * imag)
    mine = lax.axis_index("win") == 0
    keep_ref[...] = jnp.where(mine, powers[0], powers[1])
    other = jnp.where(mine, powers[1], powers[0])
    for at, ref in enumerate(send_refs):
        ref[...] = other[at * ref.shape[0] : (at + 1) * ref.shape[0]]


def finish_kernel(stations, keep_ref, *rest):
    *got_refs, spectrum_ref, beam_ref = rest
    nodes = keep_ref.shape[1]
    win = lax.axis_index("win")
    for place, refs in ((win, [keep_ref]), (1 - win, got_refs)):
        power = jnp.concatenate([ref[...] for ref in refs], axis=0)
        total = jnp.sum(power, axis=0, keepdims=True)
        at = pl.ds(pl.multiple_of(place * nodes, LANES), nodes)
        spectrum_ref[:, at] = power * (NF / total)
        beam_ref[:, at] = total * (1.0 / (NF * stations))


def on_device(traces, tables, corrections, station_table, node_ids, freq_bins):
    windows, groups, cores = (lax.axis_size(a) for a in ("win", "sta", "freq"))
    stations_dev, grid = corrections.shape
    stations = stations_dev * groups
    devices = windows * groups * cores
    nodes = grid // devices
    ntab = tables.shape[0]
    params = lambda free: pltpu.CompilerParams(vmem_limit_bytes=VMEM_LIMIT - free)
    vmem = pl.BlockSpec(memory_space=pltpu.VMEM)
    hbm = pl.BlockSpec(memory_space=pltpu.HBM)
    bins = freq_bins.reshape(1, NF)
    bins_scratch = pltpu.VMEM((1, NF), jnp.int32)

    holders = windows * cores
    merged = nodes % (holders * LANES) == 0
    pieces = nodes // (holders * LANES) if merged else 0
    height = pieces * stations_dev + 8
    blocks = pl.pallas_call(
        functools.partial(send_kernel, nodes),
        out_shape=jax.ShapeDtypeStruct((devices, height, LANES), jnp.bfloat16),
        in_specs=[hbm] * 3,
        out_specs=vmem,
        scratch_shapes=[
            bins_scratch,
            pltpu.VMEM(traces.shape, traces.dtype),
            pltpu.SemaphoreType.DMA((3,)),
        ],
        compiler_params=params(0),
        name="send",
    )(bins, traces, corrections)
    received = [lax.all_to_all(blocks, ("win", "sta", "freq"), split_axis=0, concat_axis=0, tiled=True)]
    if not merged:
        parts = corrections.reshape(stations_dev, groups, holders, nodes)
        place = lax.axis_index("freq") * windows + lax.axis_index("win")
        mine = lax.dynamic_index_in_dim(parts, place, axis=2, keepdims=False)
        corr = lax.all_to_all(mine.transpose(1, 0, 2), "sta", split_axis=0, concat_axis=0, tiled=True)
        received.append(corr.reshape(stations, nodes))

    wide = 512
    plan_width = max(LANES, stations)
    phasors = pltpu.VMEM((ntab * NF, nodes), jnp.float32)
    coefs = pltpu.VMEM((DEGREES, LANES), jnp.float32)
    plan = pltpu.VMEM((8, plan_width), jnp.float32)
    packed_shape = (packed_rows(ntab)[-1].stop, max(nodes, plan_width))
    packed = pl.pallas_call(
        prepare_kernel,
        out_shape=jax.ShapeDtypeStruct(packed_shape, jnp.float32),
        in_specs=[hbm] * 4,
        out_specs=hbm,
        scratch_shapes=[
            bins_scratch,
            pltpu.VMEM((1, stations), jnp.int32),
            pltpu.VMEM((max(nodes // LANES, 8), LANES), jnp.int32),
            pltpu.VMEM(tables.shape, tables.dtype),
            phasors,
            phasors,
            coefs,
            plan,
            pltpu.VMEM((grid // wide * ntab, 3 * wide), jnp.bfloat16),
            pltpu.VMEM((3 * wide, nodes), jnp.bfloat16),
            pltpu.SemaphoreType.DMA((3 + 2 * ntab,)),
            pltpu.SemaphoreType.DMA((TABLE_PIECES,)),
        ],
        compiler_params=params(512 * 1024),
        name="prepare",
    )(bins, station_table.reshape(1, stations), node_ids.reshape(grid // LANES, LANES), tables)

    places = (stations // 8 + ntab // 2 + 2) // 2 * 16
    half = jax.ShapeDtypeStruct((NF, nodes), jnp.float32)
    rows = 2 * windows * 2 * NF
    basis = pltpu.VMEM((2 * DEGREES * 8, nodes), jnp.bfloat16)
    part = jax.ShapeDtypeStruct((NF // PARTS, nodes), jnp.float32)
    keep, *sends = pl.pallas_call(
        functools.partial(image_kernel, merged, stations_dev),
        out_shape=[half] + [part] * PARTS,
        in_specs=[hbm] + [vmem] * len(received),
        out_specs=[vmem] * (1 + PARTS),
        scratch_shapes=[
            pltpu.SMEM((8, plan_width), jnp.float32),
            plan,
            coefs,
            phasors,
            phasors,
            pltpu.SemaphoreType.DMA((3 + ntab // 2,)),
            pltpu.VMEM((places, nodes), jnp.float32),
            pltpu.VMEM((places, rows), jnp.float32),
            pltpu.VMEM((places // 8, 2 * rows, 2 * DEGREES * 8), jnp.bfloat16),
            pltpu.VMEM((rows // 2, nodes), jnp.float32),
            basis,
            basis,
        ],
        compiler_params=params(23 * 512 * 1024),
        name="image",
    )(packed, *received)
    got = [lax.ppermute(send, "win", [(0, 1), (1, 0)]) for send in sends]
    spectrum, beam_power = pl.pallas_call(
        functools.partial(finish_kernel, stations),
        out_shape=[
            jax.ShapeDtypeStruct((NF, windows * nodes), jnp.float32),
            jax.ShapeDtypeStruct((1, windows * nodes), jnp.float32),
        ],
        in_specs=[vmem] * (1 + PARTS),
        out_specs=[vmem, vmem],
        compiler_params=params(32 * 1024 * 1024),
        name="finish",
    )(keep, *got)
    return spectrum, beam_power.reshape(windows * nodes)


def solution(mesh):
    return jax.shard_map(
        on_device,
        mesh=mesh,
        in_specs=(P(("win", "sta"), "freq"), P(), P("sta", None), P(), P(), P()),
        out_specs=(P("win", ("sta", "freq")), P(("win", "sta", "freq"))),
        check_vma=False,
    )
```

```python
import functools
import math

import jax
import jax.numpy as jnp
import numpy as np
from jax import lax
from jax.experimental import pallas as pl
from jax.experimental.pallas import tpu as pltpu
from jax.sharding import PartitionSpec as P

NT = 5120
NF = 16
NTAB = 16
LANES = 128
DEGREES = 32
FINE = 24
REACH = 1.5
TABLE_PIECES = 4
ROUNDER = 1.5 * 2.0**15
VMEM_LIMIT = 64 * 1024 * 1024 - 64 * 1024


def chebyshev_fit(func, degree, low, high):
    fit = np.polynomial.chebyshev.Chebyshev.interpolate(func, degree, domain=[low, high])
    return [float(v) for v in fit.convert(kind=np.polynomial.Polynomial).coef]


SIN_HALF = chebyshev_fit(lambda z: np.pi * np.sinc(np.sqrt(z)), 4, 0.0, 0.25)
COS_HALF = chebyshev_fit(lambda z: np.cos(np.pi * np.sqrt(z)), 4, 0.0, 0.25)


def horner(coefs, arg):
    total = coefs[-1]
    for coef in coefs[-2::-1]:
        total = total * arg + coef
    return total


def turn_parts(rest):
    square = rest * rest
    root = math.sqrt(2.0)
    sine_half = rest * horner([root * c for c in SIN_HALF], square)
    cos_half = horner([root * c for c in COS_HALF], square)
    return sine_half * sine_half, sine_half * cos_half


def cos_sin(turns):
    versine, sine = turn_parts(turns - jnp.round(turns))
    return 1.0 - versine, sine


def bins_column(bins_ref):
    rows = lax.broadcasted_iota(jnp.int32, (NF, NF), 0)
    lanes = lax.broadcasted_iota(jnp.int32, (NF, NF), 1)
    square = jnp.broadcast_to(bins_ref[...].astype(jnp.float32), (NF, NF))
    return jnp.sum(jnp.where(rows == lanes, square, 0.0), axis=1, keepdims=True)


def split_bf16(value, terms):
    pieces = []
    for term in range(terms):
        piece = value.astype(jnp.bfloat16)
        pieces.append(piece)
        if term < terms - 1:
            value = value - piece.astype(jnp.float32)
    return pieces


def start_all(copies):
    for copy in copies:
        copy.start()
    return copies


def send_kernel(nodes, bins_hbm, traces_hbm, corr_hbm, out_ref, bins_ref, traces_ref, sems):
    devices, height, _ = out_ref.shape
    stations_dev, half_length = traces_ref.shape
    pieces = (height - 8) // stations_dev
    windows, groups, cores = (lax.axis_size(a) for a in ("win", "sta", "freq"))
    place = lax.axis_index("win") * cores + lax.axis_index("freq")
    small = start_all(
        [
            pltpu.make_async_copy(bins_hbm, bins_ref, sems.at[0]),
            pltpu.make_async_copy(traces_hbm, traces_ref, sems.at[1]),
        ]
    )
    copies = []
    for dev in range(devices):
        win, sta, core = dev // (groups * cores), dev // cores % groups, dev % cores
        first = ((sta * cores + core) * windows + win) * nodes
        for piece in range(pieces):
            at = pl.multiple_of(first + (place * pieces + piece) * LANES, LANES)
            to = out_ref.at[dev, pl.ds(piece * stations_dev, stations_dev), :]
            copies.append(pltpu.make_async_copy(corr_hbm.at[:, pl.ds(at, LANES)], to, sems.at[2]))
    start_all(copies)
    start = lax.axis_index("freq") * half_length
    small[0].wait()
    bins = bins_column(bins_ref)
    pos = (start + lax.broadcasted_iota(jnp.int32, (NF, half_length), 1)).astype(jnp.float32)
    product = bins * pos
    turns = jnp.round(product * (1.0 / NT))
    rest = (product - turns * NT) * (1.0 / NT)
    versine, sine = turn_parts(rest)
    scale = 1.0 / math.sqrt(NT)
    table = jnp.concatenate([(1.0 - versine) * scale, sine * -scale], axis=0)
    both = jnp.concatenate(split_bf16(table, 2), axis=0)
    small[1].wait()
    sums = lax.dot_general(
        both, traces_ref[...], (((1,), (1,)), ((), ())), preferred_element_type=jnp.float32
    )
    sums = (sums[: 2 * NF] + sums[2 * NF :]).T
    terms = [term.astype(jnp.float32) for term in split_bf16(sums, 2)]
    tile = jnp.concatenate([term[at : at + 8] for term in terms for at in range(0, stations_dev, 8)], axis=1)
    tile = tile.astype(jnp.bfloat16)
    for dev in range(devices):
        out_ref[dev, height - 8 :, :] = tile
    if copies:
        filled = out_ref.at[:, pl.ds(0, height - 8), :]
        pltpu.make_async_copy(filled, filled, sems.at[2]).wait()


def own_place():
    windows, cores = lax.axis_size("win"), lax.axis_size("freq")
    return (lax.axis_index("sta") * cores + lax.axis_index("freq")) * windows + lax.axis_index("win")


def pick_columns(ids_ref, tables_ref, table_copies, nodes, left_ref, right_ref):
    ntab, grid = tables_ref.shape
    count = nodes // LANES
    wide = right_ref.shape[0] // 3
    blocks = grid // wide
    ids = ids_ref[pl.ds(own_place() * count % ids_ref.shape[0], count), :]
    ids = jnp.concatenate([ids[at : at + 1] for at in range(count)], axis=1)
    low, high = ids & (wide - 1), ids >> (wide.bit_length() - 1)
    spots = lax.broadcasted_iota(jnp.int32, (wide, nodes), 0)
    ones = jnp.where(spots == low, 1.0, 0.0).astype(jnp.bfloat16)
    for term in range(3):
        right_ref[term * wide : (term + 1) * wide, :] = ones
    found = jnp.zeros((ntab, nodes), jnp.float32)
    step = blocks // len(table_copies)
    for at, copy in enumerate(table_copies):
        copy.wait()
        for block in range(at * step, (at + 1) * step):
            pieces = split_bf16(tables_ref[:, block * wide : (block + 1) * wide], 3)
            left_ref[block * ntab : (block + 1) * ntab, :] = jnp.concatenate(pieces, axis=1)
        rows = left_ref[at * step * ntab : (at + 1) * step * ntab, :]
        picked = jnp.dot(rows, right_ref[...], preferred_element_type=jnp.float32)
        for block in range(step):
            part = picked[block * ntab : (block + 1) * ntab]
            found = jnp.where(high == at * step + block, part, found)
    return found


def chebyshev_coefs(bins_ref):
    shape = (DEGREES, DEGREES)
    degree = lax.broadcasted_iota(jnp.int32, shape, 0)
    node = lax.broadcasted_iota(jnp.int32, shape, 1)
    period = 4 * DEGREES
    weight, _ = cos_sin((degree * (2 * node + 1) & (period - 1)).astype(jnp.float32) * (1.0 / period))
    weight = weight * jnp.where(degree == 0, 1.0 / DEGREES, 2.0 / DEGREES)
    even = jnp.where(degree % 2 == 0, weight, 0.0)
    odd = jnp.where(degree % 2 == 1, weight, 0.0)
    row = bins_ref[...].astype(jnp.float32)
    bins = jnp.concatenate([row] * (LANES // NF), axis=1)
    at = lax.broadcasted_iota(jnp.int32, (DEGREES, LANES), 0).astype(jnp.float32)
    spot, _ = cos_sin((2.0 * at + 1.0) * (1.0 / period))
    cosine, sine = cos_sin(bins * (spot * (REACH / 256.0)))
    dot = functools.partial(jnp.dot, precision=lax.Precision.HIGHEST, preferred_element_type=jnp.float32)
    return dot(even, cosine) + dot(odd, sine)


def station_plan(table_row, width):
    count = table_row.shape[1]
    shape = (count, count)
    here = lax.broadcasted_iota(jnp.int32, shape, 0)
    there = lax.broadcasted_iota(jnp.int32, shape, 1)
    column_of = lambda row: jnp.sum(jnp.where(here == there, jnp.broadcast_to(row, shape), 0), axis=1, keepdims=True)
    table_column = column_of(table_row)
    same = (table_column == table_row) & (here < there)
    within = jnp.sum(jnp.where(same, 1, 0), axis=0, keepdims=True)
    place_row = within
    spot = jnp.zeros((1, 1), jnp.int32)
    held = jnp.zeros((1, 1), jnp.int32)
    for table in range(NTAB):
        size = jnp.sum(jnp.where(table_row == table, 1, 0), axis=1, keepdims=True)
        some = size > 0
        edge = (spot & 7) == 0
        skip = some & (held >= 2) & ~edge
        spot = jnp.where(skip, (spot + 7) >> 3 << 3, spot)
        held = jnp.where(skip | edge, 0, held)
        after = spot + size
        place_row = place_row + jnp.where(table_row == table, spot, 0)
        held = jnp.where(some, jnp.where(after >> 3 == spot >> 3, held + 1, 1), held)
        spot = after
    groups = (spot + 7) >> 3
    place_column = column_of(place_row)
    group = lax.broadcasted_iota(jnp.int32, (count, width), 1)
    inside = place_column >> 3 == group
    first = jnp.sum(jnp.where(place_column == group * 8, table_column, 0), axis=0, keepdims=True)
    last = jnp.max(jnp.where(inside, table_column, 0), axis=0, keepdims=True)
    length = jnp.sum(jnp.where(inside & (table_column == first), 1, 0), axis=0, keepdims=True)
    rows = [first, last, length, jnp.broadcast_to(groups, (1, width))]
    if width > count:
        place_row = jnp.concatenate([place_row, jnp.zeros((1, width - count), jnp.int32)], axis=1)
    rows += [place_row, jnp.zeros((3, width), jnp.int32)]
    return jnp.concatenate(rows, axis=0).astype(jnp.float32)


def packed_rows(ntab):
    ends = [ntab * NF, 2 * ntab * NF, 2 * ntab * NF + DEGREES, 2 * ntab * NF + DEGREES + 8]
    return [slice(start, end) for start, end in zip([0] + ends, ends)]


def prepare_kernel(bins_hbm, table_hbm, ids_hbm, tables_hbm, out_hbm, *rest):
    bins_ref, table_ref, ids_ref, tables_ref, cos_ref, sin_ref, coef_ref, plan_ref = rest[:8]
    left_ref, right_ref, sems, table_sems = rest[8:]
    ntab = tables_ref.shape[0]
    nodes = cos_ref.shape[1]
    near = ids_ref.shape[0]
    first = pl.multiple_of(own_place() * (nodes // LANES) // near * near, 8)
    ins = start_all(
        [
            pltpu.make_async_copy(ids_hbm.at[pl.ds(first, near), :], ids_ref, sems.at[0]),
            pltpu.make_async_copy(bins_hbm, bins_ref, sems.at[1]),
            pltpu.make_async_copy(table_hbm, table_ref, sems.at[2]),
        ]
    )
    piece = tables_ref.shape[1] // TABLE_PIECES
    table_copies = []
    for at in range(TABLE_PIECES):
        part = (slice(None), pl.ds(at * piece, piece))
        table_copies.append(pltpu.make_async_copy(tables_hbm.at[part], tables_ref.at[part], table_sems.at[at]))
    start_all(table_copies)
    for copy in ins:
        copy.wait()
    cos_at, sin_at, coef_at, plan_at = packed_rows(ntab)
    coef_ref[...] = chebyshev_coefs(bins_ref)
    plan_ref[...] = station_plan(table_ref[...], plan_ref.shape[1])
    outs = start_all(
        [
            pltpu.make_async_copy(coef_ref, out_hbm.at[coef_at, pl.ds(0, LANES)], sems.at[0]),
            pltpu.make_async_copy(plan_ref, out_hbm.at[plan_at, pl.ds(0, plan_ref.shape[1])], sems.at[1]),
        ]
    )
    turns = pick_columns(ids_ref, tables_ref, table_copies, nodes, left_ref, right_ref) * (1.0 / 256.0)
    bins = bins_column(bins_ref)
    for table in range(ntab):
        cosine, sine = cos_sin(bins * turns[table : table + 1])
        at = pl.ds(table * NF, NF)
        cos_ref[at, :] = cosine
        sin_ref[at, :] = sine
        outs += start_all(
            [
                pltpu.make_async_copy(
                    cos_ref.at[at, :], out_hbm.at[pl.ds(cos_at.start + table * NF, NF), pl.ds(0, nodes)],
                    sems.at[3 + 2 * table],
                ),
                pltpu.make_async_copy(
                    sin_ref.at[at, :], out_hbm.at[pl.ds(sin_at.start + table * NF, NF), pl.ds(0, nodes)],
                    sems.at[4 + 2 * table],
                ),
            ]
        )
    for copy in outs:
        copy.wait()


def image_kernel(merged, stations_dev, packed_hbm, block_ref, *rest):
    corr_ref, rest = (None, rest) if merged else (rest[0], rest[1:])
    keep_ref, send_ref, plan_ref, place_of_ref, coef_ref, cos_ref, sin_ref, sems = rest[:8]
    place_ref, weight_ref, left_ref, sums_ref, basis_a, basis_b = rest[8:]
    places, nodes = place_ref.shape
    windows, groups, cores = (lax.axis_size(a) for a in ("win", "sta", "freq"))
    stations = stations_dev * groups
    cos_at, sin_at, coef_at, plan_at = packed_rows(cos_ref.shape[0] // NF)
    width = plan_ref.shape[1]
    copies = start_all(
        [
            pltpu.make_async_copy(packed_hbm.at[plan_at, pl.ds(0, width)], place_of_ref, sems.at[0]),
            pltpu.make_async_copy(packed_hbm.at[plan_at, pl.ds(0, width)], plan_ref, sems.at[1]),
            pltpu.make_async_copy(packed_hbm.at[coef_at, pl.ds(0, LANES)], coef_ref, sems.at[2]),
        ]
        + [
            pltpu.make_async_copy(
                packed_hbm.at[pl.ds(at.start + first, 4 * NF), pl.ds(0, nodes)],
                ref.at[pl.ds(first, 4 * NF), :],
                sems.at[3 + 2 * (first // (4 * NF)) + which],
            )
            for first in range(0, NTAB * NF, 4 * NF)
            for which, (at, ref) in enumerate(((cos_at, cos_ref), (sin_at, sin_ref)))
        ]
    )
    height = block_ref.shape[1]
    rows_of = lambda win, core: [(win * groups + group) * cores + core for group in range(groups)]

    even, odd = [], []
    for win in range(windows):
        value = []
        for group in range(groups):
            tile = None
            for core in range(cores):
                part = block_ref[(win * groups + group) * cores + core, height - 8 :, :].astype(jnp.float32)
                tile = part if tile is None else tile + part
            tile = tile[:, : LANES // 2] + tile[:, LANES // 2 :]
            value += [tile[:, 2 * NF * piece : 2 * NF * (piece + 1)] for piece in range(stations_dev // 8)]
        value = jnp.concatenate(value, axis=0)
        even.append(value)
        odd.append(jnp.concatenate([-value[:, NF:], value[:, :NF]], axis=1))
    spectra = jnp.concatenate(even + odd, axis=1)
    if merged:
        parts = []
        for win in range(windows):
            for core in range(cores):
                for first in range(0, height - 8, stations_dev):
                    rows = [block_ref[at, first : first + stations_dev, :] for at in rows_of(win, core)]
                    parts.append(jnp.concatenate(rows, axis=0))
        corr = jnp.concatenate(parts, axis=1)
    else:
        corr = corr_ref[...]

    copies[0].wait()
    place_row = place_of_ref[4:5, :stations].astype(jnp.int32)
    sorter = lax.broadcasted_iota(jnp.int32, (places, stations), 0) == place_row
    sorter = jnp.where(sorter, 1.0, 0.0).astype(jnp.bfloat16)
    found = None
    for piece in split_bf16(spectra, 3):
        part = jnp.dot(sorter, piece, preferred_element_type=jnp.float32)
        found = part if found is None else found + part
    weight_ref[...] = found
    place_ref[...] = jnp.dot(sorter, corr, preferred_element_type=jnp.float32) * (1.0 / REACH)
    sums_ref[...] = jnp.zeros_like(sums_ref)
    chunk = min(256, nodes)
    depth = DEGREES * 8
    lanes = windows * 2 * NF
    for copy in copies[1:3]:
        copy.wait()

    spot = (lax.broadcasted_iota(jnp.int32, (lanes, LANES), 1) & 7).astype(jnp.float32)

    def make_left(pair):
        top = weight_ref[pl.ds(pl.multiple_of(pair * 16, 16), 8), :]
        bottom = weight_ref[pl.ds(pl.multiple_of(pair * 16 + 8, 8), 8), :]
        sides = [
            jnp.concatenate([top[:, :lanes], bottom[:, :lanes]], axis=1),
            jnp.concatenate([top[:, lanes:], bottom[:, lanes:]], axis=1),
        ]
        per = LANES // 8
        for half in range(DEGREES // per):
            tall = jnp.concatenate(
                [sides[k % 2] * coef_ref[k : k + 1, :] for k in range(half * per, (half + 1) * per)], axis=0
            )
            turned = tall.T
            first = half * LANES
            fine = min(FINE * 8 - first, LANES)
            for which in range(2):
                group = 2 * pair + which
                mask = spot < plan_ref[2, group]
                value = turned[which * lanes : (which + 1) * lanes]
                value = jnp.concatenate([jnp.where(mask, value, 0.0), jnp.where(mask, 0.0, value)], axis=0)
                high, low = split_bf16(value, 2)
                if fine == LANES:
                    parts = [(first, high), (depth + first, high), (2 * FINE * 8 + first + LANES, low)]
                else:
                    mixed = [high[:, :fine].astype(jnp.float32), low[:, :fine].astype(jnp.float32)]
                    parts = [(first, high), (depth + first, jnp.concatenate(mixed, axis=1).astype(jnp.bfloat16))]
                for at, part in parts:
                    left_ref[group, :, at : at + LANES] = part

    used = plan_ref[3, 0].astype(jnp.int32)
    sure = stations // 16
    if sure <= 8:
        for pair in range(sure):
            make_left(pair)
    else:
        lax.fori_loop(0, sure, lambda pair, carry: (make_left(pair), carry)[1], 0)
    lax.fori_loop(sure, (used + 1) // 2, lambda pair, carry: (make_left(pair), carry)[1], 0)
    def basis_steps(group, basis_ref):
        arg = place_ref[pl.ds(pl.multiple_of(group * 8, 8), 8), :]
        twice = arg + arg
        before, now = jnp.ones_like(arg), arg
        for degree in range(0, DEGREES, 2):
            pair = jnp.concatenate([before, now], axis=0)
            if degree < FINE:
                high = (pair + ROUNDER) - ROUNDER
                basis_ref[depth + degree * 8 : depth + degree * 8 + 16, :] = (pair - high).astype(jnp.bfloat16)
                pair = high
            basis_ref[degree * 8 : degree * 8 + 16, :] = pair.astype(jnp.bfloat16)
            before = twice * now - before
            now = twice * before - now
            if degree % 8 == 6:
                yield

    def run(steps):
        for _ in steps:
            pass

    def add_group(group, basis_ref, steps):
        left = left_ref[group]
        tables = [plan_ref[slot, group].astype(jnp.int32) for slot in range(2)]
        phasor_rows = [pl.ds(pl.multiple_of(table * NF, NF), NF) for table in tables]
        fine = FINE * 8
        for first in range(0, nodes, chunk):
            at = slice(first, first + chunk)
            right = [
                basis_ref[: depth + fine, at],
                basis_ref[LANES:fine, at],
                basis_ref[:LANES, at],
            ]
            got = jnp.dot(left, jnp.concatenate(right, axis=0), preferred_element_type=jnp.float32)
            next(steps, None)
            for win in range(windows):
                row = win * 2 * NF
                real_sum, imag_sum = sums_ref[row : row + NF, at], sums_ref[row + NF : row + 2 * NF, at]
                for slot, rows in enumerate(phasor_rows):
                    cosine, sine = cos_ref[rows, at], sin_ref[rows, at]
                    real = got[slot * lanes + row : slot * lanes + row + NF]
                    imag = got[slot * lanes + row + NF : slot * lanes + row + 2 * NF]
                    real_sum += real * cosine - imag * sine
                    imag_sum += real * sine + imag * cosine
                sums_ref[row : row + NF, at], sums_ref[row + NF : row + 2 * NF, at] = real_sum, imag_sum
        run(steps)

    run(basis_steps(0, basis_a))
    for copy in copies[3:]:
        copy.wait()

    def body(pair, carry):
        group = pair * 2
        add_group(group, basis_a, basis_steps(group + 1, basis_b))
        add_group(group + 1, basis_b, basis_steps(jnp.minimum(group + 2, places // 8 - 1), basis_a))
        return carry

    lax.fori_loop(0, used // 2, body, 0)

    @pl.when(used % 2 == 1)
    def _():
        add_group(used - 1, basis_a, iter(()))

    powers = []
    for win in range(windows):
        row = win * 2 * NF
        real, imag = sums_ref[row : row + NF, :], sums_ref[row + NF : row + 2 * NF, :]
        powers.append(real * real + imag * imag)
    mine = lax.axis_index("win") == 0
    keep_ref[...] = jnp.where(mine, powers[0], powers[1])
    send_ref[...] = jnp.where(mine, powers[1], powers[0])


def finish_kernel(stations, keep_ref, got_ref, spectrum_ref, beam_ref):
    nodes = keep_ref.shape[1]
    win = lax.axis_index("win")
    for place, ref in ((win, keep_ref), (1 - win, got_ref)):
        power = ref[...]
        total = jnp.sum(power, axis=0, keepdims=True)
        at = pl.ds(pl.multiple_of(place * nodes, LANES), nodes)
        spectrum_ref[:, at] = power * (NF / total)
        beam_ref[:, at] = total * (1.0 / (NF * stations))


def on_device(traces, tables, corrections, station_table, node_ids, freq_bins):
    windows, groups, cores = (lax.axis_size(a) for a in ("win", "sta", "freq"))
    stations_dev, grid = corrections.shape
    stations = stations_dev * groups
    devices = windows * groups * cores
    nodes = grid // devices
    ntab = tables.shape[0]
    params = lambda free: pltpu.CompilerParams(vmem_limit_bytes=VMEM_LIMIT - free)
    vmem = pl.BlockSpec(memory_space=pltpu.VMEM)
    hbm = pl.BlockSpec(memory_space=pltpu.HBM)
    bins = freq_bins.reshape(1, NF)
    bins_scratch = pltpu.VMEM((1, NF), jnp.int32)

    holders = windows * cores
    merged = nodes % (holders * LANES) == 0
    pieces = nodes // (holders * LANES) if merged else 0
    height = pieces * stations_dev + 8
    blocks = pl.pallas_call(
        functools.partial(send_kernel, nodes),
        out_shape=jax.ShapeDtypeStruct((devices, height, LANES), jnp.bfloat16),
        in_specs=[hbm] * 3,
        out_specs=vmem,
        scratch_shapes=[
            bins_scratch,
            pltpu.VMEM(traces.shape, traces.dtype),
            pltpu.SemaphoreType.DMA((3,)),
        ],
        compiler_params=params(0),
        name="send",
    )(bins, traces, corrections)
    received = [lax.all_to_all(blocks, ("win", "sta", "freq"), split_axis=0, concat_axis=0, tiled=True)]
    if not merged:
        parts = corrections.reshape(stations_dev, groups, holders, nodes)
        place = lax.axis_index("freq") * windows + lax.axis_index("win")
        mine = lax.dynamic_index_in_dim(parts, place, axis=2, keepdims=False)
        corr = lax.all_to_all(mine.transpose(1, 0, 2), "sta", split_axis=0, concat_axis=0, tiled=True)
        received.append(corr.reshape(stations, nodes))

    wide = 512
    plan_width = max(LANES, stations)
    phasors = pltpu.VMEM((ntab * NF, nodes), jnp.float32)
    coefs = pltpu.VMEM((DEGREES, LANES), jnp.float32)
    plan = pltpu.VMEM((8, plan_width), jnp.float32)
    packed_shape = (packed_rows(ntab)[-1].stop, max(nodes, plan_width))
    packed = pl.pallas_call(
        prepare_kernel,
        out_shape=jax.ShapeDtypeStruct(packed_shape, jnp.float32),
        in_specs=[hbm] * 4,
        out_specs=hbm,
        scratch_shapes=[
            bins_scratch,
            pltpu.VMEM((1, stations), jnp.int32),
            pltpu.VMEM((max(nodes // LANES, 8), LANES), jnp.int32),
            pltpu.VMEM(tables.shape, tables.dtype),
            phasors,
            phasors,
            coefs,
            plan,
            pltpu.VMEM((grid // wide * ntab, 3 * wide), jnp.bfloat16),
            pltpu.VMEM((3 * wide, nodes), jnp.bfloat16),
            pltpu.SemaphoreType.DMA((3 + 2 * ntab,)),
            pltpu.SemaphoreType.DMA((TABLE_PIECES,)),
        ],
        compiler_params=params(512 * 1024),
        name="prepare",
    )(bins, station_table.reshape(1, stations), node_ids.reshape(grid // LANES, LANES), tables)

    places = (stations // 8 + ntab // 2 + 2) // 2 * 16
    half = jax.ShapeDtypeStruct((NF, nodes), jnp.float32)
    rows = 2 * windows * 2 * NF
    basis = pltpu.VMEM(((DEGREES + FINE) * 8, nodes), jnp.bfloat16)
    keep, send = pl.pallas_call(
        functools.partial(image_kernel, merged, stations_dev),
        out_shape=[half, half],
        in_specs=[hbm] + [vmem] * len(received),
        out_specs=[vmem, vmem],
        scratch_shapes=[
            pltpu.SMEM((8, plan_width), jnp.float32),
            plan,
            coefs,
            phasors,
            phasors,
            pltpu.SemaphoreType.DMA((3 + ntab // 2,)),
            pltpu.VMEM((places, nodes), jnp.float32),
            pltpu.VMEM((places, rows), jnp.float32),
            pltpu.VMEM((places // 8, rows, (DEGREES + 2 * FINE) * 8), jnp.bfloat16),
            pltpu.VMEM((rows // 2, nodes), jnp.float32),
            basis,
            basis,
        ],
        compiler_params=params(23 * 512 * 1024),
        name="image",
    )(packed, *received)
    got = lax.ppermute(send, "win", [(0, 1), (1, 0)])
    spectrum, beam_power = pl.pallas_call(
        functools.partial(finish_kernel, stations),
        out_shape=[
            jax.ShapeDtypeStruct((NF, windows * nodes), jnp.float32),
            jax.ShapeDtypeStruct((1, windows * nodes), jnp.float32),
        ],
        in_specs=[vmem, vmem],
        out_specs=[vmem, vmem],
        compiler_params=params(32 * 1024 * 1024),
        name="finish",
    )(keep, got)
    return spectrum, beam_power.reshape(windows * nodes)


def solution(mesh):
    return jax.shard_map(
        on_device,
        mesh=mesh,
        in_specs=(P(("win", "sta"), "freq"), P(), P("sta", None), P(), P(), P()),
        out_specs=(P("win", ("sta", "freq")), P(("win", "sta", "freq"))),
        check_vma=False,
    )
```

```python
import functools
import math

import jax
import jax.numpy as jnp
import numpy as np
from jax import lax
from jax.experimental import pallas as pl
from jax.experimental.pallas import tpu as pltpu
from jax.sharding import PartitionSpec as P

NT = 5120
NF = 16
NTAB = 16
LANES = 128
DEGREES = 32
FINE = 24
REACH = 1.5
TABLE_PIECES = 4
VMEM_LIMIT = 64 * 1024 * 1024 - 64 * 1024


def chebyshev_fit(func, degree, low, high):
    fit = np.polynomial.chebyshev.Chebyshev.interpolate(func, degree, domain=[low, high])
    return [float(v) for v in fit.convert(kind=np.polynomial.Polynomial).coef]


SIN_HALF = chebyshev_fit(lambda z: np.pi * np.sinc(np.sqrt(z)), 4, 0.0, 0.25)
COS_HALF = chebyshev_fit(lambda z: np.cos(np.pi * np.sqrt(z)), 4, 0.0, 0.25)


def horner(coefs, arg):
    total = coefs[-1]
    for coef in coefs[-2::-1]:
        total = total * arg + coef
    return total


def turn_parts(rest):
    square = rest * rest
    root = math.sqrt(2.0)
    sine_half = rest * horner([root * c for c in SIN_HALF], square)
    cos_half = horner([root * c for c in COS_HALF], square)
    return sine_half * sine_half, sine_half * cos_half


def cos_sin(turns):
    versine, sine = turn_parts(turns - jnp.round(turns))
    return 1.0 - versine, sine


def bins_column(bins_ref):
    rows = lax.broadcasted_iota(jnp.int32, (NF, NF), 0)
    lanes = lax.broadcasted_iota(jnp.int32, (NF, NF), 1)
    square = jnp.broadcast_to(bins_ref[...].astype(jnp.float32), (NF, NF))
    return jnp.sum(jnp.where(rows == lanes, square, 0.0), axis=1, keepdims=True)


def split_bf16(value, terms):
    pieces = []
    for term in range(terms):
        piece = value.astype(jnp.bfloat16)
        pieces.append(piece)
        if term < terms - 1:
            value = value - piece.astype(jnp.float32)
    return pieces


def start_all(copies):
    for copy in copies:
        copy.start()
    return copies


def send_kernel(nodes, bins_hbm, traces_hbm, corr_hbm, out_ref, bins_ref, traces_ref, sems):
    devices, height, _ = out_ref.shape
    stations_dev, half_length = traces_ref.shape
    pieces = (height - 8) // stations_dev
    windows, groups, cores = (lax.axis_size(a) for a in ("win", "sta", "freq"))
    place = lax.axis_index("win") * cores + lax.axis_index("freq")
    small = start_all(
        [
            pltpu.make_async_copy(bins_hbm, bins_ref, sems.at[0]),
            pltpu.make_async_copy(traces_hbm, traces_ref, sems.at[1]),
        ]
    )
    copies = []
    for dev in range(devices):
        win, sta, core = dev // (groups * cores), dev // cores % groups, dev % cores
        first = ((sta * cores + core) * windows + win) * nodes
        for piece in range(pieces):
            at = pl.multiple_of(first + (place * pieces + piece) * LANES, LANES)
            to = out_ref.at[dev, pl.ds(piece * stations_dev, stations_dev), :]
            copies.append(pltpu.make_async_copy(corr_hbm.at[:, pl.ds(at, LANES)], to, sems.at[2]))
    start_all(copies)
    start = lax.axis_index("freq") * half_length
    small[0].wait()
    bins = bins_column(bins_ref)
    pos = (start + lax.broadcasted_iota(jnp.int32, (NF, half_length), 1)).astype(jnp.float32)
    product = bins * pos
    turns = jnp.round(product * (1.0 / NT))
    rest = (product - turns * NT) * (1.0 / NT)
    versine, sine = turn_parts(rest)
    scale = 1.0 / math.sqrt(NT)
    table = jnp.concatenate([(1.0 - versine) * scale, sine * -scale], axis=0)
    both = jnp.concatenate(split_bf16(table, 2), axis=0)
    small[1].wait()
    sums = lax.dot_general(
        both, traces_ref[...], (((1,), (1,)), ((), ())), preferred_element_type=jnp.float32
    )
    sums = (sums[: 2 * NF] + sums[2 * NF :]).T
    terms = [term.astype(jnp.float32) for term in split_bf16(sums, 2)]
    tile = jnp.concatenate([term[at : at + 8] for term in terms for at in range(0, stations_dev, 8)], axis=1)
    tile = tile.astype(jnp.bfloat16)
    for dev in range(devices):
        out_ref[dev, height - 8 :, :] = tile
    if copies:
        filled = out_ref.at[:, pl.ds(0, height - 8), :]
        pltpu.make_async_copy(filled, filled, sems.at[2]).wait()


def own_place():
    windows, cores = lax.axis_size("win"), lax.axis_size("freq")
    return (lax.axis_index("sta") * cores + lax.axis_index("freq")) * windows + lax.axis_index("win")


def pick_columns(ids_ref, tables_ref, table_copies, nodes, left_ref, right_ref):
    ntab, grid = tables_ref.shape
    count = nodes // LANES
    wide = right_ref.shape[0] // 3
    blocks = grid // wide
    ids = ids_ref[pl.ds(own_place() * count % ids_ref.shape[0], count), :]
    ids = jnp.concatenate([ids[at : at + 1] for at in range(count)], axis=1)
    low, high = ids & (wide - 1), ids >> (wide.bit_length() - 1)
    spots = lax.broadcasted_iota(jnp.int32, (wide, nodes), 0)
    ones = jnp.where(spots == low, 1.0, 0.0).astype(jnp.bfloat16)
    for term in range(3):
        right_ref[term * wide : (term + 1) * wide, :] = ones
    found = jnp.zeros((ntab, nodes), jnp.float32)
    step = blocks // len(table_copies)
    for at, copy in enumerate(table_copies):
        copy.wait()
        for block in range(at * step, (at + 1) * step):
            pieces = split_bf16(tables_ref[:, block * wide : (block + 1) * wide], 3)
            left_ref[block * ntab : (block + 1) * ntab, :] = jnp.concatenate(pieces, axis=1)
        rows = left_ref[at * step * ntab : (at + 1) * step * ntab, :]
        picked = jnp.dot(rows, right_ref[...], preferred_element_type=jnp.float32)
        for block in range(step):
            part = picked[block * ntab : (block + 1) * ntab]
            found = jnp.where(high == at * step + block, part, found)
    return found


def product_coefs(bins_ref):
    shape = (DEGREES, DEGREES)
    degree = lax.broadcasted_iota(jnp.int32, shape, 0)
    node = lax.broadcasted_iota(jnp.int32, shape, 1)
    period = 4 * DEGREES
    weight, _ = cos_sin((degree * (2 * node + 1) & (period - 1)).astype(jnp.float32) * (1.0 / period))
    weight = weight * jnp.where(degree == 0, 1.0 / DEGREES, 2.0 / DEGREES)
    even = jnp.where(degree % 2 == 0, weight, 0.0)
    odd = jnp.where(degree % 2 == 1, weight, 0.0)
    row = bins_ref[...].astype(jnp.float32)
    bins = jnp.concatenate([row] * (LANES // NF), axis=1)
    at = lax.broadcasted_iota(jnp.int32, (DEGREES, LANES), 0).astype(jnp.float32)
    spot, _ = cos_sin((2.0 * at + 1.0) * (1.0 / period))
    cosine, sine = cos_sin(bins * (spot * (REACH / 256.0)))
    dot = functools.partial(jnp.dot, precision=lax.Precision.HIGHEST, preferred_element_type=jnp.float32)
    coefs = dot(even, cosine) + dot(odd, sine)
    for first in range(DEGREES - 8, 0, -8):
        mirror = (degree + node == 2 * first) & (node > first) & (node < first + 8)
        coefs = coefs - dot(jnp.where(mirror, 1.0, 0.0), coefs)
    twice = (at >= 8.0) & ((at.astype(jnp.int32) & 7) != 0)
    return jnp.where(twice, 2.0 * coefs, coefs)


def station_plan(table_row, width):
    count = table_row.shape[1]
    shape = (count, count)
    here = lax.broadcasted_iota(jnp.int32, shape, 0)
    there = lax.broadcasted_iota(jnp.int32, shape, 1)
    column_of = lambda row: jnp.sum(jnp.where(here == there, jnp.broadcast_to(row, shape), 0), axis=1, keepdims=True)
    table_column = column_of(table_row)
    same = (table_column == table_row) & (here < there)
    within = jnp.sum(jnp.where(same, 1, 0), axis=0, keepdims=True)
    place_row = within
    spot = jnp.zeros((1, 1), jnp.int32)
    held = jnp.zeros((1, 1), jnp.int32)
    for table in range(NTAB):
        size = jnp.sum(jnp.where(table_row == table, 1, 0), axis=1, keepdims=True)
        some = size > 0
        edge = (spot & 7) == 0
        skip = some & (held >= 2) & ~edge
        spot = jnp.where(skip, (spot + 7) >> 3 << 3, spot)
        held = jnp.where(skip | edge, 0, held)
        after = spot + size
        place_row = place_row + jnp.where(table_row == table, spot, 0)
        held = jnp.where(some, jnp.where(after >> 3 == spot >> 3, held + 1, 1), held)
        spot = after
    groups = (spot + 7) >> 3
    place_column = column_of(place_row)
    group = lax.broadcasted_iota(jnp.int32, (count, width), 1)
    inside = place_column >> 3 == group
    first = jnp.sum(jnp.where(place_column == group * 8, table_column, 0), axis=0, keepdims=True)
    last = jnp.max(jnp.where(inside, table_column, 0), axis=0, keepdims=True)
    length = jnp.sum(jnp.where(inside & (table_column == first), 1, 0), axis=0, keepdims=True)
    rows = [first, last, length, jnp.broadcast_to(groups, (1, width))]
    if width > count:
        place_row = jnp.concatenate([place_row, jnp.zeros((1, width - count), jnp.int32)], axis=1)
    rows += [place_row, jnp.zeros((3, width), jnp.int32)]
    return jnp.concatenate(rows, axis=0).astype(jnp.float32)


def packed_rows(ntab):
    ends = [ntab * NF, 2 * ntab * NF, 2 * ntab * NF + DEGREES, 2 * ntab * NF + DEGREES + 8]
    return [slice(start, end) for start, end in zip([0] + ends, ends)]


def prepare_kernel(bins_hbm, table_hbm, ids_hbm, tables_hbm, out_hbm, *rest):
    bins_ref, table_ref, ids_ref, tables_ref, cos_ref, sin_ref, coef_ref, plan_ref = rest[:8]
    left_ref, right_ref, sems, table_sems = rest[8:]
    ntab = tables_ref.shape[0]
    nodes = cos_ref.shape[1]
    near = ids_ref.shape[0]
    first = pl.multiple_of(own_place() * (nodes // LANES) // near * near, 8)
    ins = start_all(
        [
            pltpu.make_async_copy(ids_hbm.at[pl.ds(first, near), :], ids_ref, sems.at[0]),
            pltpu.make_async_copy(bins_hbm, bins_ref, sems.at[1]),
            pltpu.make_async_copy(table_hbm, table_ref, sems.at[2]),
        ]
    )
    piece = tables_ref.shape[1] // TABLE_PIECES
    table_copies = []
    for at in range(TABLE_PIECES):
        part = (slice(None), pl.ds(at * piece, piece))
        table_copies.append(pltpu.make_async_copy(tables_hbm.at[part], tables_ref.at[part], table_sems.at[at]))
    start_all(table_copies)
    for copy in ins:
        copy.wait()
    cos_at, sin_at, coef_at, plan_at = packed_rows(ntab)
    coef_ref[...] = product_coefs(bins_ref)
    plan_ref[...] = station_plan(table_ref[...], plan_ref.shape[1])
    outs = start_all(
        [
            pltpu.make_async_copy(coef_ref, out_hbm.at[coef_at, pl.ds(0, LANES)], sems.at[0]),
            pltpu.make_async_copy(plan_ref, out_hbm.at[plan_at, pl.ds(0, plan_ref.shape[1])], sems.at[1]),
        ]
    )
    turns = pick_columns(ids_ref, tables_ref, table_copies, nodes, left_ref, right_ref) * (1.0 / 256.0)
    bins = bins_column(bins_ref)
    for table in range(ntab):
        cosine, sine = cos_sin(bins * turns[table : table + 1])
        at = pl.ds(table * NF, NF)
        cos_ref[at, :] = cosine
        sin_ref[at, :] = sine
        outs += start_all(
            [
                pltpu.make_async_copy(
                    cos_ref.at[at, :], out_hbm.at[pl.ds(cos_at.start + table * NF, NF), pl.ds(0, nodes)],
                    sems.at[3 + 2 * table],
                ),
                pltpu.make_async_copy(
                    sin_ref.at[at, :], out_hbm.at[pl.ds(sin_at.start + table * NF, NF), pl.ds(0, nodes)],
                    sems.at[4 + 2 * table],
                ),
            ]
        )
    for copy in outs:
        copy.wait()


def image_kernel(merged, stations_dev, packed_hbm, block_ref, *rest):
    corr_ref, rest = (None, rest) if merged else (rest[0], rest[1:])
    keep_ref, send_ref, plan_ref, place_of_ref, coef_ref, cos_ref, sin_ref, sems = rest[:8]
    place_ref, weight_ref, left_ref, sums_ref, basis_a, basis_b = rest[8:]
    places, nodes = place_ref.shape
    windows, groups, cores = (lax.axis_size(a) for a in ("win", "sta", "freq"))
    stations = stations_dev * groups
    cos_at, sin_at, coef_at, plan_at = packed_rows(cos_ref.shape[0] // NF)
    width = plan_ref.shape[1]
    copies = start_all(
        [
            pltpu.make_async_copy(packed_hbm.at[plan_at, pl.ds(0, width)], place_of_ref, sems.at[0]),
            pltpu.make_async_copy(packed_hbm.at[plan_at, pl.ds(0, width)], plan_ref, sems.at[1]),
            pltpu.make_async_copy(packed_hbm.at[coef_at, pl.ds(0, LANES)], coef_ref, sems.at[2]),
        ]
        + [
            pltpu.make_async_copy(
                packed_hbm.at[pl.ds(at.start + first, 4 * NF), pl.ds(0, nodes)],
                ref.at[pl.ds(first, 4 * NF), :],
                sems.at[3 + 2 * (first // (4 * NF)) + which],
            )
            for first in range(0, NTAB * NF, 4 * NF)
            for which, (at, ref) in enumerate(((cos_at, cos_ref), (sin_at, sin_ref)))
        ]
    )
    height = block_ref.shape[1]
    rows_of = lambda win, core: [(win * groups + group) * cores + core for group in range(groups)]

    even, odd = [], []
    for win in range(windows):
        value = []
        for group in range(groups):
            tile = None
            for core in range(cores):
                part = block_ref[(win * groups + group) * cores + core, height - 8 :, :].astype(jnp.float32)
                tile = part if tile is None else tile + part
            tile = tile[:, : LANES // 2] + tile[:, LANES // 2 :]
            value += [tile[:, 2 * NF * piece : 2 * NF * (piece + 1)] for piece in range(stations_dev // 8)]
        value = jnp.concatenate(value, axis=0)
        even.append(value)
        odd.append(jnp.concatenate([-value[:, NF:], value[:, :NF]], axis=1))
    spectra = jnp.concatenate(even + odd, axis=1)
    if merged:
        parts = []
        for win in range(windows):
            for core in range(cores):
                for first in range(0, height - 8, stations_dev):
                    rows = [block_ref[at, first : first + stations_dev, :] for at in rows_of(win, core)]
                    parts.append(jnp.concatenate(rows, axis=0))
        corr = jnp.concatenate(parts, axis=1)
    else:
        corr = corr_ref[...]

    copies[0].wait()
    place_row = place_of_ref[4:5, :stations].astype(jnp.int32)
    sorter = lax.broadcasted_iota(jnp.int32, (places, stations), 0) == place_row
    sorter = jnp.where(sorter, 1.0, 0.0).astype(jnp.bfloat16)
    found = None
    for piece in split_bf16(spectra, 3):
        part = jnp.dot(sorter, piece, preferred_element_type=jnp.float32)
        found = part if found is None else found + part
    weight_ref[...] = found
    place_ref[...] = jnp.dot(sorter, corr, preferred_element_type=jnp.float32) * (1.0 / REACH)
    sums_ref[...] = jnp.zeros_like(sums_ref)
    chunk = min(256, nodes)
    depth = DEGREES * 8
    lanes = windows * 2 * NF
    for copy in copies[1:3]:
        copy.wait()

    spot = (lax.broadcasted_iota(jnp.int32, (lanes, LANES), 1) & 7).astype(jnp.float32)

    def make_left(pair):
        top = weight_ref[pl.ds(pl.multiple_of(pair * 16, 16), 8), :]
        bottom = weight_ref[pl.ds(pl.multiple_of(pair * 16 + 8, 8), 8), :]
        sides = [
            jnp.concatenate([top[:, :lanes], bottom[:, :lanes]], axis=1),
            jnp.concatenate([top[:, lanes:], bottom[:, lanes:]], axis=1),
        ]
        per = LANES // 8
        for half in range(DEGREES // per):
            tall = jnp.concatenate(
                [sides[k % 2] * coef_ref[k : k + 1, :] for k in range(half * per, (half + 1) * per)], axis=0
            )
            turned = tall.T
            first = half * LANES
            fine = min(FINE * 8 - first, LANES)
            for which in range(2):
                group = 2 * pair + which
                mask = spot < plan_ref[2, group]
                value = turned[which * lanes : (which + 1) * lanes]
                value = jnp.concatenate([jnp.where(mask, value, 0.0), jnp.where(mask, 0.0, value)], axis=0)
                high, low = split_bf16(value, 2)
                if fine == LANES:
                    parts = [(first, high), (depth + first, high), (2 * FINE * 8 + first + LANES, low)]
                else:
                    mixed = [high[:, :fine].astype(jnp.float32), low[:, :fine].astype(jnp.float32)]
                    parts = [(first, high), (depth + first, jnp.concatenate(mixed, axis=1).astype(jnp.bfloat16))]
                for at, part in parts:
                    left_ref[group, :, at : at + LANES] = part

    used = plan_ref[3, 0].astype(jnp.int32)
    sure = stations // 16
    if sure <= 8:
        for pair in range(sure):
            make_left(pair)
    else:
        lax.fori_loop(0, sure, lambda pair, carry: (make_left(pair), carry)[1], 0)
    lax.fori_loop(sure, (used + 1) // 2, lambda pair, carry: (make_left(pair), carry)[1], 0)
    def make_basis(group, basis_ref, at):
        arg = place_ref[pl.ds(pl.multiple_of(group * 8, 8), 8), at]
        twice = arg + arg
        low = [jnp.ones_like(arg), arg]
        while len(low) < 8:
            low.append(twice * low[-1] - low[-2])
        eight = (low[4] + low[4]) * low[4] - 1.0
        sixteen = (eight + eight) * eight - 1.0
        steps = [None, eight, sixteen, (sixteen + sixteen - 1.0) * eight]
        for degree in range(0, DEGREES, 2):
            pair = []
            for factor in low[degree % 8 : degree % 8 + 2]:
                step = steps[degree // 8]
                pair.append(factor if step is None else step if factor is low[0] else factor * step)
            pair = jnp.concatenate(pair, axis=0)
            for term, value in enumerate(split_bf16(pair, 2 if degree < FINE else 1)):
                basis_ref[term * depth + degree * 8 : term * depth + degree * 8 + 16, at] = value

    def add_group(group, basis_ref, next_basis):
        left = left_ref[group]
        tables = [plan_ref[slot, group].astype(jnp.int32) for slot in range(2)]
        phasor_rows = [pl.ds(pl.multiple_of(table * NF, NF), NF) for table in tables]
        fine = FINE * 8
        for first in range(0, nodes, chunk):
            at = slice(first, first + chunk)
            right = [
                basis_ref[: depth + fine, at],
                basis_ref[LANES:fine, at],
                basis_ref[:LANES, at],
            ]
            got = jnp.dot(left, jnp.concatenate(right, axis=0), preferred_element_type=jnp.float32)
            if next_basis is not None:
                make_basis(group + 1, next_basis, at)
            for win in range(windows):
                row = win * 2 * NF
                real_sum, imag_sum = sums_ref[row : row + NF, at], sums_ref[row + NF : row + 2 * NF, at]
                for slot, rows in enumerate(phasor_rows):
                    cosine, sine = cos_ref[rows, at], sin_ref[rows, at]
                    real = got[slot * lanes + row : slot * lanes + row + NF]
                    imag = got[slot * lanes + row + NF : slot * lanes + row + 2 * NF]
                    real_sum += real * cosine - imag * sine
                    imag_sum += real * sine + imag * cosine
                sums_ref[row : row + NF, at], sums_ref[row + NF : row + 2 * NF, at] = real_sum, imag_sum

    for first in range(0, nodes, chunk):
        make_basis(0, basis_a, slice(first, first + chunk))
    for copy in copies[3:]:
        copy.wait()

    def body(pair, carry):
        group = pair * 2
        add_group(group, basis_a, basis_b)
        add_group(group + 1, basis_b, basis_a)
        return carry

    lax.fori_loop(0, used // 2, body, 0)

    @pl.when(used % 2 == 1)
    def _():
        add_group(used - 1, basis_a, None)

    powers = []
    for win in range(windows):
        row = win * 2 * NF
        real, imag = sums_ref[row : row + NF, :], sums_ref[row + NF : row + 2 * NF, :]
        powers.append(real * real + imag * imag)
    mine = lax.axis_index("win") == 0
    keep_ref[...] = jnp.where(mine, powers[0], powers[1])
    send_ref[...] = jnp.where(mine, powers[1], powers[0])


def finish_kernel(stations, keep_ref, got_ref, spectrum_ref, beam_ref):
    nodes = keep_ref.shape[1]
    win = lax.axis_index("win")
    for place, ref in ((win, keep_ref), (1 - win, got_ref)):
        power = ref[...]
        total = jnp.sum(power, axis=0, keepdims=True)
        at = pl.ds(pl.multiple_of(place * nodes, LANES), nodes)
        spectrum_ref[:, at] = power * (NF / total)
        beam_ref[:, at] = total * (1.0 / (NF * stations))


def on_device(traces, tables, corrections, station_table, node_ids, freq_bins):
    windows, groups, cores = (lax.axis_size(a) for a in ("win", "sta", "freq"))
    stations_dev, grid = corrections.shape
    stations = stations_dev * groups
    devices = windows * groups * cores
    nodes = grid // devices
    ntab = tables.shape[0]
    params = lambda free: pltpu.CompilerParams(vmem_limit_bytes=VMEM_LIMIT - free)
    vmem = pl.BlockSpec(memory_space=pltpu.VMEM)
    hbm = pl.BlockSpec(memory_space=pltpu.HBM)
    bins = freq_bins.reshape(1, NF)
    bins_scratch = pltpu.VMEM((1, NF), jnp.int32)

    holders = windows * cores
    merged = nodes % (holders * LANES) == 0
    pieces = nodes // (holders * LANES) if merged else 0
    height = pieces * stations_dev + 8
    blocks = pl.pallas_call(
        functools.partial(send_kernel, nodes),
        out_shape=jax.ShapeDtypeStruct((devices, height, LANES), jnp.bfloat16),
        in_specs=[hbm] * 3,
        out_specs=vmem,
        scratch_shapes=[
            bins_scratch,
            pltpu.VMEM(traces.shape, traces.dtype),
            pltpu.SemaphoreType.DMA((3,)),
        ],
        compiler_params=params(0),
        name="send",
    )(bins, traces, corrections)
    received = [lax.all_to_all(blocks, ("win", "sta", "freq"), split_axis=0, concat_axis=0, tiled=True)]
    if not merged:
        parts = corrections.reshape(stations_dev, groups, holders, nodes)
        place = lax.axis_index("freq") * windows + lax.axis_index("win")
        mine = lax.dynamic_index_in_dim(parts, place, axis=2, keepdims=False)
        corr = lax.all_to_all(mine.transpose(1, 0, 2), "sta", split_axis=0, concat_axis=0, tiled=True)
        received.append(corr.reshape(stations, nodes))

    wide = 512
    plan_width = max(LANES, stations)
    phasors = pltpu.VMEM((ntab * NF, nodes), jnp.float32)
    coefs = pltpu.VMEM((DEGREES, LANES), jnp.float32)
    plan = pltpu.VMEM((8, plan_width), jnp.float32)
    packed_shape = (packed_rows(ntab)[-1].stop, max(nodes, plan_width))
    packed = pl.pallas_call(
        prepare_kernel,
        out_shape=jax.ShapeDtypeStruct(packed_shape, jnp.float32),
        in_specs=[hbm] * 4,
        out_specs=hbm,
        scratch_shapes=[
            bins_scratch,
            pltpu.VMEM((1, stations), jnp.int32),
            pltpu.VMEM((max(nodes // LANES, 8), LANES), jnp.int32),
            pltpu.VMEM(tables.shape, tables.dtype),
            phasors,
            phasors,
            coefs,
            plan,
            pltpu.VMEM((grid // wide * ntab, 3 * wide), jnp.bfloat16),
            pltpu.VMEM((3 * wide, nodes), jnp.bfloat16),
            pltpu.SemaphoreType.DMA((3 + 2 * ntab,)),
            pltpu.SemaphoreType.DMA((TABLE_PIECES,)),
        ],
        compiler_params=params(512 * 1024),
        name="prepare",
    )(bins, station_table.reshape(1, stations), node_ids.reshape(grid // LANES, LANES), tables)

    places = (stations // 8 + ntab // 2 + 3) // 2 * 16
    half = jax.ShapeDtypeStruct((NF, nodes), jnp.float32)
    rows = 2 * windows * 2 * NF
    basis = pltpu.VMEM(((DEGREES + FINE) * 8, nodes), jnp.bfloat16)
    keep, send = pl.pallas_call(
        functools.partial(image_kernel, merged, stations_dev),
        out_shape=[half, half],
        in_specs=[hbm] + [vmem] * len(received),
        out_specs=[vmem, vmem],
        scratch_shapes=[
            pltpu.SMEM((8, plan_width), jnp.float32),
            plan,
            coefs,
            phasors,
            phasors,
            pltpu.SemaphoreType.DMA((3 + ntab // 2,)),
            pltpu.VMEM((places, nodes), jnp.float32),
            pltpu.VMEM((places, rows), jnp.float32),
            pltpu.VMEM((places // 8, rows, (DEGREES + 2 * FINE) * 8), jnp.bfloat16),
            pltpu.VMEM((rows // 2, nodes), jnp.float32),
            basis,
            basis,
        ],
        compiler_params=params(23 * 512 * 1024),
        name="image",
    )(packed, *received)
    got = lax.ppermute(send, "win", [(0, 1), (1, 0)])
    spectrum, beam_power = pl.pallas_call(
        functools.partial(finish_kernel, stations),
        out_shape=[
            jax.ShapeDtypeStruct((NF, windows * nodes), jnp.float32),
            jax.ShapeDtypeStruct((1, windows * nodes), jnp.float32),
        ],
        in_specs=[vmem, vmem],
        out_specs=[vmem, vmem],
        compiler_params=params(32 * 1024 * 1024),
        name="finish",
    )(keep, got)
    return spectrum, beam_power.reshape(windows * nodes)


def solution(mesh):
    return jax.shard_map(
        on_device,
        mesh=mesh,
        in_specs=(P(("win", "sta"), "freq"), P(), P("sta", None), P(), P(), P()),
        out_specs=(P("win", ("sta", "freq")), P(("win", "sta", "freq"))),
        check_vma=False,
    )
```

```python
import functools
import math

import jax
import jax.numpy as jnp
import numpy as np
from jax import lax
from jax.experimental import pallas as pl
from jax.experimental.pallas import tpu as pltpu
from jax.sharding import PartitionSpec as P

NT = 5120
NF = 16
NTAB = 16
LANES = 128
DEGREES = 32
FINE = 24
REACH = 1.5
TABLE_PIECES = 4
VMEM_LIMIT = 64 * 1024 * 1024 - 64 * 1024


def chebyshev_fit(func, degree, low, high):
    fit = np.polynomial.chebyshev.Chebyshev.interpolate(func, degree, domain=[low, high])
    return [float(v) for v in fit.convert(kind=np.polynomial.Polynomial).coef]


SIN_HALF = chebyshev_fit(lambda z: np.pi * np.sinc(np.sqrt(z)), 4, 0.0, 0.25)
COS_HALF = chebyshev_fit(lambda z: np.cos(np.pi * np.sqrt(z)), 4, 0.0, 0.25)


def horner(coefs, arg):
    total = coefs[-1]
    for coef in coefs[-2::-1]:
        total = total * arg + coef
    return total


def turn_parts(rest):
    square = rest * rest
    root = math.sqrt(2.0)
    sine_half = rest * horner([root * c for c in SIN_HALF], square)
    cos_half = horner([root * c for c in COS_HALF], square)
    return sine_half * sine_half, sine_half * cos_half


def cos_sin(turns):
    versine, sine = turn_parts(turns - jnp.round(turns))
    return 1.0 - versine, sine


def bins_column(bins_ref):
    rows = lax.broadcasted_iota(jnp.int32, (NF, NF), 0)
    lanes = lax.broadcasted_iota(jnp.int32, (NF, NF), 1)
    square = jnp.broadcast_to(bins_ref[...].astype(jnp.float32), (NF, NF))
    return jnp.sum(jnp.where(rows == lanes, square, 0.0), axis=1, keepdims=True)


def split_bf16(value, terms):
    pieces = []
    for term in range(terms):
        piece = value.astype(jnp.bfloat16)
        pieces.append(piece)
        if term < terms - 1:
            value = value - piece.astype(jnp.float32)
    return pieces


def start_all(copies):
    for copy in copies:
        copy.start()
    return copies


def send_kernel(nodes, bins_hbm, traces_hbm, corr_hbm, out_ref, bins_ref, traces_ref, sems):
    devices, height, _ = out_ref.shape
    stations_dev, half_length = traces_ref.shape
    pieces = (height - 8) // stations_dev
    windows, groups, cores = (lax.axis_size(a) for a in ("win", "sta", "freq"))
    place = lax.axis_index("win") * cores + lax.axis_index("freq")
    small = start_all(
        [
            pltpu.make_async_copy(bins_hbm, bins_ref, sems.at[0]),
            pltpu.make_async_copy(traces_hbm, traces_ref, sems.at[1]),
        ]
    )
    copies = []
    for dev in range(devices):
        win, sta, core = dev // (groups * cores), dev // cores % groups, dev % cores
        first = ((sta * cores + core) * windows + win) * nodes
        for piece in range(pieces):
            at = pl.multiple_of(first + (place * pieces + piece) * LANES, LANES)
            to = out_ref.at[dev, pl.ds(piece * stations_dev, stations_dev), :]
            copies.append(pltpu.make_async_copy(corr_hbm.at[:, pl.ds(at, LANES)], to, sems.at[2]))
    start_all(copies)
    start = lax.axis_index("freq") * half_length
    small[0].wait()
    bins = bins_column(bins_ref)
    pos = (start + lax.broadcasted_iota(jnp.int32, (NF, half_length), 1)).astype(jnp.float32)
    product = bins * pos
    turns = jnp.round(product * (1.0 / NT))
    rest = (product - turns * NT) * (1.0 / NT)
    versine, sine = turn_parts(rest)
    scale = 1.0 / math.sqrt(NT)
    table = jnp.concatenate([(1.0 - versine) * scale, sine * -scale], axis=0)
    both = jnp.concatenate(split_bf16(table, 2), axis=0)
    small[1].wait()
    sums = lax.dot_general(
        both, traces_ref[...], (((1,), (1,)), ((), ())), preferred_element_type=jnp.float32
    )
    sums = (sums[: 2 * NF] + sums[2 * NF :]).T
    terms = [term.astype(jnp.float32) for term in split_bf16(sums, 2)]
    tile = jnp.concatenate([term[at : at + 8] for term in terms for at in range(0, stations_dev, 8)], axis=1)
    tile = tile.astype(jnp.bfloat16)
    for dev in range(devices):
        out_ref[dev, height - 8 :, :] = tile
    if copies:
        filled = out_ref.at[:, pl.ds(0, height - 8), :]
        pltpu.make_async_copy(filled, filled, sems.at[2]).wait()


def own_place():
    windows, cores = lax.axis_size("win"), lax.axis_size("freq")
    return (lax.axis_index("sta") * cores + lax.axis_index("freq")) * windows + lax.axis_index("win")


def pick_columns(ids_ref, tables_ref, table_copies, nodes, left_ref, right_ref):
    ntab, grid = tables_ref.shape
    count = nodes // LANES
    wide = right_ref.shape[0] // 3
    blocks = grid // wide
    ids = ids_ref[pl.ds(own_place() * count % ids_ref.shape[0], count), :]
    ids = jnp.concatenate([ids[at : at + 1] for at in range(count)], axis=1)
    low, high = ids & (wide - 1), ids >> (wide.bit_length() - 1)
    spots = lax.broadcasted_iota(jnp.int32, (wide, nodes), 0)
    ones = jnp.where(spots == low, 1.0, 0.0).astype(jnp.bfloat16)
    for term in range(3):
        right_ref[term * wide : (term + 1) * wide, :] = ones
    found = jnp.zeros((ntab, nodes), jnp.float32)
    step = blocks // len(table_copies)
    for at, copy in enumerate(table_copies):
        copy.wait()
        for block in range(at * step, (at + 1) * step):
            pieces = split_bf16(tables_ref[:, block * wide : (block + 1) * wide], 3)
            left_ref[block * ntab : (block + 1) * ntab, :] = jnp.concatenate(pieces, axis=1)
        rows = left_ref[at * step * ntab : (at + 1) * step * ntab, :]
        picked = jnp.dot(rows, right_ref[...], preferred_element_type=jnp.float32)
        for block in range(step):
            part = picked[block * ntab : (block + 1) * ntab]
            found = jnp.where(high == at * step + block, part, found)
    return found


def product_coefs(bins_ref):
    shape = (DEGREES, DEGREES)
    degree = lax.broadcasted_iota(jnp.int32, shape, 0)
    node = lax.broadcasted_iota(jnp.int32, shape, 1)
    period = 4 * DEGREES
    weight, _ = cos_sin((degree * (2 * node + 1) & (period - 1)).astype(jnp.float32) * (1.0 / period))
    weight = weight * jnp.where(degree == 0, 1.0 / DEGREES, 2.0 / DEGREES)
    even = jnp.where(degree % 2 == 0, weight, 0.0)
    odd = jnp.where(degree % 2 == 1, weight, 0.0)
    row = bins_ref[...].astype(jnp.float32)
    bins = jnp.concatenate([row] * (LANES // NF), axis=1)
    at = lax.broadcasted_iota(jnp.int32, (DEGREES, LANES), 0).astype(jnp.float32)
    spot, _ = cos_sin((2.0 * at + 1.0) * (1.0 / period))
    cosine, sine = cos_sin(bins * (spot * (REACH / 256.0)))
    dot = functools.partial(jnp.dot, precision=lax.Precision.HIGHEST, preferred_element_type=jnp.float32)
    coefs = dot(even, cosine) + dot(odd, sine)
    for first in range(DEGREES - 8, 0, -8):
        mirror = (degree + node == 2 * first) & (node > first) & (node < first + 8)
        coefs = coefs - dot(jnp.where(mirror, 1.0, 0.0), coefs)
    twice = (at >= 8.0) & ((at.astype(jnp.int32) & 7) != 0)
    return jnp.where(twice, 2.0 * coefs, coefs)


def station_plan(table_row, width):
    count = table_row.shape[1]
    shape = (count, count)
    here = lax.broadcasted_iota(jnp.int32, shape, 0)
    there = lax.broadcasted_iota(jnp.int32, shape, 1)
    column_of = lambda row: jnp.sum(jnp.where(here == there, jnp.broadcast_to(row, shape), 0), axis=1, keepdims=True)
    table_column = column_of(table_row)
    same = (table_column == table_row) & (here < there)
    within = jnp.sum(jnp.where(same, 1, 0), axis=0, keepdims=True)
    place_row = within
    spot = jnp.zeros((1, 1), jnp.int32)
    held = jnp.zeros((1, 1), jnp.int32)
    for table in range(NTAB):
        size = jnp.sum(jnp.where(table_row == table, 1, 0), axis=1, keepdims=True)
        some = size > 0
        edge = (spot & 7) == 0
        skip = some & (held >= 2) & ~edge
        spot = jnp.where(skip, (spot + 7) >> 3 << 3, spot)
        held = jnp.where(skip | edge, 0, held)
        after = spot + size
        place_row = place_row + jnp.where(table_row == table, spot, 0)
        held = jnp.where(some, jnp.where(after >> 3 == spot >> 3, held + 1, 1), held)
        spot = after
    groups = (spot + 7) >> 3
    place_column = column_of(place_row)
    group = lax.broadcasted_iota(jnp.int32, (count, width), 1)
    inside = place_column >> 3 == group
    first = jnp.sum(jnp.where(place_column == group * 8, table_column, 0), axis=0, keepdims=True)
    last = jnp.max(jnp.where(inside, table_column, 0), axis=0, keepdims=True)
    length = jnp.sum(jnp.where(inside & (table_column == first), 1, 0), axis=0, keepdims=True)
    rows = [first, last, length, jnp.broadcast_to(groups, (1, width))]
    if width > count:
        place_row = jnp.concatenate([place_row, jnp.zeros((1, width - count), jnp.int32)], axis=1)
    rows += [place_row, jnp.zeros((3, width), jnp.int32)]
    return jnp.concatenate(rows, axis=0).astype(jnp.float32)


def packed_rows(ntab):
    ends = [ntab * NF, 2 * ntab * NF, 2 * ntab * NF + DEGREES, 2 * ntab * NF + DEGREES + 8]
    return [slice(start, end) for start, end in zip([0] + ends, ends)]


def prepare_kernel(bins_hbm, table_hbm, ids_hbm, tables_hbm, out_hbm, *rest):
    bins_ref, table_ref, ids_ref, tables_ref, cos_ref, sin_ref, coef_ref, plan_ref = rest[:8]
    left_ref, right_ref, sems, table_sems = rest[8:]
    ntab = tables_ref.shape[0]
    nodes = cos_ref.shape[1]
    near = ids_ref.shape[0]
    first = pl.multiple_of(own_place() * (nodes // LANES) // near * near, 8)
    ins = start_all(
        [
            pltpu.make_async_copy(ids_hbm.at[pl.ds(first, near), :], ids_ref, sems.at[0]),
            pltpu.make_async_copy(bins_hbm, bins_ref, sems.at[1]),
            pltpu.make_async_copy(table_hbm, table_ref, sems.at[2]),
        ]
    )
    piece = tables_ref.shape[1] // TABLE_PIECES
    table_copies = []
    for at in range(TABLE_PIECES):
        part = (slice(None), pl.ds(at * piece, piece))
        table_copies.append(pltpu.make_async_copy(tables_hbm.at[part], tables_ref.at[part], table_sems.at[at]))
    start_all(table_copies)
    for copy in ins:
        copy.wait()
    cos_at, sin_at, coef_at, plan_at = packed_rows(ntab)
    coef_ref[...] = product_coefs(bins_ref)
    plan_ref[...] = station_plan(table_ref[...], plan_ref.shape[1])
    outs = start_all(
        [
            pltpu.make_async_copy(coef_ref, out_hbm.at[coef_at, pl.ds(0, LANES)], sems.at[0]),
            pltpu.make_async_copy(plan_ref, out_hbm.at[plan_at, pl.ds(0, plan_ref.shape[1])], sems.at[1]),
        ]
    )
    turns = pick_columns(ids_ref, tables_ref, table_copies, nodes, left_ref, right_ref) * (1.0 / 256.0)
    bins = bins_column(bins_ref)
    for table in range(ntab):
        cosine, sine = cos_sin(bins * turns[table : table + 1])
        at = pl.ds(table * NF, NF)
        cos_ref[at, :] = cosine
        sin_ref[at, :] = sine
        outs += start_all(
            [
                pltpu.make_async_copy(
                    cos_ref.at[at, :], out_hbm.at[pl.ds(cos_at.start + table * NF, NF), pl.ds(0, nodes)],
                    sems.at[3 + 2 * table],
                ),
                pltpu.make_async_copy(
                    sin_ref.at[at, :], out_hbm.at[pl.ds(sin_at.start + table * NF, NF), pl.ds(0, nodes)],
                    sems.at[4 + 2 * table],
                ),
            ]
        )
    for copy in outs:
        copy.wait()


def image_kernel(merged, stations_dev, packed_hbm, block_ref, *rest):
    corr_ref, rest = (None, rest) if merged else (rest[0], rest[1:])
    keep_ref, send_ref, plan_ref, place_of_ref, coef_ref, cos_ref, sin_ref, sems = rest[:8]
    place_ref, weight_ref, left_ref, sums_ref = rest[8:]
    places, nodes = place_ref.shape
    windows, groups, cores = (lax.axis_size(a) for a in ("win", "sta", "freq"))
    stations = stations_dev * groups
    cos_at, sin_at, coef_at, plan_at = packed_rows(cos_ref.shape[0] // NF)
    width = plan_ref.shape[1]
    copies = start_all(
        [
            pltpu.make_async_copy(packed_hbm.at[plan_at, pl.ds(0, width)], place_of_ref, sems.at[0]),
            pltpu.make_async_copy(packed_hbm.at[plan_at, pl.ds(0, width)], plan_ref, sems.at[1]),
            pltpu.make_async_copy(packed_hbm.at[coef_at, pl.ds(0, LANES)], coef_ref, sems.at[2]),
        ]
        + [
            pltpu.make_async_copy(
                packed_hbm.at[pl.ds(at.start + first, 4 * NF), pl.ds(0, nodes)],
                ref.at[pl.ds(first, 4 * NF), :],
                sems.at[3 + 2 * (first // (4 * NF)) + which],
            )
            for first in range(0, NTAB * NF, 4 * NF)
            for which, (at, ref) in enumerate(((cos_at, cos_ref), (sin_at, sin_ref)))
        ]
    )
    height = block_ref.shape[1]
    rows_of = lambda win, core: [(win * groups + group) * cores + core for group in range(groups)]

    even, odd = [], []
    for win in range(windows):
        value = []
        for group in range(groups):
            tile = None
            for core in range(cores):
                part = block_ref[(win * groups + group) * cores + core, height - 8 :, :].astype(jnp.float32)
                tile = part if tile is None else tile + part
            tile = tile[:, : LANES // 2] + tile[:, LANES // 2 :]
            value += [tile[:, 2 * NF * piece : 2 * NF * (piece + 1)] for piece in range(stations_dev // 8)]
        value = jnp.concatenate(value, axis=0)
        even.append(value)
        odd.append(jnp.concatenate([-value[:, NF:], value[:, :NF]], axis=1))
    spectra = jnp.concatenate(even + odd, axis=1)
    if merged:
        parts = []
        for win in range(windows):
            for core in range(cores):
                for first in range(0, height - 8, stations_dev):
                    rows = [block_ref[at, first : first + stations_dev, :] for at in rows_of(win, core)]
                    parts.append(jnp.concatenate(rows, axis=0))
        corr = jnp.concatenate(parts, axis=1)
    else:
        corr = corr_ref[...]

    copies[0].wait()
    place_row = place_of_ref[4:5, :stations].astype(jnp.int32)
    sorter = lax.broadcasted_iota(jnp.int32, (places, stations), 0) == place_row
    sorter = jnp.where(sorter, 1.0, 0.0).astype(jnp.bfloat16)
    found = None
    for piece in split_bf16(spectra, 3):
        part = jnp.dot(sorter, piece, preferred_element_type=jnp.float32)
        found = part if found is None else found + part
    weight_ref[...] = found
    place_ref[...] = jnp.dot(sorter, corr, preferred_element_type=jnp.float32) * (1.0 / REACH)
    sums_ref[...] = jnp.zeros_like(sums_ref)
    chunk = min(256, nodes)
    depth = DEGREES * 8
    lanes = windows * 2 * NF
    for copy in copies[1:3]:
        copy.wait()

    rows = 2 * lanes
    spot = (lax.broadcasted_iota(jnp.int32, (lanes, LANES), 1) & 7).astype(jnp.float32)

    def make_left(pair):
        top = weight_ref[pl.ds(pl.multiple_of(pair * 16, 16), 8), :]
        bottom = weight_ref[pl.ds(pl.multiple_of(pair * 16 + 8, 8), 8), :]
        sides = [
            jnp.concatenate([top[:, :lanes], bottom[:, :lanes]], axis=1),
            jnp.concatenate([top[:, lanes:], bottom[:, lanes:]], axis=1),
        ]
        per = LANES // 8
        for half in range(DEGREES // per):
            tall = jnp.concatenate(
                [sides[k % 2] * coef_ref[k : k + 1, :] for k in range(half * per, (half + 1) * per)], axis=0
            )
            turned = tall.T
            first = half * LANES
            fine = min(FINE * 8 - first, LANES)
            for which in range(2):
                group = 2 * pair + which
                mask = spot < plan_ref[2, group]
                value = turned[which * lanes : (which + 1) * lanes]
                value = jnp.concatenate([jnp.where(mask, value, 0.0), jnp.where(mask, 0.0, value)], axis=0)
                high, low = split_bf16(value, 2)
                left_ref[group, :rows, first : first + LANES] = high
                left_ref[group, rows:, first : first + LANES] = low
                if fine < LANES:
                    lane = lax.broadcasted_iota(jnp.int32, high.shape, 1)
                    high = jnp.where(lane < fine, high.astype(jnp.float32), 0.0).astype(jnp.bfloat16)
                left_ref[group, :rows, depth + first : depth + first + LANES] = high
                left_ref[group, rows:, depth + first : depth + first + LANES] = jnp.zeros_like(low)

    used = plan_ref[3, 0].astype(jnp.int32)
    sure = stations // 16
    if sure <= 8:
        for pair in range(sure):
            make_left(pair)
    else:
        lax.fori_loop(0, sure, lambda pair, carry: (make_left(pair), carry)[1], 0)
    lax.fori_loop(sure, (used + 1) // 2, lambda pair, carry: (make_left(pair), carry)[1], 0)
    def basis_of(group, at):
        arg = place_ref[pl.ds(pl.multiple_of(group * 8, 8), 8), at]
        twice = arg + arg
        low = [jnp.ones_like(arg), arg]
        while len(low) < 8:
            low.append(twice * low[-1] - low[-2])
        eight = (low[4] + low[4]) * low[4] - 1.0
        sixteen = (eight + eight) * eight - 1.0
        steps = [None, eight, sixteen, (sixteen + sixteen - 1.0) * eight]
        terms = [[], []]
        for degree in range(0, DEGREES, 2):
            pair = []
            for factor in low[degree % 8 : degree % 8 + 2]:
                step = steps[degree // 8]
                pair.append(factor if step is None else step if factor is low[0] else factor * step)
            pair = jnp.concatenate(pair, axis=0)
            for term, value in enumerate(split_bf16(pair, 2 if degree < FINE else 1)):
                terms[term].append(value)
        spare = jnp.zeros((depth - FINE * 8, chunk), jnp.bfloat16)
        return jnp.concatenate(terms[0] + terms[1] + [spare], axis=0)

    def add_group(group):
        left = left_ref[group]
        tables = [plan_ref[slot, group].astype(jnp.int32) for slot in range(2)]
        phasor_rows = [pl.ds(pl.multiple_of(table * NF, NF), NF) for table in tables]
        for first in range(0, nodes, chunk):
            at = slice(first, first + chunk)
            got = jnp.dot(left, basis_of(group, at), preferred_element_type=jnp.float32)
            got = got[: 2 * lanes] + got[2 * lanes :]
            for win in range(windows):
                row = win * 2 * NF
                real_sum, imag_sum = sums_ref[row : row + NF, at], sums_ref[row + NF : row + 2 * NF, at]
                for slot, rows in enumerate(phasor_rows):
                    cosine, sine = cos_ref[rows, at], sin_ref[rows, at]
                    real = got[slot * lanes + row : slot * lanes + row + NF]
                    imag = got[slot * lanes + row + NF : slot * lanes + row + 2 * NF]
                    real_sum += real * cosine - imag * sine
                    imag_sum += real * sine + imag * cosine
                sums_ref[row : row + NF, at], sums_ref[row + NF : row + 2 * NF, at] = real_sum, imag_sum

    for copy in copies[3:]:
        copy.wait()

    def body(pair, carry):
        add_group(pair * 2)
        add_group(pair * 2 + 1)
        return carry

    lax.fori_loop(0, used // 2, body, 0)

    @pl.when(used % 2 == 1)
    def _():
        add_group(used - 1)

    powers = []
    for win in range(windows):
        row = win * 2 * NF
        real, imag = sums_ref[row : row + NF, :], sums_ref[row + NF : row + 2 * NF, :]
        powers.append(real * real + imag * imag)
    mine = lax.axis_index("win") == 0
    keep_ref[...] = jnp.where(mine, powers[0], powers[1])
    send_ref[...] = jnp.where(mine, powers[1], powers[0])


def finish_kernel(stations, keep_ref, got_ref, spectrum_ref, beam_ref):
    nodes = keep_ref.shape[1]
    win = lax.axis_index("win")
    for place, ref in ((win, keep_ref), (1 - win, got_ref)):
        power = ref[...]
        total = jnp.sum(power, axis=0, keepdims=True)
        at = pl.ds(pl.multiple_of(place * nodes, LANES), nodes)
        spectrum_ref[:, at] = power * (NF / total)
        beam_ref[:, at] = total * (1.0 / (NF * stations))


def on_device(traces, tables, corrections, station_table, node_ids, freq_bins):
    windows, groups, cores = (lax.axis_size(a) for a in ("win", "sta", "freq"))
    stations_dev, grid = corrections.shape
    stations = stations_dev * groups
    devices = windows * groups * cores
    nodes = grid // devices
    ntab = tables.shape[0]
    params = lambda free: pltpu.CompilerParams(vmem_limit_bytes=VMEM_LIMIT - free)
    vmem = pl.BlockSpec(memory_space=pltpu.VMEM)
    hbm = pl.BlockSpec(memory_space=pltpu.HBM)
    bins = freq_bins.reshape(1, NF)
    bins_scratch = pltpu.VMEM((1, NF), jnp.int32)

    holders = windows * cores
    merged = nodes % (holders * LANES) == 0
    pieces = nodes // (holders * LANES) if merged else 0
    height = pieces * stations_dev + 8
    blocks = pl.pallas_call(
        functools.partial(send_kernel, nodes),
        out_shape=jax.ShapeDtypeStruct((devices, height, LANES), jnp.bfloat16),
        in_specs=[hbm] * 3,
        out_specs=vmem,
        scratch_shapes=[
            bins_scratch,
            pltpu.VMEM(traces.shape, traces.dtype),
            pltpu.SemaphoreType.DMA((3,)),
        ],
        compiler_params=params(0),
        name="send",
    )(bins, traces, corrections)
    received = [lax.all_to_all(blocks, ("win", "sta", "freq"), split_axis=0, concat_axis=0, tiled=True)]
    if not merged:
        parts = corrections.reshape(stations_dev, groups, holders, nodes)
        place = lax.axis_index("freq") * windows + lax.axis_index("win")
        mine = lax.dynamic_index_in_dim(parts, place, axis=2, keepdims=False)
        corr = lax.all_to_all(mine.transpose(1, 0, 2), "sta", split_axis=0, concat_axis=0, tiled=True)
        received.append(corr.reshape(stations, nodes))

    wide = 512
    plan_width = max(LANES, stations)
    phasors = pltpu.VMEM((ntab * NF, nodes), jnp.float32)
    coefs = pltpu.VMEM((DEGREES, LANES), jnp.float32)
    plan = pltpu.VMEM((8, plan_width), jnp.float32)
    packed_shape = (packed_rows(ntab)[-1].stop, max(nodes, plan_width))
    packed = pl.pallas_call(
        prepare_kernel,
        out_shape=jax.ShapeDtypeStruct(packed_shape, jnp.float32),
        in_specs=[hbm] * 4,
        out_specs=hbm,
        scratch_shapes=[
            bins_scratch,
            pltpu.VMEM((1, stations), jnp.int32),
            pltpu.VMEM((max(nodes // LANES, 8), LANES), jnp.int32),
            pltpu.VMEM(tables.shape, tables.dtype),
            phasors,
            phasors,
            coefs,
            plan,
            pltpu.VMEM((grid // wide * ntab, 3 * wide), jnp.bfloat16),
            pltpu.VMEM((3 * wide, nodes), jnp.bfloat16),
            pltpu.SemaphoreType.DMA((3 + 2 * ntab,)),
            pltpu.SemaphoreType.DMA((TABLE_PIECES,)),
        ],
        compiler_params=params(512 * 1024),
        name="prepare",
    )(bins, station_table.reshape(1, stations), node_ids.reshape(grid // LANES, LANES), tables)

    places = (stations // 8 + ntab // 2 + 3) // 2 * 16
    half = jax.ShapeDtypeStruct((NF, nodes), jnp.float32)
    rows = 2 * windows * 2 * NF
    keep, send = pl.pallas_call(
        functools.partial(image_kernel, merged, stations_dev),
        out_shape=[half, half],
        in_specs=[hbm] + [vmem] * len(received),
        out_specs=[vmem, vmem],
        scratch_shapes=[
            pltpu.SMEM((8, plan_width), jnp.float32),
            plan,
            coefs,
            phasors,
            phasors,
            pltpu.SemaphoreType.DMA((3 + ntab // 2,)),
            pltpu.VMEM((places, nodes), jnp.float32),
            pltpu.VMEM((places, rows), jnp.float32),
            pltpu.VMEM((places // 8, 2 * rows, 2 * DEGREES * 8), jnp.bfloat16),
            pltpu.VMEM((rows // 2, nodes), jnp.float32),
        ],
        compiler_params=params(23 * 512 * 1024),
        name="image",
    )(packed, *received)
    got = lax.ppermute(send, "win", [(0, 1), (1, 0)])
    spectrum, beam_power = pl.pallas_call(
        functools.partial(finish_kernel, stations),
        out_shape=[
            jax.ShapeDtypeStruct((NF, windows * nodes), jnp.float32),
            jax.ShapeDtypeStruct((1, windows * nodes), jnp.float32),
        ],
        in_specs=[vmem, vmem],
        out_specs=[vmem, vmem],
        compiler_params=params(32 * 1024 * 1024),
        name="finish",
    )(keep, got)
    return spectrum, beam_power.reshape(windows * nodes)


def solution(mesh):
    return jax.shard_map(
        on_device,
        mesh=mesh,
        in_specs=(P(("win", "sta"), "freq"), P(), P("sta", None), P(), P(), P()),
        out_specs=(P("win", ("sta", "freq")), P(("win", "sta", "freq"))),
        check_vma=False,
    )
```

```python
import functools
import math

import jax
import jax.numpy as jnp
import numpy as np
from jax import lax
from jax.experimental import pallas as pl
from jax.experimental.pallas import tpu as pltpu
from jax.sharding import PartitionSpec as P

NT = 5120
NF = 16
NTAB = 16
LANES = 128
DEGREES = 32
FINE = 24
REACH = 1.5
TABLE_PIECES = 4
VMEM_LIMIT = 64 * 1024 * 1024 - 64 * 1024


def chebyshev_fit(func, degree, low, high):
    fit = np.polynomial.chebyshev.Chebyshev.interpolate(func, degree, domain=[low, high])
    return [float(v) for v in fit.convert(kind=np.polynomial.Polynomial).coef]


SIN_HALF = chebyshev_fit(lambda z: np.pi * np.sinc(np.sqrt(z)), 4, 0.0, 0.25)
COS_HALF = chebyshev_fit(lambda z: np.cos(np.pi * np.sqrt(z)), 4, 0.0, 0.25)


def horner(coefs, arg):
    total = coefs[-1]
    for coef in coefs[-2::-1]:
        total = total * arg + coef
    return total


def turn_parts(rest):
    square = rest * rest
    root = math.sqrt(2.0)
    sine_half = rest * horner([root * c for c in SIN_HALF], square)
    cos_half = horner([root * c for c in COS_HALF], square)
    return sine_half * sine_half, sine_half * cos_half


def cos_sin(turns):
    versine, sine = turn_parts(turns - jnp.round(turns))
    return 1.0 - versine, sine


def bins_column(bins_ref):
    rows = lax.broadcasted_iota(jnp.int32, (NF, NF), 0)
    lanes = lax.broadcasted_iota(jnp.int32, (NF, NF), 1)
    square = jnp.broadcast_to(bins_ref[...].astype(jnp.float32), (NF, NF))
    return jnp.sum(jnp.where(rows == lanes, square, 0.0), axis=1, keepdims=True)


def split_bf16(value, terms):
    pieces = []
    for term in range(terms):
        piece = value.astype(jnp.bfloat16)
        pieces.append(piece)
        if term < terms - 1:
            value = value - piece.astype(jnp.float32)
    return pieces


def start_all(copies):
    for copy in copies:
        copy.start()
    return copies


def send_kernel(nodes, bins_hbm, traces_hbm, corr_hbm, out_hbm, out_ref, bins_ref, traces_ref, sems):
    devices, height, _ = out_ref.shape
    stations_dev, half_length = traces_ref.shape
    pieces = (height - 8) // stations_dev
    windows, groups, cores = (lax.axis_size(a) for a in ("win", "sta", "freq"))
    place = lax.axis_index("win") * cores + lax.axis_index("freq")
    small = start_all(
        [
            pltpu.make_async_copy(bins_hbm, bins_ref, sems.at[0]),
            pltpu.make_async_copy(traces_hbm, traces_ref, sems.at[1]),
        ]
    )
    copies = []
    for dev in range(devices):
        win, sta, core = dev // (groups * cores), dev // cores % groups, dev % cores
        first = ((sta * cores + core) * windows + win) * nodes
        for piece in range(pieces):
            at = pl.multiple_of(first + (place * pieces + piece) * LANES, LANES)
            to = out_ref.at[dev, pl.ds(piece * stations_dev, stations_dev), :]
            copies.append(pltpu.make_async_copy(corr_hbm.at[:, pl.ds(at, LANES)], to, sems.at[2]))
    start_all(copies)
    start = lax.axis_index("freq") * half_length
    small[0].wait()
    bins = bins_column(bins_ref)
    pos = (start + lax.broadcasted_iota(jnp.int32, (NF, half_length), 1)).astype(jnp.float32)
    product = bins * pos
    turns = jnp.round(product * (1.0 / NT))
    rest = (product - turns * NT) * (1.0 / NT)
    versine, sine = turn_parts(rest)
    scale = 1.0 / math.sqrt(NT)
    table = jnp.concatenate([(1.0 - versine) * scale, sine * -scale], axis=0)
    both = jnp.concatenate(split_bf16(table, 2), axis=0)
    parts = [pl.ds(0, height - 8), pl.ds(height - 8, 8)]
    outs = [
        pltpu.make_async_copy(out_ref.at[:, part, :], out_hbm.at[:, part, :], sems.at[3 + at])
        for at, part in enumerate(parts)
    ]
    if copies:
        filled = out_ref.at[:, parts[0], :]
        pltpu.make_async_copy(filled, filled, sems.at[2]).wait()
        outs[0].start()
    small[1].wait()
    sums = lax.dot_general(
        both, traces_ref[...], (((1,), (1,)), ((), ())), preferred_element_type=jnp.float32
    )
    sums = (sums[: 2 * NF] + sums[2 * NF :]).T
    terms = [term.astype(jnp.float32) for term in split_bf16(sums, 2)]
    tile = jnp.concatenate([term[at : at + 8] for term in terms for at in range(0, stations_dev, 8)], axis=1)
    tile = tile.astype(jnp.bfloat16)
    for dev in range(devices):
        out_ref[dev, height - 8 :, :] = tile
    outs[1].start()
    for copy in outs if copies else outs[1:]:
        copy.wait()


def own_place():
    windows, cores = lax.axis_size("win"), lax.axis_size("freq")
    return (lax.axis_index("sta") * cores + lax.axis_index("freq")) * windows + lax.axis_index("win")


def pick_columns(ids_ref, tables_ref, table_copies, nodes, left_ref, right_ref):
    ntab, grid = tables_ref.shape
    count = nodes // LANES
    wide = right_ref.shape[0] // 3
    blocks = grid // wide
    ids = ids_ref[pl.ds(own_place() * count % ids_ref.shape[0], count), :]
    ids = jnp.concatenate([ids[at : at + 1] for at in range(count)], axis=1)
    low, high = ids & (wide - 1), ids >> (wide.bit_length() - 1)
    spots = lax.broadcasted_iota(jnp.int32, (wide, nodes), 0)
    ones = jnp.where(spots == low, 1.0, 0.0).astype(jnp.bfloat16)
    for term in range(3):
        right_ref[term * wide : (term + 1) * wide, :] = ones
    found = jnp.zeros((ntab, nodes), jnp.float32)
    step = blocks // len(table_copies)
    for at, copy in enumerate(table_copies):
        copy.wait()
        for block in range(at * step, (at + 1) * step):
            pieces = split_bf16(tables_ref[:, block * wide : (block + 1) * wide], 3)
            left_ref[block * ntab : (block + 1) * ntab, :] = jnp.concatenate(pieces, axis=1)
        rows = left_ref[at * step * ntab : (at + 1) * step * ntab, :]
        picked = jnp.dot(rows, right_ref[...], preferred_element_type=jnp.float32)
        for block in range(step):
            part = picked[block * ntab : (block + 1) * ntab]
            found = jnp.where(high == at * step + block, part, found)
    return found


def product_coefs(bins_ref):
    shape = (DEGREES, DEGREES)
    degree = lax.broadcasted_iota(jnp.int32, shape, 0)
    node = lax.broadcasted_iota(jnp.int32, shape, 1)
    period = 4 * DEGREES
    weight, _ = cos_sin((degree * (2 * node + 1) & (period - 1)).astype(jnp.float32) * (1.0 / period))
    weight = weight * jnp.where(degree == 0, 1.0 / DEGREES, 2.0 / DEGREES)
    even = jnp.where(degree % 2 == 0, weight, 0.0)
    odd = jnp.where(degree % 2 == 1, weight, 0.0)
    row = bins_ref[...].astype(jnp.float32)
    bins = jnp.concatenate([row] * (LANES // NF), axis=1)
    at = lax.broadcasted_iota(jnp.int32, (DEGREES, LANES), 0).astype(jnp.float32)
    spot, _ = cos_sin((2.0 * at + 1.0) * (1.0 / period))
    cosine, sine = cos_sin(bins * (spot * (REACH / 256.0)))
    dot = functools.partial(jnp.dot, precision=lax.Precision.HIGHEST, preferred_element_type=jnp.float32)
    coefs = dot(even, cosine) + dot(odd, sine)
    for first in range(DEGREES - 8, 0, -8):
        mirror = (degree + node == 2 * first) & (node > first) & (node < first + 8)
        coefs = coefs - dot(jnp.where(mirror, 1.0, 0.0), coefs)
    twice = (at >= 8.0) & ((at.astype(jnp.int32) & 7) != 0)
    return jnp.where(twice, 2.0 * coefs, coefs)


def station_plan(table_row, width):
    count = table_row.shape[1]
    shape = (count, count)
    here = lax.broadcasted_iota(jnp.int32, shape, 0)
    there = lax.broadcasted_iota(jnp.int32, shape, 1)
    column_of = lambda row: jnp.sum(jnp.where(here == there, jnp.broadcast_to(row, shape), 0), axis=1, keepdims=True)
    table_column = column_of(table_row)
    same = (table_column == table_row) & (here < there)
    within = jnp.sum(jnp.where(same, 1, 0), axis=0, keepdims=True)
    place_row = within
    spot = jnp.zeros((1, 1), jnp.int32)
    held = jnp.zeros((1, 1), jnp.int32)
    for table in range(NTAB):
        size = jnp.sum(jnp.where(table_row == table, 1, 0), axis=1, keepdims=True)
        some = size > 0
        edge = (spot & 7) == 0
        skip = some & (held >= 2) & ~edge
        spot = jnp.where(skip, (spot + 7) >> 3 << 3, spot)
        held = jnp.where(skip | edge, 0, held)
        after = spot + size
        place_row = place_row + jnp.where(table_row == table, spot, 0)
        held = jnp.where(some, jnp.where(after >> 3 == spot >> 3, held + 1, 1), held)
        spot = after
    groups = (spot + 7) >> 3
    place_column = column_of(place_row)
    group = lax.broadcasted_iota(jnp.int32, (count, width), 1)
    inside = place_column >> 3 == group
    first = jnp.sum(jnp.where(place_column == group * 8, table_column, 0), axis=0, keepdims=True)
    last = jnp.max(jnp.where(inside, table_column, 0), axis=0, keepdims=True)
    length = jnp.sum(jnp.where(inside & (table_column == first), 1, 0), axis=0, keepdims=True)
    rows = [first, last, length, jnp.broadcast_to(groups, (1, width))]
    if width > count:
        place_row = jnp.concatenate([place_row, jnp.zeros((1, width - count), jnp.int32)], axis=1)
    rows += [place_row, jnp.zeros((3, width), jnp.int32)]
    return jnp.concatenate(rows, axis=0).astype(jnp.float32)


def packed_rows(ntab):
    ends = [ntab * NF, 2 * ntab * NF, 2 * ntab * NF + DEGREES, 2 * ntab * NF + DEGREES + 8]
    return [slice(start, end) for start, end in zip([0] + ends, ends)]


def prepare_kernel(bins_hbm, table_hbm, ids_hbm, tables_hbm, out_hbm, *rest):
    bins_ref, table_ref, ids_ref, tables_ref, cos_ref, sin_ref, coef_ref, plan_ref = rest[:8]
    left_ref, right_ref, sems, table_sems = rest[8:]
    ntab = tables_ref.shape[0]
    nodes = cos_ref.shape[1]
    near = ids_ref.shape[0]
    first = pl.multiple_of(own_place() * (nodes // LANES) // near * near, 8)
    ins = start_all(
        [
            pltpu.make_async_copy(ids_hbm.at[pl.ds(first, near), :], ids_ref, sems.at[0]),
            pltpu.make_async_copy(bins_hbm, bins_ref, sems.at[1]),
            pltpu.make_async_copy(table_hbm, table_ref, sems.at[2]),
        ]
    )
    piece = tables_ref.shape[1] // TABLE_PIECES
    table_copies = []
    for at in range(TABLE_PIECES):
        part = (slice(None), pl.ds(at * piece, piece))
        table_copies.append(pltpu.make_async_copy(tables_hbm.at[part], tables_ref.at[part], table_sems.at[at]))
    start_all(table_copies)
    for copy in ins:
        copy.wait()
    cos_at, sin_at, coef_at, plan_at = packed_rows(ntab)
    coef_ref[...] = product_coefs(bins_ref)
    plan_ref[...] = station_plan(table_ref[...], plan_ref.shape[1])
    outs = start_all(
        [
            pltpu.make_async_copy(coef_ref, out_hbm.at[coef_at, pl.ds(0, LANES)], sems.at[0]),
            pltpu.make_async_copy(plan_ref, out_hbm.at[plan_at, pl.ds(0, plan_ref.shape[1])], sems.at[1]),
        ]
    )
    turns = pick_columns(ids_ref, tables_ref, table_copies, nodes, left_ref, right_ref) * (1.0 / 256.0)
    bins = bins_column(bins_ref)
    for table in range(ntab):
        cosine, sine = cos_sin(bins * turns[table : table + 1])
        at = pl.ds(table * NF, NF)
        cos_ref[at, :] = cosine
        sin_ref[at, :] = sine
        outs += start_all(
            [
                pltpu.make_async_copy(
                    cos_ref.at[at, :], out_hbm.at[pl.ds(cos_at.start + table * NF, NF), pl.ds(0, nodes)],
                    sems.at[3 + 2 * table],
                ),
                pltpu.make_async_copy(
                    sin_ref.at[at, :], out_hbm.at[pl.ds(sin_at.start + table * NF, NF), pl.ds(0, nodes)],
                    sems.at[4 + 2 * table],
                ),
            ]
        )
    for copy in outs:
        copy.wait()


def image_kernel(merged, stations_dev, packed_hbm, block_ref, *rest):
    corr_ref, rest = (None, rest) if merged else (rest[0], rest[1:])
    keep_ref, send_ref, plan_ref, place_of_ref, coef_ref, cos_ref, sin_ref, sems = rest[:8]
    place_ref, weight_ref, left_ref, sums_ref = rest[8:]
    places, nodes = place_ref.shape
    windows, groups, cores = (lax.axis_size(a) for a in ("win", "sta", "freq"))
    stations = stations_dev * groups
    cos_at, sin_at, coef_at, plan_at = packed_rows(cos_ref.shape[0] // NF)
    width = plan_ref.shape[1]
    copies = start_all(
        [
            pltpu.make_async_copy(packed_hbm.at[plan_at, pl.ds(0, width)], place_of_ref, sems.at[0]),
            pltpu.make_async_copy(packed_hbm.at[plan_at, pl.ds(0, width)], plan_ref, sems.at[1]),
            pltpu.make_async_copy(packed_hbm.at[coef_at, pl.ds(0, LANES)], coef_ref, sems.at[2]),
        ]
        + [
            pltpu.make_async_copy(
                packed_hbm.at[pl.ds(at.start + first, 4 * NF), pl.ds(0, nodes)],
                ref.at[pl.ds(first, 4 * NF), :],
                sems.at[3 + 2 * (first // (4 * NF)) + which],
            )
            for first in range(0, NTAB * NF, 4 * NF)
            for which, (at, ref) in enumerate(((cos_at, cos_ref), (sin_at, sin_ref)))
        ]
    )
    height = block_ref.shape[1]
    rows_of = lambda win, core: [(win * groups + group) * cores + core for group in range(groups)]

    even, odd = [], []
    for win in range(windows):
        value = []
        for group in range(groups):
            tile = None
            for core in range(cores):
                part = block_ref[(win * groups + group) * cores + core, height - 8 :, :].astype(jnp.float32)
                tile = part if tile is None else tile + part
            tile = tile[:, : LANES // 2] + tile[:, LANES // 2 :]
            value += [tile[:, 2 * NF * piece : 2 * NF * (piece + 1)] for piece in range(stations_dev // 8)]
        value = jnp.concatenate(value, axis=0)
        even.append(value)
        odd.append(jnp.concatenate([-value[:, NF:], value[:, :NF]], axis=1))
    spectra = jnp.concatenate(even + odd, axis=1)
    if merged:
        parts = []
        for win in range(windows):
            for core in range(cores):
                for first in range(0, height - 8, stations_dev):
                    rows = [block_ref[at, first : first + stations_dev, :] for at in rows_of(win, core)]
                    parts.append(jnp.concatenate(rows, axis=0))
        corr = jnp.concatenate(parts, axis=1)
    else:
        corr = corr_ref[...]

    copies[0].wait()
    place_row = place_of_ref[4:5, :stations].astype(jnp.int32)
    sorter = lax.broadcasted_iota(jnp.int32, (places, stations), 0) == place_row
    sorter = jnp.where(sorter, 1.0, 0.0).astype(jnp.bfloat16)
    found = None
    for piece in split_bf16(spectra, 3):
        part = jnp.dot(sorter, piece, preferred_element_type=jnp.float32)
        found = part if found is None else found + part
    weight_ref[...] = found
    place_ref[...] = jnp.dot(sorter, corr, preferred_element_type=jnp.float32) * (1.0 / REACH)
    sums_ref[...] = jnp.zeros_like(sums_ref)
    chunk = min(256, nodes)
    depth = DEGREES * 8
    lanes = windows * 2 * NF
    for copy in copies[1:3]:
        copy.wait()

    spot = (lax.broadcasted_iota(jnp.int32, (lanes, LANES), 1) & 7).astype(jnp.float32)

    def make_left(pair):
        top = weight_ref[pl.ds(pl.multiple_of(pair * 16, 16), 8), :]
        bottom = weight_ref[pl.ds(pl.multiple_of(pair * 16 + 8, 8), 8), :]
        sides = [
            jnp.concatenate([top[:, :lanes], bottom[:, :lanes]], axis=1),
            jnp.concatenate([top[:, lanes:], bottom[:, lanes:]], axis=1),
        ]
        per = LANES // 8
        for half in range(DEGREES // per):
            tall = jnp.concatenate(
                [sides[k % 2] * coef_ref[k : k + 1, :] for k in range(half * per, (half + 1) * per)], axis=0
            )
            turned = tall.T
            first = half * LANES
            fine = min(FINE * 8 - first, LANES)
            for which in range(2):
                group = 2 * pair + which
                mask = spot < plan_ref[2, group]
                value = turned[which * lanes : (which + 1) * lanes]
                value = jnp.concatenate([jnp.where(mask, value, 0.0), jnp.where(mask, 0.0, value)], axis=0)
                high, low = split_bf16(value, 2)
                if fine == LANES:
                    parts = [(first, high), (depth + first, high), (2 * FINE * 8 + first + LANES, low)]
                else:
                    mixed = [high[:, :fine].astype(jnp.float32), low[:, :fine].astype(jnp.float32)]
                    parts = [(first, high), (depth + first, jnp.concatenate(mixed, axis=1).astype(jnp.bfloat16))]
                for at, part in parts:
                    left_ref[group, :, at : at + LANES] = part

    used = plan_ref[3, 0].astype(jnp.int32)
    sure = stations // 16
    if sure <= 8:
        for pair in range(sure):
            make_left(pair)
    else:
        lax.fori_loop(0, sure, lambda pair, carry: (make_left(pair), carry)[1], 0)
    lax.fori_loop(sure, (used + 1) // 2, lambda pair, carry: (make_left(pair), carry)[1], 0)
    def basis_of(group, at):
        arg = place_ref[pl.ds(pl.multiple_of(group * 8, 8), 8), at]
        twice = arg + arg
        low = [jnp.ones_like(arg), arg]
        while len(low) < 8:
            low.append(twice * low[-1] - low[-2])
        eight = (low[4] + low[4]) * low[4] - 1.0
        sixteen = (eight + eight) * eight - 1.0
        steps = [None, eight, sixteen, (sixteen + sixteen - 1.0) * eight]
        terms = [[], []]
        for degree in range(0, DEGREES, 2):
            pair = []
            for factor in low[degree % 8 : degree % 8 + 2]:
                step = steps[degree // 8]
                pair.append(factor if step is None else step if factor is low[0] else factor * step)
            pair = jnp.concatenate(pair, axis=0)
            for term, value in enumerate(split_bf16(pair, 2 if degree < FINE else 1)):
                terms[term].append(value)
        high, low = terms
        return jnp.concatenate(high + low + high[8 : FINE // 2] + high[:8], axis=0)

    def add_group(group):
        left = left_ref[group]
        tables = [plan_ref[slot, group].astype(jnp.int32) for slot in range(2)]
        phasor_rows = [pl.ds(pl.multiple_of(table * NF, NF), NF) for table in tables]
        for first in range(0, nodes, chunk):
            at = slice(first, first + chunk)
            got = jnp.dot(left, basis_of(group, at), preferred_element_type=jnp.float32)
            for win in range(windows):
                row = win * 2 * NF
                real_sum, imag_sum = sums_ref[row : row + NF, at], sums_ref[row + NF : row + 2 * NF, at]
                for slot, rows in enumerate(phasor_rows):
                    cosine, sine = cos_ref[rows, at], sin_ref[rows, at]
                    real = got[slot * lanes + row : slot * lanes + row + NF]
                    imag = got[slot * lanes + row + NF : slot * lanes + row + 2 * NF]
                    real_sum += real * cosine - imag * sine
                    imag_sum += real * sine + imag * cosine
                sums_ref[row : row + NF, at], sums_ref[row + NF : row + 2 * NF, at] = real_sum, imag_sum

    for copy in copies[3:]:
        copy.wait()

    def body(pair, carry):
        add_group(pair * 2)
        add_group(pair * 2 + 1)
        return carry

    lax.fori_loop(0, used // 2, body, 0)

    @pl.when(used % 2 == 1)
    def _():
        add_group(used - 1)

    powers = []
    for win in range(windows):
        row = win * 2 * NF
        real, imag = sums_ref[row : row + NF, :], sums_ref[row + NF : row + 2 * NF, :]
        powers.append(real * real + imag * imag)
    mine = lax.axis_index("win") == 0
    keep_ref[...] = jnp.where(mine, powers[0], powers[1])
    send_ref[...] = jnp.where(mine, powers[1], powers[0])


def finish_kernel(stations, keep_ref, got_ref, spectrum_ref, beam_ref):
    nodes = keep_ref.shape[1]
    win = lax.axis_index("win")
    for place, ref in ((win, keep_ref), (1 - win, got_ref)):
        power = ref[...]
        total = jnp.sum(power, axis=0, keepdims=True)
        at = pl.ds(pl.multiple_of(place * nodes, LANES), nodes)
        spectrum_ref[:, at] = power * (NF / total)
        beam_ref[:, at] = total * (1.0 / (NF * stations))


def on_device(traces, tables, corrections, station_table, node_ids, freq_bins):
    windows, groups, cores = (lax.axis_size(a) for a in ("win", "sta", "freq"))
    stations_dev, grid = corrections.shape
    stations = stations_dev * groups
    devices = windows * groups * cores
    nodes = grid // devices
    ntab = tables.shape[0]
    params = lambda free: pltpu.CompilerParams(vmem_limit_bytes=VMEM_LIMIT - free)
    vmem = pl.BlockSpec(memory_space=pltpu.VMEM)
    hbm = pl.BlockSpec(memory_space=pltpu.HBM)
    bins = freq_bins.reshape(1, NF)
    bins_scratch = pltpu.VMEM((1, NF), jnp.int32)

    holders = windows * cores
    merged = nodes % (holders * LANES) == 0
    pieces = nodes // (holders * LANES) if merged else 0
    height = pieces * stations_dev + 8
    blocks = pl.pallas_call(
        functools.partial(send_kernel, nodes),
        out_shape=jax.ShapeDtypeStruct((devices, height, LANES), jnp.bfloat16),
        in_specs=[hbm] * 3,
        out_specs=hbm,
        scratch_shapes=[
            pltpu.VMEM((devices, height, LANES), jnp.bfloat16),
            bins_scratch,
            pltpu.VMEM(traces.shape, traces.dtype),
            pltpu.SemaphoreType.DMA((5,)),
        ],
        compiler_params=params(0),
        name="send",
    )(bins, traces, corrections)
    received = [lax.all_to_all(blocks, ("win", "sta", "freq"), split_axis=0, concat_axis=0, tiled=True)]
    if not merged:
        parts = corrections.reshape(stations_dev, groups, holders, nodes)
        place = lax.axis_index("freq") * windows + lax.axis_index("win")
        mine = lax.dynamic_index_in_dim(parts, place, axis=2, keepdims=False)
        corr = lax.all_to_all(mine.transpose(1, 0, 2), "sta", split_axis=0, concat_axis=0, tiled=True)
        received.append(corr.reshape(stations, nodes))

    wide = 512
    plan_width = max(LANES, stations)
    phasors = pltpu.VMEM((ntab * NF, nodes), jnp.float32)
    coefs = pltpu.VMEM((DEGREES, LANES), jnp.float32)
    plan = pltpu.VMEM((8, plan_width), jnp.float32)
    packed_shape = (packed_rows(ntab)[-1].stop, max(nodes, plan_width))
    packed = pl.pallas_call(
        prepare_kernel,
        out_shape=jax.ShapeDtypeStruct(packed_shape, jnp.float32),
        in_specs=[hbm] * 4,
        out_specs=hbm,
        scratch_shapes=[
            bins_scratch,
            pltpu.VMEM((1, stations), jnp.int32),
            pltpu.VMEM((max(nodes // LANES, 8), LANES), jnp.int32),
            pltpu.VMEM(tables.shape, tables.dtype),
            phasors,
            phasors,
            coefs,
            plan,
            pltpu.VMEM((grid // wide * ntab, 3 * wide), jnp.bfloat16),
            pltpu.VMEM((3 * wide, nodes), jnp.bfloat16),
            pltpu.SemaphoreType.DMA((3 + 2 * ntab,)),
            pltpu.SemaphoreType.DMA((TABLE_PIECES,)),
        ],
        compiler_params=params(512 * 1024),
        name="prepare",
    )(bins, station_table.reshape(1, stations), node_ids.reshape(grid // LANES, LANES), tables)

    places = (stations // 8 + ntab // 2 + 3) // 2 * 16
    half = jax.ShapeDtypeStruct((NF, nodes), jnp.float32)
    rows = 2 * windows * 2 * NF
    keep, send = pl.pallas_call(
        functools.partial(image_kernel, merged, stations_dev),
        out_shape=[half, half],
        in_specs=[hbm] + [vmem] * len(received),
        out_specs=[vmem, vmem],
        scratch_shapes=[
            pltpu.SMEM((8, plan_width), jnp.float32),
            plan,
            coefs,
            phasors,
            phasors,
            pltpu.SemaphoreType.DMA((3 + ntab // 2,)),
            pltpu.VMEM((places, nodes), jnp.float32),
            pltpu.VMEM((places, rows), jnp.float32),
            pltpu.VMEM((places // 8, rows, (DEGREES + 2 * FINE) * 8), jnp.bfloat16),
            pltpu.VMEM((rows // 2, nodes), jnp.float32),
        ],
        compiler_params=params(23 * 512 * 1024),
        name="image",
    )(packed, *received)
    got = lax.ppermute(send, "win", [(0, 1), (1, 0)])
    spectrum, beam_power = pl.pallas_call(
        functools.partial(finish_kernel, stations),
        out_shape=[
            jax.ShapeDtypeStruct((NF, windows * nodes), jnp.float32),
            jax.ShapeDtypeStruct((1, windows * nodes), jnp.float32),
        ],
        in_specs=[vmem, vmem],
        out_specs=[vmem, vmem],
        compiler_params=params(32 * 1024 * 1024),
        name="finish",
    )(keep, got)
    return spectrum, beam_power.reshape(windows * nodes)


def solution(mesh):
    return jax.shard_map(
        on_device,
        mesh=mesh,
        in_specs=(P(("win", "sta"), "freq"), P(), P("sta", None), P(), P(), P()),
        out_specs=(P("win", ("sta", "freq")), P(("win", "sta", "freq"))),
        check_vma=False,
    )
```

```python
import functools
import math

import jax
import jax.numpy as jnp
import numpy as np
from jax import lax
from jax.experimental import pallas as pl
from jax.experimental.pallas import tpu as pltpu
from jax.sharding import PartitionSpec as P

NT = 5120
NF = 16
NTAB = 16
LANES = 128
DEGREES = 32
FINE = 24
REACH = 1.5
TABLE_PIECES = 4
VMEM_LIMIT = 64 * 1024 * 1024 - 64 * 1024


def chebyshev_fit(func, degree, low, high):
    fit = np.polynomial.chebyshev.Chebyshev.interpolate(func, degree, domain=[low, high])
    return [float(v) for v in fit.convert(kind=np.polynomial.Polynomial).coef]


SIN_HALF = chebyshev_fit(lambda z: np.pi * np.sinc(np.sqrt(z)), 4, 0.0, 0.25)
COS_HALF = chebyshev_fit(lambda z: np.cos(np.pi * np.sqrt(z)), 4, 0.0, 0.25)


def horner(coefs, arg):
    total = coefs[-1]
    for coef in coefs[-2::-1]:
        total = total * arg + coef
    return total


def turn_parts(rest):
    square = rest * rest
    root = math.sqrt(2.0)
    sine_half = rest * horner([root * c for c in SIN_HALF], square)
    cos_half = horner([root * c for c in COS_HALF], square)
    return sine_half * sine_half, sine_half * cos_half


def cos_sin(turns):
    versine, sine = turn_parts(turns - jnp.round(turns))
    return 1.0 - versine, sine


def bins_column(bins_ref):
    rows = lax.broadcasted_iota(jnp.int32, (NF, NF), 0)
    lanes = lax.broadcasted_iota(jnp.int32, (NF, NF), 1)
    square = jnp.broadcast_to(bins_ref[...].astype(jnp.float32), (NF, NF))
    return jnp.sum(jnp.where(rows == lanes, square, 0.0), axis=1, keepdims=True)


def split_bf16(value, terms):
    pieces = []
    for term in range(terms):
        piece = value.astype(jnp.bfloat16)
        pieces.append(piece)
        if term < terms - 1:
            value = value - piece.astype(jnp.float32)
    return pieces


def start_all(copies):
    for copy in copies:
        copy.start()
    return copies


def send_kernel(nodes, bins_hbm, traces_hbm, corr_hbm, out_ref, bins_ref, traces_ref, sems):
    devices, height, _ = out_ref.shape
    stations_dev, half_length = traces_ref.shape
    pieces = (height - 8) // stations_dev
    windows, groups, cores = (lax.axis_size(a) for a in ("win", "sta", "freq"))
    place = lax.axis_index("win") * cores + lax.axis_index("freq")
    small = start_all(
        [
            pltpu.make_async_copy(bins_hbm, bins_ref, sems.at[0]),
            pltpu.make_async_copy(traces_hbm, traces_ref, sems.at[1]),
        ]
    )
    copies = []
    for dev in range(devices):
        win, sta, core = dev // (groups * cores), dev // cores % groups, dev % cores
        first = ((sta * cores + core) * windows + win) * nodes
        for piece in range(pieces):
            at = pl.multiple_of(first + (place * pieces + piece) * LANES, LANES)
            to = out_ref.at[dev, pl.ds(piece * stations_dev, stations_dev), :]
            copies.append(pltpu.make_async_copy(corr_hbm.at[:, pl.ds(at, LANES)], to, sems.at[2]))
    start_all(copies)
    start = lax.axis_index("freq") * half_length
    small[0].wait()
    bins = bins_column(bins_ref)
    pos = (start + lax.broadcasted_iota(jnp.int32, (NF, half_length), 1)).astype(jnp.float32)
    product = bins * pos
    turns = jnp.round(product * (1.0 / NT))
    rest = (product - turns * NT) * (1.0 / NT)
    versine, sine = turn_parts(rest)
    scale = 1.0 / math.sqrt(NT)
    table = jnp.concatenate([(1.0 - versine) * scale, sine * -scale], axis=0)
    both = jnp.concatenate(split_bf16(table, 2), axis=0)
    small[1].wait()
    sums = lax.dot_general(
        both, traces_ref[...], (((1,), (1,)), ((), ())), preferred_element_type=jnp.float32
    )
    sums = (sums[: 2 * NF] + sums[2 * NF :]).T
    terms = [term.astype(jnp.float32) for term in split_bf16(sums, 2)]
    tile = jnp.concatenate([term[at : at + 8] for term in terms for at in range(0, stations_dev, 8)], axis=1)
    tile = tile.astype(jnp.bfloat16)
    for dev in range(devices):
        out_ref[dev, height - 8 :, :] = tile
    if copies:
        filled = out_ref.at[:, pl.ds(0, height - 8), :]
        pltpu.make_async_copy(filled, filled, sems.at[2]).wait()


def own_place():
    windows, cores = lax.axis_size("win"), lax.axis_size("freq")
    return (lax.axis_index("sta") * cores + lax.axis_index("freq")) * windows + lax.axis_index("win")


def pick_columns(ids_ref, tables_ref, table_copies, nodes, left_ref, right_ref):
    ntab, grid = tables_ref.shape
    count = nodes // LANES
    wide = right_ref.shape[0] // 3
    blocks = grid // wide
    ids = ids_ref[pl.ds(own_place() * count % ids_ref.shape[0], count), :]
    ids = jnp.concatenate([ids[at : at + 1] for at in range(count)], axis=1)
    low, high = ids & (wide - 1), ids >> (wide.bit_length() - 1)
    spots = lax.broadcasted_iota(jnp.int32, (wide, nodes), 0)
    ones = jnp.where(spots == low, 1.0, 0.0).astype(jnp.bfloat16)
    for term in range(3):
        right_ref[term * wide : (term + 1) * wide, :] = ones
    found = jnp.zeros((ntab, nodes), jnp.float32)
    step = blocks // len(table_copies)
    for at, copy in enumerate(table_copies):
        copy.wait()
        for block in range(at * step, (at + 1) * step):
            pieces = split_bf16(tables_ref[:, block * wide : (block + 1) * wide], 3)
            left_ref[block * ntab : (block + 1) * ntab, :] = jnp.concatenate(pieces, axis=1)
        rows = left_ref[at * step * ntab : (at + 1) * step * ntab, :]
        picked = jnp.dot(rows, right_ref[...], preferred_element_type=jnp.float32)
        for block in range(step):
            part = picked[block * ntab : (block + 1) * ntab]
            found = jnp.where(high == at * step + block, part, found)
    return found


def product_coefs(bins_ref):
    shape = (DEGREES, DEGREES)
    degree = lax.broadcasted_iota(jnp.int32, shape, 0)
    node = lax.broadcasted_iota(jnp.int32, shape, 1)
    period = 4 * DEGREES
    weight, _ = cos_sin((degree * (2 * node + 1) & (period - 1)).astype(jnp.float32) * (1.0 / period))
    weight = weight * jnp.where(degree == 0, 1.0 / DEGREES, 2.0 / DEGREES)
    even = jnp.where(degree % 2 == 0, weight, 0.0)
    odd = jnp.where(degree % 2 == 1, weight, 0.0)
    row = bins_ref[...].astype(jnp.float32)
    bins = jnp.concatenate([row] * (LANES // NF), axis=1)
    at = lax.broadcasted_iota(jnp.int32, (DEGREES, LANES), 0).astype(jnp.float32)
    spot, _ = cos_sin((2.0 * at + 1.0) * (1.0 / period))
    cosine, sine = cos_sin(bins * (spot * (REACH / 256.0)))
    dot = functools.partial(jnp.dot, precision=lax.Precision.HIGHEST, preferred_element_type=jnp.float32)
    coefs = dot(even, cosine) + dot(odd, sine)
    for first in range(DEGREES - 8, 0, -8):
        mirror = (degree + node == 2 * first) & (node > first) & (node < first + 8)
        coefs = coefs - dot(jnp.where(mirror, 1.0, 0.0), coefs)
    twice = (at >= 8.0) & ((at.astype(jnp.int32) & 7) != 0)
    return jnp.where(twice, 2.0 * coefs, coefs)


def station_plan(table_row, width):
    count = table_row.shape[1]
    shape = (count, count)
    here = lax.broadcasted_iota(jnp.int32, shape, 0)
    there = lax.broadcasted_iota(jnp.int32, shape, 1)
    column_of = lambda row: jnp.sum(jnp.where(here == there, jnp.broadcast_to(row, shape), 0), axis=1, keepdims=True)
    table_column = column_of(table_row)
    same = (table_column == table_row) & (here < there)
    within = jnp.sum(jnp.where(same, 1, 0), axis=0, keepdims=True)
    place_row = within
    spot = jnp.zeros((1, 1), jnp.int32)
    held = jnp.zeros((1, 1), jnp.int32)
    for table in range(NTAB):
        size = jnp.sum(jnp.where(table_row == table, 1, 0), axis=1, keepdims=True)
        some = size > 0
        edge = (spot & 7) == 0
        skip = some & (held >= 2) & ~edge
        spot = jnp.where(skip, (spot + 7) >> 3 << 3, spot)
        held = jnp.where(skip | edge, 0, held)
        after = spot + size
        place_row = place_row + jnp.where(table_row == table, spot, 0)
        held = jnp.where(some, jnp.where(after >> 3 == spot >> 3, held + 1, 1), held)
        spot = after
    groups = (spot + 7) >> 3
    place_column = column_of(place_row)
    group = lax.broadcasted_iota(jnp.int32, (count, width), 1)
    inside = place_column >> 3 == group
    first = jnp.sum(jnp.where(place_column == group * 8, table_column, 0), axis=0, keepdims=True)
    last = jnp.max(jnp.where(inside, table_column, 0), axis=0, keepdims=True)
    length = jnp.sum(jnp.where(inside & (table_column == first), 1, 0), axis=0, keepdims=True)
    rows = [first, last, length, jnp.broadcast_to(groups, (1, width))]
    if width > count:
        place_row = jnp.concatenate([place_row, jnp.zeros((1, width - count), jnp.int32)], axis=1)
    rows += [place_row, jnp.zeros((3, width), jnp.int32)]
    return jnp.concatenate(rows, axis=0).astype(jnp.float32)


def packed_rows(ntab):
    ends = [ntab * NF, 2 * ntab * NF, 2 * ntab * NF + DEGREES, 2 * ntab * NF + DEGREES + 8]
    return [slice(start, end) for start, end in zip([0] + ends, ends)]


def prepare_kernel(bins_hbm, table_hbm, ids_hbm, tables_hbm, out_hbm, *rest):
    bins_ref, table_ref, ids_ref, tables_ref, cos_ref, sin_ref, coef_ref, plan_ref = rest[:8]
    left_ref, right_ref, sems, table_sems = rest[8:]
    ntab = tables_ref.shape[0]
    nodes = cos_ref.shape[1]
    near = ids_ref.shape[0]
    first = pl.multiple_of(own_place() * (nodes // LANES) // near * near, 8)
    ins = start_all(
        [
            pltpu.make_async_copy(ids_hbm.at[pl.ds(first, near), :], ids_ref, sems.at[0]),
            pltpu.make_async_copy(bins_hbm, bins_ref, sems.at[1]),
            pltpu.make_async_copy(table_hbm, table_ref, sems.at[2]),
        ]
    )
    piece = tables_ref.shape[1] // TABLE_PIECES
    table_copies = []
    for at in range(TABLE_PIECES):
        part = (slice(None), pl.ds(at * piece, piece))
        table_copies.append(pltpu.make_async_copy(tables_hbm.at[part], tables_ref.at[part], table_sems.at[at]))
    start_all(table_copies)
    for copy in ins:
        copy.wait()
    cos_at, sin_at, coef_at, plan_at = packed_rows(ntab)
    coef_ref[...] = product_coefs(bins_ref)
    plan_ref[...] = station_plan(table_ref[...], plan_ref.shape[1])
    outs = start_all(
        [
            pltpu.make_async_copy(coef_ref, out_hbm.at[coef_at, pl.ds(0, LANES)], sems.at[0]),
            pltpu.make_async_copy(plan_ref, out_hbm.at[plan_at, pl.ds(0, plan_ref.shape[1])], sems.at[1]),
        ]
    )
    turns = pick_columns(ids_ref, tables_ref, table_copies, nodes, left_ref, right_ref) * (1.0 / 256.0)
    bins = bins_column(bins_ref)
    for table in range(ntab):
        cosine, sine = cos_sin(bins * turns[table : table + 1])
        at = pl.ds(table * NF, NF)
        cos_ref[at, :] = cosine
        sin_ref[at, :] = sine
        outs += start_all(
            [
                pltpu.make_async_copy(
                    cos_ref.at[at, :], out_hbm.at[pl.ds(cos_at.start + table * NF, NF), pl.ds(0, nodes)],
                    sems.at[3 + 2 * table],
                ),
                pltpu.make_async_copy(
                    sin_ref.at[at, :], out_hbm.at[pl.ds(sin_at.start + table * NF, NF), pl.ds(0, nodes)],
                    sems.at[4 + 2 * table],
                ),
            ]
        )
    for copy in outs:
        copy.wait()


def image_kernel(merged, stations_dev, packed_hbm, block_ref, *rest):
    corr_ref, rest = (None, rest) if merged else (rest[0], rest[1:])
    keep_ref, send_ref, plan_ref, place_of_ref, coef_ref, cos_ref, sin_ref, sems = rest[:8]
    place_ref, weight_ref, left_ref, sums_ref, basis_a, basis_b = rest[8:]
    places, nodes = place_ref.shape
    windows, groups, cores = (lax.axis_size(a) for a in ("win", "sta", "freq"))
    stations = stations_dev * groups
    cos_at, sin_at, coef_at, plan_at = packed_rows(cos_ref.shape[0] // NF)
    width = plan_ref.shape[1]
    copies = start_all(
        [
            pltpu.make_async_copy(packed_hbm.at[plan_at, pl.ds(0, width)], place_of_ref, sems.at[0]),
            pltpu.make_async_copy(packed_hbm.at[plan_at, pl.ds(0, width)], plan_ref, sems.at[1]),
            pltpu.make_async_copy(packed_hbm.at[coef_at, pl.ds(0, LANES)], coef_ref, sems.at[2]),
        ]
        + [
            pltpu.make_async_copy(
                packed_hbm.at[pl.ds(at.start + first, 4 * NF), pl.ds(0, nodes)],
                ref.at[pl.ds(first, 4 * NF), :],
                sems.at[3 + 2 * (first // (4 * NF)) + which],
            )
            for first in range(0, NTAB * NF, 4 * NF)
            for which, (at, ref) in enumerate(((cos_at, cos_ref), (sin_at, sin_ref)))
        ]
    )
    height = block_ref.shape[1]
    rows_of = lambda win, core: [(win * groups + group) * cores + core for group in range(groups)]

    even, odd = [], []
    for win in range(windows):
        value = []
        for group in range(groups):
            tile = None
            for core in range(cores):
                part = block_ref[(win * groups + group) * cores + core, height - 8 :, :].astype(jnp.float32)
                tile = part if tile is None else tile + part
            tile = tile[:, : LANES // 2] + tile[:, LANES // 2 :]
            value += [tile[:, 2 * NF * piece : 2 * NF * (piece + 1)] for piece in range(stations_dev // 8)]
        value = jnp.concatenate(value, axis=0)
        even.append(value)
        odd.append(jnp.concatenate([-value[:, NF:], value[:, :NF]], axis=1))
    spectra = jnp.concatenate(even + odd, axis=1)
    if merged:
        parts = []
        for win in range(windows):
            for core in range(cores):
                for first in range(0, height - 8, stations_dev):
                    rows = [block_ref[at, first : first + stations_dev, :] for at in rows_of(win, core)]
                    parts.append(jnp.concatenate(rows, axis=0))
        corr = jnp.concatenate(parts, axis=1)
    else:
        corr = corr_ref[...]

    copies[0].wait()
    place_row = place_of_ref[4:5, :stations].astype(jnp.int32)
    sorter = lax.broadcasted_iota(jnp.int32, (places, stations), 0) == place_row
    sorter = jnp.where(sorter, 1.0, 0.0).astype(jnp.bfloat16)
    found = None
    for piece in split_bf16(spectra, 3):
        part = jnp.dot(sorter, piece, preferred_element_type=jnp.float32)
        found = part if found is None else found + part
    weight_ref[...] = found
    place_ref[...] = jnp.dot(sorter, corr, preferred_element_type=jnp.float32) * (1.0 / REACH)
    sums_ref[...] = jnp.zeros_like(sums_ref)
    chunk = min(256, nodes)
    depth = DEGREES * 8
    lanes = windows * 2 * NF
    for copy in copies[1:3]:
        copy.wait()

    spot = (lax.broadcasted_iota(jnp.int32, (lanes, LANES), 1) & 7).astype(jnp.float32)

    def make_left(pair):
        top = weight_ref[pl.ds(pl.multiple_of(pair * 16, 16), 8), :]
        bottom = weight_ref[pl.ds(pl.multiple_of(pair * 16 + 8, 8), 8), :]
        sides = [
            jnp.concatenate([top[:, :lanes], bottom[:, :lanes]], axis=1),
            jnp.concatenate([top[:, lanes:], bottom[:, lanes:]], axis=1),
        ]
        per = LANES // 8
        for half in range(DEGREES // per):
            tall = jnp.concatenate(
                [sides[k % 2] * coef_ref[k : k + 1, :] for k in range(half * per, (half + 1) * per)], axis=0
            )
            turned = tall.T
            first = half * LANES
            fine = min(FINE * 8 - first, LANES)
            for which in range(2):
                group = 2 * pair + which
                mask = spot < plan_ref[2, group]
                value = turned[which * lanes : (which + 1) * lanes]
                value = jnp.concatenate([jnp.where(mask, value, 0.0), jnp.where(mask, 0.0, value)], axis=0)
                high, low = split_bf16(value, 2)
                if fine == LANES:
                    parts = [(first, high), (depth + first, high), (2 * FINE * 8 + first + LANES, low)]
                else:
                    mixed = [high[:, :fine].astype(jnp.float32), low[:, :fine].astype(jnp.float32)]
                    parts = [(first, high), (depth + first, jnp.concatenate(mixed, axis=1).astype(jnp.bfloat16))]
                for at, part in parts:
                    left_ref[group, :, at : at + LANES] = part

    used = plan_ref[3, 0].astype(jnp.int32)
    sure = stations // 16
    if sure <= 8:
        for pair in range(sure):
            make_left(pair)
    else:
        lax.fori_loop(0, sure, lambda pair, carry: (make_left(pair), carry)[1], 0)
    lax.fori_loop(sure, (used + 1) // 2, lambda pair, carry: (make_left(pair), carry)[1], 0)
    def make_basis(group, basis_ref, at):
        arg = place_ref[pl.ds(pl.multiple_of(group * 8, 8), 8), at]
        twice = arg + arg
        low = [jnp.ones_like(arg), arg]
        while len(low) < 8:
            low.append(twice * low[-1] - low[-2])
        eight = (low[4] + low[4]) * low[4] - 1.0
        sixteen = (eight + eight) * eight - 1.0
        steps = [None, eight, sixteen, (sixteen + sixteen - 1.0) * eight]
        for degree in range(0, DEGREES, 2):
            pair = []
            for factor in low[degree % 8 : degree % 8 + 2]:
                step = steps[degree // 8]
                pair.append(factor if step is None else step if factor is low[0] else factor * step)
            pair = jnp.concatenate(pair, axis=0)
            for term, value in enumerate(split_bf16(pair, 2 if degree < FINE else 1)):
                basis_ref[term * depth + degree * 8 : term * depth + degree * 8 + 16, at] = value

    def add_group(group, basis_ref, next_basis):
        left = left_ref[group]
        tables = [plan_ref[slot, group].astype(jnp.int32) for slot in range(2)]
        phasor_rows = [pl.ds(pl.multiple_of(table * NF, NF), NF) for table in tables]
        fine = FINE * 8
        for first in range(0, nodes, chunk):
            at = slice(first, first + chunk)
            right = [
                basis_ref[: depth + fine, at],
                basis_ref[LANES:fine, at],
                basis_ref[:LANES, at],
            ]
            got = jnp.dot(left, jnp.concatenate(right, axis=0), preferred_element_type=jnp.float32)
            if next_basis is not None:
                for part in range(first, first + chunk, LANES):
                    make_basis(group + 1, next_basis, slice(part, part + LANES))
            for win in range(windows):
                row = win * 2 * NF
                real_sum, imag_sum = sums_ref[row : row + NF, at], sums_ref[row + NF : row + 2 * NF, at]
                for slot, rows in enumerate(phasor_rows):
                    cosine, sine = cos_ref[rows, at], sin_ref[rows, at]
                    real = got[slot * lanes + row : slot * lanes + row + NF]
                    imag = got[slot * lanes + row + NF : slot * lanes + row + 2 * NF]
                    real_sum += real * cosine - imag * sine
                    imag_sum += real * sine + imag * cosine
                sums_ref[row : row + NF, at], sums_ref[row + NF : row + 2 * NF, at] = real_sum, imag_sum

    for first in range(0, nodes, LANES):
        make_basis(0, basis_a, slice(first, first + LANES))
    for copy in copies[3:]:
        copy.wait()

    def body(pair, carry):
        group = pair * 2
        add_group(group, basis_a, basis_b)
        add_group(group + 1, basis_b, basis_a)
        return carry

    lax.fori_loop(0, used // 2, body, 0)

    @pl.when(used % 2 == 1)
    def _():
        add_group(used - 1, basis_a, None)

    powers = []
    for win in range(windows):
        row = win * 2 * NF
        real, imag = sums_ref[row : row + NF, :], sums_ref[row + NF : row + 2 * NF, :]
        powers.append(real * real + imag * imag)
    mine = lax.axis_index("win") == 0
    keep_ref[...] = jnp.where(mine, powers[0], powers[1])
    send_ref[...] = jnp.where(mine, powers[1], powers[0])


def finish_kernel(stations, keep_ref, got_ref, spectrum_ref, beam_ref):
    nodes = keep_ref.shape[1]
    win = lax.axis_index("win")
    for place, ref in ((win, keep_ref), (1 - win, got_ref)):
        power = ref[...]
        total = jnp.sum(power, axis=0, keepdims=True)
        at = pl.ds(pl.multiple_of(place * nodes, LANES), nodes)
        spectrum_ref[:, at] = power * (NF / total)
        beam_ref[:, at] = total * (1.0 / (NF * stations))


def on_device(traces, tables, corrections, station_table, node_ids, freq_bins):
    windows, groups, cores = (lax.axis_size(a) for a in ("win", "sta", "freq"))
    stations_dev, grid = corrections.shape
    stations = stations_dev * groups
    devices = windows * groups * cores
    nodes = grid // devices
    ntab = tables.shape[0]
    params = lambda free: pltpu.CompilerParams(vmem_limit_bytes=VMEM_LIMIT - free)
    vmem = pl.BlockSpec(memory_space=pltpu.VMEM)
    hbm = pl.BlockSpec(memory_space=pltpu.HBM)
    bins = freq_bins.reshape(1, NF)
    bins_scratch = pltpu.VMEM((1, NF), jnp.int32)

    holders = windows * cores
    merged = nodes % (holders * LANES) == 0
    pieces = nodes // (holders * LANES) if merged else 0
    height = pieces * stations_dev + 8
    blocks = pl.pallas_call(
        functools.partial(send_kernel, nodes),
        out_shape=jax.ShapeDtypeStruct((devices, height, LANES), jnp.bfloat16),
        in_specs=[hbm] * 3,
        out_specs=vmem,
        scratch_shapes=[
            bins_scratch,
            pltpu.VMEM(traces.shape, traces.dtype),
            pltpu.SemaphoreType.DMA((3,)),
        ],
        compiler_params=params(0),
        name="send",
    )(bins, traces, corrections)
    received = [lax.all_to_all(blocks, ("win", "sta", "freq"), split_axis=0, concat_axis=0, tiled=True)]
    if not merged:
        parts = corrections.reshape(stations_dev, groups, holders, nodes)
        place = lax.axis_index("freq") * windows + lax.axis_index("win")
        mine = lax.dynamic_index_in_dim(parts, place, axis=2, keepdims=False)
        corr = lax.all_to_all(mine.transpose(1, 0, 2), "sta", split_axis=0, concat_axis=0, tiled=True)
        received.append(corr.reshape(stations, nodes))

    wide = 512
    plan_width = max(LANES, stations)
    phasors = pltpu.VMEM((ntab * NF, nodes), jnp.float32)
    coefs = pltpu.VMEM((DEGREES, LANES), jnp.float32)
    plan = pltpu.VMEM((8, plan_width), jnp.float32)
    packed_shape = (packed_rows(ntab)[-1].stop, max(nodes, plan_width))
    packed = pl.pallas_call(
        prepare_kernel,
        out_shape=jax.ShapeDtypeStruct(packed_shape, jnp.float32),
        in_specs=[hbm] * 4,
        out_specs=hbm,
        scratch_shapes=[
            bins_scratch,
            pltpu.VMEM((1, stations), jnp.int32),
            pltpu.VMEM((max(nodes // LANES, 8), LANES), jnp.int32),
            pltpu.VMEM(tables.shape, tables.dtype),
            phasors,
            phasors,
            coefs,
            plan,
            pltpu.VMEM((grid // wide * ntab, 3 * wide), jnp.bfloat16),
            pltpu.VMEM((3 * wide, nodes), jnp.bfloat16),
            pltpu.SemaphoreType.DMA((3 + 2 * ntab,)),
            pltpu.SemaphoreType.DMA((TABLE_PIECES,)),
        ],
        compiler_params=params(512 * 1024),
        name="prepare",
    )(bins, station_table.reshape(1, stations), node_ids.reshape(grid // LANES, LANES), tables)

    places = (stations // 8 + ntab // 2 + 3) // 2 * 16
    half = jax.ShapeDtypeStruct((NF, nodes), jnp.float32)
    rows = 2 * windows * 2 * NF
    basis = pltpu.VMEM(((DEGREES + FINE) * 8, nodes), jnp.bfloat16)
    keep, send = pl.pallas_call(
        functools.partial(image_kernel, merged, stations_dev),
        out_shape=[half, half],
        in_specs=[hbm] + [vmem] * len(received),
        out_specs=[vmem, vmem],
        scratch_shapes=[
            pltpu.SMEM((8, plan_width), jnp.float32),
            plan,
            coefs,
            phasors,
            phasors,
            pltpu.SemaphoreType.DMA((3 + ntab // 2,)),
            pltpu.VMEM((places, nodes), jnp.float32),
            pltpu.VMEM((places, rows), jnp.float32),
            pltpu.VMEM((places // 8, rows, (DEGREES + 2 * FINE) * 8), jnp.bfloat16),
            pltpu.VMEM((rows // 2, nodes), jnp.float32),
            basis,
            basis,
        ],
        compiler_params=params(23 * 512 * 1024),
        name="image",
    )(packed, *received)
    got = lax.ppermute(send, "win", [(0, 1), (1, 0)])
    spectrum, beam_power = pl.pallas_call(
        functools.partial(finish_kernel, stations),
        out_shape=[
            jax.ShapeDtypeStruct((NF, windows * nodes), jnp.float32),
            jax.ShapeDtypeStruct((1, windows * nodes), jnp.float32),
        ],
        in_specs=[vmem, vmem],
        out_specs=[vmem, vmem],
        compiler_params=params(32 * 1024 * 1024),
        name="finish",
    )(keep, got)
    return spectrum, beam_power.reshape(windows * nodes)


def solution(mesh):
    return jax.shard_map(
        on_device,
        mesh=mesh,
        in_specs=(P(("win", "sta"), "freq"), P(), P("sta", None), P(), P(), P()),
        out_specs=(P("win", ("sta", "freq")), P(("win", "sta", "freq"))),
        check_vma=False,
    )
```

```python
import functools
import math

import jax
import jax.numpy as jnp
import numpy as np
from jax import lax
from jax.experimental import pallas as pl
from jax.experimental.pallas import tpu as pltpu
from jax.sharding import PartitionSpec as P

NT = 5120
NF = 16
NTAB = 16
LANES = 128
DEGREES = 32
FINE = 24
REACH = 1.5
TABLE_PIECES = 4
VMEM_LIMIT = 64 * 1024 * 1024 - 64 * 1024


def chebyshev_fit(func, degree, low, high):
    fit = np.polynomial.chebyshev.Chebyshev.interpolate(func, degree, domain=[low, high])
    return [float(v) for v in fit.convert(kind=np.polynomial.Polynomial).coef]


SIN_HALF = chebyshev_fit(lambda z: np.pi * np.sinc(np.sqrt(z)), 4, 0.0, 0.25)
COS_HALF = chebyshev_fit(lambda z: np.cos(np.pi * np.sqrt(z)), 4, 0.0, 0.25)


def horner(coefs, arg):
    total = coefs[-1]
    for coef in coefs[-2::-1]:
        total = total * arg + coef
    return total


def turn_parts(rest):
    square = rest * rest
    root = math.sqrt(2.0)
    sine_half = rest * horner([root * c for c in SIN_HALF], square)
    cos_half = horner([root * c for c in COS_HALF], square)
    return sine_half * sine_half, sine_half * cos_half


def cos_sin(turns):
    versine, sine = turn_parts(turns - jnp.round(turns))
    return 1.0 - versine, sine


def bins_column(bins_ref):
    rows = lax.broadcasted_iota(jnp.int32, (NF, NF), 0)
    lanes = lax.broadcasted_iota(jnp.int32, (NF, NF), 1)
    square = jnp.broadcast_to(bins_ref[...].astype(jnp.float32), (NF, NF))
    return jnp.sum(jnp.where(rows == lanes, square, 0.0), axis=1, keepdims=True)


def split_bf16(value, terms):
    pieces = []
    for term in range(terms):
        piece = value.astype(jnp.bfloat16)
        pieces.append(piece)
        if term < terms - 1:
            value = value - piece.astype(jnp.float32)
    return pieces


def start_all(copies):
    for copy in copies:
        copy.start()
    return copies


def send_kernel(nodes, bins_hbm, traces_hbm, corr_hbm, out_ref, bins_ref, traces_ref, sems):
    devices, height, _ = out_ref.shape
    stations_dev, half_length = traces_ref.shape
    pieces = (height - 8) // stations_dev
    windows, groups, cores = (lax.axis_size(a) for a in ("win", "sta", "freq"))
    place = lax.axis_index("win") * cores + lax.axis_index("freq")
    small = start_all(
        [
            pltpu.make_async_copy(bins_hbm, bins_ref, sems.at[0]),
            pltpu.make_async_copy(traces_hbm, traces_ref, sems.at[1]),
        ]
    )
    copies = []
    for dev in range(devices):
        win, sta, core = dev // (groups * cores), dev // cores % groups, dev % cores
        first = ((sta * cores + core) * windows + win) * nodes
        for piece in range(pieces):
            at = pl.multiple_of(first + (place * pieces + piece) * LANES, LANES)
            to = out_ref.at[dev, pl.ds(piece * stations_dev, stations_dev), :]
            copies.append(pltpu.make_async_copy(corr_hbm.at[:, pl.ds(at, LANES)], to, sems.at[2]))
    start_all(copies)
    start = lax.axis_index("freq") * half_length
    small[0].wait()
    bins = bins_column(bins_ref)
    pos = (start + lax.broadcasted_iota(jnp.int32, (NF, half_length), 1)).astype(jnp.float32)
    product = bins * pos
    turns = jnp.round(product * (1.0 / NT))
    rest = (product - turns * NT) * (1.0 / NT)
    versine, sine = turn_parts(rest)
    scale = 1.0 / math.sqrt(NT)
    table = jnp.concatenate([(1.0 - versine) * scale, sine * -scale], axis=0)
    both = jnp.concatenate(split_bf16(table, 2), axis=0)
    small[1].wait()
    sums = lax.dot_general(
        both, traces_ref[...], (((1,), (1,)), ((), ())), preferred_element_type=jnp.float32
    )
    sums = (sums[: 2 * NF] + sums[2 * NF :]).T
    terms = [term.astype(jnp.float32) for term in split_bf16(sums, 2)]
    tile = jnp.concatenate([term[at : at + 8] for term in terms for at in range(0, stations_dev, 8)], axis=1)
    tile = tile.astype(jnp.bfloat16)
    for dev in range(devices):
        out_ref[dev, height - 8 :, :] = tile
    if copies:
        filled = out_ref.at[:, pl.ds(0, height - 8), :]
        pltpu.make_async_copy(filled, filled, sems.at[2]).wait()


def own_place():
    windows, cores = lax.axis_size("win"), lax.axis_size("freq")
    return (lax.axis_index("sta") * cores + lax.axis_index("freq")) * windows + lax.axis_index("win")


def pick_columns(ids_ref, tables_ref, table_copies, nodes, left_ref, right_ref):
    ntab, grid = tables_ref.shape
    count = nodes // LANES
    wide = right_ref.shape[0] // 3
    blocks = grid // wide
    ids = ids_ref[pl.ds(own_place() * count % ids_ref.shape[0], count), :]
    ids = jnp.concatenate([ids[at : at + 1] for at in range(count)], axis=1)
    low, high = ids & (wide - 1), ids >> (wide.bit_length() - 1)
    spots = lax.broadcasted_iota(jnp.int32, (wide, nodes), 0)
    ones = jnp.where(spots == low, 1.0, 0.0).astype(jnp.bfloat16)
    for term in range(3):
        right_ref[term * wide : (term + 1) * wide, :] = ones
    found = jnp.zeros((ntab, nodes), jnp.float32)
    step = blocks // len(table_copies)
    for at, copy in enumerate(table_copies):
        copy.wait()
        for block in range(at * step, (at + 1) * step):
            pieces = split_bf16(tables_ref[:, block * wide : (block + 1) * wide], 3)
            left_ref[block * ntab : (block + 1) * ntab, :] = jnp.concatenate(pieces, axis=1)
        rows = left_ref[at * step * ntab : (at + 1) * step * ntab, :]
        picked = jnp.dot(rows, right_ref[...], preferred_element_type=jnp.float32)
        for block in range(step):
            part = picked[block * ntab : (block + 1) * ntab]
            found = jnp.where(high == at * step + block, part, found)
    return found


def product_coefs(bins_ref):
    shape = (DEGREES, DEGREES)
    degree = lax.broadcasted_iota(jnp.int32, shape, 0)
    node = lax.broadcasted_iota(jnp.int32, shape, 1)
    period = 4 * DEGREES
    weight, _ = cos_sin((degree * (2 * node + 1) & (period - 1)).astype(jnp.float32) * (1.0 / period))
    weight = weight * jnp.where(degree == 0, 1.0 / DEGREES, 2.0 / DEGREES)
    even = jnp.where(degree % 2 == 0, weight, 0.0)
    odd = jnp.where(degree % 2 == 1, weight, 0.0)
    row = bins_ref[...].astype(jnp.float32)
    bins = jnp.concatenate([row] * (LANES // NF), axis=1)
    at = lax.broadcasted_iota(jnp.int32, (DEGREES, LANES), 0).astype(jnp.float32)
    spot, _ = cos_sin((2.0 * at + 1.0) * (1.0 / period))
    cosine, sine = cos_sin(bins * (spot * (REACH / 256.0)))
    dot = functools.partial(jnp.dot, precision=lax.Precision.HIGHEST, preferred_element_type=jnp.float32)
    coefs = dot(even, cosine) + dot(odd, sine)
    for first in range(DEGREES - 8, 0, -8):
        mirror = (degree + node == 2 * first) & (node > first) & (node < first + 8)
        coefs = coefs - dot(jnp.where(mirror, 1.0, 0.0), coefs)
    twice = (at >= 8.0) & ((at.astype(jnp.int32) & 7) != 0)
    return jnp.where(twice, 2.0 * coefs, coefs)


def station_plan(table_row, width):
    count = table_row.shape[1]
    shape = (count, count)
    here = lax.broadcasted_iota(jnp.int32, shape, 0)
    there = lax.broadcasted_iota(jnp.int32, shape, 1)
    column_of = lambda row: jnp.sum(jnp.where(here == there, jnp.broadcast_to(row, shape), 0), axis=1, keepdims=True)
    table_column = column_of(table_row)
    same = (table_column == table_row) & (here < there)
    within = jnp.sum(jnp.where(same, 1, 0), axis=0, keepdims=True)
    place_row = within
    spot = jnp.zeros((1, 1), jnp.int32)
    held = jnp.zeros((1, 1), jnp.int32)
    for table in range(NTAB):
        size = jnp.sum(jnp.where(table_row == table, 1, 0), axis=1, keepdims=True)
        some = size > 0
        edge = (spot & 7) == 0
        skip = some & (held >= 2) & ~edge
        spot = jnp.where(skip, (spot + 7) >> 3 << 3, spot)
        held = jnp.where(skip | edge, 0, held)
        after = spot + size
        place_row = place_row + jnp.where(table_row == table, spot, 0)
        held = jnp.where(some, jnp.where(after >> 3 == spot >> 3, held + 1, 1), held)
        spot = after
    groups = (spot + 7) >> 3
    place_column = column_of(place_row)
    group = lax.broadcasted_iota(jnp.int32, (count, width), 1)
    inside = place_column >> 3 == group
    first = jnp.sum(jnp.where(place_column == group * 8, table_column, 0), axis=0, keepdims=True)
    last = jnp.max(jnp.where(inside, table_column, 0), axis=0, keepdims=True)
    length = jnp.sum(jnp.where(inside & (table_column == first), 1, 0), axis=0, keepdims=True)
    rows = [first, last, length, jnp.broadcast_to(groups, (1, width))]
    if width > count:
        place_row = jnp.concatenate([place_row, jnp.zeros((1, width - count), jnp.int32)], axis=1)
    rows += [place_row, jnp.zeros((3, width), jnp.int32)]
    return jnp.concatenate(rows, axis=0).astype(jnp.float32)


def packed_rows(ntab):
    ends = [ntab * NF, 2 * ntab * NF, 2 * ntab * NF + DEGREES, 2 * ntab * NF + DEGREES + 8]
    return [slice(start, end) for start, end in zip([0] + ends, ends)]


def prepare_kernel(bins_hbm, table_hbm, ids_hbm, tables_hbm, out_hbm, *rest):
    bins_ref, table_ref, ids_ref, tables_ref, cos_ref, sin_ref, coef_ref, plan_ref = rest[:8]
    left_ref, right_ref, sems, table_sems = rest[8:]
    ntab = tables_ref.shape[0]
    nodes = cos_ref.shape[1]
    near = ids_ref.shape[0]
    first = pl.multiple_of(own_place() * (nodes // LANES) // near * near, 8)
    ins = start_all(
        [
            pltpu.make_async_copy(ids_hbm.at[pl.ds(first, near), :], ids_ref, sems.at[0]),
            pltpu.make_async_copy(bins_hbm, bins_ref, sems.at[1]),
            pltpu.make_async_copy(table_hbm, table_ref, sems.at[2]),
        ]
    )
    piece = tables_ref.shape[1] // TABLE_PIECES
    table_copies = []
    for at in range(TABLE_PIECES):
        part = (slice(None), pl.ds(at * piece, piece))
        table_copies.append(pltpu.make_async_copy(tables_hbm.at[part], tables_ref.at[part], table_sems.at[at]))
    start_all(table_copies)
    for copy in ins:
        copy.wait()
    cos_at, sin_at, coef_at, plan_at = packed_rows(ntab)
    coef_ref[...] = product_coefs(bins_ref)
    plan_ref[...] = station_plan(table_ref[...], plan_ref.shape[1])
    outs = start_all(
        [
            pltpu.make_async_copy(coef_ref, out_hbm.at[coef_at, pl.ds(0, LANES)], sems.at[0]),
            pltpu.make_async_copy(plan_ref, out_hbm.at[plan_at, pl.ds(0, plan_ref.shape[1])], sems.at[1]),
        ]
    )
    turns = pick_columns(ids_ref, tables_ref, table_copies, nodes, left_ref, right_ref) * (1.0 / 256.0)
    bins = bins_column(bins_ref)
    for table in range(ntab):
        cosine, sine = cos_sin(bins * turns[table : table + 1])
        at = pl.ds(table * NF, NF)
        cos_ref[at, :] = cosine
        sin_ref[at, :] = sine
        outs += start_all(
            [
                pltpu.make_async_copy(
                    cos_ref.at[at, :], out_hbm.at[pl.ds(cos_at.start + table * NF, NF), pl.ds(0, nodes)],
                    sems.at[3 + 2 * table],
                ),
                pltpu.make_async_copy(
                    sin_ref.at[at, :], out_hbm.at[pl.ds(sin_at.start + table * NF, NF), pl.ds(0, nodes)],
                    sems.at[4 + 2 * table],
                ),
            ]
        )
    for copy in outs:
        copy.wait()


def image_kernel(merged, stations_dev, packed_hbm, block_ref, *rest):
    corr_ref, rest = (None, rest) if merged else (rest[0], rest[1:])
    keep_ref, send_ref, plan_ref, place_of_ref, coef_ref, cos_ref, sin_ref, sems = rest[:8]
    place_ref, weight_ref, left_ref, sums_ref, basis_a, basis_b = rest[8:]
    places, nodes = place_ref.shape
    windows, groups, cores = (lax.axis_size(a) for a in ("win", "sta", "freq"))
    stations = stations_dev * groups
    cos_at, sin_at, coef_at, plan_at = packed_rows(cos_ref.shape[0] // NF)
    width = plan_ref.shape[1]
    copies = start_all(
        [
            pltpu.make_async_copy(packed_hbm.at[plan_at, pl.ds(0, width)], place_of_ref, sems.at[0]),
            pltpu.make_async_copy(packed_hbm.at[plan_at, pl.ds(0, width)], plan_ref, sems.at[1]),
            pltpu.make_async_copy(packed_hbm.at[coef_at, pl.ds(0, LANES)], coef_ref, sems.at[2]),
        ]
        + [
            pltpu.make_async_copy(
                packed_hbm.at[pl.ds(at.start + first, 4 * NF), pl.ds(0, nodes)],
                ref.at[pl.ds(first, 4 * NF), :],
                sems.at[3 + 2 * (first // (4 * NF)) + which],
            )
            for first in range(0, NTAB * NF, 4 * NF)
            for which, (at, ref) in enumerate(((cos_at, cos_ref), (sin_at, sin_ref)))
        ]
    )
    height = block_ref.shape[1]
    rows_of = lambda win, core: [(win * groups + group) * cores + core for group in range(groups)]

    even, odd = [], []
    for win in range(windows):
        value = []
        for group in range(groups):
            tile = None
            for core in range(cores):
                part = block_ref[(win * groups + group) * cores + core, height - 8 :, :].astype(jnp.float32)
                tile = part if tile is None else tile + part
            tile = tile[:, : LANES // 2] + tile[:, LANES // 2 :]
            value += [tile[:, 2 * NF * piece : 2 * NF * (piece + 1)] for piece in range(stations_dev // 8)]
        value = jnp.concatenate(value, axis=0)
        even.append(value)
        odd.append(jnp.concatenate([-value[:, NF:], value[:, :NF]], axis=1))
    spectra = jnp.concatenate(even + odd, axis=1)
    if merged:
        parts = []
        for win in range(windows):
            for core in range(cores):
                for first in range(0, height - 8, stations_dev):
                    rows = [block_ref[at, first : first + stations_dev, :] for at in rows_of(win, core)]
                    parts.append(jnp.concatenate(rows, axis=0))
        corr = jnp.concatenate(parts, axis=1)
    else:
        corr = corr_ref[...]

    copies[0].wait()
    place_row = place_of_ref[4:5, :stations].astype(jnp.int32)
    sorter = lax.broadcasted_iota(jnp.int32, (places, stations), 0) == place_row
    sorter = jnp.where(sorter, 1.0, 0.0).astype(jnp.bfloat16)
    found = None
    for piece in split_bf16(spectra, 3):
        part = jnp.dot(sorter, piece, preferred_element_type=jnp.float32)
        found = part if found is None else found + part
    weight_ref[...] = found
    place_ref[...] = jnp.dot(sorter, corr, preferred_element_type=jnp.float32) * (1.0 / REACH)
    sums_ref[...] = jnp.zeros_like(sums_ref)
    chunk, broad = min(256, nodes), min(512, nodes)
    depth = DEGREES * 8
    lanes = windows * 2 * NF
    for copy in copies[1:3]:
        copy.wait()

    spot = (lax.broadcasted_iota(jnp.int32, (lanes, LANES), 1) & 7).astype(jnp.float32)

    def make_left(pair):
        top = weight_ref[pl.ds(pl.multiple_of(pair * 16, 16), 8), :]
        bottom = weight_ref[pl.ds(pl.multiple_of(pair * 16 + 8, 8), 8), :]
        sides = [
            jnp.concatenate([top[:, :lanes], bottom[:, :lanes]], axis=1),
            jnp.concatenate([top[:, lanes:], bottom[:, lanes:]], axis=1),
        ]
        per = LANES // 8
        for half in range(DEGREES // per):
            tall = jnp.concatenate(
                [sides[k % 2] * coef_ref[k : k + 1, :] for k in range(half * per, (half + 1) * per)], axis=0
            )
            turned = tall.T
            first = half * LANES
            fine = min(FINE * 8 - first, LANES)
            for which in range(2):
                group = 2 * pair + which
                mask = spot < plan_ref[2, group]
                value = turned[which * lanes : (which + 1) * lanes]
                value = jnp.concatenate([jnp.where(mask, value, 0.0), jnp.where(mask, 0.0, value)], axis=0)
                high, low = split_bf16(value, 2)
                if fine == LANES:
                    parts = [(first, high), (depth + first, high), (2 * FINE * 8 + first + LANES, low)]
                else:
                    mixed = [high[:, :fine].astype(jnp.float32), low[:, :fine].astype(jnp.float32)]
                    parts = [(first, high), (depth + first, jnp.concatenate(mixed, axis=1).astype(jnp.bfloat16))]
                for at, part in parts:
                    left_ref[group, :, at : at + LANES] = part

    used = plan_ref[3, 0].astype(jnp.int32)
    sure = stations // 16
    if sure <= 8:
        for pair in range(sure):
            make_left(pair)
    else:
        lax.fori_loop(0, sure, lambda pair, carry: (make_left(pair), carry)[1], 0)
    lax.fori_loop(sure, (used + 1) // 2, lambda pair, carry: (make_left(pair), carry)[1], 0)
    def make_basis(group, basis_ref, at):
        arg = place_ref[pl.ds(pl.multiple_of(group * 8, 8), 8), at]
        twice = arg + arg
        low = [jnp.ones_like(arg), arg]
        while len(low) < 8:
            low.append(twice * low[-1] - low[-2])
        eight = (low[4] + low[4]) * low[4] - 1.0
        sixteen = (eight + eight) * eight - 1.0
        steps = [None, eight, sixteen, (sixteen + sixteen - 1.0) * eight]
        for degree in range(0, DEGREES, 2):
            pair = []
            for factor in low[degree % 8 : degree % 8 + 2]:
                step = steps[degree // 8]
                pair.append(factor if step is None else step if factor is low[0] else factor * step)
            pair = jnp.concatenate(pair, axis=0)
            for term, value in enumerate(split_bf16(pair, 2 if degree < FINE else 1)):
                basis_ref[term * depth + degree * 8 : term * depth + degree * 8 + 16, at] = value

    def add_group(group, basis_ref, next_basis):
        left = left_ref[group]
        tables = [plan_ref[slot, group].astype(jnp.int32) for slot in range(2)]
        phasor_rows = [pl.ds(pl.multiple_of(table * NF, NF), NF) for table in tables]
        fine = FINE * 8
        for first in range(0, nodes, chunk):
            at = slice(first, first + chunk)
            right = [
                basis_ref[: depth + fine, at],
                basis_ref[LANES:fine, at],
                basis_ref[:LANES, at],
            ]
            got = jnp.dot(left, jnp.concatenate(right, axis=0), preferred_element_type=jnp.float32)
            if next_basis is not None and first % broad == 0:
                make_basis(group + 1, next_basis, slice(first, first + broad))
            for win in range(windows):
                row = win * 2 * NF
                real_sum, imag_sum = sums_ref[row : row + NF, at], sums_ref[row + NF : row + 2 * NF, at]
                for slot, rows in enumerate(phasor_rows):
                    cosine, sine = cos_ref[rows, at], sin_ref[rows, at]
                    real = got[slot * lanes + row : slot * lanes + row + NF]
                    imag = got[slot * lanes + row + NF : slot * lanes + row + 2 * NF]
                    real_sum += real * cosine - imag * sine
                    imag_sum += real * sine + imag * cosine
                sums_ref[row : row + NF, at], sums_ref[row + NF : row + 2 * NF, at] = real_sum, imag_sum

    for first in range(0, nodes, broad):
        make_basis(0, basis_a, slice(first, first + broad))
    for copy in copies[3:]:
        copy.wait()

    def body(pair, carry):
        group = pair * 2
        add_group(group, basis_a, basis_b)
        add_group(group + 1, basis_b, basis_a)
        return carry

    lax.fori_loop(0, used // 2, body, 0)

    @pl.when(used % 2 == 1)
    def _():
        add_group(used - 1, basis_a, None)

    powers = []
    for win in range(windows):
        row = win * 2 * NF
        real, imag = sums_ref[row : row + NF, :], sums_ref[row + NF : row + 2 * NF, :]
        powers.append(real * real + imag * imag)
    mine = lax.axis_index("win") == 0
    keep_ref[...] = jnp.where(mine, powers[0], powers[1])
    send_ref[...] = jnp.where(mine, powers[1], powers[0])


def finish_kernel(stations, keep_ref, got_ref, spectrum_ref, beam_ref):
    nodes = keep_ref.shape[1]
    win = lax.axis_index("win")
    for place, ref in ((win, keep_ref), (1 - win, got_ref)):
        power = ref[...]
        total = jnp.sum(power, axis=0, keepdims=True)
        at = pl.ds(pl.multiple_of(place * nodes, LANES), nodes)
        spectrum_ref[:, at] = power * (NF / total)
        beam_ref[:, at] = total * (1.0 / (NF * stations))


def on_device(traces, tables, corrections, station_table, node_ids, freq_bins):
    windows, groups, cores = (lax.axis_size(a) for a in ("win", "sta", "freq"))
    stations_dev, grid = corrections.shape
    stations = stations_dev * groups
    devices = windows * groups * cores
    nodes = grid // devices
    ntab = tables.shape[0]
    params = lambda free: pltpu.CompilerParams(vmem_limit_bytes=VMEM_LIMIT - free)
    vmem = pl.BlockSpec(memory_space=pltpu.VMEM)
    hbm = pl.BlockSpec(memory_space=pltpu.HBM)
    bins = freq_bins.reshape(1, NF)
    bins_scratch = pltpu.VMEM((1, NF), jnp.int32)

    holders = windows * cores
    merged = nodes % (holders * LANES) == 0
    pieces = nodes // (holders * LANES) if merged else 0
    height = pieces * stations_dev + 8
    blocks = pl.pallas_call(
        functools.partial(send_kernel, nodes),
        out_shape=jax.ShapeDtypeStruct((devices, height, LANES), jnp.bfloat16),
        in_specs=[hbm] * 3,
        out_specs=vmem,
        scratch_shapes=[
            bins_scratch,
            pltpu.VMEM(traces.shape, traces.dtype),
            pltpu.SemaphoreType.DMA((3,)),
        ],
        compiler_params=params(0),
        name="send",
    )(bins, traces, corrections)
    received = [lax.all_to_all(blocks, ("win", "sta", "freq"), split_axis=0, concat_axis=0, tiled=True)]
    if not merged:
        parts = corrections.reshape(stations_dev, groups, holders, nodes)
        place = lax.axis_index("freq") * windows + lax.axis_index("win")
        mine = lax.dynamic_index_in_dim(parts, place, axis=2, keepdims=False)
        corr = lax.all_to_all(mine.transpose(1, 0, 2), "sta", split_axis=0, concat_axis=0, tiled=True)
        received.append(corr.reshape(stations, nodes))

    wide = 512
    plan_width = max(LANES, stations)
    phasors = pltpu.VMEM((ntab * NF, nodes), jnp.float32)
    coefs = pltpu.VMEM((DEGREES, LANES), jnp.float32)
    plan = pltpu.VMEM((8, plan_width), jnp.float32)
    packed_shape = (packed_rows(ntab)[-1].stop, max(nodes, plan_width))
    packed = pl.pallas_call(
        prepare_kernel,
        out_shape=jax.ShapeDtypeStruct(packed_shape, jnp.float32),
        in_specs=[hbm] * 4,
        out_specs=hbm,
        scratch_shapes=[
            bins_scratch,
            pltpu.VMEM((1, stations), jnp.int32),
            pltpu.VMEM((max(nodes // LANES, 8), LANES), jnp.int32),
            pltpu.VMEM(tables.shape, tables.dtype),
            phasors,
            phasors,
            coefs,
            plan,
            pltpu.VMEM((grid // wide * ntab, 3 * wide), jnp.bfloat16),
            pltpu.VMEM((3 * wide, nodes), jnp.bfloat16),
            pltpu.SemaphoreType.DMA((3 + 2 * ntab,)),
            pltpu.SemaphoreType.DMA((TABLE_PIECES,)),
        ],
        compiler_params=params(512 * 1024),
        name="prepare",
    )(bins, station_table.reshape(1, stations), node_ids.reshape(grid // LANES, LANES), tables)

    places = (stations // 8 + ntab // 2 + 3) // 2 * 16
    half = jax.ShapeDtypeStruct((NF, nodes), jnp.float32)
    rows = 2 * windows * 2 * NF
    basis = pltpu.VMEM(((DEGREES + FINE) * 8, nodes), jnp.bfloat16)
    keep, send = pl.pallas_call(
        functools.partial(image_kernel, merged, stations_dev),
        out_shape=[half, half],
        in_specs=[hbm] + [vmem] * len(received),
        out_specs=[vmem, vmem],
        scratch_shapes=[
            pltpu.SMEM((8, plan_width), jnp.float32),
            plan,
            coefs,
            phasors,
            phasors,
            pltpu.SemaphoreType.DMA((3 + ntab // 2,)),
            pltpu.VMEM((places, nodes), jnp.float32),
            pltpu.VMEM((places, rows), jnp.float32),
            pltpu.VMEM((places // 8, rows, (DEGREES + 2 * FINE) * 8), jnp.bfloat16),
            pltpu.VMEM((rows // 2, nodes), jnp.float32),
            basis,
            basis,
        ],
        compiler_params=params(23 * 512 * 1024),
        name="image",
    )(packed, *received)
    got = lax.ppermute(send, "win", [(0, 1), (1, 0)])
    spectrum, beam_power = pl.pallas_call(
        functools.partial(finish_kernel, stations),
        out_shape=[
            jax.ShapeDtypeStruct((NF, windows * nodes), jnp.float32),
            jax.ShapeDtypeStruct((1, windows * nodes), jnp.float32),
        ],
        in_specs=[vmem, vmem],
        out_specs=[vmem, vmem],
        compiler_params=params(32 * 1024 * 1024),
        name="finish",
    )(keep, got)
    return spectrum, beam_power.reshape(windows * nodes)


def solution(mesh):
    return jax.shard_map(
        on_device,
        mesh=mesh,
        in_specs=(P(("win", "sta"), "freq"), P(), P("sta", None), P(), P(), P()),
        out_specs=(P("win", ("sta", "freq")), P(("win", "sta", "freq"))),
        check_vma=False,
    )
```

```python
import functools
import math

import jax
import jax.numpy as jnp
import numpy as np
from jax import lax
from jax.experimental import pallas as pl
from jax.experimental.pallas import tpu as pltpu
from jax.sharding import PartitionSpec as P

NT = 5120
NF = 16
NTAB = 16
LANES = 128
DEGREES = 32
FINE = 24
REACH = 1.5
TABLE_PIECES = 4
VMEM_LIMIT = 64 * 1024 * 1024 - 64 * 1024


def chebyshev_fit(func, degree, low, high):
    fit = np.polynomial.chebyshev.Chebyshev.interpolate(func, degree, domain=[low, high])
    return [float(v) for v in fit.convert(kind=np.polynomial.Polynomial).coef]


SIN_HALF = chebyshev_fit(lambda z: np.pi * np.sinc(np.sqrt(z)), 4, 0.0, 0.25)
COS_HALF = chebyshev_fit(lambda z: np.cos(np.pi * np.sqrt(z)), 4, 0.0, 0.25)


def horner(coefs, arg):
    total = coefs[-1]
    for coef in coefs[-2::-1]:
        total = total * arg + coef
    return total


def turn_parts(rest):
    square = rest * rest
    root = math.sqrt(2.0)
    sine_half = rest * horner([root * c for c in SIN_HALF], square)
    cos_half = horner([root * c for c in COS_HALF], square)
    return sine_half * sine_half, sine_half * cos_half


def cos_sin(turns):
    versine, sine = turn_parts(turns - jnp.round(turns))
    return 1.0 - versine, sine


def bins_column(bins_ref):
    rows = lax.broadcasted_iota(jnp.int32, (NF, NF), 0)
    lanes = lax.broadcasted_iota(jnp.int32, (NF, NF), 1)
    square = jnp.broadcast_to(bins_ref[...].astype(jnp.float32), (NF, NF))
    return jnp.sum(jnp.where(rows == lanes, square, 0.0), axis=1, keepdims=True)


def split_bf16(value, terms):
    pieces = []
    for term in range(terms):
        piece = value.astype(jnp.bfloat16)
        pieces.append(piece)
        if term < terms - 1:
            value = value - piece.astype(jnp.float32)
    return pieces


def start_all(copies):
    for copy in copies:
        copy.start()
    return copies


def send_kernel(nodes, bins_hbm, traces_hbm, corr_hbm, out_ref, bins_ref, traces_ref, sems):
    devices, height, _ = out_ref.shape
    stations_dev, half_length = traces_ref.shape
    pieces = (height - 8) // stations_dev
    windows, groups, cores = (lax.axis_size(a) for a in ("win", "sta", "freq"))
    place = lax.axis_index("win") * cores + lax.axis_index("freq")
    small = start_all(
        [
            pltpu.make_async_copy(bins_hbm, bins_ref, sems.at[0]),
            pltpu.make_async_copy(traces_hbm, traces_ref, sems.at[1]),
        ]
    )
    copies = []
    for dev in range(devices):
        win, sta, core = dev // (groups * cores), dev // cores % groups, dev % cores
        first = ((sta * cores + core) * windows + win) * nodes
        for piece in range(pieces):
            at = pl.multiple_of(first + (place * pieces + piece) * LANES, LANES)
            to = out_ref.at[dev, pl.ds(piece * stations_dev, stations_dev), :]
            copies.append(pltpu.make_async_copy(corr_hbm.at[:, pl.ds(at, LANES)], to, sems.at[2]))
    start_all(copies)
    start = lax.axis_index("freq") * half_length
    small[0].wait()
    bins = bins_column(bins_ref)
    pos = (start + lax.broadcasted_iota(jnp.int32, (NF, half_length), 1)).astype(jnp.float32)
    product = bins * pos
    turns = jnp.round(product * (1.0 / NT))
    rest = (product - turns * NT) * (1.0 / NT)
    versine, sine = turn_parts(rest)
    scale = 1.0 / math.sqrt(NT)
    table = jnp.concatenate([(1.0 - versine) * scale, sine * -scale], axis=0)
    both = jnp.concatenate(split_bf16(table, 2), axis=0)
    small[1].wait()
    sums = lax.dot_general(
        both, traces_ref[...], (((1,), (1,)), ((), ())), preferred_element_type=jnp.float32
    )
    sums = (sums[: 2 * NF] + sums[2 * NF :]).T
    terms = [term.astype(jnp.float32) for term in split_bf16(sums, 2)]
    tile = jnp.concatenate([term[at : at + 8] for term in terms for at in range(0, stations_dev, 8)], axis=1)
    tile = tile.astype(jnp.bfloat16)
    for dev in range(devices):
        out_ref[dev, height - 8 :, :] = tile
    if copies:
        filled = out_ref.at[:, pl.ds(0, height - 8), :]
        pltpu.make_async_copy(filled, filled, sems.at[2]).wait()


def own_place():
    windows, cores = lax.axis_size("win"), lax.axis_size("freq")
    return (lax.axis_index("sta") * cores + lax.axis_index("freq")) * windows + lax.axis_index("win")


def pick_columns(ids_ref, tables_ref, table_copies, nodes, left_ref, right_ref):
    ntab, grid = tables_ref.shape
    count = nodes // LANES
    wide = right_ref.shape[0] // 3
    blocks = grid // wide
    ids = ids_ref[pl.ds(own_place() * count % ids_ref.shape[0], count), :]
    ids = jnp.concatenate([ids[at : at + 1] for at in range(count)], axis=1)
    low, high = ids & (wide - 1), ids >> (wide.bit_length() - 1)
    spots = lax.broadcasted_iota(jnp.int32, (wide, nodes), 0)
    ones = jnp.where(spots == low, 1.0, 0.0).astype(jnp.bfloat16)
    for term in range(3):
        right_ref[term * wide : (term + 1) * wide, :] = ones
    found = jnp.zeros((ntab, nodes), jnp.float32)
    step = blocks // len(table_copies)
    for at, copy in enumerate(table_copies):
        copy.wait()
        for block in range(at * step, (at + 1) * step):
            pieces = split_bf16(tables_ref[:, block * wide : (block + 1) * wide], 3)
            left_ref[block * ntab : (block + 1) * ntab, :] = jnp.concatenate(pieces, axis=1)
        rows = left_ref[at * step * ntab : (at + 1) * step * ntab, :]
        picked = jnp.dot(rows, right_ref[...], preferred_element_type=jnp.float32)
        for block in range(step):
            part = picked[block * ntab : (block + 1) * ntab]
            found = jnp.where(high == at * step + block, part, found)
    return found


def chebyshev_coefs(bins_ref):
    shape = (DEGREES, DEGREES)
    degree = lax.broadcasted_iota(jnp.int32, shape, 0)
    node = lax.broadcasted_iota(jnp.int32, shape, 1)
    period = 4 * DEGREES
    weight, _ = cos_sin((degree * (2 * node + 1) & (period - 1)).astype(jnp.float32) * (1.0 / period))
    weight = weight * jnp.where(degree == 0, 1.0 / DEGREES, 2.0 / DEGREES)
    even = jnp.where(degree % 2 == 0, weight, 0.0)
    odd = jnp.where(degree % 2 == 1, weight, 0.0)
    row = bins_ref[...].astype(jnp.float32)
    bins = jnp.concatenate([row] * (LANES // NF), axis=1)
    at = lax.broadcasted_iota(jnp.int32, (DEGREES, LANES), 0).astype(jnp.float32)
    spot, _ = cos_sin((2.0 * at + 1.0) * (1.0 / period))
    cosine, sine = cos_sin(bins * (spot * (REACH / 256.0)))
    dot = functools.partial(jnp.dot, precision=lax.Precision.HIGHEST, preferred_element_type=jnp.float32)
    return dot(even, cosine) + dot(odd, sine)


def station_plan(table_row, width):
    count = table_row.shape[1]
    shape = (count, count)
    here = lax.broadcasted_iota(jnp.int32, shape, 0)
    there = lax.broadcasted_iota(jnp.int32, shape, 1)
    column_of = lambda row: jnp.sum(jnp.where(here == there, jnp.broadcast_to(row, shape), 0), axis=1, keepdims=True)
    table_column = column_of(table_row)
    same = (table_column == table_row) & (here < there)
    within = jnp.sum(jnp.where(same, 1, 0), axis=0, keepdims=True)
    place_row = within
    spot = jnp.zeros((1, 1), jnp.int32)
    held = jnp.zeros((1, 1), jnp.int32)
    for table in range(NTAB):
        size = jnp.sum(jnp.where(table_row == table, 1, 0), axis=1, keepdims=True)
        some = size > 0
        edge = (spot & 7) == 0
        skip = some & (held >= 2) & ~edge
        spot = jnp.where(skip, (spot + 7) >> 3 << 3, spot)
        held = jnp.where(skip | edge, 0, held)
        after = spot + size
        place_row = place_row + jnp.where(table_row == table, spot, 0)
        held = jnp.where(some, jnp.where(after >> 3 == spot >> 3, held + 1, 1), held)
        spot = after
    groups = (spot + 7) >> 3
    place_column = column_of(place_row)
    group = lax.broadcasted_iota(jnp.int32, (count, width), 1)
    inside = place_column >> 3 == group
    first = jnp.sum(jnp.where(place_column == group * 8, table_column, 0), axis=0, keepdims=True)
    last = jnp.max(jnp.where(inside, table_column, 0), axis=0, keepdims=True)
    length = jnp.sum(jnp.where(inside & (table_column == first), 1, 0), axis=0, keepdims=True)
    rows = [first, last, length, jnp.broadcast_to(groups, (1, width))]
    if width > count:
        place_row = jnp.concatenate([place_row, jnp.zeros((1, width - count), jnp.int32)], axis=1)
    rows += [place_row, jnp.zeros((3, width), jnp.int32)]
    return jnp.concatenate(rows, axis=0).astype(jnp.float32)


def packed_rows(ntab):
    ends = [ntab * NF, 2 * ntab * NF, 2 * ntab * NF + DEGREES, 2 * ntab * NF + DEGREES + 8]
    return [slice(start, end) for start, end in zip([0] + ends, ends)]


def prepare_kernel(bins_hbm, table_hbm, ids_hbm, tables_hbm, out_hbm, *rest):
    bins_ref, table_ref, ids_ref, tables_ref, cos_ref, sin_ref, coef_ref, plan_ref = rest[:8]
    left_ref, right_ref, sems, table_sems = rest[8:]
    ntab = tables_ref.shape[0]
    nodes = cos_ref.shape[1]
    near = ids_ref.shape[0]
    first = pl.multiple_of(own_place() * (nodes // LANES) // near * near, 8)
    ins = start_all(
        [
            pltpu.make_async_copy(ids_hbm.at[pl.ds(first, near), :], ids_ref, sems.at[0]),
            pltpu.make_async_copy(bins_hbm, bins_ref, sems.at[1]),
            pltpu.make_async_copy(table_hbm, table_ref, sems.at[2]),
        ]
    )
    piece = tables_ref.shape[1] // TABLE_PIECES
    table_copies = []
    for at in range(TABLE_PIECES):
        part = (slice(None), pl.ds(at * piece, piece))
        table_copies.append(pltpu.make_async_copy(tables_hbm.at[part], tables_ref.at[part], table_sems.at[at]))
    start_all(table_copies)
    for copy in ins:
        copy.wait()
    cos_at, sin_at, coef_at, plan_at = packed_rows(ntab)
    coef_ref[...] = chebyshev_coefs(bins_ref)
    plan_ref[...] = station_plan(table_ref[...], plan_ref.shape[1])
    outs = start_all(
        [
            pltpu.make_async_copy(coef_ref, out_hbm.at[coef_at, pl.ds(0, LANES)], sems.at[0]),
            pltpu.make_async_copy(plan_ref, out_hbm.at[plan_at, pl.ds(0, plan_ref.shape[1])], sems.at[1]),
        ]
    )
    turns = pick_columns(ids_ref, tables_ref, table_copies, nodes, left_ref, right_ref) * (1.0 / 256.0)
    bins = bins_column(bins_ref)
    for table in range(ntab):
        cosine, sine = cos_sin(bins * turns[table : table + 1])
        at = pl.ds(table * NF, NF)
        cos_ref[at, :] = cosine
        sin_ref[at, :] = sine
        outs += start_all(
            [
                pltpu.make_async_copy(
                    cos_ref.at[at, :], out_hbm.at[pl.ds(cos_at.start + table * NF, NF), pl.ds(0, nodes)],
                    sems.at[3 + 2 * table],
                ),
                pltpu.make_async_copy(
                    sin_ref.at[at, :], out_hbm.at[pl.ds(sin_at.start + table * NF, NF), pl.ds(0, nodes)],
                    sems.at[4 + 2 * table],
                ),
            ]
        )
    for copy in outs:
        copy.wait()


def image_kernel(merged, stations_dev, packed_hbm, block_ref, *rest):
    corr_ref, rest = (None, rest) if merged else (rest[0], rest[1:])
    keep_ref, send_ref, plan_ref, place_of_ref, coef_ref, cos_ref, sin_ref, sems = rest[:8]
    place_ref, weight_ref, left_ref, sums_ref, basis_a, basis_b = rest[8:]
    places, nodes = place_ref.shape
    windows, groups, cores = (lax.axis_size(a) for a in ("win", "sta", "freq"))
    stations = stations_dev * groups
    cos_at, sin_at, coef_at, plan_at = packed_rows(cos_ref.shape[0] // NF)
    width = plan_ref.shape[1]
    copies = start_all(
        [
            pltpu.make_async_copy(packed_hbm.at[plan_at, pl.ds(0, width)], place_of_ref, sems.at[0]),
            pltpu.make_async_copy(packed_hbm.at[plan_at, pl.ds(0, width)], plan_ref, sems.at[1]),
            pltpu.make_async_copy(packed_hbm.at[coef_at, pl.ds(0, LANES)], coef_ref, sems.at[2]),
        ]
        + [
            pltpu.make_async_copy(
                packed_hbm.at[pl.ds(at.start + first, 4 * NF), pl.ds(0, nodes)],
                ref.at[pl.ds(first, 4 * NF), :],
                sems.at[3 + 2 * (first // (4 * NF)) + which],
            )
            for first in range(0, NTAB * NF, 4 * NF)
            for which, (at, ref) in enumerate(((cos_at, cos_ref), (sin_at, sin_ref)))
        ]
    )
    height = block_ref.shape[1]
    rows_of = lambda win, core: [(win * groups + group) * cores + core for group in range(groups)]

    even, odd = [], []
    for win in range(windows):
        value = []
        for group in range(groups):
            tile = None
            for core in range(cores):
                part = block_ref[(win * groups + group) * cores + core, height - 8 :, :].astype(jnp.float32)
                tile = part if tile is None else tile + part
            tile = tile[:, : LANES // 2] + tile[:, LANES // 2 :]
            value += [tile[:, 2 * NF * piece : 2 * NF * (piece + 1)] for piece in range(stations_dev // 8)]
        value = jnp.concatenate(value, axis=0)
        even.append(value)
        odd.append(jnp.concatenate([-value[:, NF:], value[:, :NF]], axis=1))
    spectra = jnp.concatenate(even + odd, axis=1)
    if merged:
        parts = []
        for win in range(windows):
            for core in range(cores):
                for first in range(0, height - 8, stations_dev):
                    rows = [block_ref[at, first : first + stations_dev, :] for at in rows_of(win, core)]
                    parts.append(jnp.concatenate(rows, axis=0))
        corr = jnp.concatenate(parts, axis=1)
    else:
        corr = corr_ref[...]

    copies[0].wait()
    place_row = place_of_ref[4:5, :stations].astype(jnp.int32)
    sorter = lax.broadcasted_iota(jnp.int32, (places, stations), 0) == place_row
    sorter = jnp.where(sorter, 1.0, 0.0).astype(jnp.bfloat16)
    found = None
    for piece in split_bf16(spectra, 3):
        part = jnp.dot(sorter, piece, preferred_element_type=jnp.float32)
        found = part if found is None else found + part
    weight_ref[...] = found
    place_ref[...] = jnp.dot(sorter, corr, preferred_element_type=jnp.float32) * (1.0 / REACH)
    sums_ref[...] = jnp.zeros_like(sums_ref)
    chunk = min(256, nodes)
    depth = DEGREES * 8
    lanes = windows * 2 * NF
    for copy in copies[1:3]:
        copy.wait()

    spot = (lax.broadcasted_iota(jnp.int32, (lanes, LANES), 1) & 7).astype(jnp.float32)

    def make_left(pair):
        top = weight_ref[pl.ds(pl.multiple_of(pair * 16, 16), 8), :]
        bottom = weight_ref[pl.ds(pl.multiple_of(pair * 16 + 8, 8), 8), :]
        sides = [
            jnp.concatenate([top[:, :lanes], bottom[:, :lanes]], axis=1),
            jnp.concatenate([top[:, lanes:], bottom[:, lanes:]], axis=1),
        ]
        per = LANES // 8
        for half in range(DEGREES // per):
            tall = jnp.concatenate(
                [sides[k % 2] * coef_ref[k : k + 1, :] for k in range(half * per, (half + 1) * per)], axis=0
            )
            turned = tall.T
            first = half * LANES
            fine = min(FINE * 8 - first, LANES)
            for which in range(2):
                group = 2 * pair + which
                mask = spot < plan_ref[2, group]
                value = turned[which * lanes : (which + 1) * lanes]
                value = jnp.concatenate([jnp.where(mask, value, 0.0), jnp.where(mask, 0.0, value)], axis=0)
                high, low = split_bf16(value, 2)
                if fine == LANES:
                    parts = [(first, high), (depth + first, high), (2 * FINE * 8 + first + LANES, low)]
                else:
                    mixed = [high[:, :fine].astype(jnp.float32), low[:, :fine].astype(jnp.float32)]
                    parts = [(first, high), (depth + first, jnp.concatenate(mixed, axis=1).astype(jnp.bfloat16))]
                for at, part in parts:
                    left_ref[group, :, at : at + LANES] = part

    used = plan_ref[3, 0].astype(jnp.int32)
    sure = stations // 16
    if sure <= 8:
        for pair in range(sure):
            make_left(pair)
    else:
        lax.fori_loop(0, sure, lambda pair, carry: (make_left(pair), carry)[1], 0)
    lax.fori_loop(sure, (used + 1) // 2, lambda pair, carry: (make_left(pair), carry)[1], 0)
    def basis_steps(group, basis_ref):
        arg = place_ref[pl.ds(pl.multiple_of(group * 8, 8), 8), :]
        twice = arg + arg
        before, now = jnp.ones_like(arg), arg
        for degree in range(0, DEGREES, 2):
            pair = jnp.concatenate([before, now], axis=0)
            terms = split_bf16(pair, 2 if degree < FINE else 1)
            for term, value in enumerate(terms):
                basis_ref[term * depth + degree * 8 : term * depth + degree * 8 + 16, :] = value
            before = twice * now - before
            now = twice * before - now
            if degree % 8 == 6:
                yield

    def run(steps):
        for _ in steps:
            pass

    def add_group(group, basis_ref, steps):
        left = left_ref[group]
        tables = [plan_ref[slot, group].astype(jnp.int32) for slot in range(2)]
        phasor_rows = [pl.ds(pl.multiple_of(table * NF, NF), NF) for table in tables]
        fine = FINE * 8
        for first in range(0, nodes, chunk):
            at = slice(first, first + chunk)
            right = [
                basis_ref[: depth + fine, at],
                basis_ref[LANES:fine, at],
                basis_ref[:LANES, at],
            ]
            got = jnp.dot(left, jnp.concatenate(right, axis=0), preferred_element_type=jnp.float32)
            next(steps, None)
            for win in range(windows):
                row = win * 2 * NF
                real_sum, imag_sum = sums_ref[row : row + NF, at], sums_ref[row + NF : row + 2 * NF, at]
                for slot, rows in enumerate(phasor_rows):
                    cosine, sine = cos_ref[rows, at], sin_ref[rows, at]
                    real = got[slot * lanes + row : slot * lanes + row + NF]
                    imag = got[slot * lanes + row + NF : slot * lanes + row + 2 * NF]
                    real_sum += real * cosine - imag * sine
                    imag_sum += real * sine + imag * cosine
                sums_ref[row : row + NF, at], sums_ref[row + NF : row + 2 * NF, at] = real_sum, imag_sum
        run(steps)

    run(basis_steps(0, basis_a))
    for copy in copies[3:]:
        copy.wait()

    def body(pair, carry):
        group = pair * 2
        add_group(group, basis_a, basis_steps(group + 1, basis_b))
        add_group(group + 1, basis_b, basis_steps(jnp.minimum(group + 2, places // 8 - 1), basis_a))
        return carry

    lax.fori_loop(0, used // 2, body, 0)

    @pl.when(used % 2 == 1)
    def _():
        add_group(used - 1, basis_a, iter(()))

    powers = []
    for win in range(windows):
        row = win * 2 * NF
        real, imag = sums_ref[row : row + NF, :], sums_ref[row + NF : row + 2 * NF, :]
        powers.append(real * real + imag * imag)
    mine = lax.axis_index("win") == 0
    keep_ref[...] = jnp.where(mine, powers[0], powers[1])
    send_ref[...] = jnp.where(mine, powers[1], powers[0])


def finish_kernel(stations, keep_ref, got_ref, spectrum_ref, beam_ref):
    nodes = keep_ref.shape[1]
    win = lax.axis_index("win")
    for place, ref in ((win, keep_ref), (1 - win, got_ref)):
        power = ref[...]
        total = jnp.sum(power, axis=0, keepdims=True)
        at = pl.ds(pl.multiple_of(place * nodes, LANES), nodes)
        spectrum_ref[:, at] = power * (NF / total)
        beam_ref[:, at] = total * (1.0 / (NF * stations))


def on_device(traces, tables, corrections, station_table, node_ids, freq_bins):
    windows, groups, cores = (lax.axis_size(a) for a in ("win", "sta", "freq"))
    stations_dev, grid = corrections.shape
    stations = stations_dev * groups
    devices = windows * groups * cores
    nodes = grid // devices
    ntab = tables.shape[0]
    params = lambda free: pltpu.CompilerParams(vmem_limit_bytes=VMEM_LIMIT - free)
    vmem = pl.BlockSpec(memory_space=pltpu.VMEM)
    hbm = pl.BlockSpec(memory_space=pltpu.HBM)
    bins = freq_bins.reshape(1, NF)
    bins_scratch = pltpu.VMEM((1, NF), jnp.int32)

    holders = windows * cores
    merged = nodes % (holders * LANES) == 0
    pieces = nodes // (holders * LANES) if merged else 0
    height = pieces * stations_dev + 8
    blocks = pl.pallas_call(
        functools.partial(send_kernel, nodes),
        out_shape=jax.ShapeDtypeStruct((devices, height, LANES), jnp.bfloat16),
        in_specs=[hbm] * 3,
        out_specs=vmem,
        scratch_shapes=[
            bins_scratch,
            pltpu.VMEM(traces.shape, traces.dtype),
            pltpu.SemaphoreType.DMA((3,)),
        ],
        compiler_params=params(0),
        name="send",
    )(bins, traces, corrections)
    received = [lax.all_to_all(blocks, ("win", "sta", "freq"), split_axis=0, concat_axis=0, tiled=True)]
    if not merged:
        parts = corrections.reshape(stations_dev, groups, holders, nodes)
        place = lax.axis_index("freq") * windows + lax.axis_index("win")
        mine = lax.dynamic_index_in_dim(parts, place, axis=2, keepdims=False)
        corr = lax.all_to_all(mine.transpose(1, 0, 2), "sta", split_axis=0, concat_axis=0, tiled=True)
        received.append(corr.reshape(stations, nodes))

    wide = 512
    plan_width = max(LANES, stations)
    phasors = pltpu.VMEM((ntab * NF, nodes), jnp.float32)
    coefs = pltpu.VMEM((DEGREES, LANES), jnp.float32)
    plan = pltpu.VMEM((8, plan_width), jnp.float32)
    packed_shape = (packed_rows(ntab)[-1].stop, max(nodes, plan_width))
    packed = pl.pallas_call(
        prepare_kernel,
        out_shape=jax.ShapeDtypeStruct(packed_shape, jnp.float32),
        in_specs=[hbm] * 4,
        out_specs=hbm,
        scratch_shapes=[
            bins_scratch,
            pltpu.VMEM((1, stations), jnp.int32),
            pltpu.VMEM((max(nodes // LANES, 8), LANES), jnp.int32),
            pltpu.VMEM(tables.shape, tables.dtype),
            phasors,
            phasors,
            coefs,
            plan,
            pltpu.VMEM((grid // wide * ntab, 3 * wide), jnp.bfloat16),
            pltpu.VMEM((3 * wide, nodes), jnp.bfloat16),
            pltpu.SemaphoreType.DMA((3 + 2 * ntab,)),
            pltpu.SemaphoreType.DMA((TABLE_PIECES,)),
        ],
        compiler_params=params(512 * 1024),
        name="prepare",
    )(bins, station_table.reshape(1, stations), node_ids.reshape(grid // LANES, LANES), tables)

    places = (stations // 8 + ntab // 2 + 2) // 2 * 16
    half = jax.ShapeDtypeStruct((NF, nodes), jnp.float32)
    rows = 2 * windows * 2 * NF
    basis = pltpu.VMEM(((DEGREES + FINE) * 8, nodes), jnp.bfloat16)
    keep, send = pl.pallas_call(
        functools.partial(image_kernel, merged, stations_dev),
        out_shape=[half, half],
        in_specs=[hbm] + [vmem] * len(received),
        out_specs=[vmem, vmem],
        scratch_shapes=[
            pltpu.SMEM((8, plan_width), jnp.float32),
            plan,
            coefs,
            phasors,
            phasors,
            pltpu.SemaphoreType.DMA((3 + ntab // 2,)),
            pltpu.VMEM((places, nodes), jnp.float32),
            pltpu.VMEM((places, rows), jnp.float32),
            pltpu.VMEM((places // 8, rows, (DEGREES + 2 * FINE) * 8), jnp.bfloat16),
            pltpu.VMEM((rows // 2, nodes), jnp.float32),
            basis,
            basis,
        ],
        compiler_params=params(23 * 512 * 1024),
        name="image",
    )(packed, *received)
    got = lax.ppermute(send, "win", [(0, 1), (1, 0)])
    spectrum, beam_power = pl.pallas_call(
        functools.partial(finish_kernel, stations),
        out_shape=[
            jax.ShapeDtypeStruct((NF, windows * nodes), jnp.float32),
            jax.ShapeDtypeStruct((1, windows * nodes), jnp.float32),
        ],
        in_specs=[vmem, vmem],
        out_specs=[vmem, vmem],
        compiler_params=params(32 * 1024 * 1024),
        name="finish",
    )(keep, got)
    return spectrum, beam_power.reshape(windows * nodes)


def solution(mesh):
    return jax.shard_map(
        on_device,
        mesh=mesh,
        in_specs=(P(("win", "sta"), "freq"), P(), P("sta", None), P(), P(), P()),
        out_specs=(P("win", ("sta", "freq")), P(("win", "sta", "freq"))),
        check_vma=False,
    )
```

```python
import functools
import math

import jax
import jax.numpy as jnp
import numpy as np
from jax import lax
from jax.experimental import pallas as pl
from jax.experimental.pallas import tpu as pltpu
from jax.sharding import PartitionSpec as P

NT = 5120
NF = 16
NTAB = 16
LANES = 128
DEGREES = 32
FINE = 24
REACH = 1.5
TABLE_PIECES = 4
VMEM_LIMIT = 64 * 1024 * 1024 - 64 * 1024


def chebyshev_fit(func, degree, low, high):
    fit = np.polynomial.chebyshev.Chebyshev.interpolate(func, degree, domain=[low, high])
    return [float(v) for v in fit.convert(kind=np.polynomial.Polynomial).coef]


SIN_HALF = chebyshev_fit(lambda z: np.pi * np.sinc(np.sqrt(z)), 4, 0.0, 0.25)
COS_HALF = chebyshev_fit(lambda z: np.cos(np.pi * np.sqrt(z)), 4, 0.0, 0.25)


def horner(coefs, arg):
    total = coefs[-1]
    for coef in coefs[-2::-1]:
        total = total * arg + coef
    return total


def turn_parts(rest):
    square = rest * rest
    root = math.sqrt(2.0)
    sine_half = rest * horner([root * c for c in SIN_HALF], square)
    cos_half = horner([root * c for c in COS_HALF], square)
    return sine_half * sine_half, sine_half * cos_half


def cos_sin(turns):
    versine, sine = turn_parts(turns - jnp.round(turns))
    return 1.0 - versine, sine


def bins_column(bins_ref):
    rows = lax.broadcasted_iota(jnp.int32, (NF, NF), 0)
    lanes = lax.broadcasted_iota(jnp.int32, (NF, NF), 1)
    square = jnp.broadcast_to(bins_ref[...].astype(jnp.float32), (NF, NF))
    return jnp.sum(jnp.where(rows == lanes, square, 0.0), axis=1, keepdims=True)


def split_bf16(value, terms):
    pieces = []
    for term in range(terms):
        piece = value.astype(jnp.bfloat16)
        pieces.append(piece)
        if term < terms - 1:
            value = value - piece.astype(jnp.float32)
    return pieces


def start_all(copies):
    for copy in copies:
        copy.start()
    return copies


def send_kernel(nodes, bins_hbm, traces_hbm, corr_hbm, out_ref, bins_ref, traces_ref, sems):
    devices, height, _ = out_ref.shape
    stations_dev, half_length = traces_ref.shape
    pieces = (height - 8) // stations_dev
    windows, groups, cores = (lax.axis_size(a) for a in ("win", "sta", "freq"))
    place = lax.axis_index("win") * cores + lax.axis_index("freq")
    small = start_all(
        [
            pltpu.make_async_copy(bins_hbm, bins_ref, sems.at[0]),
            pltpu.make_async_copy(traces_hbm, traces_ref, sems.at[1]),
        ]
    )
    copies = []
    for dev in range(devices):
        win, sta, core = dev // (groups * cores), dev // cores % groups, dev % cores
        first = ((sta * cores + core) * windows + win) * nodes
        for piece in range(pieces):
            at = pl.multiple_of(first + (place * pieces + piece) * LANES, LANES)
            to = out_ref.at[dev, pl.ds(piece * stations_dev, stations_dev), :]
            copies.append(pltpu.make_async_copy(corr_hbm.at[:, pl.ds(at, LANES)], to, sems.at[2]))
    start_all(copies)
    start = lax.axis_index("freq") * half_length
    small[0].wait()
    bins = bins_column(bins_ref)
    pos = (start + lax.broadcasted_iota(jnp.int32, (NF, half_length), 1)).astype(jnp.float32)
    product = bins * pos
    turns = jnp.round(product * (1.0 / NT))
    rest = (product - turns * NT) * (1.0 / NT)
    versine, sine = turn_parts(rest)
    scale = 1.0 / math.sqrt(NT)
    table = jnp.concatenate([(1.0 - versine) * scale, sine * -scale], axis=0)
    both = jnp.concatenate(split_bf16(table, 2), axis=0)
    small[1].wait()
    sums = lax.dot_general(
        both, traces_ref[...], (((1,), (1,)), ((), ())), preferred_element_type=jnp.float32
    )
    sums = (sums[: 2 * NF] + sums[2 * NF :]).T
    terms = [term.astype(jnp.float32) for term in split_bf16(sums, 2)]
    tile = jnp.concatenate([term[at : at + 8] for term in terms for at in range(0, stations_dev, 8)], axis=1)
    tile = tile.astype(jnp.bfloat16)
    for dev in range(devices):
        out_ref[dev, height - 8 :, :] = tile
    if copies:
        filled = out_ref.at[:, pl.ds(0, height - 8), :]
        pltpu.make_async_copy(filled, filled, sems.at[2]).wait()


def own_place():
    windows, cores = lax.axis_size("win"), lax.axis_size("freq")
    return (lax.axis_index("sta") * cores + lax.axis_index("freq")) * windows + lax.axis_index("win")


def pick_columns(ids_ref, tables_ref, table_copies, nodes, left_ref, right_ref):
    ntab, grid = tables_ref.shape
    count = nodes // LANES
    wide = right_ref.shape[0] // 3
    blocks = grid // wide
    ids = ids_ref[pl.ds(own_place() * count % ids_ref.shape[0], count), :]
    ids = jnp.concatenate([ids[at : at + 1] for at in range(count)], axis=1)
    low, high = ids & (wide - 1), ids >> (wide.bit_length() - 1)
    spots = lax.broadcasted_iota(jnp.int32, (wide, nodes), 0)
    ones = jnp.where(spots == low, 1.0, 0.0).astype(jnp.bfloat16)
    for term in range(3):
        right_ref[term * wide : (term + 1) * wide, :] = ones
    found = jnp.zeros((ntab, nodes), jnp.float32)
    step = blocks // len(table_copies)
    for at, copy in enumerate(table_copies):
        copy.wait()
        for block in range(at * step, (at + 1) * step):
            pieces = split_bf16(tables_ref[:, block * wide : (block + 1) * wide], 3)
            left_ref[block * ntab : (block + 1) * ntab, :] = jnp.concatenate(pieces, axis=1)
        rows = left_ref[at * step * ntab : (at + 1) * step * ntab, :]
        picked = jnp.dot(rows, right_ref[...], preferred_element_type=jnp.float32)
        for block in range(step):
            part = picked[block * ntab : (block + 1) * ntab]
            found = jnp.where(high == at * step + block, part, found)
    return found


def chebyshev_coefs(bins_ref):
    shape = (DEGREES, DEGREES)
    degree = lax.broadcasted_iota(jnp.int32, shape, 0)
    node = lax.broadcasted_iota(jnp.int32, shape, 1)
    period = 4 * DEGREES
    weight, _ = cos_sin((degree * (2 * node + 1) & (period - 1)).astype(jnp.float32) * (1.0 / period))
    weight = weight * jnp.where(degree == 0, 1.0 / DEGREES, 2.0 / DEGREES)
    even = jnp.where(degree % 2 == 0, weight, 0.0)
    odd = jnp.where(degree % 2 == 1, weight, 0.0)
    row = bins_ref[...].astype(jnp.float32)
    bins = jnp.concatenate([row] * (LANES // NF), axis=1)
    at = lax.broadcasted_iota(jnp.int32, (DEGREES, LANES), 0).astype(jnp.float32)
    spot, _ = cos_sin((2.0 * at + 1.0) * (1.0 / period))
    cosine, sine = cos_sin(bins * (spot * (REACH / 256.0)))
    dot = functools.partial(jnp.dot, precision=lax.Precision.HIGHEST, preferred_element_type=jnp.float32)
    return dot(even, cosine) + dot(odd, sine)


def station_plan(table_row, width):
    count = table_row.shape[1]
    shape = (count, count)
    here = lax.broadcasted_iota(jnp.int32, shape, 0)
    there = lax.broadcasted_iota(jnp.int32, shape, 1)
    column_of = lambda row: jnp.sum(jnp.where(here == there, jnp.broadcast_to(row, shape), 0), axis=1, keepdims=True)
    table_column = column_of(table_row)
    same = (table_column == table_row) & (here < there)
    within = jnp.sum(jnp.where(same, 1, 0), axis=0, keepdims=True)
    place_row = within
    spot = jnp.zeros((1, 1), jnp.int32)
    held = jnp.zeros((1, 1), jnp.int32)
    for table in range(NTAB):
        size = jnp.sum(jnp.where(table_row == table, 1, 0), axis=1, keepdims=True)
        some = size > 0
        edge = (spot & 7) == 0
        skip = some & (held >= 2) & ~edge
        spot = jnp.where(skip, (spot + 7) >> 3 << 3, spot)
        held = jnp.where(skip | edge, 0, held)
        after = spot + size
        place_row = place_row + jnp.where(table_row == table, spot, 0)
        held = jnp.where(some, jnp.where(after >> 3 == spot >> 3, held + 1, 1), held)
        spot = after
    groups = (spot + 7) >> 3
    place_column = column_of(place_row)
    group = lax.broadcasted_iota(jnp.int32, (count, width), 1)
    inside = place_column >> 3 == group
    first = jnp.sum(jnp.where(place_column == group * 8, table_column, 0), axis=0, keepdims=True)
    last = jnp.max(jnp.where(inside, table_column, 0), axis=0, keepdims=True)
    length = jnp.sum(jnp.where(inside & (table_column == first), 1, 0), axis=0, keepdims=True)
    rows = [first, last, length, jnp.broadcast_to(groups, (1, width))]
    if width > count:
        place_row = jnp.concatenate([place_row, jnp.zeros((1, width - count), jnp.int32)], axis=1)
    rows += [place_row, jnp.zeros((3, width), jnp.int32)]
    return jnp.concatenate(rows, axis=0).astype(jnp.float32)


def packed_rows(ntab):
    ends = [ntab * NF, 2 * ntab * NF, 2 * ntab * NF + DEGREES, 2 * ntab * NF + DEGREES + 8]
    return [slice(start, end) for start, end in zip([0] + ends, ends)]


def prepare_kernel(bins_hbm, table_hbm, ids_hbm, tables_hbm, out_hbm, *rest):
    bins_ref, table_ref, ids_ref, tables_ref, cos_ref, sin_ref, coef_ref, plan_ref = rest[:8]
    left_ref, right_ref, sems, table_sems = rest[8:]
    ntab = tables_ref.shape[0]
    nodes = cos_ref.shape[1]
    near = ids_ref.shape[0]
    first = pl.multiple_of(own_place() * (nodes // LANES) // near * near, 8)
    ins = start_all(
        [
            pltpu.make_async_copy(ids_hbm.at[pl.ds(first, near), :], ids_ref, sems.at[0]),
            pltpu.make_async_copy(bins_hbm, bins_ref, sems.at[1]),
            pltpu.make_async_copy(table_hbm, table_ref, sems.at[2]),
        ]
    )
    piece = tables_ref.shape[1] // TABLE_PIECES
    table_copies = []
    for at in range(TABLE_PIECES):
        part = (slice(None), pl.ds(at * piece, piece))
        table_copies.append(pltpu.make_async_copy(tables_hbm.at[part], tables_ref.at[part], table_sems.at[at]))
    start_all(table_copies)
    for copy in ins:
        copy.wait()
    cos_at, sin_at, coef_at, plan_at = packed_rows(ntab)
    coef_ref[...] = chebyshev_coefs(bins_ref)
    plan_ref[...] = station_plan(table_ref[...], plan_ref.shape[1])
    outs = start_all(
        [
            pltpu.make_async_copy(coef_ref, out_hbm.at[coef_at, pl.ds(0, LANES)], sems.at[0]),
            pltpu.make_async_copy(plan_ref, out_hbm.at[plan_at, pl.ds(0, plan_ref.shape[1])], sems.at[1]),
        ]
    )
    turns = pick_columns(ids_ref, tables_ref, table_copies, nodes, left_ref, right_ref) * (1.0 / 256.0)
    bins = bins_column(bins_ref)
    for table in range(ntab):
        cosine, sine = cos_sin(bins * turns[table : table + 1])
        at = pl.ds(table * NF, NF)
        cos_ref[at, :] = cosine
        sin_ref[at, :] = sine
        outs += start_all(
            [
                pltpu.make_async_copy(
                    cos_ref.at[at, :], out_hbm.at[pl.ds(cos_at.start + table * NF, NF), pl.ds(0, nodes)],
                    sems.at[3 + 2 * table],
                ),
                pltpu.make_async_copy(
                    sin_ref.at[at, :], out_hbm.at[pl.ds(sin_at.start + table * NF, NF), pl.ds(0, nodes)],
                    sems.at[4 + 2 * table],
                ),
            ]
        )
    for copy in outs:
        copy.wait()


def image_kernel(merged, stations_dev, packed_hbm, block_ref, *rest):
    corr_ref, rest = (None, rest) if merged else (rest[0], rest[1:])
    keep_ref, send_ref, plan_ref, place_of_ref, coef_ref, cos_ref, sin_ref, sems = rest[:8]
    place_ref, weight_ref, left_ref, sums_ref, basis_a, basis_b = rest[8:]
    places, nodes = place_ref.shape
    windows, groups, cores = (lax.axis_size(a) for a in ("win", "sta", "freq"))
    stations = stations_dev * groups
    cos_at, sin_at, coef_at, plan_at = packed_rows(cos_ref.shape[0] // NF)
    width = plan_ref.shape[1]
    copies = start_all(
        [
            pltpu.make_async_copy(packed_hbm.at[plan_at, pl.ds(0, width)], place_of_ref, sems.at[0]),
            pltpu.make_async_copy(packed_hbm.at[plan_at, pl.ds(0, width)], plan_ref, sems.at[1]),
            pltpu.make_async_copy(packed_hbm.at[coef_at, pl.ds(0, LANES)], coef_ref, sems.at[2]),
        ]
        + [
            pltpu.make_async_copy(
                packed_hbm.at[pl.ds(at.start + first, 4 * NF), pl.ds(0, nodes)],
                ref.at[pl.ds(first, 4 * NF), :],
                sems.at[3 + 2 * (first // (4 * NF)) + which],
            )
            for first in range(0, NTAB * NF, 4 * NF)
            for which, (at, ref) in enumerate(((cos_at, cos_ref), (sin_at, sin_ref)))
        ]
    )
    height = block_ref.shape[1]
    rows_of = lambda win, core: [(win * groups + group) * cores + core for group in range(groups)]

    even, odd = [], []
    for win in range(windows):
        value = []
        for group in range(groups):
            tile = None
            for core in range(cores):
                part = block_ref[(win * groups + group) * cores + core, height - 8 :, :].astype(jnp.float32)
                tile = part if tile is None else tile + part
            tile = tile[:, : LANES // 2] + tile[:, LANES // 2 :]
            value += [tile[:, 2 * NF * piece : 2 * NF * (piece + 1)] for piece in range(stations_dev // 8)]
        value = jnp.concatenate(value, axis=0)
        even.append(value)
        odd.append(jnp.concatenate([-value[:, NF:], value[:, :NF]], axis=1))
    spectra = jnp.concatenate(even + odd, axis=1)
    if merged:
        parts = []
        for win in range(windows):
            for core in range(cores):
                for first in range(0, height - 8, stations_dev):
                    rows = [block_ref[at, first : first + stations_dev, :] for at in rows_of(win, core)]
                    parts.append(jnp.concatenate(rows, axis=0))
        corr = jnp.concatenate(parts, axis=1)
    else:
        corr = corr_ref[...]

    copies[0].wait()
    place_row = place_of_ref[4:5, :stations].astype(jnp.int32)
    sorter = lax.broadcasted_iota(jnp.int32, (places, stations), 0) == place_row
    sorter = jnp.where(sorter, 1.0, 0.0).astype(jnp.bfloat16)
    found = None
    for piece in split_bf16(spectra, 3):
        part = jnp.dot(sorter, piece, preferred_element_type=jnp.float32)
        found = part if found is None else found + part
    weight_ref[...] = found
    place_ref[...] = jnp.dot(sorter, corr, preferred_element_type=jnp.float32) * (1.0 / REACH)
    sums_ref[...] = jnp.zeros_like(sums_ref)
    chunk = min(256, nodes)
    depth = DEGREES * 8
    lanes = windows * 2 * NF
    for copy in copies[1:3]:
        copy.wait()

    spot = (lax.broadcasted_iota(jnp.int32, (lanes, LANES), 1) & 7).astype(jnp.float32)

    def make_left(pair):
        top = weight_ref[pl.ds(pl.multiple_of(pair * 16, 16), 8), :]
        bottom = weight_ref[pl.ds(pl.multiple_of(pair * 16 + 8, 8), 8), :]
        sides = [
            jnp.concatenate([top[:, :lanes], bottom[:, :lanes]], axis=1),
            jnp.concatenate([top[:, lanes:], bottom[:, lanes:]], axis=1),
        ]
        per = LANES // 8
        for half in range(DEGREES // per):
            tall = jnp.concatenate(
                [sides[k % 2] * coef_ref[k : k + 1, :] for k in range(half * per, (half + 1) * per)], axis=0
            )
            turned = tall.T
            first = half * LANES
            fine = min(FINE * 8 - first, LANES)
            for which in range(2):
                group = 2 * pair + which
                mask = spot < plan_ref[2, group]
                value = turned[which * lanes : (which + 1) * lanes]
                value = jnp.concatenate([jnp.where(mask, value, 0.0), jnp.where(mask, 0.0, value)], axis=0)
                high, low = split_bf16(value, 2)
                if fine == LANES:
                    parts = [(first, high), (depth + first, high), (2 * FINE * 8 + first + LANES, low)]
                else:
                    mixed = [high[:, :fine].astype(jnp.float32), low[:, :fine].astype(jnp.float32)]
                    parts = [(first, high), (depth + first, jnp.concatenate(mixed, axis=1).astype(jnp.bfloat16))]
                for at, part in parts:
                    left_ref[group, :, at : at + LANES] = part

    used = plan_ref[3, 0].astype(jnp.int32)
    sure = stations // 16
    if sure <= 8:
        for pair in range(sure):
            make_left(pair)
    else:
        lax.fori_loop(0, sure, lambda pair, carry: (make_left(pair), carry)[1], 0)
    lax.fori_loop(sure, (used + 1) // 2, lambda pair, carry: (make_left(pair), carry)[1], 0)
    def basis_steps(group, basis_ref):
        arg = place_ref[pl.ds(pl.multiple_of(group * 8, 8), 8), :]
        twice = arg + arg
        before, now = jnp.ones_like(arg), arg
        for degree in range(0, DEGREES, 2):
            pair = jnp.concatenate([before, now], axis=0)
            terms = split_bf16(pair, 2 if degree < FINE else 1)
            for term, value in enumerate(terms):
                basis_ref[term * depth + degree * 8 : term * depth + degree * 8 + 16, :] = value
            before = twice * now - before
            now = twice * before - now
            if degree % 8 == 6:
                yield

    def run(steps):
        for _ in steps:
            pass

    def add_group(group, basis_ref, steps):
        left = left_ref[group]
        tables = [plan_ref[slot, group].astype(jnp.int32) for slot in range(2)]
        phasor_rows = [pl.ds(pl.multiple_of(table * NF, NF), NF) for table in tables]
        fine = FINE * 8
        for first in range(0, nodes, chunk):
            at = slice(first, first + chunk)
            right = [
                basis_ref[: depth + fine, at],
                basis_ref[LANES:fine, at],
                basis_ref[:LANES, at],
            ]
            got = jnp.dot(left, jnp.concatenate(right, axis=0), preferred_element_type=jnp.float32)
            run(steps)
            for win in range(windows):
                row = win * 2 * NF
                real_sum, imag_sum = sums_ref[row : row + NF, at], sums_ref[row + NF : row + 2 * NF, at]
                for slot, rows in enumerate(phasor_rows):
                    cosine, sine = cos_ref[rows, at], sin_ref[rows, at]
                    real = got[slot * lanes + row : slot * lanes + row + NF]
                    imag = got[slot * lanes + row + NF : slot * lanes + row + 2 * NF]
                    real_sum += real * cosine - imag * sine
                    imag_sum += real * sine + imag * cosine
                sums_ref[row : row + NF, at], sums_ref[row + NF : row + 2 * NF, at] = real_sum, imag_sum

    run(basis_steps(0, basis_a))
    for copy in copies[3:]:
        copy.wait()

    def body(pair, carry):
        group = pair * 2
        add_group(group, basis_a, basis_steps(group + 1, basis_b))
        add_group(group + 1, basis_b, basis_steps(jnp.minimum(group + 2, places // 8 - 1), basis_a))
        return carry

    lax.fori_loop(0, used // 2, body, 0)

    @pl.when(used % 2 == 1)
    def _():
        add_group(used - 1, basis_a, iter(()))

    powers = []
    for win in range(windows):
        row = win * 2 * NF
        real, imag = sums_ref[row : row + NF, :], sums_ref[row + NF : row + 2 * NF, :]
        powers.append(real * real + imag * imag)
    mine = lax.axis_index("win") == 0
    keep_ref[...] = jnp.where(mine, powers[0], powers[1])
    send_ref[...] = jnp.where(mine, powers[1], powers[0])


def finish_kernel(stations, keep_ref, got_ref, spectrum_ref, beam_ref):
    nodes = keep_ref.shape[1]
    win = lax.axis_index("win")
    for place, ref in ((win, keep_ref), (1 - win, got_ref)):
        power = ref[...]
        total = jnp.sum(power, axis=0, keepdims=True)
        at = pl.ds(pl.multiple_of(place * nodes, LANES), nodes)
        spectrum_ref[:, at] = power * (NF / total)
        beam_ref[:, at] = total * (1.0 / (NF * stations))


def on_device(traces, tables, corrections, station_table, node_ids, freq_bins):
    windows, groups, cores = (lax.axis_size(a) for a in ("win", "sta", "freq"))
    stations_dev, grid = corrections.shape
    stations = stations_dev * groups
    devices = windows * groups * cores
    nodes = grid // devices
    ntab = tables.shape[0]
    params = lambda free: pltpu.CompilerParams(vmem_limit_bytes=VMEM_LIMIT - free)
    vmem = pl.BlockSpec(memory_space=pltpu.VMEM)
    hbm = pl.BlockSpec(memory_space=pltpu.HBM)
    bins = freq_bins.reshape(1, NF)
    bins_scratch = pltpu.VMEM((1, NF), jnp.int32)

    holders = windows * cores
    merged = nodes % (holders * LANES) == 0
    pieces = nodes // (holders * LANES) if merged else 0
    height = pieces * stations_dev + 8
    blocks = pl.pallas_call(
        functools.partial(send_kernel, nodes),
        out_shape=jax.ShapeDtypeStruct((devices, height, LANES), jnp.bfloat16),
        in_specs=[hbm] * 3,
        out_specs=vmem,
        scratch_shapes=[
            bins_scratch,
            pltpu.VMEM(traces.shape, traces.dtype),
            pltpu.SemaphoreType.DMA((3,)),
        ],
        compiler_params=params(0),
        name="send",
    )(bins, traces, corrections)
    received = [lax.all_to_all(blocks, ("win", "sta", "freq"), split_axis=0, concat_axis=0, tiled=True)]
    if not merged:
        parts = corrections.reshape(stations_dev, groups, holders, nodes)
        place = lax.axis_index("freq") * windows + lax.axis_index("win")
        mine = lax.dynamic_index_in_dim(parts, place, axis=2, keepdims=False)
        corr = lax.all_to_all(mine.transpose(1, 0, 2), "sta", split_axis=0, concat_axis=0, tiled=True)
        received.append(corr.reshape(stations, nodes))

    wide = 512
    plan_width = max(LANES, stations)
    phasors = pltpu.VMEM((ntab * NF, nodes), jnp.float32)
    coefs = pltpu.VMEM((DEGREES, LANES), jnp.float32)
    plan = pltpu.VMEM((8, plan_width), jnp.float32)
    packed_shape = (packed_rows(ntab)[-1].stop, max(nodes, plan_width))
    packed = pl.pallas_call(
        prepare_kernel,
        out_shape=jax.ShapeDtypeStruct(packed_shape, jnp.float32),
        in_specs=[hbm] * 4,
        out_specs=hbm,
        scratch_shapes=[
            bins_scratch,
            pltpu.VMEM((1, stations), jnp.int32),
            pltpu.VMEM((max(nodes // LANES, 8), LANES), jnp.int32),
            pltpu.VMEM(tables.shape, tables.dtype),
            phasors,
            phasors,
            coefs,
            plan,
            pltpu.VMEM((grid // wide * ntab, 3 * wide), jnp.bfloat16),
            pltpu.VMEM((3 * wide, nodes), jnp.bfloat16),
            pltpu.SemaphoreType.DMA((3 + 2 * ntab,)),
            pltpu.SemaphoreType.DMA((TABLE_PIECES,)),
        ],
        compiler_params=params(512 * 1024),
        name="prepare",
    )(bins, station_table.reshape(1, stations), node_ids.reshape(grid // LANES, LANES), tables)

    places = (stations // 8 + ntab // 2 + 2) // 2 * 16
    half = jax.ShapeDtypeStruct((NF, nodes), jnp.float32)
    rows = 2 * windows * 2 * NF
    basis = pltpu.VMEM(((DEGREES + FINE) * 8, nodes), jnp.bfloat16)
    keep, send = pl.pallas_call(
        functools.partial(image_kernel, merged, stations_dev),
        out_shape=[half, half],
        in_specs=[hbm] + [vmem] * len(received),
        out_specs=[vmem, vmem],
        scratch_shapes=[
            pltpu.SMEM((8, plan_width), jnp.float32),
            plan,
            coefs,
            phasors,
            phasors,
            pltpu.SemaphoreType.DMA((3 + ntab // 2,)),
            pltpu.VMEM((places, nodes), jnp.float32),
            pltpu.VMEM((places, rows), jnp.float32),
            pltpu.VMEM((places // 8, rows, (DEGREES + 2 * FINE) * 8), jnp.bfloat16),
            pltpu.VMEM((rows // 2, nodes), jnp.float32),
            basis,
            basis,
        ],
        compiler_params=params(23 * 512 * 1024),
        name="image",
    )(packed, *received)
    got = lax.ppermute(send, "win", [(0, 1), (1, 0)])
    spectrum, beam_power = pl.pallas_call(
        functools.partial(finish_kernel, stations),
        out_shape=[
            jax.ShapeDtypeStruct((NF, windows * nodes), jnp.float32),
            jax.ShapeDtypeStruct((1, windows * nodes), jnp.float32),
        ],
        in_specs=[vmem, vmem],
        out_specs=[vmem, vmem],
        compiler_params=params(32 * 1024 * 1024),
        name="finish",
    )(keep, got)
    return spectrum, beam_power.reshape(windows * nodes)


def solution(mesh):
    return jax.shard_map(
        on_device,
        mesh=mesh,
        in_specs=(P(("win", "sta"), "freq"), P(), P("sta", None), P(), P(), P()),
        out_specs=(P("win", ("sta", "freq")), P(("win", "sta", "freq"))),
        check_vma=False,
    )
```
